128 devices in a mesh: ctx: 16 (over x_lo, z, core), wsh: 8 (over y, x_hi).
Axes of the slice: x: 4 (x_hi: 2, x_lo: 2; x = x_hi * 2 + x_lo), y: 4, z: 4, core: 2. Of those that a mesh axis runs over, the one named last changes fastest.
Arguments:
- inputs: bfloat16 [8, 2048, 2048], P('wsh', 'ctx'), may hold values from -6 to 6
- output_cotangent: bfloat16 [8, 2048, 2048], P('wsh', 'ctx'), may hold values from -6 to 6
- block_index_per_position: int32 [8, 2048], P('wsh'), may hold values from 0 to 15, never falling along the last dimension, each value on 1 to 256 neighbouring positions
- adapter_index_per_run: int32 [8, 16], P('wsh', 'ctx'), may hold values from 0 to 7
- norm_gain: bfloat16 [2048], P('wsh'), may hold values from 0.5 to 1.5
- norm_bias: bfloat16 [2048], P('wsh'), may hold values from -4 to 4
- query_weight: bfloat16 [2048, 2048], P('wsh'), may hold values from -0.125 to 0.125
- key_weight: bfloat16 [2048, 2048], P('wsh'), may hold values from -0.125 to 0.125
- value_weight: bfloat16 [2048, 2048], P('wsh'), may hold values from -0.125 to 0.125
- dense_weight: bfloat16 [2048, 2048], P('wsh'), may hold values from -0.5 to 0.5
- query_bias: bfloat16 [2048], P('wsh'), may hold values from -4 to 4
- key_bias: bfloat16 [2048], P('wsh'), may hold values from -4 to 4
- value_bias: bfloat16 [2048], P('wsh'), may hold values from -4 to 4
- dense_bias: bfloat16 [2048], P('wsh'), may hold values from -4 to 4
- feedforward_in_weight: bfloat16 [2048, 8192], P('wsh'), may hold values from -0.125 to 0.125
- feedforward_in_bias: bfloat16 [8192], P('wsh'), may hold values from -4 to 4
- feedforward_out_weight: bfloat16 [8192, 2048], P('wsh'), may hold values from -0.0625 to 0.0625
- feedforward_out_bias: bfloat16 [2048], P('wsh'), may hold values from -4 to 4
- adapter_attention_down: bfloat16 [8, 3, 16, 2048], P('wsh'), may hold values from -0.125 to 0.125
- adapter_attention_up: bfloat16 [8, 3, 16, 2048], P('wsh'), may hold values from -1.5 to 1.5
- adapter_dense_down: bfloat16 [8, 16, 2048], P('wsh'), may hold values from -0.5 to 0.5
- adapter_dense_up: bfloat16 [8, 16, 2048], P('wsh'), may hold values from -1.5 to 1.5
- adapter_feedforward_in_down: bfloat16 [8, 16, 2048], P('wsh'), may hold values from -0.125 to 0.125
- adapter_feedforward_in_up: bfloat16 [8, 16, 8192], P('wsh'), may hold values from -1.5 to 1.5
- adapter_feedforward_out_down: bfloat16 [8, 16, 8192], P('wsh'), may hold values from -0.0625 to 0.0625
- adapter_feedforward_out_up: bfloat16 [8, 16, 2048], P('wsh'), may hold values from -1.5 to 1.5
Outputs:
- outputs: bfloat16 [8, 2048, 2048], P('wsh', 'ctx')
- grad_inputs: bfloat16 [8, 2048, 2048], P('wsh', 'ctx')
- grad_down_qkv: float32 [8, 3, 16, 2048], P('wsh')
- grad_up_qkv: float32 [8, 3, 16, 2048], P('wsh')
- dense_down_gradient: float32 [8, 16, 2048], P('wsh')
- dense_up_gradient: float32 [8, 16, 2048], P('wsh')
- feedforward_in_down_gradient: float32 [8, 16, 2048], P('wsh')
- feedforward_in_up_gradient: float32 [8, 16, 8192], P('wsh')
- feedforward_out_down_gradient: float32 [8, 16, 8192], P('wsh')
- feedforward_out_up_gradient: float32 [8, 16, 2048], P('wsh')
The draws below stay inside these ranges and needn't reach their ends.
Inputs may be any that keep to these rules, and one draw needn't show every extreme that they name: `block_index_per_position`: block numbers never fall along a sequence; each block holds 1 to 256 positions and one holds exactly 256.
All inputs are finite; a program needn't handle non-finite values.
Results may differ from the reference program's by a relative error of at most 0.02.
Values may be sent and summed in bfloat16 or wider, within the bound.
No kernel may reach another device: no remote copies, remote signals or barrier semaphores. Data moves between devices by JAX's collectives and lax.ppermute only.
A program may use at most 320 MiB of HBM per device.

```python
import math
import jax
import jax.numpy as jnp
import numpy as np
from jax import lax

MODEL_WIDTH = 2048
FEEDFWD_UNITS = 8192
HEADS = 32
HEAD_DIM = 64
ROT = 32
ADAPTER_RANK = 16
ADAPTER_COUNT = 8
BLOCK = 256
TOK_DEV = 128
SEQS = 8
RUNS = 16
LENGTH = 2048


def plant(array, rng, least, high):
    spot = [jax.random.randint(jax.random.fold_in(rng, axis), (), 0, length) for axis, length in enumerate(array.shape)]
    longest = array.shape.index(max(array.shape))
    next_to = spot[:longest] + [(spot[longest] + 1) % array.shape[longest]] + spot[longest + 1:]
    return array.at[tuple(spot)].set(least).at[tuple(next_to)].set(high)


def steps_of(stream_key, shape, shards, smallest, top_value):
    level, own = 1.0, jax.random.fold_in(stream_key, 6)
    for position, parts in shards:
        heights = jnp.exp(jax.random.uniform(jax.random.fold_in(own, position), (parts,), jnp.float32, smallest / len(shards), top_value / len(shards)))
        level = level * jnp.repeat(heights, shape[position] // parts).reshape([-1 if axis == position else 1 for axis in range(len(shape))])
    return level


def profile(amount, total, reach, slope):
    loads = [(1 << 20) // math.isqrt(standing ** slope) + 1 for standing in range(2, amount + 1)]
    spare, holding = total - reach - (amount - 1), [1] * (amount - 1)
    while spare > 0:
        candidates = [i for i in range(amount - 1) if holding[i] < reach]
        whole, left = sum([loads[i] for i in candidates]), spare
        for i in candidates:
            addition = min(reach - holding[i], max(1, left * loads[i] // whole), spare)
            holding[i] = holding[i] + addition
            spare = spare - addition
    return np.array([reach] + holding)


def uneven(key, amount, total, bound, lean):
    if amount == 2:
        one = jax.random.randint(key, (), max(1, total - bound), min(bound, total - 1) + 1)
        return jnp.stack([one, total - one])
    tallies = jnp.asarray(profile(amount, total, bound, lean), jnp.int32)
    twos = (amount - 1) // 2
    donor, receiver = tallies[1:1 + 2 * twos:2], tallies[2:2 + 2 * twos:2]
    slack = jnp.minimum(donor - 1, bound - receiver)
    passed = jax.random.randint(jax.random.fold_in(key, 1), (twos,), 0, 1 << 20) % (slack + 1)
    tallies = tallies.at[1:1 + 2 * twos:2].set(donor - passed).at[2:2 + 2 * twos:2].set(receiver + passed)
    return tallies[jax.random.permutation(jax.random.fold_in(key, 2), amount)]


def centred(key, dims, width, limit, split=(), held_as=jnp.bfloat16):
    entries = jax.random.normal(key, dims, jnp.float32) * width
    if len(split) > 0:
        entries = steps_of(key, dims, split, -0.22, 0.18) * entries
    return jnp.clip(entries, min=-limit, max=limit).astype(held_as)


def setup_inputs(seed: int = 0) -> dict:
    key_of = jax.random.split(jax.random.key(seed), 27)
    inputs = centred(key_of[0], (SEQS, LENGTH, MODEL_WIDTH), 1.0, 6.0, ((0, 8), (1, 16)))
    output_cotangent = centred(key_of[1], (SEQS, LENGTH, MODEL_WIDTH), 1.0, 6.0, ((0, 8), (1, 16)))
    block_index_per_position = jax.vmap(lambda own: jnp.searchsorted(jnp.cumsum(uneven(own, LENGTH // (BLOCK // 2), LENGTH, BLOCK, 0)), jnp.arange(LENGTH), side="right"))(jax.random.split(key_of[2], SEQS)).reshape((SEQS, LENGTH)).astype(jnp.int32)
    adapter_index_per_run = plant(jax.random.randint(key_of[3], (SEQS, RUNS), 0, ADAPTER_COUNT), jax.random.fold_in(key_of[3], 1), 0, ADAPTER_COUNT - 1).astype(jnp.int32)
    norm_gain = jnp.clip(1.0 + 0.1 * jax.random.normal(key_of[4], (MODEL_WIDTH,), jnp.float32), 0.5, 1.5).astype(jnp.bfloat16)
    norm_bias = centred(key_of[5], (MODEL_WIDTH,), 0.3, 4.0, ((0, 8),))
    query_weight = centred(key_of[6], (MODEL_WIDTH, MODEL_WIDTH), MODEL_WIDTH ** -0.5, 0.125, ((0, 8),))
    key_weight = centred(key_of[7], (MODEL_WIDTH, MODEL_WIDTH), MODEL_WIDTH ** -0.5, 0.125, ((0, 8),))
    value_weight = centred(key_of[8], (MODEL_WIDTH, MODEL_WIDTH), MODEL_WIDTH ** -0.5, 0.125, ((0, 8),))
    dense_weight = centred(key_of[9], (MODEL_WIDTH, MODEL_WIDTH), (MODEL_WIDTH // 16) ** -0.5, 0.5, ((0, 8),))
    query_bias = centred(key_of[10], (MODEL_WIDTH,), 0.3, 4.0, ((0, 8),))
    key_bias = centred(key_of[11], (MODEL_WIDTH,), 0.3, 4.0, ((0, 8),))
    value_bias = centred(key_of[12], (MODEL_WIDTH,), 0.3, 4.0, ((0, 8),))
    dense_bias = centred(key_of[13], (MODEL_WIDTH,), 0.3, 4.0, ((0, 8),))
    feedforward_in_weight = centred(key_of[14], (MODEL_WIDTH, FEEDFWD_UNITS), MODEL_WIDTH ** -0.5, 0.125, ((0, 8),))
    feedforward_in_bias = centred(key_of[15], (FEEDFWD_UNITS,), 0.3, 4.0, ((0, 8),))
    feedforward_out_weight = centred(key_of[16], (FEEDFWD_UNITS, MODEL_WIDTH), FEEDFWD_UNITS ** -0.5, 0.0625, ((0, 8),))
    feedforward_out_bias = centred(key_of[17], (MODEL_WIDTH,), 0.3, 4.0, ((0, 8),))
    adapter_attention_down = centred(key_of[18], (ADAPTER_COUNT, 3, ADAPTER_RANK, MODEL_WIDTH), MODEL_WIDTH ** -0.5, 0.125, ((0, 8),))
    adapter_attention_up = centred(key_of[19], (ADAPTER_COUNT, 3, ADAPTER_RANK, MODEL_WIDTH), ADAPTER_RANK ** -0.5, 1.5, ((0, 8),))
    adapter_dense_down = centred(key_of[20], (ADAPTER_COUNT, ADAPTER_RANK, MODEL_WIDTH), (MODEL_WIDTH // 16) ** -0.5, 0.5, ((0, 8),))
    adapter_dense_up = centred(key_of[21], (ADAPTER_COUNT, ADAPTER_RANK, MODEL_WIDTH), ADAPTER_RANK ** -0.5, 1.5, ((0, 8),))
    adapter_feedforward_in_down = centred(key_of[22], (ADAPTER_COUNT, ADAPTER_RANK, MODEL_WIDTH), MODEL_WIDTH ** -0.5, 0.125, ((0, 8),))
    adapter_feedforward_in_up = centred(key_of[23], (ADAPTER_COUNT, ADAPTER_RANK, FEEDFWD_UNITS), ADAPTER_RANK ** -0.5, 1.5, ((0, 8),))
    adapter_feedforward_out_down = centred(key_of[24], (ADAPTER_COUNT, ADAPTER_RANK, FEEDFWD_UNITS), FEEDFWD_UNITS ** -0.5, 0.0625, ((0, 8),))
    adapter_feedforward_out_up = centred(key_of[25], (ADAPTER_COUNT, ADAPTER_RANK, MODEL_WIDTH), ADAPTER_RANK ** -0.5, 1.5, ((0, 8),))
    return {"inputs": inputs, "output_cotangent": output_cotangent, "block_index_per_position": block_index_per_position, "adapter_index_per_run": adapter_index_per_run, "norm_gain": norm_gain, "norm_bias": norm_bias, "query_weight": query_weight, "key_weight": key_weight, "value_weight": value_weight, "dense_weight": dense_weight, "query_bias": query_bias, "key_bias": key_bias, "value_bias": value_bias, "dense_bias": dense_bias, "feedforward_in_weight": feedforward_in_weight, "feedforward_in_bias": feedforward_in_bias, "feedforward_out_weight": feedforward_out_weight, "feedforward_out_bias": feedforward_out_bias, "adapter_attention_down": adapter_attention_down, "adapter_attention_up": adapter_attention_up, "adapter_dense_down": adapter_dense_down, "adapter_dense_up": adapter_dense_up, "adapter_feedforward_in_down": adapter_feedforward_in_down, "adapter_feedforward_in_up": adapter_feedforward_in_up, "adapter_feedforward_out_down": adapter_feedforward_out_down, "adapter_feedforward_out_up": adapter_feedforward_out_up}


EPSILON = 1e-05
GELU_SCALE = 0.7978845608028654
NEGATIVE = -1e+30
HIGHEST = lax.Precision.HIGHEST

@jax.custom_vjp
def low(v):
    return lax.optimization_barrier(v.astype(jnp.bfloat16)).astype(jnp.float32)

@jax.custom_vjp
def lowrank_backward(v):
    return v

def low_keep(v):
    return (low(v), None)

def low_pass(kept, grad):
    return (grad,)

def back_keep(v):
    return (v, None)

def back_low(kept, grad):
    return (low(grad),)
low.defvjp(low_keep, low_pass)
lowrank_backward.defvjp(back_keep, back_low)

def gelu_tanh(values):
    return 0.5 * values * (1.0 + jnp.tanh(GELU_SCALE * (values + 0.044715 * values * values * values)))

def layer_norm(values, gain, shift):
    center = values - lax.optimization_barrier(jnp.mean(values, axis=-1, keepdims=True))
    spread = lax.optimization_barrier(jnp.mean(center * center, axis=-1, keepdims=True))
    return center * lax.rsqrt(spread + EPSILON) * gain + shift

def rotate(field, positions, direction):
    token_count = field.shape[0]
    shaped = field.reshape(token_count, HEADS, HEAD_DIM)
    middle = ROT // 2
    rates = 10000.0 ** (-2.0 * jnp.arange(middle, dtype=jnp.float32) / ROT)
    angles = positions.astype(jnp.float32)[:, None] * rates[None, :]
    cosine = jnp.cos(angles)[:, None, :]
    sine = direction * jnp.sin(angles)[:, None, :]
    leading = shaped[:, :, :middle]
    trailing = shaped[:, :, middle:ROT]
    turned = jnp.concatenate([leading * cosine - trailing * sine, trailing * cosine + leading * sine, shaped[:, :, ROT:]], axis=2)
    return turned.reshape(token_count, HEADS * HEAD_DIM)

def adapter_projection(inputs, weight_matrix, bias_vector, down_matrix_per_run, up_matrix_per_run):
    shaped = inputs.reshape(RUNS, TOK_DEV, inputs.shape[-1])
    inner = jnp.einsum('ntd,nrd->ntr', shaped, down_matrix_per_run, precision=HIGHEST)
    inner = low(lowrank_backward(inner))
    extra = jnp.einsum('ntr,nro->nto', inner, up_matrix_per_run, precision=HIGHEST).reshape(LENGTH, up_matrix_per_run.shape[-1])
    return jnp.dot(inputs, weight_matrix, precision=HIGHEST) + bias_vector + extra

def attention(queries, keys, values, block_row):
    key_heads = keys.reshape(LENGTH, HEADS, HEAD_DIM)
    value_heads = values.reshape(LENGTH, HEADS, HEAD_DIM)
    block_rows = 512 if LENGTH % 512 == 0 else LENGTH
    block_count = LENGTH // block_rows

    @jax.checkpoint
    def one_block(element):
        query_block, query_ids = element
        scores = jnp.einsum('thd,shd->hts', query_block, key_heads, precision=HIGHEST) * HEAD_DIM ** (-0.5)
        scores = lowrank_backward(scores)
        allowed = (block_row[None, :] <= query_ids[:, None])[None]
        scores = jnp.where(allowed, scores, NEGATIVE)
        largest = lax.optimization_barrier(jnp.max(scores, axis=2, keepdims=True))
        expos = jnp.where(allowed, jnp.exp(scores - largest), 0.0)
        probs = low(expos / lax.optimization_barrier(jnp.sum(expos, axis=2, keepdims=True)))
        return jnp.einsum('hts,shd->thd', probs, value_heads, precision=HIGHEST)
    query_blocks = queries.reshape(block_count, block_rows, HEADS, HEAD_DIM)
    id_blocks = block_row.reshape(block_count, block_rows)
    result = lax.map(one_block, (query_blocks, id_blocks))
    return result.reshape(LENGTH, HEADS * HEAD_DIM)

def forward(inputs, adapter_tables, frozen, block_row, run_index_per_token):
    gain, shift, query_weight, key_weight, value_weight, dense_weight, query_bias, key_bias, value_bias, dense_bias, feedforward_in_weight, feedforward_in_bias, feedforward_out_weight, feedforward_out_bias = frozen
    attention_down_matrix, attention_up_matrix, dense_down_matrix, dense_up_matrix, feedforward_in_down, feedforward_in_up, feedforward_out_down, feedforward_out_up = adapter_tables
    positions = jnp.arange(LENGTH, dtype=jnp.int32)
    normalized_input = low(layer_norm(inputs, gain, shift))
    down_matrix_per_run = attention_down_matrix[run_index_per_token]
    up_matrix_per_run = attention_up_matrix[run_index_per_token]
    query_preactivation = lowrank_backward(adapter_projection(normalized_input, query_weight, query_bias, down_matrix_per_run[:, 0], up_matrix_per_run[:, 0]))
    key_preactivation = lowrank_backward(adapter_projection(normalized_input, key_weight, key_bias, down_matrix_per_run[:, 1], up_matrix_per_run[:, 1]))
    value_preactivation = lowrank_backward(adapter_projection(normalized_input, value_weight, value_bias, down_matrix_per_run[:, 2], up_matrix_per_run[:, 2]))
    queries = low(rotate(query_preactivation, positions, 1.0))
    keys = low(rotate(key_preactivation, positions, 1.0))
    values = low(value_preactivation)
    attended_values = low(lowrank_backward(attention(queries, keys, values, block_row)))
    attention_output = adapter_projection(attended_values, dense_weight, dense_bias, dense_down_matrix[run_index_per_token], dense_up_matrix[run_index_per_token])
    feedforward_preactivation = lowrank_backward(adapter_projection(normalized_input, feedforward_in_weight, feedforward_in_bias, feedforward_in_down[run_index_per_token], feedforward_in_up[run_index_per_token]))
    activated_hidden = low(gelu_tanh(feedforward_preactivation))
    feedforward_output = adapter_projection(activated_hidden, feedforward_out_weight, feedforward_out_bias, feedforward_out_down[run_index_per_token], feedforward_out_up[run_index_per_token])
    return inputs + attention_output + feedforward_output

def widen_rows(values):
    return values.astype(jnp.float32)

def reference(inputs, output_cotangent, block_index_per_position, adapter_index_per_run, norm_gain, norm_bias, query_weight, key_weight, value_weight, dense_weight, query_bias, key_bias, value_bias, dense_bias, feedforward_in_weight, feedforward_in_bias, feedforward_out_weight, feedforward_out_bias, adapter_attention_down, adapter_attention_up, adapter_dense_down, adapter_dense_up, adapter_feedforward_in_down, adapter_feedforward_in_up, adapter_feedforward_out_down, adapter_feedforward_out_up):
    frozen = (widen_rows(norm_gain), widen_rows(norm_bias), widen_rows(query_weight), widen_rows(key_weight), widen_rows(value_weight), widen_rows(dense_weight), widen_rows(query_bias), widen_rows(key_bias), widen_rows(value_bias), widen_rows(dense_bias), widen_rows(feedforward_in_weight), widen_rows(feedforward_in_bias), widen_rows(feedforward_out_weight), widen_rows(feedforward_out_bias))
    adapter_tables = (widen_rows(adapter_attention_down), widen_rows(adapter_attention_up), widen_rows(adapter_dense_down), widen_rows(adapter_dense_up), widen_rows(adapter_feedforward_in_down), widen_rows(adapter_feedforward_in_up), widen_rows(adapter_feedforward_out_down), widen_rows(adapter_feedforward_out_up))

    def visit(sums, element):
        seq_inputs, seq_grad, block_row, run_index_per_token = element

        def apply(values, members):
            return forward(values, members, frozen, block_row, run_index_per_token)
        result, pullback = jax.vjp(apply, widen_rows(seq_inputs), adapter_tables)
        grad_in, grad_members = pullback(widen_rows(seq_grad))
        sums = jax.tree.map(jnp.add, sums, grad_members)
        return (sums, (result.astype(jnp.bfloat16), grad_in.astype(jnp.bfloat16)))
    zeros = jax.tree.map(jnp.zeros_like, adapter_tables)
    sums, stacked = lax.scan(visit, zeros, (inputs, output_cotangent, block_index_per_position, adapter_index_per_run))
    return (stacked[0], stacked[1], sums[0], sums[1], sums[2], sums[3], sums[4], sums[5], sums[6], sums[7])
```

```python
import functools

import jax
import jax.numpy as jnp
import numpy as np
from jax import lax
from jax.experimental import pallas as pl
from jax.experimental.pallas import tpu as pltpu
from jax.sharding import Mesh, PartitionSpec as P

ADAPTERS = 8
RANK = 16
EPSILON = 1e-05
GELU_SCALE = 0.7978845608028654
NEGATIVE = -1e30
SCALE = 64 ** -0.5
BF = jnp.bfloat16
F32 = jnp.float32
WSH = ("y", "xh")
TP = ("xl", "z")
CTX = ("xl", "z", "c")
VMEM_LIMIT = 58 * 1024 * 1024


def nn(a, b):
    return lax.dot_general(a, b, (((1,), (0,)), ((), ())), preferred_element_type=F32)


def nt(a, b):
    return lax.dot_general(a, b, (((1,), (1,)), ((), ())), preferred_element_type=F32)


def tn(a, b):
    return lax.dot_general(a, b, (((0,), (0,)), ((), ())), preferred_element_type=F32)


def adapter_mask(aid, columns):
    col = lax.broadcasted_iota(jnp.int32, (aid.shape[0], columns), 1)
    return (lax.shift_right_logical(col, 4) & 7) == aid.astype(jnp.int32)


def turn(values, cosine, sine):
    width = values.shape[1]
    lane = lax.broadcasted_iota(jnp.int32, values.shape, 1) & 63
    partner = jnp.where(
        lane < 16, pltpu.roll(values, width - 16, 1), pltpu.roll(values, 16, 1)
    )
    return values * cosine + partner * sine


def k1_body(x_ref, wqkv_ref, down_ref, up_ref, misc_ref, bias_ref, cos_ref, sin_ref, hb_ref, inner_ref, qkv_ref):
    x = x_ref[:, :2048].astype(F32)
    aid = x_ref[:, 2048:2049].astype(F32)
    mean = jnp.mean(x, axis=1, keepdims=True)
    center = x - mean
    spread = jnp.mean(center * center, axis=1, keepdims=True)
    h = center * lax.rsqrt(spread + EPSILON) * misc_ref[0:1, :] + misc_ref[1:2, :]
    hb = h.astype(BF)
    hb_ref[...] = hb
    inner = nt(hb, down_ref[...])
    inner = jnp.where(adapter_mask(aid, 512), inner, 0.0).astype(BF)
    inner_ref[...] = inner
    cosine = jnp.concatenate([cos_ref[...]] * 2, axis=1)
    sine = jnp.concatenate([sin_ref[...]] * 2, axis=1)
    for p in range(3):
        cols = slice(256 * p, 256 * p + 256)
        pre = nn(hb, wqkv_ref[:, cols]) + nn(inner[:, 128 * p : 128 * p + 128], up_ref[:, cols])
        pre = pre + bias_ref[:, cols]
        if p < 2:
            pre = turn(pre, cosine, sine)
        low = pre.astype(BF)
        qkv_ref[0, p] = low[:, :128]
        qkv_ref[1, p] = low[:, 128:]


def whole(shape):
    return pl.BlockSpec(shape, lambda t: (0,) * len(shape))


def k1(xg, wqkv, downs, ups, misc, bias, cosine, sine):
    rows = 256
    return pl.pallas_call(
        k1_body,
        grid=(1024 // rows,),
        in_specs=[
            pl.BlockSpec((rows, 2176), lambda t: (t, 0)),
            whole((2048, 768)),
            whole((512, 2048)),
            whole((128, 768)),
            whole((2, 2048)),
            whole((1, 768)),
            pl.BlockSpec((rows, 128), lambda t: (t, 0)),
            pl.BlockSpec((rows, 128), lambda t: (t, 0)),
        ],
        out_specs=[
            pl.BlockSpec((rows, 2048), lambda t: (t, 0)),
            pl.BlockSpec((rows, 512), lambda t: (t, 0)),
            pl.BlockSpec((2, 3, rows, 128), lambda t: (0, 0, t, 0)),
        ],
        out_shape=[
            jax.ShapeDtypeStruct((1024, 2048), BF),
            jax.ShapeDtypeStruct((1024, 512), BF),
            jax.ShapeDtypeStruct((2, 3, 1024, 128), BF),
        ],
        compiler_params=pltpu.CompilerParams(vmem_limit_bytes=VMEM_LIMIT),
        name="norm_qkv",
    )(xg, wqkv, downs, ups, misc, bias, cosine, sine)


def k1b_body(dy_ref, aid_ref, wd_ref, ud_ref, dd_ref, dob_ref, ginner_ref):
    dy = dy_ref[...]
    aid = aid_ref[:, 0:1].astype(F32)
    ginner = jnp.where(adapter_mask(aid, 128), nt(dy, ud_ref[...]), 0.0).astype(BF)
    ginner_ref[...] = ginner
    dob = (nt(dy, wd_ref[...]) + nn(ginner, dd_ref[...])).astype(BF)
    dob_ref[0] = dob[:, :128]
    dob_ref[1] = dob[:, 128:]


def k1b(dyg, aid, wd, ud, dd):
    rows = 256
    return pl.pallas_call(
        k1b_body,
        grid=(1024 // rows,),
        in_specs=[
            pl.BlockSpec((rows, 2048), lambda t: (t, 0)),
            pl.BlockSpec((rows, 128), lambda t: (t, 0)),
            whole((256, 2048)),
            whole((128, 2048)),
            whole((128, 256)),
        ],
        out_specs=[
            pl.BlockSpec((2, rows, 128), lambda t: (0, t, 0)),
            pl.BlockSpec((rows, 128), lambda t: (t, 0)),
        ],
        out_shape=[
            jax.ShapeDtypeStruct((2, 1024, 128), BF),
            jax.ShapeDtypeStruct((1024, 128), BF),
        ],
        compiler_params=pltpu.CompilerParams(vmem_limit_bytes=VMEM_LIMIT),
        name="attention_output_grad",
    )(dyg, aid, wd, ud, dd)


def k3_body(qkvd_ref, idrow_ref, idcol_ref, cos_ref, sin_ref, out_ref, kt_s, vt_s, dk_s, dv_s):
    kt_s[...] = qkvd_ref[1].T
    vt_s[...] = qkvd_ref[2].T
    dk_s[...] = jnp.zeros_like(dk_s)
    dv_s[...] = jnp.zeros_like(dv_s)
    tile = 256
    lane = lax.broadcasted_iota(jnp.int32, (tile, 128), 1)
    for t in range(8):
        rows = slice(tile * t, tile * t + tile)
        length = min(tile * (t + 2), 2048)
        free = tile * t
        q = qkvd_ref[0, rows]
        dob = qkvd_ref[3, rows]
        query_ids = idrow_ref[0:1, rows]
        allowed = idcol_ref[free:length, 0:1] <= query_ids
        o_parts, dq_parts = [], []
        for h in range(2):
            mine = (lane >= 64 * h) & (lane < 64 * h + 64)
            qh = jnp.where(mine, q, jnp.zeros_like(q))
            dh = jnp.where(mine, dob, jnp.zeros_like(dob))
            s_tail = jnp.where(allowed, nt(qkvd_ref[1, free:length], qh), NEGATIVE)
            largest = jnp.max(s_tail, axis=0, keepdims=True)
            if free:
                s_head = nt(qkvd_ref[1, :free], qh)
                largest = jnp.maximum(largest, jnp.max(s_head, axis=0, keepdims=True))
                s = jnp.concatenate([s_head, s_tail], axis=0)
            else:
                s = s_tail
            e = jnp.exp((s - largest) * SCALE)
            recip = 1.0 / jnp.sum(e, axis=0, keepdims=True)
            p = e * recip
            pb = p.astype(BF)
            ot = nn(vt_s[64 * h : 64 * h + 64, :length], pb)
            dp = nt(qkvd_ref[2, :length], dh)
            delta = jnp.sum(p * dp, axis=0, keepdims=True)
            ds = (p * (dp - delta)).astype(BF)
            dqt = nn(kt_s[64 * h : 64 * h + 64, :length], ds)
            dk_s[:length] += nn(ds, qh)
            dv_s[:length] += nn(pb, dh)
            o_parts.append(ot)
            dq_parts.append(dqt)
        o = jnp.concatenate(o_parts, axis=0).T
        dq = jnp.concatenate(dq_parts, axis=0).T * SCALE
        out_ref[0, rows] = o.astype(BF)
        out_ref[1, rows] = turn(dq, cos_ref[rows], -sin_ref[rows]).astype(BF)
    out_ref[2] = turn(dk_s[...] * SCALE, cos_ref[...], -sin_ref[...]).astype(BF)
    out_ref[3] = dv_s[...].astype(BF)


def k3(qkvd, idrow, idcol, cosine, sine):
    return pl.pallas_call(
        k3_body,
        out_shape=jax.ShapeDtypeStruct((4, 2048, 128), BF),
        scratch_shapes=[
            pltpu.VMEM((128, 2048), BF),
            pltpu.VMEM((128, 2048), BF),
            pltpu.VMEM((2048, 128), F32),
            pltpu.VMEM((2048, 128), F32),
        ],
        compiler_params=pltpu.CompilerParams(vmem_limit_bytes=VMEM_LIMIT),
        name="attention",
    )(qkvd, idrow, idcol, cosine, sine)


def k2_body(
    hb_ref, dy_ref, aid_ref, inner_ref, gdense_ref, att_ref,
    w1_ref, w2_ref, wd_ref, wqkv_ref, down_ref, up_ref, up1_ref, d2_ref, u2_ref, ud_ref, dd_ref, b1_ref, fold_ref,
    out_ref, dh_ref, small_ref, gup1_ref, gd2_ref, gqkv_ref, gdd_ref,
):
    step = pl.program_id(0)
    hb = hb_ref[...]
    dy = dy_ref[...]
    aid = aid_ref[:, 0:1].astype(F32)
    keep = adapter_mask(aid, 128)
    inner = inner_ref[...]

    def masked(v):
        return jnp.where(keep, v, 0.0).astype(BF)

    f = nn(hb, w1_ref[...]) + nn(inner[:, 384:512], up1_ref[...]) + b1_ref[...]
    square = f * f
    th = jnp.tanh(GELU_SCALE * f * (1.0 + 0.044715 * square))
    half = 0.5 * (1.0 + th)
    gb = (f * half).astype(BF)
    slope = half + 0.5 * f * (1.0 - th * th) * GELU_SCALE * (1.0 + 3 * 0.044715 * square)
    ob = att_ref[0]
    inner2 = masked(nt(gb, d2_ref[...]))
    innerd = masked(nt(ob, dd_ref[...]))
    out = nn(gb, w2_ref[...]) + nn(inner2, u2_ref[...]) + nn(ob, wd_ref[...]) + nn(innerd, ud_ref[...])
    out_ref[...] = out.astype(BF)
    ginner2 = masked(nt(dy, u2_ref[...]))
    dg = nt(dy, w2_ref[...]) + nn(ginner2, d2_ref[...])
    df = (dg * slope).astype(BF)
    ginner1 = masked(nt(df, up1_ref[...]))
    dh = nt(df, w1_ref[...])
    small = []
    gqkv = []
    for p in range(3):
        cols = slice(256 * p, 256 * p + 256)
        dpre = att_ref[p + 1]
        ginner = masked(nt(dpre, up_ref[:, cols]))
        small.append(ginner)
        dh = dh + nt(dpre, wqkv_ref[:, cols])
        gqkv.append(tn(inner[:, 128 * p : 128 * p + 128], dpre))
    small.append(ginner1)
    dh = dh + nn(jnp.concatenate(small, axis=1), down_ref[...])
    dh_ref[...] = dh.astype(BF)
    small = jnp.concatenate(small + [innerd, inner2], axis=1)
    small_ref[...] = nn(small, fold_ref[...]).astype(BF)
    gup1 = tn(inner[:, 384:512], df)
    gd2 = tn(ginner2, gb)
    gdd = tn(gdense_ref[...], ob)
    gqkv = jnp.concatenate(gqkv, axis=1)

    @pl.when(step == 0)
    def _():
        gup1_ref[...] = gup1
        gd2_ref[...] = gd2
        gdd_ref[...] = gdd
        gqkv_ref[...] = gqkv

    @pl.when(step > 0)
    def _():
        gup1_ref[...] += gup1
        gd2_ref[...] += gd2
        gdd_ref[...] += gdd
        gqkv_ref[...] += gqkv


def k2(hb, dyg, aid, inner, gdense, att, w1, w2, wd, wqkv, downs, ups, up1, d2, u2, ud, dd, b1, fold):
    rows = 256

    def once(shape):
        return pl.BlockSpec(shape, lambda t: (0,) * len(shape), pipeline_mode=pl.Buffered(1))

    return pl.pallas_call(
        k2_body,
        grid=(1024 // rows,),
        in_specs=[
            pl.BlockSpec((rows, 2048), lambda t: (t, 0)),
            pl.BlockSpec((rows, 2048), lambda t: (t, 0)),
            pl.BlockSpec((rows, 128), lambda t: (t, 0)),
            pl.BlockSpec((rows, 512), lambda t: (t, 0)),
            pl.BlockSpec((rows, 128), lambda t: (t, 0)),
            pl.BlockSpec((4, rows, 256), lambda t: (0, t, 0)),
            once((2048, 1024)),
            once((1024, 2048)),
            once((256, 2048)),
            once((2048, 768)),
            once((512, 2048)),
            once((128, 768)),
            once((128, 1024)),
            once((128, 1024)),
            once((128, 2048)),
            once((128, 2048)),
            once((128, 256)),
            once((1, 1024)),
            once((768, 128)),
        ],
        out_specs=[
            pl.BlockSpec((rows, 2048), lambda t: (t, 0)),
            pl.BlockSpec((rows, 2048), lambda t: (t, 0)),
            pl.BlockSpec((rows, 128), lambda t: (t, 0)),
            whole((128, 1024)),
            whole((128, 1024)),
            whole((128, 768)),
            whole((128, 256)),
        ],
        out_shape=[
            jax.ShapeDtypeStruct((1024, 2048), BF),
            jax.ShapeDtypeStruct((1024, 2048), BF),
            jax.ShapeDtypeStruct((1024, 128), BF),
            jax.ShapeDtypeStruct((128, 1024), F32),
            jax.ShapeDtypeStruct((128, 1024), F32),
            jax.ShapeDtypeStruct((128, 768), F32),
            jax.ShapeDtypeStruct((128, 256), F32),
        ],
        compiler_params=pltpu.CompilerParams(vmem_limit_bytes=VMEM_LIMIT),
        name="feed_forward_both_ways",
    )(hb, dyg, aid, inner, gdense, att, w1, w2, wd, wqkv, downs, ups, up1, d2, u2, ud, dd, b1, fold)


def k5_body(small_ref, aid_ref, hb_ref, dy_ref, spread_ref, gdown_ref, gup_ref):
    aid = aid_ref[:, 0:1].astype(F32)
    wide = jnp.where(adapter_mask(aid, 768), nn(small_ref[...], spread_ref[...]), 0.0).astype(BF)
    gdown_ref[...] = tn(wide[:, :512], hb_ref[...])
    gup_ref[...] = tn(wide[:, 512:], dy_ref[...])


def k5(small, aid, hb_cols, dy_cols, spread):
    return pl.pallas_call(
        k5_body,
        out_shape=[
            jax.ShapeDtypeStruct((512, 256), F32),
            jax.ShapeDtypeStruct((256, 256), F32),
        ],
        compiler_params=pltpu.CompilerParams(vmem_limit_bytes=VMEM_LIMIT),
        name="adapter_grads",
    )(small, aid, hb_cols, dy_cols, spread)


def rotary_tables():
    lane = np.arange(128) % 64
    rate = np.where(lane < 32, 10000.0 ** (-2.0 * (lane % 16) / 32.0), 0.0).astype(np.float32)
    sign = np.where(lane < 16, -1.0, 1.0).astype(np.float32)
    angles = jnp.arange(2048, dtype=jnp.int32).astype(F32)[:, None] * jnp.asarray(rate)[None, :]
    return jnp.cos(angles), jnp.sin(angles) * jnp.asarray(sign)[None, :]


def fold_matrix():
    row = np.arange(768)
    target = (row // 128) * 16 + row % 16
    return jnp.asarray((target[:, None] == np.arange(128)[None, :]).astype(np.float32)).astype(BF)


def halves(a):
    m = a.shape[1] // 2
    return jnp.concatenate([a[:, :m], a[:, m:]], axis=0)


def gather_pair(own, single):
    xh = lax.axis_index("xh")
    other = lax.ppermute(own, "xh", [(0, 1), (1, 0)])
    first = jnp.where(xh == 0, own, other)
    second = jnp.where(xh == 0, other, own)
    parts = [first, second]
    if single is not None:
        parts.append(single)
    packed = jnp.concatenate(parts, axis=0)
    rows = own.shape[0]
    g = lax.all_gather(packed, ("y", "c"), axis=0, tiled=False)
    g = g.reshape((4, 2) + packed.shape)
    main = g[:, :, : 2 * rows].reshape(4, 2, 2, rows, packed.shape[1])
    main = main.transpose(0, 2, 1, 3, 4).reshape(8, 2, rows, packed.shape[1])
    return main, g[:, :, 2 * rows :]


def local(
    inputs,
    output_cotangent,
    block_index_per_position,
    adapter_index_per_run,
    norm_gain,
    norm_bias,
    query_weight,
    key_weight,
    value_weight,
    dense_weight,
    query_bias,
    key_bias,
    value_bias,
    dense_bias,
    feedforward_in_weight,
    feedforward_in_bias,
    feedforward_out_weight,
    feedforward_out_bias,
    adapter_attention_down,
    adapter_attention_up,
    adapter_dense_down,
    adapter_dense_up,
    adapter_feedforward_in_down,
    adapter_feedforward_in_up,
    adapter_feedforward_out_down,
    adapter_feedforward_out_up,
):
    xl, z, c = lax.axis_index("xl"), lax.axis_index("z"), lax.axis_index("c")
    xh = lax.axis_index("xh")
    j = xl * 4 + z
    x_own = inputs[0]
    dy_own = output_cotangent[0]
    run_adapter = adapter_index_per_run[0, 0].astype(F32).astype(BF)
    block_row = block_index_per_position[0]

    def row_half(a):
        n = a.shape[0] // 2
        return lax.dynamic_slice_in_dim(a, c * n, n, 0)

    def col_half(a):
        n = a.shape[1] // 2
        return lax.dynamic_slice_in_dim(a, c * n, n, 1)

    def head_cols(a):
        return jnp.concatenate(
            [lax.dynamic_slice_in_dim(a, (2 * i + xl) * 256 + z * 64, 64, 1) for i in range(4)], axis=1
        )

    def hidden_cols(a):
        return jnp.concatenate(
            [lax.dynamic_slice_in_dim(a, 1024 * w + 128 * j, 128, 1) for w in range(8)], axis=1
        )

    qkv_half = jnp.concatenate(
        [head_cols(row_half(a)) for a in (query_weight, key_weight, value_weight)], axis=1
    )
    downs_own = jnp.concatenate([adapter_attention_down[0].reshape(48, 2048), adapter_feedforward_in_down[0]], axis=0)
    downs_half = row_half(downs_own)
    side = jnp.concatenate([downs_half[:16, 256 * b : 256 * b + 256] for b in range(8)], axis=0)
    ups16 = jnp.concatenate(
        [head_cols(adapter_attention_up[0, p]) for p in range(3)] + [head_cols(adapter_dense_down[0])], axis=1
    )

    def head_bias(a):
        return lax.dynamic_slice_in_dim(a, z * 64, 64, 0)

    row0 = jnp.concatenate([norm_gain, norm_bias, dense_bias, feedforward_out_bias])
    row1 = jnp.concatenate(
        [
            head_bias(query_bias),
            head_bias(key_bias),
            head_bias(value_bias),
            jnp.zeros((64,), BF),
            lax.dynamic_slice_in_dim(feedforward_in_bias, 128 * j, 128, 0),
            jnp.zeros((640,), BF),
        ]
    )
    misc16 = jnp.concatenate([row0[None], row1[None], jnp.zeros((14, 1024), BF)], axis=0)
    own1 = jnp.concatenate(
        [
            jnp.concatenate([qkv_half, side], axis=1),
            halves(downs_half[16:32]),
            jnp.where(c == 0, ups16, misc16),
            col_half(adapter_dense_up[0]),
        ],
        axis=0,
    )
    dense_rows = row_half(lax.dynamic_slice_in_dim(dense_weight, 64 * z, 64, 0))
    dense_piece = halves(dense_rows)
    dense_other = lax.ppermute(dense_piece, "xh", [(0, 1), (1, 0)])
    dense_piece = jnp.where(xh == xl, dense_piece, dense_other)

    own2 = jnp.concatenate(
        [
            hidden_cols(row_half(feedforward_in_weight)),
            hidden_cols(jnp.where(c == 0, adapter_feedforward_in_up[0], adapter_feedforward_out_down[0])),
            halves(row_half(lax.dynamic_slice_in_dim(feedforward_out_weight, 128 * j, 128, 0))),
            col_half(adapter_feedforward_out_up[0]),
        ],
        axis=0,
    )

    x_send = jnp.concatenate([x_own, jnp.full((128, 128), run_adapter, BF)], axis=1)
    xg = lax.all_gather(x_send, TP, axis=0, tiled=True)
    g1, dense_g = gather_pair(own1, dense_piece)
    dyg = lax.all_gather(dy_own, TP, axis=0, tiled=True)
    g2, _ = gather_pair(own2, None)

    wqkv = g1[:, :, :128, :768].reshape(2048, 768)
    first = g1[:, :, :128, 768:].reshape(8, 2, 8, 16, 256).transpose(1, 0, 3, 2, 4).reshape(2, 1, 128, 2048)
    second = g1[:, :, 128:160].reshape(8, 2, 2, 16, 1024).transpose(1, 0, 3, 2, 4).reshape(2, 1, 128, 2048)
    downs = jnp.concatenate([first, second], axis=1).reshape(512, 2048)
    ups = g1[:, 0, 160:176, :768].reshape(128, 768)
    dd = g1[:, 0, 160:176, 768:].reshape(128, 256)
    misc = g1[:, 1, 160, :].reshape(8, 4, 256).transpose(1, 0, 2).reshape(4, 2048).astype(F32)
    rest = g1[:, 1, 161, :].astype(F32)
    head_b = lax.dynamic_index_in_dim(rest[:, :192].reshape(4, 2, 3, 64), xl, 1, keepdims=False)
    bias_qkv = head_b.transpose(1, 0, 2).reshape(1, 768)
    b1 = rest[:, 256:384].reshape(1, 1024)
    ud = g1[:, :, 176:192].transpose(0, 2, 1, 3).reshape(128, 2048)
    wd = dense_g.reshape(4, 2, 2, 32, 1024).transpose(0, 1, 3, 2, 4).reshape(256, 2048)
    w1 = g2[:, :, :128].reshape(2048, 1024)
    up1 = g2[:, 0, 128:144].reshape(128, 1024)
    d2 = g2[:, 1, 128:144].reshape(128, 1024)
    w2 = g2[:, :, 144:272].reshape(8, 2, 2, 64, 1024).transpose(0, 1, 3, 2, 4).reshape(1024, 2048)
    u2 = g2[:, :, 272:288].transpose(0, 2, 1, 3).reshape(128, 2048)

    cos_all, sin_all = rotary_tables()

    def my_tokens(a):
        return lax.dynamic_index_in_dim(a.reshape(8, 2, 128, 128), c, 1, keepdims=False).reshape(1024, 128)

    hb, inner, qkv2 = k1(xg, wqkv, downs, ups, misc[:2], bias_qkv, my_tokens(cos_all), my_tokens(sin_all))
    aid = xg[:, 2048:]
    dob2, gdense = k1b(dyg, aid, wd, ud, dd)

    swap = [(0, 1), (1, 0)]
    both = jnp.concatenate([qkv2, dob2[:, None]], axis=1)
    mine = lax.dynamic_index_in_dim(both, c, 0, keepdims=False)
    theirs = lax.ppermute(lax.dynamic_index_in_dim(both, 1 - c, 0, keepdims=False), "c", swap)
    even = jnp.where(c == 0, mine, theirs).reshape(4, 8, 1, 128, 128)
    odd = jnp.where(c == 0, theirs, mine).reshape(4, 8, 1, 128, 128)
    qkvd = jnp.concatenate([even, odd], axis=2).reshape(4, 2048, 128)
    idrow = jnp.broadcast_to(block_row[None, :], (8, 2048))
    idcol = jnp.broadcast_to(block_row[:, None], (2048, 128))
    att = k3(qkvd, idrow, idcol, cos_all, sin_all)
    att = att.reshape(4, 8, 2, 128, 128)
    mine = lax.dynamic_index_in_dim(att, c, 2, keepdims=False).reshape(4, 1024, 128)
    theirs = lax.ppermute(
        lax.dynamic_index_in_dim(att, 1 - c, 2, keepdims=False).reshape(4, 1024, 128), "c", swap
    )
    att = jnp.concatenate([jnp.where(c == 0, mine, theirs), jnp.where(c == 0, theirs, mine)], axis=2)

    fold = fold_matrix()
    out_part, dh_part, small, gup1, gd2, gqkv, gdd = k2(
        hb, dyg, aid, inner, gdense, att, w1, w2, wd, wqkv, downs, ups, up1, d2, u2, ud, dd, b1, fold
    )
    out_sum = lax.psum_scatter(out_part, TP, scatter_dimension=0, tiled=True)
    dh_sum = lax.psum_scatter(dh_part, TP, scatter_dimension=0, tiled=True)

    small = lax.all_to_all(small.reshape(8, 128, 128), TP, 0, 0, tiled=True)
    small = jnp.sum(small.astype(F32), axis=0).astype(BF)
    small = lax.all_to_all(jnp.broadcast_to(small[None], (8, 128, 128)), TP, 0, 0, tiled=True).reshape(1024, 128)
    hb_cols = lax.dynamic_slice_in_dim(hb, 256 * j, 256, 1)
    dy_cols = lax.dynamic_slice_in_dim(dyg, 256 * j, 256, 1)
    gdown, gup = k5(small, aid, hb_cols, dy_cols, fold.T)

    gdown = gdown.reshape(4, 8, 16, 256).transpose(1, 2, 0, 3).reshape(8, 16, 1024)
    gqkvd = jnp.concatenate([gqkv, gdd], axis=1).reshape(8, 16, 1024)
    gup = gup.reshape(2, 8, 16, 256).transpose(1, 2, 0, 3).reshape(8, 16, 512)
    gup = jnp.concatenate([gup, jnp.zeros_like(gup)], axis=2)
    grads = jnp.concatenate([gdown, gqkvd, gup1.reshape(8, 16, 1024), gd2.reshape(8, 16, 1024), gup], axis=1)
    keep = lax.dynamic_slice_in_dim(grads, 40 * c, 40, 1)
    send = lax.dynamic_slice_in_dim(grads, 40 * (1 - c), 40, 1).astype(BF)
    grads = (keep + lax.ppermute(send, "c", swap).astype(F32)).astype(BF)
    grads = lax.all_to_all(grads, WSH, 0, 0, tiled=True)
    grads = jnp.sum(grads.astype(F32), axis=0).astype(BF)
    grads = lax.all_to_all(jnp.broadcast_to(grads[None], (16, 40, 1024)), CTX, 0, 0, tiled=True)
    grads = grads.reshape(8, 80, 1024).astype(F32)

    def from_heads(a):
        return a.reshape(2, 4, 16, 4, 64).transpose(2, 3, 0, 1, 4).reshape(16, 2048)

    def from_blocks(a):
        return a.transpose(1, 0, 2).reshape(16, 2048)

    def from_hidden(a):
        return a.reshape(8, 16, 8, 128).transpose(1, 2, 0, 3).reshape(16, 8192)

    downs_g = [from_blocks(grads[:, :16, 256 * p : 256 * p + 256]) for p in range(4)]
    ups_g = [from_heads(grads[:, 16:32, 256 * p : 256 * p + 256]) for p in range(4)]
    gup1 = from_hidden(grads[:, 32:48])
    gd2 = from_hidden(grads[:, 48:64])
    gud = from_blocks(grads[:, 64:80, :256])
    gu2 = from_blocks(grads[:, 64:80, 256:512])

    source = x_own.astype(F32)
    outputs = (source + out_sum.astype(F32) + misc[2:3] + misc[3:4]).astype(BF)[None]
    mean = jnp.mean(source, axis=1, keepdims=True)
    center = source - mean
    inv = lax.rsqrt(jnp.mean(center * center, axis=1, keepdims=True) + EPSILON)
    hn = center * inv
    e = dh_sum.astype(F32) * misc[0:1]
    dx = (e - jnp.mean(e, axis=1, keepdims=True) - hn * jnp.mean(e * hn, axis=1, keepdims=True)) * inv
    grad_inputs = (dy_own.astype(F32) + dx).astype(BF)[None]
    return (
        outputs,
        grad_inputs,
        jnp.stack(downs_g[:3])[None],
        jnp.stack(ups_g[:3])[None],
        ups_g[3][None],
        gud[None],
        downs_g[3][None],
        gup1[None],
        gd2[None],
        gu2[None],
    )


def solution(mesh):
    fine = Mesh(np.asarray(mesh.devices).reshape(2, 4, 2, 4, 2), ("xl", "z", "c", "y", "xh"))
    tokens = P(WSH, CTX, None)
    w1 = P(WSH)
    w2 = P(WSH, None)
    w3 = P(WSH, None, None)
    w4 = P(WSH, None, None, None)
    placed = (tokens, tokens, w2, P(WSH, CTX)) + (w1, w1, w2, w2, w2, w2, w1, w1, w1, w1, w2, w1, w2, w1)
    placed = placed + (w4, w4, w3, w3, w3, w3, w3, w3)
    return jax.shard_map(
        local,
        mesh=fine,
        in_specs=placed,
        out_specs=(tokens, tokens, w4, w4, w3, w3, w3, w3, w3, w3),
        check_vma=False,
    )
```

```python
import functools

import jax
import jax.numpy as jnp
import numpy as np
from jax import lax
from jax.experimental import pallas as pl
from jax.experimental.pallas import tpu as pltpu
from jax.sharding import Mesh, PartitionSpec as P

ADAPTERS = 8
RANK = 16
EPSILON = 1e-05
GELU_SCALE = 0.7978845608028654
NEGATIVE = -1e30
SCALE = 64 ** -0.5
BF = jnp.bfloat16
F32 = jnp.float32
WSH = ("y", "xh")
TP = ("xl", "z")
CTX = ("xl", "z", "c")
VMEM_LIMIT = 58 * 1024 * 1024


def nn(a, b):
    return lax.dot_general(a, b, (((1,), (0,)), ((), ())), preferred_element_type=F32)


def nt(a, b):
    return lax.dot_general(a, b, (((1,), (1,)), ((), ())), preferred_element_type=F32)


def tn(a, b):
    return lax.dot_general(a, b, (((0,), (0,)), ((), ())), preferred_element_type=F32)


def adapter_mask(aid, columns):
    col = lax.broadcasted_iota(jnp.int32, (aid.shape[0], columns), 1)
    return (lax.shift_right_logical(col, 4) & 7) == aid.astype(jnp.int32)


def turn(values, cosine, sine):
    width = values.shape[1]
    lane = lax.broadcasted_iota(jnp.int32, values.shape, 1) & 63
    partner = jnp.where(
        lane < 16, pltpu.roll(values, width - 16, 1), pltpu.roll(values, 16, 1)
    )
    return values * cosine + partner * sine


ANY = pl.BlockSpec(memory_space=pl.ANY)
SMEM = pl.BlockSpec(memory_space=pltpu.SMEM)
VM = pl.BlockSpec(memory_space=pltpu.VMEM)
PARAMS = pltpu.CompilerParams(vmem_limit_bytes=VMEM_LIMIT)
MAIN = 208
SECOND = 288


def whole(shape):
    return pl.BlockSpec(shape, lambda t: (0,) * len(shape), pipeline_mode=pl.Buffered(1))


def start_all(pairs, sem):
    for source, target in pairs:
        pltpu.make_async_copy(source, target, sem).start()


def wait_all(target, sem):
    pltpu.make_async_copy(target, target, sem).wait()


def pieces_qkv(g1, target):
    return [
        (
            g1.at[y, c, pl.ds(MAIN * xh, 128), pl.ds(0, 768)],
            target.at[pl.ds((2 * y + xh) * 256 + c * 128, 128), :],
        )
        for y in range(4)
        for xh in range(2)
        for c in range(2)
    ]


def pieces_downs(g1, target):
    return [
        (
            g1.at[:, c, pl.ds(MAIN * xh + 128 + 32 * i + 16 * b, 16), :],
            target.at[c, i, :, xh, :, pl.ds(1024 * b, 1024)],
        )
        for c in range(2)
        for i in range(2)
        for xh in range(2)
        for b in range(2)
    ]


def pieces_rank(g, base, stride, target, row):
    return [
        (
            g.at[y, c, pl.ds(stride * xh + base, 16), :],
            target.at[pl.ds(row + (2 * y + xh) * 16, 16), pl.ds(1024 * c, 1024)],
        )
        for y in range(4)
        for xh in range(2)
        for c in range(2)
    ]


def pieces_dense(g1, target, row):
    return [
        (
            g1.at[y, c, pl.ds(2 * MAIN + 32 * b, 32), :],
            target.at[pl.ds(row + 64 * y + 32 * c, 32), pl.ds(1024 * b, 1024)],
        )
        for y in range(4)
        for c in range(2)
        for b in range(2)
    ]


def pieces_w1(g2, target):
    return [
        (
            g2.at[y, c, pl.ds(SECOND * xh, 128), :],
            target.at[pl.ds((2 * y + xh) * 256 + c * 128, 128), :],
        )
        for y in range(4)
        for xh in range(2)
        for c in range(2)
    ]


def pieces_sixteen(g2, c, target, row):
    return [
        (
            g2.at[y, c, pl.ds(SECOND * xh + 128, 16), :],
            target.at[pl.ds(row + (2 * y + xh) * 16, 16), :],
        )
        for y in range(4)
        for xh in range(2)
    ]


def pieces_w2(g2, target):
    return [
        (
            g2.at[y, c, pl.ds(SECOND * xh + 144 + 64 * b, 64), :],
            target.at[pl.ds((2 * y + xh) * 128 + c * 64, 64), pl.ds(1024 * b, 1024)],
        )
        for y in range(4)
        for xh in range(2)
        for c in range(2)
        for b in range(2)
    ]


def block_diagonal(source, target):
    target[...] = jnp.zeros_like(target)
    for p in range(3):
        cols = slice(256 * p, 256 * p + 256)
        target[128 * p : 128 * p + 128, cols] = source[:, cols]


def k1_body(*refs):
    blocks, refs = refs[:8], refs[8:]
    (scal_ref, g1_ref, up_ref, misc_ref, bias_ref, cos_ref, sin_ref,
     hb_ref, inner_ref, keep_ref, send_ref, aid_ref, x_s, w_s, down_s, up_s, x_sem, w_sem) = refs
    step = pl.program_id(0)

    @pl.when(step == 0)
    def _():
        for i in range(2):
            pltpu.make_async_copy(blocks[i], x_s.at[0, i], x_sem.at[i]).start()
        start_all(pieces_downs(g1_ref, down_s), w_sem.at[0])
        start_all(pieces_qkv(g1_ref, w_s.at[:, pl.ds(0, 768)]), w_sem.at[1])
        for i in range(2, 8):
            pltpu.make_async_copy(blocks[i], x_s.at[i // 2, i % 2], x_sem.at[i]).start()

    for i in range(2):
        target = x_s.at[step, i]
        pltpu.make_async_copy(target, target, x_sem.at[2 * step + i]).wait()
    tile = x_s[step].reshape(256, 2176)
    x = tile[:, :2048].astype(F32)
    aid_ref[...] = tile[:, 2048:]
    aid = tile[:, 2048:2049].astype(F32)
    mean = jnp.mean(x, axis=1, keepdims=True)
    center = x - mean
    spread = jnp.mean(center * center, axis=1, keepdims=True)
    h = center * lax.rsqrt(spread + EPSILON) * misc_ref[0:1, :] + misc_ref[1:2, :]
    hb = h.astype(BF)
    hb_ref[...] = hb

    @pl.when(step == 0)
    def _():
        block_diagonal(up_ref, up_s)
        wait_all(down_s, w_sem.at[0])
        w_s[:, 768:] = down_s[...].reshape(512, 2048).T
        wait_all(w_s.at[:, pl.ds(0, 768)], w_sem.at[1])

    pre_all = nn(hb, w_s[...])
    inner = jnp.where(adapter_mask(aid, 512), pre_all[:, 768:], 0.0).astype(BF)
    inner_ref[...] = inner
    pre_all = pre_all[:, :768] + nn(inner[:, :384], up_s[...]) + bias_ref[...]
    first_core = scal_ref[8] == 0
    cosine = jnp.concatenate([cos_ref[...]] * 2, axis=1)
    sine = jnp.concatenate([sin_ref[...]] * 2, axis=1)
    for p in range(3):
        cols = slice(256 * p, 256 * p + 256)
        pre = pre_all[:, cols]
        if p < 2:
            pre = turn(pre, cosine, sine)
        low = pre.astype(BF)
        keep_ref[p] = jnp.where(first_core, low[:, :128], low[:, 128:])
        send_ref[p] = jnp.where(first_core, low[:, 128:], low[:, :128])


def k1(blocks, scal, g1, ups, misc, bias, cosine, sine):
    rows = 256
    return pl.pallas_call(
        k1_body,
        grid=(4,),
        in_specs=[ANY] * 8
        + [
            SMEM,
            ANY,
            whole((128, 768)),
            whole((2, 2048)),
            whole((1, 768)),
            pl.BlockSpec((rows, 128), lambda t: (t, 0)),
            pl.BlockSpec((rows, 128), lambda t: (t, 0)),
        ],
        out_specs=[
            pl.BlockSpec((rows, 2048), lambda t: (t, 0)),
            pl.BlockSpec((rows, 512), lambda t: (t, 0)),
            pl.BlockSpec((3, rows, 128), lambda t: (0, t, 0)),
            pl.BlockSpec((3, rows, 128), lambda t: (0, t, 0)),
            pl.BlockSpec((rows, 128), lambda t: (t, 0)),
        ],
        out_shape=[
            jax.ShapeDtypeStruct((1024, 2048), BF),
            jax.ShapeDtypeStruct((1024, 512), BF),
            jax.ShapeDtypeStruct((3, 1024, 128), BF),
            jax.ShapeDtypeStruct((3, 1024, 128), BF),
            jax.ShapeDtypeStruct((1024, 128), BF),
        ],
        scratch_shapes=[
            pltpu.VMEM((4, 2, 128, 2176), BF),
            pltpu.VMEM((2048, 1280), BF),
            pltpu.VMEM((2, 2, 4, 2, 16, 2048), BF),
            pltpu.VMEM((384, 768), BF),
            pltpu.SemaphoreType.DMA((8,)),
            pltpu.SemaphoreType.DMA((2,)),
        ],
        compiler_params=PARAMS,
        cost_estimate=pl.CostEstimate(flops=6_000_000_000, bytes_accessed=20_000_000, transcendentals=0),
        name="norm_qkv",
    )(*blocks, scal, g1, ups, misc, bias, cosine, sine)


def k1b_body(*refs):
    blocks, refs = refs[:8], refs[8:]
    scal_ref, aid_ref, g1_ref, dd_ref, keep_ref, send_ref, ginner_ref, dy_s, w_s, dy_sem, w_sem = refs
    start_all(pieces_dense(g1_ref, w_s, 0) + pieces_rank(g1_ref, 192, MAIN, w_s, 256), w_sem)
    start_all([(blocks[i], dy_s.at[i]) for i in range(8)], dy_sem)
    wait_all(w_s, w_sem)
    wait_all(dy_s, dy_sem)
    first_core = scal_ref[8] == 0
    both = nt(dy_s[...].reshape(1024, 2048), w_s[...])
    aid = aid_ref[:, 0:1].astype(F32)
    ginner = jnp.where(adapter_mask(aid, 128), both[:, 256:], 0.0).astype(BF)
    ginner_ref[...] = ginner
    dob = (both[:, :256] + nn(ginner, dd_ref[...])).astype(BF)
    keep_ref[...] = jnp.where(first_core, dob[:, :128], dob[:, 128:])
    send_ref[...] = jnp.where(first_core, dob[:, 128:], dob[:, :128])


def k1b(blocks, scal, aid, g1, dd):
    return pl.pallas_call(
        k1b_body,
        in_specs=[ANY] * 8 + [SMEM, VM, ANY, VM],
        out_specs=[VM, VM, VM],
        out_shape=[jax.ShapeDtypeStruct((1024, 128), BF)] * 3,
        scratch_shapes=[
            pltpu.VMEM((8, 128, 2048), BF),
            pltpu.VMEM((384, 2048), BF),
            pltpu.SemaphoreType.DMA,
            pltpu.SemaphoreType.DMA,
        ],
        compiler_params=PARAMS,
        cost_estimate=pl.CostEstimate(flops=2_000_000_000, bytes_accessed=8_000_000, transcendentals=0),
        name="attention_output_grad",
    )(*blocks, scal, aid, g1, dd)


def k3_body(
    scal_ref, qkv_keep, qkv_recv, dob_keep, dob_recv, idrow_ref, idcol_ref, cos_ref, sin_ref,
    keep_out, send_out, x_s, out_s, kt_s, vt_s, dk_s, dv_s, sem, sem_out,
):
    core = scal_ref[8]
    copies = []
    for b in range(8):
        rows = pl.ds(128 * b, 128)
        spot = scal_ref[b]
        for side, (qkv, dob) in enumerate(((qkv_keep, dob_keep), (qkv_recv, dob_recv))):
            parity = core if side == 0 else 1 - core
            copies.append((qkv.at[:, rows, :], x_s.at[pl.ds(0, 3), spot, parity]))
            copies.append((dob.at[rows, :], x_s.at[3, spot, parity]))
    start_all(copies, sem)
    dk_s[...] = jnp.zeros_like(dk_s)
    dv_s[...] = jnp.zeros_like(dv_s)
    wait_all(x_s, sem)
    kt_s[...] = x_s[1].reshape(2048, 128).T
    vt_s[...] = x_s[2].reshape(2048, 128).T
    tile = 256
    lane = lax.broadcasted_iota(jnp.int32, (tile, 128), 1)

    def span(i, start, stop):
        return x_s[i, start // 256 : stop // 256].reshape(stop - start, 128)

    for t in range(8):
        start, stop = tile * t, tile * t + tile
        length = min(stop + tile, 2048)
        q = span(0, start, stop)
        dob = span(3, start, stop)
        zero = jnp.zeros_like(q)
        q2 = jnp.concatenate([jnp.where(lane < 64, q, zero), jnp.where(lane < 64, zero, q)], axis=0)
        d2 = jnp.concatenate([jnp.where(lane < 64, dob, zero), jnp.where(lane < 64, zero, dob)], axis=0)
        query_ids = idrow_ref[0:1, start:stop]
        query_ids = jnp.concatenate([query_ids, query_ids], axis=1)
        allowed = idcol_ref[start:length, 0:1] <= query_ids
        s = jnp.where(allowed, nt(span(1, start, length), q2), NEGATIVE)
        largest = jnp.max(s, axis=0, keepdims=True)
        if start:
            s_head = nt(span(1, 0, start), q2)
            largest = jnp.maximum(largest, jnp.max(s_head, axis=0, keepdims=True))
            s = jnp.concatenate([s_head, s], axis=0)
        e = jnp.exp((s - largest) * SCALE)
        recip = 1.0 / jnp.sum(e, axis=0, keepdims=True)
        p = e * recip
        pb = p.astype(BF)
        dp = nt(span(2, 0, length), d2)
        delta = jnp.sum(p * dp, axis=0, keepdims=True)
        ds = (p * (dp - delta)).astype(BF)
        dk_s[:length] += nn(ds, q2)
        dv_s[:length] += nn(pb, d2)
        ot = nn(vt_s[:, :length], pb)
        dqt = nn(kt_s[:, :length], ds)
        o_parts = [ot[:64, :256], ot[64:, 256:]]
        dq_parts = [dqt[:64, :256], dqt[64:, 256:]]
        o = jnp.concatenate(o_parts, axis=0).T
        dq = jnp.concatenate(dq_parts, axis=0).T * SCALE
        rows = slice(start, stop)
        out_s[0, t] = o.astype(BF).reshape(2, 128, 128)
        out_s[1, t] = turn(dq, cos_ref[rows], -sin_ref[rows]).astype(BF).reshape(2, 128, 128)
    out_s[2] = turn(dk_s[...] * SCALE, cos_ref[...], -sin_ref[...]).astype(BF).reshape(8, 2, 128, 128)
    out_s[3] = dv_s[...].astype(BF).reshape(8, 2, 128, 128)
    copies = []
    for b in range(8):
        rows = pl.ds(128 * b, 128)
        spot = scal_ref[b]
        copies.append((out_s.at[:, spot, core], keep_out.at[:, rows, :]))
        copies.append((out_s.at[:, spot, 1 - core], send_out.at[:, rows, :]))
    start_all(copies, sem_out)
    wait_all(out_s, sem_out)


def k3(scal, qkv_keep, qkv_recv, dob_keep, dob_recv, idrow, idcol, cosine, sine):
    vm = pl.BlockSpec(memory_space=pltpu.VMEM)
    return pl.pallas_call(
        k3_body,
        in_specs=[SMEM] + [ANY] * 4 + [vm] * 4,
        out_specs=[ANY, ANY],
        out_shape=[jax.ShapeDtypeStruct((4, 1024, 128), BF)] * 2,
        scratch_shapes=[
            pltpu.VMEM((4, 8, 2, 128, 128), BF),
            pltpu.VMEM((4, 8, 2, 128, 128), BF),
            pltpu.VMEM((128, 2048), BF),
            pltpu.VMEM((128, 2048), BF),
            pltpu.VMEM((2048, 128), F32),
            pltpu.VMEM((2048, 128), F32),
            pltpu.SemaphoreType.DMA,
            pltpu.SemaphoreType.DMA,
        ],
        compiler_params=PARAMS,
        cost_estimate=pl.CostEstimate(flops=15_000_000_000, bytes_accessed=8_000_000, transcendentals=5_000_000),
        name="attention",
    )(scal, qkv_keep, qkv_recv, dob_keep, dob_recv, idrow, idcol, cosine, sine)


def heads_of(keep_ref, recv_ref, i, first_core):
    a, b = keep_ref[i], recv_ref[i]
    return jnp.concatenate([jnp.where(first_core, a, b), jnp.where(first_core, b, a)], axis=1)


def tile_spec(width, rows=256):
    return pl.BlockSpec((rows, width), lambda t, s: (t, 0))


def const_spec(shape):
    return pl.BlockSpec(shape, lambda t, s: (0,) * len(shape), pipeline_mode=pl.Buffered(1))


def placed_spec(width):
    return pl.BlockSpec((2, 1, 128, width), lambda t, s: (0, s[12 + t], 0, 0))


def place(ref, xl, value):
    ref[xl, 0] = value[:128]
    ref[1 - xl, 0] = value[128:]


def accumulate(step, pairs):
    @pl.when(step == 0)
    def _():
        for ref, value in pairs:
            ref[...] = value

    @pl.when(step > 0)
    def _():
        for ref, value in pairs:
            ref[...] += value


def k2a_body(
    scal_ref, hb_ref, aid_ref, inner_ref, gdense_ref, keep_ref, recv_ref, g1_ref, g2_ref, dd_ref, b1_ref, fold_ref,
    out_ref, gb_ref, slope_ref, small_ref, gdd_ref,
    w1_s, wout_s, d2_s, rest_s, sems,
):
    step = pl.program_id(0)

    @pl.when(step == 0)
    def _():
        start_all(pieces_w1(g2_ref, w1_s) + pieces_sixteen(g2_ref, 0, w1_s, 2048), sems.at[0])
        start_all(pieces_sixteen(g2_ref, 1, d2_s, 0), sems.at[1])
        start_all(pieces_w2(g2_ref, wout_s) + pieces_dense(g1_ref, wout_s, 1024), sems.at[2])
        start_all(
            pieces_rank(g2_ref, 272, SECOND, rest_s, 0) + pieces_rank(g1_ref, 192, MAIN, rest_s, 128), sems.at[3]
        )
        wout_s[:, 2048:] = jnp.zeros((1280, 256), BF)
        wout_s[1024:, 2176:] = dd_ref[...].T
        wait_all(d2_s, sems.at[1])
        wout_s[:1024, 2048:2176] = d2_s[...].T
        wait_all(w1_s, sems.at[0])

    keep = adapter_mask(aid_ref[:, 0:1].astype(F32), 256)
    f = nn(jnp.concatenate([hb_ref[...], inner_ref[...]], axis=1), w1_s[...]) + b1_ref[...]
    square = f * f
    th = jnp.tanh(GELU_SCALE * f * (1.0 + 0.044715 * square))
    half = 0.5 * (1.0 + th)
    gb = (f * half).astype(BF)
    gb_ref[...] = gb
    slope = half + (0.5 * GELU_SCALE) * f * (1.0 - th * th) * (1.0 + 3 * 0.044715 * square)
    slope_ref[...] = slope.astype(BF)
    ob = heads_of(keep_ref, recv_ref, 0, scal_ref[8] == 0)

    @pl.when(step == 0)
    def _():
        wait_all(wout_s.at[:, pl.ds(0, 2048)], sems.at[2])
        wait_all(rest_s, sems.at[3])

    total = nn(jnp.concatenate([gb, ob], axis=1), wout_s[...])
    low = jnp.where(keep, total[:, 2048:], 0.0).astype(BF)
    out = (total[:, :2048] + nn(low, rest_s[...])).astype(BF)
    place(out_ref, scal_ref[10], out)
    small_ref[...] = nn(low, fold_ref[...]).astype(BF)
    accumulate(step, [(gdd_ref, tn(gdense_ref[...], ob))])


def k2a(scal, hb, aid, inner, gdense, keep, recv, g1, g2, dd, b1, fold):
    return pl.pallas_call(
        k2a_body,
        grid_spec=pltpu.PrefetchScalarGridSpec(
            num_scalar_prefetch=1,
            grid=(4,),
            in_specs=[
                tile_spec(2048),
                tile_spec(128),
                pl.BlockSpec((256, 128), lambda t, s: (t, 3)),
                tile_spec(128),
                pl.BlockSpec((1, 256, 128), lambda t, s: (0, t, 0)),
                pl.BlockSpec((1, 256, 128), lambda t, s: (0, t, 0)),
                ANY,
                ANY,
                const_spec((128, 256)),
                const_spec((1, 1024)),
                const_spec((256, 128)),
            ],
            out_specs=[
                placed_spec(2048),
                tile_spec(1024),
                tile_spec(1024),
                tile_spec(128),
                const_spec((128, 256)),
            ],
            scratch_shapes=[
                pltpu.VMEM((2176, 1024), BF),
                pltpu.VMEM((1280, 2304), BF),
                pltpu.VMEM((128, 1024), BF),
                pltpu.VMEM((256, 2048), BF),
                pltpu.SemaphoreType.DMA((4,)),
            ],
        ),
        out_shape=[
            jax.ShapeDtypeStruct((2, 4, 128, 2048), BF),
            jax.ShapeDtypeStruct((1024, 1024), BF),
            jax.ShapeDtypeStruct((1024, 1024), BF),
            jax.ShapeDtypeStruct((1024, 128), BF),
            jax.ShapeDtypeStruct((128, 256), F32),
        ],
        compiler_params=PARAMS,
        cost_estimate=pl.CostEstimate(flops=12_000_000_000, bytes_accessed=24_000_000, transcendentals=1_000_000),
        name="feed_forward",
    )(scal, hb, aid, inner, gdense, keep, recv, g1, g2, dd, b1, fold)


def k2b_body(scal_ref, *refs):
    blocks, refs = refs[:8], refs[8:]
    (aid_ref, inner_ref, keep_ref, recv_ref, gb_ref, slope_ref, small_in_ref, g1_ref, g2_ref, up_ref, fold_ref,
     near_ref, owns_ref, sides_ref, small_ref, gup1_ref, gd2_ref, gqkv_ref,
     dy_s, w1_s, w2_s, d2_s, wqkv_s, down_s, dy_sem, sems) = refs
    step = pl.program_id(0)

    @pl.when(step == 0)
    def _():
        for i in range(2):
            pltpu.make_async_copy(blocks[i], dy_s.at[0, i], dy_sem.at[i]).start()
        start_all(pieces_w2(g2_ref, w2_s) + pieces_rank(g2_ref, 272, SECOND, w2_s, 1024), sems.at[0])
        start_all(pieces_sixteen(g2_ref, 1, d2_s, 0), sems.at[1])
        start_all(pieces_w1(g2_ref, w1_s) + pieces_sixteen(g2_ref, 0, w1_s, 2048), sems.at[2])
        start_all(pieces_qkv(g1_ref, wqkv_s), sems.at[3])
        start_all(pieces_downs(g1_ref, down_s), sems.at[4])
        for i in range(2, 8):
            pltpu.make_async_copy(blocks[i], dy_s.at[i // 2, i % 2], dy_sem.at[i]).start()
        block_diagonal(up_ref, wqkv_s.at[pl.ds(2048, 384)])
        wait_all(w2_s, sems.at[0])
        wait_all(d2_s, sems.at[1])

    for i in range(2):
        target = dy_s.at[step, i]
        pltpu.make_async_copy(target, target, dy_sem.at[2 * step + i]).wait()
    aid = aid_ref[:, 0:1].astype(F32)
    first_core = scal_ref[8] == 0
    inner = inner_ref[...]
    dy = dy_s[step].reshape(256, 2048)
    wide = nt(dy, w2_s[...])
    ginner2 = jnp.where(adapter_mask(aid, 128), wide[:, 1024:], 0.0).astype(BF)
    dg = wide[:, :1024] + nn(ginner2, d2_s[...])
    df = (dg * slope_ref[...].astype(F32)).astype(BF)

    @pl.when(step == 0)
    def _():
        wait_all(w1_s, sems.at[2])
        wait_all(wqkv_s.at[pl.ds(0, 2048)], sems.at[3])
        wait_all(down_s, sems.at[4])

    wide = nt(df, w1_s[...])
    dpre = jnp.concatenate([heads_of(keep_ref, recv_ref, p, first_core) for p in (1, 2, 3)], axis=1)
    wider = nt(dpre, wqkv_s[...])
    small = jnp.concatenate([wider[:, 2048:], wide[:, 2048:]], axis=1)
    small = jnp.where(adapter_mask(aid, 512), small, 0.0).astype(BF)
    dh = wide[:, :2048] + wider[:, :2048] + nn(small, down_s[...].reshape(512, 2048))
    dh = dh.astype(BF)
    near_ref[0] = dh[:128, :1024]
    near_ref[1] = dh[128:, :1024]
    owns_ref[0] = dh[:128, 1024:]
    sides_ref[0] = dh[128:, 1024:]
    place(small_ref, scal_ref[10], (nn(small, fold_ref[...]) + small_in_ref[...].astype(F32)).astype(BF))
    gqkv = [tn(inner[:, 128 * p : 128 * p + 128], dpre[:, 256 * p : 256 * p + 256]) for p in range(3)]
    accumulate(
        step,
        [
            (gup1_ref, tn(inner[:, 384:], df)),
            (gd2_ref, tn(ginner2, gb_ref[...])),
            (gqkv_ref, jnp.concatenate(gqkv, axis=1)),
        ],
    )


def k2b(blocks, scal, aid, inner, keep, recv, gb, slope, small, g1, g2, ups, fold):
    return pl.pallas_call(
        k2b_body,
        grid_spec=pltpu.PrefetchScalarGridSpec(
            num_scalar_prefetch=1,
            grid=(4,),
            in_specs=[ANY] * 8
            + [
                tile_spec(128),
                tile_spec(512),
                pl.BlockSpec((4, 256, 128), lambda t, s: (0, t, 0)),
                pl.BlockSpec((4, 256, 128), lambda t, s: (0, t, 0)),
                tile_spec(1024),
                tile_spec(1024),
                tile_spec(128),
                ANY,
                ANY,
                const_spec((128, 768)),
                const_spec((512, 128)),
            ],
            out_specs=[
                pl.BlockSpec((2, 128, 1024), lambda t, s: (t, 0, 0)),
                pl.BlockSpec((1, 128, 1024), lambda t, s: (t, 0, 0)),
                pl.BlockSpec((1, 128, 1024), lambda t, s: (t, 0, 0)),
                placed_spec(128),
                const_spec((128, 1024)),
                const_spec((128, 1024)),
                const_spec((128, 768)),
            ],
            scratch_shapes=[
                pltpu.VMEM((4, 2, 128, 2048), BF),
                pltpu.VMEM((2176, 1024), BF),
                pltpu.VMEM((1152, 2048), BF),
                pltpu.VMEM((128, 1024), BF),
                pltpu.VMEM((2432, 768), BF),
                pltpu.VMEM((2, 2, 4, 2, 16, 2048), BF),
                pltpu.SemaphoreType.DMA((8,)),
                pltpu.SemaphoreType.DMA((5,)),
            ],
        ),
        out_shape=[
            jax.ShapeDtypeStruct((8, 128, 1024), BF),
            jax.ShapeDtypeStruct((4, 128, 1024), BF),
            jax.ShapeDtypeStruct((4, 128, 1024), BF),
            jax.ShapeDtypeStruct((2, 4, 128, 128), BF),
            jax.ShapeDtypeStruct((128, 1024), F32),
            jax.ShapeDtypeStruct((128, 1024), F32),
            jax.ShapeDtypeStruct((128, 768), F32),
        ],
        compiler_params=PARAMS,
        cost_estimate=pl.CostEstimate(flops=17_000_000_000, bytes_accessed=36_000_000, transcendentals=0),
        name="feed_forward_grad",
    )(scal, *blocks, aid, inner, keep, recv, gb, slope, small, g1, g2, ups, fold)


def k5_body(scal_ref, small_ref, aid_ref, hb_ref, spread_ref, *refs):
    blocks, refs = refs[:8], refs[8:]
    gdown_ref, gup_ref, dy_s, sem = refs
    column = pl.multiple_of(256 * scal_ref[9], 256)
    start_all([(blocks[b].at[:, pl.ds(column, 256)], dy_s.at[b]) for b in range(8)], sem)
    small = jnp.concatenate([small_ref[scal_ref[b]] for b in range(8)], axis=0)
    aid = aid_ref[:, 0:1].astype(F32)
    wide = jnp.where(adapter_mask(aid, 768), nn(small, spread_ref[...]), 0.0).astype(BF)
    gdown_ref[...] = tn(wide[:, :512], hb_ref[...])
    wait_all(dy_s, sem)
    gup_ref[...] = tn(wide[:, 512:], dy_s[...].reshape(1024, 256))


def k5(scal, small, aid, hb, spread, blocks):
    def const(shape):
        return pl.BlockSpec(shape, lambda t, s: (0,) * len(shape))

    return pl.pallas_call(
        k5_body,
        grid_spec=pltpu.PrefetchScalarGridSpec(
            num_scalar_prefetch=1,
            grid=(1,),
            in_specs=[
                const((8, 128, 128)),
                const((1024, 128)),
                pl.BlockSpec((1024, 256), lambda t, s: (0, s[9])),
                const((128, 768)),
            ]
            + [ANY] * 8,
            out_specs=[const((512, 256)), const((256, 256))],
            scratch_shapes=[pltpu.VMEM((8, 128, 256), BF), pltpu.SemaphoreType.DMA],
        ),
        out_shape=[
            jax.ShapeDtypeStruct((512, 256), F32),
            jax.ShapeDtypeStruct((256, 256), F32),
        ],
        compiler_params=PARAMS,
        name="adapter_grads",
    )(scal, small, aid, hb, spread, *blocks)


def rotary_tables(positions):
    lane = np.arange(128) % 64
    rate = np.where(lane < 32, 10000.0 ** (-2.0 * (lane % 16) / 32.0), 0.0).astype(np.float32)
    sign = np.where(lane < 16, -1.0, 1.0).astype(np.float32)
    angles = positions.astype(F32)[:, None] * jnp.asarray(rate)[None, :]
    return jnp.cos(angles), jnp.sin(angles) * jnp.asarray(sign)[None, :]


def fold_matrix():
    row = np.arange(768)
    target = (row // 128) * 16 + row % 16
    return jnp.asarray((target[:, None] == np.arange(128)[None, :]).astype(np.float32)).astype(BF)


def halves(a):
    m = a.shape[1] // 2
    return jnp.concatenate([a[:, :m], a[:, m:]], axis=0)


SWAP = [(0, 1), (1, 0)]
UP = [(i, (i + 1) % 4) for i in range(4)]
DOWN = [(i, (i + 3) % 4) for i in range(4)]
Z_OFFSETS = (0, -1, 1, 2)


def together(*values):
    return lax.optimization_barrier(values)


def up(a):
    return lax.ppermute(a, "z", UP)


def down(a):
    return lax.ppermute(a, "z", DOWN)


def across(a):
    return lax.ppermute(a, "xl", SWAP)


def gather_pair(own, other, single):
    xh = lax.axis_index("xh")
    parts = [jnp.where(xh == 0, own, other), jnp.where(xh == 0, other, own)]
    if single is not None:
        parts.append(single)
    packed = jnp.concatenate(parts, axis=0)
    g = lax.all_gather(packed, ("y", "c"), axis=0, tiled=False)
    return g.reshape((4, 2) + packed.shape)


def add(*terms):
    return sum(t.astype(F32) for t in terms)


def scatter_sum(near, owns, sides):
    own, side, down_own, down_side, up_own, up_side, far_own, far_side = [near[b] for b in range(8)]
    from_side = lax.ppermute(sides, "xl", SWAP)
    via_below = lax.ppermute(far_own, "z", UP)
    via_above = lax.ppermute(far_side, "z", DOWN)
    up_side = lax.ppermute(up_side, "z", UP)
    down_own = lax.ppermute(down_own, "z", DOWN)
    up_own = lax.ppermute(add(up_own, via_below).astype(BF), "z", UP)
    down_side = lax.ppermute(add(down_side, via_above).astype(BF), "z", DOWN)
    side = lax.ppermute(add(side, up_side, down_side).astype(BF), "xl", SWAP)
    first = add(own, up_own, down_own, side)
    t = add(owns, from_side)
    far = t[3].astype(BF)
    half_up = lax.ppermute(far[:64], "z", UP)
    half_down = lax.ppermute(far[64:], "z", DOWN)
    up = jnp.concatenate([t[2, :64] + half_up.astype(F32), t[2, 64:]], axis=0).astype(BF)
    down = jnp.concatenate([t[1, :64], t[1, 64:] + half_down.astype(F32)], axis=0).astype(BF)
    second = add(t[0], lax.ppermute(up, "z", UP), lax.ppermute(down, "z", DOWN))
    return jnp.concatenate([first, second], axis=1)


def local(
    inputs,
    output_cotangent,
    block_index_per_position,
    adapter_index_per_run,
    norm_gain,
    norm_bias,
    query_weight,
    key_weight,
    value_weight,
    dense_weight,
    query_bias,
    key_bias,
    value_bias,
    dense_bias,
    feedforward_in_weight,
    feedforward_in_bias,
    feedforward_out_weight,
    feedforward_out_bias,
    adapter_attention_down,
    adapter_attention_up,
    adapter_dense_down,
    adapter_dense_up,
    adapter_feedforward_in_down,
    adapter_feedforward_in_up,
    adapter_feedforward_out_down,
    adapter_feedforward_out_up,
):
    xl, z, c = lax.axis_index("xl"), lax.axis_index("z"), lax.axis_index("c")
    xh = lax.axis_index("xh")
    j = xl * 4 + z
    x_own = inputs[0]
    dy_own = output_cotangent[0]
    run_adapter = adapter_index_per_run[0, 0].astype(F32).astype(BF)
    block_row = block_index_per_position[0]
    z_of = [lax.rem(z + o + 4, 4) for o in Z_OFFSETS]
    spots = [(xl if side == 0 else 1 - xl) * 4 + zz for zz in z_of for side in range(2)]
    scal = jnp.stack(spots + [c, j, xl, z] + z_of).astype(jnp.int32)

    def row_half(a):
        n = a.shape[0] // 2
        return lax.dynamic_slice_in_dim(a, c * n, n, 0)

    def col_half(a):
        n = a.shape[1] // 2
        return lax.dynamic_slice_in_dim(a, c * n, n, 1)

    def head_cols(a):
        return jnp.concatenate(
            [lax.dynamic_slice_in_dim(a, (2 * i + xl) * 256 + z * 64, 64, 1) for i in range(4)], axis=1
        )

    def hidden_cols(a):
        return jnp.concatenate(
            [lax.dynamic_slice_in_dim(a, 1024 * w + 128 * j, 128, 1) for w in range(8)], axis=1
        )

    qkv_half = jnp.concatenate(
        [head_cols(row_half(a)) for a in (query_weight, key_weight, value_weight)], axis=1
    )
    downs_own = jnp.concatenate([adapter_attention_down[0].reshape(48, 2048), adapter_feedforward_in_down[0]], axis=0)
    downs_half = row_half(downs_own)
    ups64 = jnp.concatenate(
        [head_cols(adapter_attention_up[0, p]) for p in range(3)] + [head_cols(adapter_dense_down[0])], axis=0
    )

    def head_bias(a):
        return lax.dynamic_slice_in_dim(a, z * 64, 64, 0)

    row1 = jnp.concatenate(
        [head_bias(query_bias), head_bias(key_bias), head_bias(value_bias), jnp.zeros((64,), BF)]
    )
    row2 = jnp.concatenate(
        [lax.dynamic_slice_in_dim(feedforward_in_bias, 128 * j, 128, 0), jnp.zeros((128,), BF)]
    )
    misc64 = jnp.concatenate(
        [
            jnp.stack([norm_gain, norm_bias, dense_bias, feedforward_out_bias, row1, row2]),
            jnp.zeros((58, 256), BF),
        ],
        axis=0,
    )
    side = jnp.concatenate([jnp.where(c == 0, ups64, misc64), jnp.zeros((64, 256), BF)], axis=0)
    own1 = jnp.concatenate(
        [
            jnp.concatenate([qkv_half, side], axis=1),
            halves(downs_half[:16]),
            halves(downs_half[16:]),
            col_half(adapter_dense_up[0]),
        ],
        axis=0,
    )
    dense_rows = row_half(lax.dynamic_slice_in_dim(dense_weight, 64 * z, 64, 0))
    dense_piece = halves(dense_rows)
    own2 = jnp.concatenate(
        [
            hidden_cols(row_half(feedforward_in_weight)),
            hidden_cols(jnp.where(c == 0, adapter_feedforward_in_up[0], adapter_feedforward_out_down[0])),
            halves(row_half(lax.dynamic_slice_in_dim(feedforward_out_weight, 128 * j, 128, 0))),
            col_half(adapter_feedforward_out_up[0]),
        ],
        axis=0,
    )

    x_send = jnp.concatenate([x_own, jnp.full((128, 128), run_adapter, BF)], axis=1)
    sent1 = jnp.concatenate([own1, dense_piece], axis=0)
    x_up, x_down, x_side, other1 = together(
        up(x_send), down(x_send), across(x_send), lax.ppermute(sent1, "xh", SWAP)
    )
    g1 = gather_pair(own1, other1[:MAIN], jnp.where(xh == xl, dense_piece, other1[MAIN:]))
    own2, x_up, x_down, x_side = together(own2, x_up, x_down, x_side)
    x_up_side, x_down_side, other2 = together(up(x_side), down(x_side), lax.ppermute(own2, "xh", SWAP))
    g2 = gather_pair(own2, other2, None)
    x_up, x_down_side, dy_own = together(x_up, x_down_side, dy_own)
    x_far, x_far_side, dy_side = together(up(x_up), down(x_down_side), across(dy_own))
    dy_own, dy_side = together(dy_own, dy_side, x_far)[:2]
    dy_up, dy_down = together(up(dy_own), down(dy_own))
    dy_side, dy_up, dy_down = together(dy_side, dy_up, dy_down)
    dy_up_side, dy_down_side = together(up(dy_side), down(dy_side))
    dy_up, dy_down_side = together(dy_up, dy_down_side)
    dy_far, dy_far_side = up(dy_up), down(dy_down_side)
    x_blocks = [x_send, x_side, x_up, x_up_side, x_down, x_down_side, x_far, x_far_side]
    dy_blocks = [dy_own, dy_side, dy_up, dy_up_side, dy_down, dy_down_side, dy_far, dy_far_side]

    def side_of(core):
        return jnp.stack(
            [g1[:, core, MAIN * h : MAIN * h + 64, 768:] for h in range(2)], axis=1
        ).reshape(8, 64, 256)

    ups_all = side_of(0).reshape(8, 4, 16, 256).transpose(1, 0, 2, 3).reshape(4, 128, 256)
    ups = jnp.concatenate([ups_all[0], ups_all[1], ups_all[2]], axis=1)
    dd = ups_all[3]
    small_all = side_of(1)[:, :6].astype(F32)
    misc = small_all[:, :4].transpose(1, 0, 2).reshape(4, 2048)
    head_b = lax.dynamic_index_in_dim(small_all[:, 4, :192].reshape(4, 2, 3, 64), xl, 1, keepdims=False)
    bias_qkv = head_b.transpose(1, 0, 2).reshape(1, 768)
    b1 = small_all[:, 5, :128].reshape(1, 1024)

    spread = jnp.stack(spots)
    my_positions = ((spread * 2 + c) * 128)[:, None] + jnp.arange(128, dtype=jnp.int32)[None, :]
    cos_mine, sin_mine = rotary_tables(my_positions.reshape(1024))
    cos_all, sin_all = rotary_tables(jnp.arange(2048, dtype=jnp.int32))

    hb, inner, qkv_keep, qkv_send, aid = k1(x_blocks, scal, g1, ups, misc[:2], bias_qkv, cos_mine, sin_mine)
    qkv_recv = lax.ppermute(qkv_send, "c", SWAP)
    dob_keep, dob_send, gdense = k1b(dy_blocks, scal, aid, g1, dd)
    dob_recv = lax.ppermute(dob_send, "c", SWAP)

    idrow = jnp.broadcast_to(block_row[None, :], (8, 2048))
    idcol = jnp.broadcast_to(block_row[:, None], (2048, 128))
    att_keep, att_send = k3(scal, qkv_keep, qkv_recv, dob_keep, dob_recv, idrow, idcol, cos_all, sin_all)
    att_recv = lax.ppermute(att_send, "c", SWAP)

    fold = fold_matrix()
    low_fold = jnp.concatenate([fold[640:], fold[512:640]], axis=0)
    out_part, gb, slope, small, gdd = k2a(
        scal, hb, aid, inner, gdense, att_keep, att_recv, g1, g2, dd, b1, low_fold
    )
    out_sum = lax.psum_scatter(out_part.reshape(1024, 2048), TP, scatter_dimension=0, tiled=True)
    near, owns, sides, small, gup1, gd2, gqkv = k2b(
        dy_blocks, scal, aid, inner, att_keep, att_recv, gb, slope, small, g1, g2, ups, fold[:512]
    )
    dh_sum = scatter_sum(near, owns, sides)

    small = lax.all_to_all(small.reshape(8, 128, 128), TP, 0, 0, tiled=True)
    small = jnp.sum(small.astype(F32), axis=0).astype(BF)
    small = lax.all_to_all(jnp.broadcast_to(small[None], (8, 128, 128)), TP, 0, 0, tiled=True)
    gdown, gup = k5(scal, small, aid, hb, fold.T, dy_blocks)

    gdown = gdown.reshape(4, 8, 16, 256).transpose(1, 2, 0, 3).reshape(8, 16, 1024)
    gqkvd = jnp.concatenate([gqkv, gdd], axis=1).reshape(8, 16, 1024)
    gup = gup.reshape(2, 8, 16, 256).transpose(1, 2, 0, 3).reshape(8, 16, 512)
    gup = jnp.concatenate([gup, jnp.zeros_like(gup)], axis=2)
    grads = jnp.concatenate([gdown, gqkvd, gup1.reshape(8, 16, 1024), gd2.reshape(8, 16, 1024), gup], axis=1)
    keep = lax.dynamic_slice_in_dim(grads, 40 * c, 40, 1)
    send = lax.dynamic_slice_in_dim(grads, 40 * (1 - c), 40, 1).astype(BF)
    grads = (keep + lax.ppermute(send, "c", SWAP).astype(F32)).astype(BF)
    grads = lax.all_to_all(grads, WSH, 0, 0, tiled=True)
    grads = jnp.sum(grads.astype(F32), axis=0).astype(BF)
    grads = lax.all_to_all(jnp.broadcast_to(grads[None], (16, 40, 1024)), CTX, 0, 0, tiled=True)
    grads = grads.reshape(8, 80, 1024).astype(F32)

    def from_heads(a):
        return a.reshape(2, 4, 16, 4, 64).transpose(2, 3, 0, 1, 4).reshape(16, 2048)

    def from_blocks(a):
        return a.transpose(1, 0, 2).reshape(16, 2048)

    def from_hidden(a):
        return a.reshape(8, 16, 8, 128).transpose(1, 2, 0, 3).reshape(16, 8192)

    downs_g = [from_blocks(grads[:, :16, 256 * p : 256 * p + 256]) for p in range(4)]
    ups_g = [from_heads(grads[:, 16:32, 256 * p : 256 * p + 256]) for p in range(4)]
    gup1 = from_hidden(grads[:, 32:48])
    gd2 = from_hidden(grads[:, 48:64])
    gud = from_blocks(grads[:, 64:80, :256])
    gu2 = from_blocks(grads[:, 64:80, 256:512])

    source = x_own.astype(F32)
    outputs = (source + out_sum.astype(F32) + misc[2:3] + misc[3:4]).astype(BF)[None]
    mean = jnp.mean(source, axis=1, keepdims=True)
    center = source - mean
    inv = lax.rsqrt(jnp.mean(center * center, axis=1, keepdims=True) + EPSILON)
    hn = center * inv
    e = dh_sum.astype(F32) * misc[0:1]
    dx = (e - jnp.mean(e, axis=1, keepdims=True) - hn * jnp.mean(e * hn, axis=1, keepdims=True)) * inv
    grad_inputs = (dy_own.astype(F32) + dx).astype(BF)[None]
    return (
        outputs,
        grad_inputs,
        jnp.stack(downs_g[:3])[None],
        jnp.stack(ups_g[:3])[None],
        ups_g[3][None],
        gud[None],
        downs_g[3][None],
        gup1[None],
        gd2[None],
        gu2[None],
    )


def solution(mesh):
    fine = Mesh(np.asarray(mesh.devices).reshape(2, 4, 2, 4, 2), ("xl", "z", "c", "y", "xh"))
    tokens = P(WSH, CTX, None)
    w1 = P(WSH)
    w2 = P(WSH, None)
    w3 = P(WSH, None, None)
    w4 = P(WSH, None, None, None)
    placed = (tokens, tokens, w2, P(WSH, CTX)) + (w1, w1, w2, w2, w2, w2, w1, w1, w1, w1, w2, w1, w2, w1)
    placed = placed + (w4, w4, w3, w3, w3, w3, w3, w3)
    return jax.shard_map(
        local,
        mesh=fine,
        in_specs=placed,
        out_specs=(tokens, tokens, w4, w4, w3, w3, w3, w3, w3, w3),
        check_vma=False,
    )
```

```python
import functools

import jax
import jax.numpy as jnp
import numpy as np
from jax import lax
from jax.experimental import pallas as pl
from jax.experimental.pallas import tpu as pltpu
from jax.sharding import Mesh, PartitionSpec as P

ADAPTERS = 8
RANK = 16
EPSILON = 1e-05
GELU_SCALE = 0.7978845608028654
NEGATIVE = -1e30
SCALE = 64 ** -0.5
BF = jnp.bfloat16
F32 = jnp.float32
WSH = ("y", "xh")
TP = ("xl", "z")
CTX = ("xl", "z", "c")
VMEM_LIMIT = 58 * 1024 * 1024


def nn(a, b):
    return lax.dot_general(a, b, (((1,), (0,)), ((), ())), preferred_element_type=F32)


def nt(a, b):
    return lax.dot_general(a, b, (((1,), (1,)), ((), ())), preferred_element_type=F32)


def tn(a, b):
    return lax.dot_general(a, b, (((0,), (0,)), ((), ())), preferred_element_type=F32)


def adapter_mask(aid, columns):
    col = lax.broadcasted_iota(jnp.int32, (aid.shape[0], columns), 1)
    return (lax.shift_right_logical(col, 4) & 7) == aid.astype(jnp.int32)


def turn(values, cosine, sine):
    width = values.shape[1]
    lane = lax.broadcasted_iota(jnp.int32, values.shape, 1) & 63
    partner = jnp.where(
        lane < 16, pltpu.roll(values, width - 16, 1), pltpu.roll(values, 16, 1)
    )
    return values * cosine + partner * sine


ANY = pl.BlockSpec(memory_space=pl.ANY)
SMEM = pl.BlockSpec(memory_space=pltpu.SMEM)
VM = pl.BlockSpec(memory_space=pltpu.VMEM)
PARAMS = pltpu.CompilerParams(vmem_limit_bytes=VMEM_LIMIT)
MAIN = 208
SECOND = 288


def whole(shape):
    return pl.BlockSpec(shape, lambda t: (0,) * len(shape), pipeline_mode=pl.Buffered(1))


def start_all(pairs, sem):
    for source, target in pairs:
        pltpu.make_async_copy(source, target, sem).start()


def wait_all(target, sem):
    pltpu.make_async_copy(target, target, sem).wait()


def token_copies(blocks, target):
    pairs = [(blocks[i], target.at[i // 2, i % 2], i) for i in range(6)]
    for i in range(4):
        pairs.append((blocks[6 + i], target.at[3, i // 2, pl.ds(64 * (i % 2), 64)], 6 + i // 2))
    return pairs


def start_tokens(blocks, target, sem, first, last):
    for source, part, i in token_copies(blocks, target):
        if first <= i < last:
            pltpu.make_async_copy(source, part, sem.at[i]).start()


def wait_tokens(target, sem, step):
    for i in range(2):
        part = target.at[step, i]
        pltpu.make_async_copy(part, part, sem.at[2 * step + i]).wait()


def pieces_qkv(g1, target):
    return [
        (
            g1.at[y, c, pl.ds(MAIN * xh, 128), pl.ds(0, 768)],
            target.at[pl.ds((2 * y + xh) * 256 + c * 128, 128), :],
        )
        for y in range(4)
        for xh in range(2)
        for c in range(2)
    ]


def pieces_downs(g1, target):
    return [
        (
            g1.at[:, c, pl.ds(MAIN * xh + 128 + 32 * i + 16 * b, 16), :],
            target.at[c, i, :, xh, :, pl.ds(1024 * b, 1024)],
        )
        for c in range(2)
        for i in range(2)
        for xh in range(2)
        for b in range(2)
    ]


def pieces_rank(g, base, stride, target, row):
    return [
        (
            g.at[y, c, pl.ds(stride * xh + base, 16), :],
            target.at[pl.ds(row + (2 * y + xh) * 16, 16), pl.ds(1024 * c, 1024)],
        )
        for y in range(4)
        for xh in range(2)
        for c in range(2)
    ]


def pieces_dense(g1, target, row):
    return [
        (
            g1.at[y, c, pl.ds(2 * MAIN + 32 * b, 32), :],
            target.at[pl.ds(row + 64 * y + 32 * c, 32), pl.ds(1024 * b, 1024)],
        )
        for y in range(4)
        for c in range(2)
        for b in range(2)
    ]


def pieces_w1(g2, target):
    return [
        (
            g2.at[y, c, pl.ds(SECOND * xh, 128), :],
            target.at[pl.ds((2 * y + xh) * 256 + c * 128, 128), :],
        )
        for y in range(4)
        for xh in range(2)
        for c in range(2)
    ]


def pieces_sixteen(g2, c, target, row):
    return [
        (
            g2.at[y, c, pl.ds(SECOND * xh + 128, 16), :],
            target.at[pl.ds(row + (2 * y + xh) * 16, 16), :],
        )
        for y in range(4)
        for xh in range(2)
    ]


def pieces_w2(g2, target):
    return [
        (
            g2.at[y, c, pl.ds(SECOND * xh + 144 + 64 * b, 64), :],
            target.at[pl.ds((2 * y + xh) * 128 + c * 64, 64), pl.ds(1024 * b, 1024)],
        )
        for y in range(4)
        for xh in range(2)
        for c in range(2)
        for b in range(2)
    ]


def block_diagonal(source, target):
    target[...] = jnp.zeros_like(target)
    for p in range(3):
        cols = slice(256 * p, 256 * p + 256)
        target[128 * p : 128 * p + 128, cols] = source[:, cols]


def k1_body(*refs):
    blocks, refs = refs[:10], refs[10:]
    (scal_ref, g1_ref, up_ref, misc_ref, bias_ref, cos_ref, sin_ref,
     hb_ref, inner_ref, keep_ref, send_ref, aid_ref, x_s, w_s, down_s, up_s, x_sem, w_sem) = refs
    step = pl.program_id(0)

    @pl.when(step == 0)
    def _():
        start_tokens(blocks, x_s, x_sem, 0, 2)
        start_all(pieces_downs(g1_ref, down_s), w_sem.at[0])
        start_all(pieces_qkv(g1_ref, w_s.at[:, pl.ds(0, 768)]), w_sem.at[1])
        start_tokens(blocks, x_s, x_sem, 2, 8)

    wait_tokens(x_s, x_sem, step)
    tile = x_s[step].reshape(256, 2176)
    x = tile[:, :2048].astype(F32)
    aid_ref[...] = tile[:, 2048:]
    aid = tile[:, 2048:2049].astype(F32)
    mean = jnp.mean(x, axis=1, keepdims=True)
    center = x - mean
    spread = jnp.mean(center * center, axis=1, keepdims=True)
    h = center * lax.rsqrt(spread + EPSILON) * misc_ref[0:1, :] + misc_ref[1:2, :]
    hb = h.astype(BF)
    hb_ref[...] = hb

    @pl.when(step == 0)
    def _():
        block_diagonal(up_ref, up_s)
        wait_all(down_s, w_sem.at[0])
        w_s[:, 768:] = down_s[...].reshape(512, 2048).T
        wait_all(w_s.at[:, pl.ds(0, 768)], w_sem.at[1])

    pre_all = nn(hb, w_s[...])
    inner = jnp.where(adapter_mask(aid, 512), pre_all[:, 768:], 0.0).astype(BF)
    inner_ref[...] = inner
    pre_all = pre_all[:, :768] + nn(inner[:, :384], up_s[...]) + bias_ref[...]
    first_core = scal_ref[8] == 0
    cosine = jnp.concatenate([cos_ref[...]] * 2, axis=1)
    sine = jnp.concatenate([sin_ref[...]] * 2, axis=1)
    for p in range(3):
        cols = slice(256 * p, 256 * p + 256)
        pre = pre_all[:, cols]
        if p < 2:
            pre = turn(pre, cosine, sine)
        low = pre.astype(BF)
        keep_ref[p] = jnp.where(first_core, low[:, :128], low[:, 128:])
        send_ref[p] = jnp.where(first_core, low[:, 128:], low[:, :128])


def k1(blocks, scal, g1, ups, misc, bias, cosine, sine):
    rows = 256
    return pl.pallas_call(
        k1_body,
        grid=(4,),
        in_specs=[ANY] * 10
        + [
            SMEM,
            ANY,
            whole((128, 768)),
            whole((2, 2048)),
            whole((1, 768)),
            pl.BlockSpec((rows, 128), lambda t: (t, 0)),
            pl.BlockSpec((rows, 128), lambda t: (t, 0)),
        ],
        out_specs=[
            pl.BlockSpec((rows, 2048), lambda t: (t, 0)),
            pl.BlockSpec((rows, 512), lambda t: (t, 0)),
            pl.BlockSpec((3, rows, 128), lambda t: (0, t, 0)),
            pl.BlockSpec((3, rows, 128), lambda t: (0, t, 0)),
            pl.BlockSpec((rows, 128), lambda t: (t, 0)),
        ],
        out_shape=[
            jax.ShapeDtypeStruct((1024, 2048), BF),
            jax.ShapeDtypeStruct((1024, 512), BF),
            jax.ShapeDtypeStruct((3, 1024, 128), BF),
            jax.ShapeDtypeStruct((3, 1024, 128), BF),
            jax.ShapeDtypeStruct((1024, 128), BF),
        ],
        scratch_shapes=[
            pltpu.VMEM((4, 2, 128, 2176), BF),
            pltpu.VMEM((2048, 1280), BF),
            pltpu.VMEM((2, 2, 4, 2, 16, 2048), BF),
            pltpu.VMEM((384, 768), BF),
            pltpu.SemaphoreType.DMA((8,)),
            pltpu.SemaphoreType.DMA((2,)),
        ],
        compiler_params=PARAMS,
        cost_estimate=pl.CostEstimate(flops=6_000_000_000, bytes_accessed=20_000_000, transcendentals=0),
        name="norm_qkv",
    )(*blocks, scal, g1, ups, misc, bias, cosine, sine)


def k1b_body(*refs):
    blocks, refs = refs[:10], refs[10:]
    scal_ref, aid_ref, g1_ref, dd_ref, keep_ref, send_ref, ginner_ref, dy_s, w_s, dy_sem, w_sem = refs
    start_all(pieces_dense(g1_ref, w_s, 0) + pieces_rank(g1_ref, 192, MAIN, w_s, 256), w_sem)
    start_tokens(blocks, dy_s, dy_sem, 0, 8)
    wait_all(w_s, w_sem)
    for step in range(4):
        wait_tokens(dy_s, dy_sem, step)
    first_core = scal_ref[8] == 0
    both = nt(dy_s[...].reshape(1024, 2048), w_s[...])
    aid = aid_ref[:, 0:1].astype(F32)
    ginner = jnp.where(adapter_mask(aid, 128), both[:, 256:], 0.0).astype(BF)
    ginner_ref[...] = ginner
    dob = (both[:, :256] + nn(ginner, dd_ref[...])).astype(BF)
    keep_ref[...] = jnp.where(first_core, dob[:, :128], dob[:, 128:])
    send_ref[...] = jnp.where(first_core, dob[:, 128:], dob[:, :128])


def k1b(blocks, scal, aid, g1, dd):
    return pl.pallas_call(
        k1b_body,
        in_specs=[ANY] * 10 + [SMEM, VM, ANY, VM],
        out_specs=[VM, VM, VM],
        out_shape=[jax.ShapeDtypeStruct((1024, 128), BF)] * 3,
        scratch_shapes=[
            pltpu.VMEM((4, 2, 128, 2048), BF),
            pltpu.VMEM((384, 2048), BF),
            pltpu.SemaphoreType.DMA((8,)),
            pltpu.SemaphoreType.DMA,
        ],
        compiler_params=PARAMS,
        cost_estimate=pl.CostEstimate(flops=2_000_000_000, bytes_accessed=8_000_000, transcendentals=0),
        name="attention_output_grad",
    )(*blocks, scal, aid, g1, dd)


def k3_body(
    scal_ref, qkv_keep, qkv_recv, dob_keep, dob_recv, idrow_ref, idcol_ref, cos_ref, sin_ref,
    keep_out, send_out, x_s, out_s, kt_s, vt_s, dk_s, dv_s, sem, sem_out,
):
    core = scal_ref[8]
    copies = []
    for b in range(8):
        rows = pl.ds(128 * b, 128)
        spot = scal_ref[b]
        for side, (qkv, dob) in enumerate(((qkv_keep, dob_keep), (qkv_recv, dob_recv))):
            parity = core if side == 0 else 1 - core
            copies.append((qkv.at[:, rows, :], x_s.at[pl.ds(0, 3), spot, parity]))
            copies.append((dob.at[rows, :], x_s.at[3, spot, parity]))
    start_all(copies, sem)
    dk_s[...] = jnp.zeros_like(dk_s)
    dv_s[...] = jnp.zeros_like(dv_s)
    wait_all(x_s, sem)
    kt_s[...] = x_s[1].reshape(2048, 128).T
    vt_s[...] = x_s[2].reshape(2048, 128).T
    tile = 256
    lane = lax.broadcasted_iota(jnp.int32, (tile, 128), 1)

    def span(i, start, stop):
        return x_s[i, start // 256 : stop // 256].reshape(stop - start, 128)

    for t in range(8):
        start, stop = tile * t, tile * t + tile
        length = min(stop + tile, 2048)
        q = span(0, start, stop)
        dob = span(3, start, stop)
        zero = jnp.zeros_like(q)
        q2 = jnp.concatenate([jnp.where(lane < 64, q, zero), jnp.where(lane < 64, zero, q)], axis=0)
        d2 = jnp.concatenate([jnp.where(lane < 64, dob, zero), jnp.where(lane < 64, zero, dob)], axis=0)
        query_ids = idrow_ref[0:1, start:stop]
        query_ids = jnp.concatenate([query_ids, query_ids], axis=1)
        allowed = idcol_ref[start:length, 0:1] <= query_ids
        s = jnp.where(allowed, nt(span(1, start, length), q2), NEGATIVE)
        largest = jnp.max(s, axis=0, keepdims=True)
        if start:
            s_head = nt(span(1, 0, start), q2)
            largest = jnp.maximum(largest, jnp.max(s_head, axis=0, keepdims=True))
            s = jnp.concatenate([s_head, s], axis=0)
        e = jnp.exp((s - largest) * SCALE)
        recip = 1.0 / jnp.sum(e, axis=0, keepdims=True)
        p = e * recip
        pb = p.astype(BF)
        dp = nt(span(2, 0, length), d2)
        delta = jnp.sum(p * dp, axis=0, keepdims=True)
        ds = (p * (dp - delta)).astype(BF)
        dk_s[:length] += nn(ds, q2)
        dv_s[:length] += nn(pb, d2)
        ot = nn(vt_s[:, :length], pb)
        dqt = nn(kt_s[:, :length], ds)
        o_parts = [ot[:64, :256], ot[64:, 256:]]
        dq_parts = [dqt[:64, :256], dqt[64:, 256:]]
        o = jnp.concatenate(o_parts, axis=0).T
        dq = jnp.concatenate(dq_parts, axis=0).T * SCALE
        rows = slice(start, stop)
        out_s[0, t] = o.astype(BF).reshape(2, 128, 128)
        out_s[1, t] = turn(dq, cos_ref[rows], -sin_ref[rows]).astype(BF).reshape(2, 128, 128)
    out_s[2] = turn(dk_s[...] * SCALE, cos_ref[...], -sin_ref[...]).astype(BF).reshape(8, 2, 128, 128)
    out_s[3] = dv_s[...].astype(BF).reshape(8, 2, 128, 128)
    copies = []
    for b in range(8):
        rows = pl.ds(128 * b, 128)
        spot = scal_ref[b]
        copies.append((out_s.at[:, spot, core], keep_out.at[:, rows, :]))
        copies.append((out_s.at[:, spot, 1 - core], send_out.at[:, rows, :]))
    start_all(copies, sem_out)
    wait_all(out_s, sem_out)


def k3(scal, qkv_keep, qkv_recv, dob_keep, dob_recv, idrow, idcol, cosine, sine):
    vm = pl.BlockSpec(memory_space=pltpu.VMEM)
    return pl.pallas_call(
        k3_body,
        in_specs=[SMEM] + [ANY] * 4 + [vm] * 4,
        out_specs=[ANY, ANY],
        out_shape=[jax.ShapeDtypeStruct((4, 1024, 128), BF)] * 2,
        scratch_shapes=[
            pltpu.VMEM((4, 8, 2, 128, 128), BF),
            pltpu.VMEM((4, 8, 2, 128, 128), BF),
            pltpu.VMEM((128, 2048), BF),
            pltpu.VMEM((128, 2048), BF),
            pltpu.VMEM((2048, 128), F32),
            pltpu.VMEM((2048, 128), F32),
            pltpu.SemaphoreType.DMA,
            pltpu.SemaphoreType.DMA,
        ],
        compiler_params=PARAMS,
        cost_estimate=pl.CostEstimate(flops=15_000_000_000, bytes_accessed=8_000_000, transcendentals=5_000_000),
        name="attention",
    )(scal, qkv_keep, qkv_recv, dob_keep, dob_recv, idrow, idcol, cosine, sine)


def heads_of(keep_ref, recv_ref, i, first_core):
    a, b = keep_ref[i], recv_ref[i]
    return jnp.concatenate([jnp.where(first_core, a, b), jnp.where(first_core, b, a)], axis=1)


def tile_spec(width, rows=256):
    return pl.BlockSpec((rows, width), lambda t, s: (t, 0))


def const_spec(shape):
    return pl.BlockSpec(shape, lambda t, s: (0,) * len(shape), pipeline_mode=pl.Buffered(1))


def placed_spec(width):
    return pl.BlockSpec((2, 1, 128, width), lambda t, s: (0, s[12 + t], 0, 0))


def place(ref, xl, value):
    ref[xl, 0] = value[:128]
    ref[1 - xl, 0] = value[128:]


def accumulate(step, pairs):
    @pl.when(step == 0)
    def _():
        for ref, value in pairs:
            ref[...] = value

    @pl.when(step > 0)
    def _():
        for ref, value in pairs:
            ref[...] += value


def k2m_body(scal_ref, *refs):
    blocks, refs = refs[:10], refs[10:]
    (hb_ref, aid_ref, inner_ref, gdense_ref, keep_ref, recv_ref, g2_ref, up_ref, dd_ref, b1_ref, fold_ref,
     gb_ref, df_ref, low_out_ref, low_in_ref, small_ref, gup1_ref, gd2_ref, gdd_ref,
     dy_s, w1_s, w2_s, d2_s, up_s, dy_sem, sems) = refs
    step = pl.program_id(0)

    @pl.when(step == 0)
    def _():
        start_all(pieces_w1(g2_ref, w1_s) + pieces_sixteen(g2_ref, 0, w1_s, 2048), sems.at[0])
        start_all(pieces_sixteen(g2_ref, 1, d2_s, 0), sems.at[1])
        start_tokens(blocks, dy_s, dy_sem, 0, 2)
        start_all(pieces_w2(g2_ref, w2_s) + pieces_rank(g2_ref, 272, SECOND, w2_s, 1024), sems.at[2])
        start_tokens(blocks, dy_s, dy_sem, 2, 8)
        block_diagonal(up_ref, up_s)
        wait_all(w1_s, sems.at[0])

    aid = aid_ref[:, 0:1].astype(F32)
    first_core = scal_ref[8] == 0
    f = nn(jnp.concatenate([hb_ref[...], inner_ref[...]], axis=1), w1_s[...]) + b1_ref[...]

    @pl.when(step == 0)
    def _():
        wait_all(w2_s, sems.at[2])
        wait_all(d2_s, sems.at[1])

    wait_tokens(dy_s, dy_sem, step)
    wide = nt(dy_s[step].reshape(256, 2048), w2_s[...])
    square = f * f
    th = jnp.tanh(GELU_SCALE * f * (1.0 + 0.044715 * square))
    half = 0.5 * (1.0 + th)
    gb = (f * half).astype(BF)
    gb_ref[...] = gb
    slope = half + (0.5 * GELU_SCALE) * f * (1.0 - th * th) * (1.0 + 3 * 0.044715 * square)
    ginner2 = jnp.where(adapter_mask(aid, 128), wide[:, 1024:], 0.0).astype(BF)
    ob = heads_of(keep_ref, recv_ref, 0, first_core)
    dpre = jnp.concatenate([heads_of(keep_ref, recv_ref, p, first_core) for p in (1, 2, 3)], axis=1)
    inner2 = nt(gb, d2_s[...])
    innerd = nt(ob, dd_ref[...])
    ginner = nt(dpre, up_s[...])
    df = ((wide[:, :1024] + nn(ginner2, d2_s[...])) * slope).astype(BF)
    df_ref[...] = df
    ginner1 = nt(df, w1_s[2048:])
    low = jnp.concatenate([ginner, ginner1, innerd, inner2], axis=1)
    low = jnp.where(adapter_mask(aid, 768), low, 0.0).astype(BF)
    low_in_ref[...] = low[:, :512]
    low_out_ref[...] = low[:, 512:]
    place(small_ref, scal_ref[10], nn(low, fold_ref[...]).astype(BF))
    accumulate(
        step,
        [
            (gup1_ref, tn(inner_ref[...], df)),
            (gd2_ref, tn(ginner2, gb)),
            (gdd_ref, tn(gdense_ref[...], ob)),
        ],
    )


def att_spec(first, count):
    return pl.BlockSpec((count, 256, 128), lambda t, s: (first, t, 0))


def k2m(blocks, scal, hb, aid, inner, gdense, keep, recv, g2, ups, dd, b1, fold):
    return pl.pallas_call(
        k2m_body,
        grid_spec=pltpu.PrefetchScalarGridSpec(
            num_scalar_prefetch=1,
            grid=(4,),
            in_specs=[ANY] * 10
            + [
                tile_spec(2048),
                tile_spec(128),
                pl.BlockSpec((256, 128), lambda t, s: (t, 3)),
                tile_spec(128),
                att_spec(0, 4),
                att_spec(0, 4),
                ANY,
                const_spec((128, 768)),
                const_spec((128, 256)),
                const_spec((1, 1024)),
                const_spec((768, 128)),
            ],
            out_specs=[
                tile_spec(1024),
                tile_spec(1024),
                tile_spec(256),
                tile_spec(512),
                placed_spec(128),
                const_spec((128, 1024)),
                const_spec((128, 1024)),
                const_spec((128, 256)),
            ],
            scratch_shapes=[
                pltpu.VMEM((4, 2, 128, 2048), BF),
                pltpu.VMEM((2176, 1024), BF),
                pltpu.VMEM((1152, 2048), BF),
                pltpu.VMEM((128, 1024), BF),
                pltpu.VMEM((384, 768), BF),
                pltpu.SemaphoreType.DMA((8,)),
                pltpu.SemaphoreType.DMA((3,)),
            ],
        ),
        out_shape=[
            jax.ShapeDtypeStruct((1024, 1024), BF),
            jax.ShapeDtypeStruct((1024, 1024), BF),
            jax.ShapeDtypeStruct((1024, 256), BF),
            jax.ShapeDtypeStruct((1024, 512), BF),
            jax.ShapeDtypeStruct((2, 4, 128, 128), BF),
            jax.ShapeDtypeStruct((128, 1024), F32),
            jax.ShapeDtypeStruct((128, 1024), F32),
            jax.ShapeDtypeStruct((128, 256), F32),
        ],
        compiler_params=PARAMS,
        cost_estimate=pl.CostEstimate(flops=14_000_000_000, bytes_accessed=30_000_000, transcendentals=1_000_000),
        name="feed_forward",
    )(scal, *blocks, hb, aid, inner, gdense, keep, recv, g2, ups, dd, b1, fold)


def k2o_body(scal_ref, gb_ref, keep_ref, recv_ref, low_ref, g1_ref, g2_ref, out_ref, w_s, sem):
    step = pl.program_id(0)

    @pl.when(step == 0)
    def _():
        start_all(
            pieces_w2(g2_ref, w_s)
            + pieces_dense(g1_ref, w_s, 1024)
            + pieces_rank(g1_ref, 192, MAIN, w_s, 1280)
            + pieces_rank(g2_ref, 272, SECOND, w_s, 1408),
            sem,
        )
        wait_all(w_s, sem)

    ob = heads_of(keep_ref, recv_ref, 0, scal_ref[8] == 0)
    out = nn(jnp.concatenate([gb_ref[...], ob, low_ref[...]], axis=1), w_s[...]).astype(BF)
    place(out_ref, scal_ref[10], out)


def k2o(scal, gb, keep, recv, low_out, g1, g2):
    return pl.pallas_call(
        k2o_body,
        grid_spec=pltpu.PrefetchScalarGridSpec(
            num_scalar_prefetch=1,
            grid=(4,),
            in_specs=[tile_spec(1024), att_spec(0, 1), att_spec(0, 1), tile_spec(256), ANY, ANY],
            out_specs=[placed_spec(2048)],
            scratch_shapes=[pltpu.VMEM((1536, 2048), BF), pltpu.SemaphoreType.DMA],
        ),
        out_shape=[jax.ShapeDtypeStruct((2, 4, 128, 2048), BF)],
        compiler_params=PARAMS,
        cost_estimate=pl.CostEstimate(flops=7_000_000_000, bytes_accessed=14_000_000, transcendentals=0),
        name="out_rows",
    )(scal, gb, keep, recv, low_out, g1, g2)[0]


def k2h_body(
    scal_ref, df_ref, keep_ref, recv_ref, low_ref, inner_ref, g1_ref, g2_ref,
    near_ref, owns_ref, sides_ref, gqkv_ref, w_s, down_s, sems,
):
    step = pl.program_id(0)

    @pl.when(step == 0)
    def _():
        start_all(
            pieces_w1(g2_ref, w_s.at[:, pl.ds(0, 1024)]) + pieces_qkv(g1_ref, w_s.at[:, pl.ds(1024, 768)]), sems.at[0]
        )
        start_all(pieces_downs(g1_ref, down_s), sems.at[1])
        wait_all(w_s, sems.at[0])
        wait_all(down_s, sems.at[1])

    first_core = scal_ref[8] == 0
    dpre = [heads_of(keep_ref, recv_ref, p, first_core) for p in (1, 2, 3)]
    dh = nt(jnp.concatenate([df_ref[...]] + dpre, axis=1), w_s[...])
    dh = (dh + nn(low_ref[...], down_s[...].reshape(512, 2048))).astype(BF)
    near_ref[0] = dh[:128, :1024]
    near_ref[1] = dh[128:, :1024]
    owns_ref[0] = dh[:128, 1024:]
    sides_ref[0] = dh[128:, 1024:]
    gqkv = [tn(inner_ref[:, 128 * p : 128 * p + 128], dpre[p]) for p in range(3)]
    accumulate(step, [(gqkv_ref, jnp.concatenate(gqkv, axis=1))])


def k2h(scal, df, keep, recv, low_in, inner, g1, g2):
    return pl.pallas_call(
        k2h_body,
        grid_spec=pltpu.PrefetchScalarGridSpec(
            num_scalar_prefetch=1,
            grid=(4,),
            in_specs=[tile_spec(1024), att_spec(0, 4), att_spec(0, 4), tile_spec(512), tile_spec(512), ANY, ANY],
            out_specs=[
                pl.BlockSpec((2, 128, 1024), lambda t, s: (t, 0, 0)),
                pl.BlockSpec((1, 128, 1024), lambda t, s: (t, 0, 0)),
                pl.BlockSpec((1, 128, 1024), lambda t, s: (t, 0, 0)),
                const_spec((128, 768)),
            ],
            scratch_shapes=[
                pltpu.VMEM((2048, 1792), BF),
                pltpu.VMEM((2, 2, 4, 2, 16, 2048), BF),
                pltpu.SemaphoreType.DMA((2,)),
            ],
        ),
        out_shape=[
            jax.ShapeDtypeStruct((8, 128, 1024), BF),
            jax.ShapeDtypeStruct((4, 128, 1024), BF),
            jax.ShapeDtypeStruct((4, 128, 1024), BF),
            jax.ShapeDtypeStruct((128, 768), F32),
        ],
        compiler_params=PARAMS,
        cost_estimate=pl.CostEstimate(flops=10_000_000_000, bytes_accessed=18_000_000, transcendentals=0),
        name="hidden_grad",
    )(scal, df, keep, recv, low_in, inner, g1, g2)


def k5_body(scal_ref, small_ref, aid_ref, hb_ref, spread_ref, gup1_ref, gd2_ref, gqkv_ref, gdd_ref, *refs):
    blocks, refs = refs[:10], refs[10:]
    keep_ref, send_ref, dy_s, sem = refs
    column = pl.multiple_of(256 * scal_ref[9], 256)
    start_all(
        [(source.at[:, pl.ds(column, 256)], part) for source, part, _ in token_copies(blocks, dy_s)], sem
    )
    first_core = scal_ref[8] == 0

    def store(section, left, right):
        kept = jnp.where(first_core, left, right)
        sent = jnp.where(first_core, right, left)
        keep_ref[:, 16 * section : 16 * section + 16] = kept.reshape(8, 16, 512)
        send_ref[:, 16 * section : 16 * section + 16] = sent.astype(BF).reshape(8, 16, 512)

    small = jnp.concatenate([small_ref[scal_ref[b]] for b in range(8)], axis=0)
    aid = aid_ref[:, 0:1].astype(F32)
    wide = jnp.where(adapter_mask(aid, 768), nn(small, spread_ref[...]), 0.0).astype(BF)
    down = tn(wide[:, :512], hb_ref[...])
    store(
        0,
        jnp.concatenate([down[:128], down[128:256]], axis=1),
        jnp.concatenate([down[256:384], down[384:]], axis=1),
    )
    store(1, gqkv_ref[:, :512], jnp.concatenate([gqkv_ref[:, 512:], gdd_ref[...]], axis=1))
    store(2, gup1_ref[:, :512], gup1_ref[:, 512:])
    store(3, gd2_ref[:, :512], gd2_ref[:, 512:])
    wait_all(dy_s, sem)
    up = tn(wide[:, 512:], dy_s[...].reshape(1024, 256))
    left = jnp.concatenate([up[:128], up[128:]], axis=1)
    store(4, left, jnp.zeros_like(left))


def k5(scal, small, aid, hb, spread, gup1, gd2, gqkv, gdd, blocks):
    def const(shape):
        return pl.BlockSpec(shape, lambda t, s: (0,) * len(shape))

    return pl.pallas_call(
        k5_body,
        grid_spec=pltpu.PrefetchScalarGridSpec(
            num_scalar_prefetch=1,
            grid=(1,),
            in_specs=[
                const((8, 128, 128)),
                const((1024, 128)),
                pl.BlockSpec((1024, 256), lambda t, s: (0, s[9])),
                const((128, 768)),
                const((128, 1024)),
                const((128, 1024)),
                const((128, 768)),
                const((128, 256)),
            ]
            + [ANY] * 10,
            out_specs=[const((8, 80, 512)), const((8, 80, 512))],
            scratch_shapes=[pltpu.VMEM((4, 2, 128, 256), BF), pltpu.SemaphoreType.DMA],
        ),
        out_shape=[jax.ShapeDtypeStruct((8, 80, 512), F32), jax.ShapeDtypeStruct((8, 80, 512), BF)],
        compiler_params=PARAMS,
        cost_estimate=pl.CostEstimate(flops=1_500_000_000, bytes_accessed=6_000_000, transcendentals=0),
        name="adapter_grads",
    )(scal, small, aid, hb, spread, gup1, gd2, gqkv, gdd, *blocks)


def kf_body(g_ref, down_ref, up_ref, dd_ref, ud_ref, f1d_ref, f1u_ref, f2d_ref, f2u_ref):
    lane = lax.broadcasted_iota(jnp.int32, (16, 128), 1)

    def part(j, half, section, start, width):
        return g_ref[2 * j + half, 16 * section : 16 * section + 16, start : start + width].astype(F32)

    for j in range(8):
        block = slice(256 * j, 256 * j + 256)
        down_ref[0, :, block] = part(j, 0, 0, 0, 256)
        down_ref[1, :, block] = part(j, 0, 0, 256, 256)
        down_ref[2, :, block] = part(j, 1, 0, 0, 256)
        f1d_ref[:, block] = part(j, 1, 0, 256, 256)
        ud_ref[:, block] = part(j, 0, 4, 0, 256)
        f2u_ref[:, block] = part(j, 0, 4, 256, 256)
        for w in range(8):
            spot = slice(1024 * w + 128 * j, 1024 * w + 128 * j + 128)
            f1u_ref[:, spot] = part(j, w // 4, 2, 128 * (w % 4), 128)
            f2d_ref[:, spot] = part(j, w // 4, 3, 128 * (w % 4), 128)
    for i in range(4):
        for x in range(2):
            for y in range(4):
                for h in range(2):
                    start = 256 * (i % 2) + 128 * (y // 2)
                    a = part(4 * x + 2 * h, i // 2, 1, start, 128)
                    b = part(4 * x + 2 * h + 1, i // 2, 1, start, 128)
                    if y % 2:
                        a = pltpu.roll(a, 64, 1)
                    else:
                        b = pltpu.roll(b, 64, 1)
                    value = jnp.where(lane < 64, a, b)
                    spot = slice(256 * (2 * y + x) + 128 * h, 256 * (2 * y + x) + 128 * h + 128)
                    if i < 3:
                        up_ref[i, :, spot] = value
                    else:
                        dd_ref[:, spot] = value


def kf(grads):
    return pl.pallas_call(
        kf_body,
        in_specs=[VM],
        out_specs=[VM] * 8,
        out_shape=[
            jax.ShapeDtypeStruct((3, 16, 2048), F32),
            jax.ShapeDtypeStruct((3, 16, 2048), F32),
            jax.ShapeDtypeStruct((16, 2048), F32),
            jax.ShapeDtypeStruct((16, 2048), F32),
            jax.ShapeDtypeStruct((16, 2048), F32),
            jax.ShapeDtypeStruct((16, 8192), F32),
            jax.ShapeDtypeStruct((16, 8192), F32),
            jax.ShapeDtypeStruct((16, 2048), F32),
        ],
        compiler_params=PARAMS,
        name="finish",
    )(grads)


def pack1_body(
    scal_ref, wq, wk, wv, wd, ad_ref, fd_ref, au_ref, dd_ref, du_ref, misc_ref, own_ref, other_ref, w_s, d_s, sem, d_sem
):
    c, z = scal_ref[8], scal_ref[11]
    start_all([(w.at[pl.ds(128 * c, 128), :], w_s.at[i]) for i, w in enumerate((wq, wk, wv))], sem)
    start_all([(wd.at[pl.ds(64 * z + 32 * c, 32), :], d_s)], d_sem)
    first_core = c == 0
    odd = lax.rem(z, 2) == 1
    targets = ((own_ref, scal_ref[10], 0), (other_ref, 1 - scal_ref[10], 1))

    def head_pair(read, rows, i, xl):
        lane = lax.broadcasted_iota(jnp.int32, (rows, 128), 1)
        parts = []
        for k in range(2):
            start = (2 * (i + k) + xl) * 256 + (z // 2) * 128
            v = read(pl.ds(pl.multiple_of(start, 128), 128)).astype(F32)
            turned = pltpu.roll(v, 64, 1)
            parts.append(jnp.where(odd, turned, v) if k == 0 else jnp.where(odd, v, turned))
        return jnp.where(lane < 64, parts[0], parts[1]).astype(BF)

    a = jnp.where(first_core, ad_ref[0], ad_ref[2])
    b = jnp.where(first_core, ad_ref[1], fd_ref[...])
    du = jnp.where(first_core, du_ref[:, :1024], du_ref[:, 1024:])
    for out_ref, xl, which in targets:
        for p in range(4):
            for i in (0, 2):
                read = (lambda s, p=p: au_ref[p, :, s]) if p < 3 else (lambda s: dd_ref[:, s])
                value = head_pair(read, 16, i, xl)
                rows = slice(16 * p, 16 * p + 16)
                cols = slice(64 * i, 64 * i + 128)
                out_ref[rows, 768 + 64 * i : 768 + 64 * i + 128] = jnp.where(
                    first_core, value, misc_ref[which, rows, cols]
                )
        out_ref[64:128, 768:] = jnp.zeros((64, 256), BF)
        out_ref[128:144] = a[:, :1024]
        out_ref[144:160] = a[:, 1024:]
        out_ref[160:176] = b[:, :1024]
        out_ref[176:192] = b[:, 1024:]
        out_ref[192:208] = du
    wait_all(d_s, d_sem)
    for out_ref, _, _ in targets:
        out_ref[208:240] = d_s[:, :1024]
        out_ref[240:272] = d_s[:, 1024:]
    wait_all(w_s, sem)
    for p in range(3):
        for i in (0, 2):
            start = 256 * p + 64 * i
            for out_ref, xl, _ in targets:
                out_ref[:128, start : start + 128] = head_pair(lambda s, p=p: w_s[p, :, s], 128, i, xl)


def pack1(scal, wq, wk, wv, wd, ad, fd, au, dd, du, misc):
    return pl.pallas_call(
        pack1_body,
        in_specs=[SMEM] + [ANY] * 4 + [VM] * 6,
        out_specs=[VM, VM],
        out_shape=[jax.ShapeDtypeStruct((272, 1024), BF)] * 2,
        scratch_shapes=[
            pltpu.VMEM((3, 128, 2048), BF),
            pltpu.VMEM((32, 2048), BF),
            pltpu.SemaphoreType.DMA,
            pltpu.SemaphoreType.DMA,
        ],
        compiler_params=PARAMS,
        cost_estimate=pl.CostEstimate(flops=1_000_000, bytes_accessed=4_000_000, transcendentals=0),
        name="pack_qkv",
    )(scal, wq, wk, wv, wd, ad, fd, au, dd, du, misc)


def pack2_body(scal_ref, w1, w2, up_ref, down_ref, up2_ref, own_ref, w1_s, w2_s, sem, sem2):
    c, j = scal_ref[8], scal_ref[9]
    start_all([(w1.at[pl.ds(128 * c, 128), :], w1_s)], sem)
    start_all([(w2.at[pl.ds(128 * j + 64 * c, 64), :], w2_s)], sem2)
    first_core = c == 0
    own_ref[272:288] = jnp.where(first_core, up2_ref[:, :1024], up2_ref[:, 1024:])

    def column(w):
        return pl.ds(pl.multiple_of(1024 * w + 128 * j, 128), 128)

    for w in range(8):
        own_ref[128:144, 128 * w : 128 * w + 128] = jnp.where(first_core, up_ref[:, column(w)], down_ref[:, column(w)])
    wait_all(w2_s, sem2)
    own_ref[144:208] = w2_s[:, :1024]
    own_ref[208:272] = w2_s[:, 1024:]
    wait_all(w1_s, sem)
    for w in range(8):
        own_ref[:128, 128 * w : 128 * w + 128] = w1_s[:, column(w)]


def pack2(scal, w1, w2, up, down, up2):
    return pl.pallas_call(
        pack2_body,
        in_specs=[SMEM, ANY, ANY, VM, VM, VM],
        out_specs=VM,
        out_shape=jax.ShapeDtypeStruct((288, 1024), BF),
        scratch_shapes=[
            pltpu.VMEM((128, 8192), BF),
            pltpu.VMEM((64, 2048), BF),
            pltpu.SemaphoreType.DMA,
            pltpu.SemaphoreType.DMA,
        ],
        compiler_params=PARAMS,
        cost_estimate=pl.CostEstimate(flops=1_000_000, bytes_accessed=4_000_000, transcendentals=0),
        name="pack_hidden",
    )(scal, w1, w2, up, down, up2)


def rotary_tables(positions):
    lane = np.arange(128) % 64
    rate = np.where(lane < 32, 10000.0 ** (-2.0 * (lane % 16) / 32.0), 0.0).astype(np.float32)
    sign = np.where(lane < 16, -1.0, 1.0).astype(np.float32)
    angles = positions.astype(F32)[:, None] * jnp.asarray(rate)[None, :]
    return jnp.cos(angles), jnp.sin(angles) * jnp.asarray(sign)[None, :]


def fold_matrix():
    row = np.arange(768)
    target = (row // 128) * 16 + row % 16
    return jnp.asarray((target[:, None] == np.arange(128)[None, :]).astype(np.float32)).astype(BF)


def halves(a):
    m = a.shape[1] // 2
    return jnp.concatenate([a[:, :m], a[:, m:]], axis=0)


SWAP = [(0, 1), (1, 0)]
FLIP = [(i, 3 - i) for i in range(4)]
UP = [(i, (i + 1) % 4) for i in range(4)]
DOWN = [(i, (i + 3) % 4) for i in range(4)]
Z_OFFSETS = (0, -1, 1, 2)


def together(*values):
    return lax.optimization_barrier(values)


def up(a):
    return lax.ppermute(a, "z", UP)


def down(a):
    return lax.ppermute(a, "z", DOWN)


def across(a):
    return lax.ppermute(a, "xl", SWAP)


def gather_pair(own, other, single):
    xh = lax.axis_index("xh")
    parts = [jnp.where(xh == 0, own, other), jnp.where(xh == 0, other, own)]
    if single is not None:
        parts.append(single)
    packed = jnp.concatenate(parts, axis=0)
    g = lax.all_gather(packed, ("y", "c"), axis=0, tiled=False)
    return g.reshape((4, 2) + packed.shape)


def add(*terms):
    return sum(t.astype(F32) for t in terms)


def scatter_sum(near, owns, sides):
    own, side, down_own, down_side, up_own, up_side, far_own, far_side = [near[b] for b in range(8)]
    from_side = lax.ppermute(sides, "xl", SWAP)
    via_below = lax.ppermute(far_own, "z", UP)
    via_above = lax.ppermute(far_side, "z", DOWN)
    up_side = lax.ppermute(up_side, "z", UP)
    down_own = lax.ppermute(down_own, "z", DOWN)
    up_own = lax.ppermute(add(up_own, via_below).astype(BF), "z", UP)
    down_side = lax.ppermute(add(down_side, via_above).astype(BF), "z", DOWN)
    side = lax.ppermute(add(side, up_side, down_side).astype(BF), "xl", SWAP)
    first = add(own, up_own, down_own, side)
    t = add(owns, from_side)
    far = t[3].astype(BF)
    half_up = lax.ppermute(far[:64], "z", UP)
    half_down = lax.ppermute(far[64:], "z", DOWN)
    up = jnp.concatenate([t[2, :64] + half_up.astype(F32), t[2, 64:]], axis=0).astype(BF)
    down = jnp.concatenate([t[1, :64], t[1, 64:] + half_down.astype(F32)], axis=0).astype(BF)
    second = add(t[0], lax.ppermute(up, "z", UP), lax.ppermute(down, "z", DOWN))
    return jnp.concatenate([first, second], axis=1)


def local(
    inputs,
    output_cotangent,
    block_index_per_position,
    adapter_index_per_run,
    norm_gain,
    norm_bias,
    query_weight,
    key_weight,
    value_weight,
    dense_weight,
    query_bias,
    key_bias,
    value_bias,
    dense_bias,
    feedforward_in_weight,
    feedforward_in_bias,
    feedforward_out_weight,
    feedforward_out_bias,
    adapter_attention_down,
    adapter_attention_up,
    adapter_dense_down,
    adapter_dense_up,
    adapter_feedforward_in_down,
    adapter_feedforward_in_up,
    adapter_feedforward_out_down,
    adapter_feedforward_out_up,
):
    xl, z, c = lax.axis_index("xl"), lax.axis_index("z"), lax.axis_index("c")
    xh = lax.axis_index("xh")
    j = xl * 4 + z
    x_own = inputs[0]
    dy_own = output_cotangent[0]
    run_adapter = adapter_index_per_run[0, 0].astype(F32).astype(BF)
    block_row = block_index_per_position[0]
    z_of = [lax.rem(z + o + 4, 4) for o in Z_OFFSETS]
    spots = [(xl if side == 0 else 1 - xl) * 4 + zz for zz in z_of for side in range(2)]
    scal = jnp.stack(spots + [c, j, xl, z] + z_of).astype(jnp.int32)

    def head_bias(a):
        return lax.dynamic_slice_in_dim(a, z * 64, 64, 0)

    row1 = jnp.concatenate(
        [head_bias(query_bias), head_bias(key_bias), head_bias(value_bias), jnp.zeros((64,), BF)]
    )
    base = jnp.stack([norm_gain, norm_bias, dense_bias, feedforward_out_bias, row1])
    misc_own = []
    for place in (j, (1 - xl) * 4 + z):
        part = lax.dynamic_slice_in_dim(feedforward_in_bias, 128 * place, 128, 0)
        misc_own.append(jnp.pad(jnp.concatenate([base, jnp.pad(part, (0, 128))[None]], axis=0), ((0, 58), (0, 0))))
    misc_own = jnp.stack(misc_own)
    sent1, for_other = pack1(
        scal,
        query_weight,
        key_weight,
        value_weight,
        dense_weight,
        adapter_attention_down[0],
        adapter_feedforward_in_down[0],
        adapter_attention_up[0],
        adapter_dense_down[0],
        adapter_dense_up[0],
        misc_own,
    )
    own2 = pack2(
        scal,
        feedforward_in_weight,
        feedforward_out_weight,
        adapter_feedforward_in_up[0],
        adapter_feedforward_out_down[0],
        adapter_feedforward_out_up[0],
    )
    spread = jnp.stack(spots)
    my_positions = ((spread * 2 + c) * 128)[:, None] + jnp.arange(128, dtype=jnp.int32)[None, :]
    tables = rotary_tables(my_positions.reshape(1024)) + rotary_tables(jnp.arange(2048, dtype=jnp.int32))
    tables = tables + (jnp.broadcast_to(block_row[:, None], (2048, 128)),)
    x_send = jnp.concatenate([x_own, jnp.full((128, 128), run_adapter, BF)], axis=1)

    x_up, x_down, x_side, other1, own2, tables = together(
        up(x_send), down(x_send), across(x_send), lax.ppermute(for_other, ("xl", "xh"), FLIP), own2, tables
    )
    g1 = gather_pair(sent1[:MAIN], other1[:MAIN], jnp.where(xh == xl, sent1[MAIN:], other1[MAIN:]))
    x_up, x_down, x_side, dy_own = together(x_up, x_down, x_side, dy_own)
    x_up_side, x_down_side, x_far_a, x_far_b, dy_side = together(
        up(x_side), down(x_side), up(x_up[:64]), down(x_down[64:]), across(dy_own)
    )
    x_far_side_a, x_far_side_b, dy_up, dy_down, other2 = together(
        across(x_far_a), across(x_far_b), up(dy_own), down(dy_own), lax.ppermute(own2, "xh", SWAP)
    )
    g2 = gather_pair(own2, other2, None)
    dy_side, dy_up, dy_down = together(dy_side, dy_up, dy_down)
    dy_far_a, dy_far_b, dy_up_side, dy_down_side = together(
        up(dy_up[:64]), down(dy_down[64:]), up(dy_side), down(dy_side)
    )
    dy_far_side_a, dy_far_side_b = across(dy_far_a), across(dy_far_b)
    x_blocks = [x_send, x_side, x_up, x_up_side, x_down, x_down_side, x_far_a, x_far_b, x_far_side_a, x_far_side_b]
    dy_blocks = [dy_own, dy_side, dy_up, dy_up_side, dy_down, dy_down_side]
    dy_blocks = dy_blocks + [dy_far_a, dy_far_b, dy_far_side_a, dy_far_side_b]

    def side_of(core):
        return jnp.stack(
            [g1[:, core, MAIN * h : MAIN * h + 64, 768:] for h in range(2)], axis=1
        ).reshape(8, 64, 256)

    ups_all = side_of(0).reshape(8, 4, 16, 256).transpose(1, 0, 2, 3).reshape(4, 128, 256)
    ups = jnp.concatenate([ups_all[0], ups_all[1], ups_all[2]], axis=1)
    dd = ups_all[3]
    small_all = side_of(1)[:, :6].astype(F32)
    misc = small_all[:, :4].transpose(1, 0, 2).reshape(4, 2048)
    head_b = lax.dynamic_index_in_dim(small_all[:, 4, :192].reshape(4, 2, 3, 64), xl, 1, keepdims=False)
    bias_qkv = head_b.transpose(1, 0, 2).reshape(1, 768)
    b1 = small_all[:, 5, :128].reshape(1, 1024)

    cos_mine, sin_mine, cos_all, sin_all, idcol = tables

    hb, inner, qkv_keep, qkv_send, aid = k1(x_blocks, scal, g1, ups, misc[:2], bias_qkv, cos_mine, sin_mine)
    qkv_recv = lax.ppermute(qkv_send, "c", SWAP)
    dob_keep, dob_send, gdense = k1b(dy_blocks, scal, aid, g1, dd)
    dob_recv = lax.ppermute(dob_send, "c", SWAP)

    idrow = jnp.broadcast_to(block_row[None, :], (8, 2048))
    att_keep, att_send = k3(scal, qkv_keep, qkv_recv, dob_keep, dob_recv, idrow, idcol, cos_all, sin_all)
    att_recv = lax.ppermute(att_send, "c", SWAP)

    fold = fold_matrix()
    gb, df, low_out, low_in, small, gup1, gd2, gdd = k2m(
        dy_blocks, scal, hb, aid, inner, gdense, att_keep, att_recv, g2, ups, dd, b1, fold
    )
    small = lax.all_to_all(small.reshape(8, 128, 128), TP, 0, 0, tiled=True)
    out_part = k2o(scal, gb, att_keep, att_recv, low_out, g1, g2)
    out_part, small, df = together(out_part, small, df)
    small = jnp.sum(small.astype(F32), axis=0).astype(BF)
    small = lax.all_to_all(jnp.broadcast_to(small[None], (8, 128, 128)), TP, 0, 0, tiled=True)
    out_sum = lax.psum_scatter(out_part.reshape(1024, 2048), TP, scatter_dimension=0, tiled=True)
    near, owns, sides, gqkv = k2h(scal, df, att_keep, att_recv, low_in, inner, g1, g2)
    dh_sum = scatter_sum(near, owns, sides)

    keep, send = k5(scal, small, aid, hb, fold.T, gup1, gd2, gqkv, gdd, dy_blocks)
    grads = (keep + lax.ppermute(send, "c", SWAP).astype(F32)).astype(BF)
    grads = lax.all_to_all(grads, WSH, 0, 0, tiled=True)
    grads = jnp.sum(grads.astype(F32), axis=0).astype(BF)
    grads = lax.all_to_all(jnp.broadcast_to(grads[None], (16, 80, 512)), CTX, 0, 0, tiled=True)
    down_qkv, up_qkv, gdd, gud, gf1d, gf1u, gf2d, gf2u = kf(grads)

    source = x_own.astype(F32)
    outputs = (source + out_sum.astype(F32) + misc[2:3] + misc[3:4]).astype(BF)[None]
    mean = jnp.mean(source, axis=1, keepdims=True)
    center = source - mean
    inv = lax.rsqrt(jnp.mean(center * center, axis=1, keepdims=True) + EPSILON)
    hn = center * inv
    e = dh_sum.astype(F32) * misc[0:1]
    dx = (e - jnp.mean(e, axis=1, keepdims=True) - hn * jnp.mean(e * hn, axis=1, keepdims=True)) * inv
    grad_inputs = (dy_own.astype(F32) + dx).astype(BF)[None]
    return (
        outputs,
        grad_inputs,
        down_qkv[None],
        up_qkv[None],
        gdd[None],
        gud[None],
        gf1d[None],
        gf1u[None],
        gf2d[None],
        gf2u[None],
    )


def solution(mesh):
    fine = Mesh(np.asarray(mesh.devices).reshape(2, 4, 2, 4, 2), ("xl", "z", "c", "y", "xh"))
    tokens = P(WSH, CTX, None)
    w1 = P(WSH)
    w2 = P(WSH, None)
    w3 = P(WSH, None, None)
    w4 = P(WSH, None, None, None)
    placed = (tokens, tokens, w2, P(WSH, CTX)) + (w1, w1, w2, w2, w2, w2, w1, w1, w1, w1, w2, w1, w2, w1)
    placed = placed + (w4, w4, w3, w3, w3, w3, w3, w3)
    return jax.shard_map(
        local,
        mesh=fine,
        in_specs=placed,
        out_specs=(tokens, tokens, w4, w4, w3, w3, w3, w3, w3, w3),
        check_vma=False,
    )
```

```python
import functools

import jax
import jax.numpy as jnp
import numpy as np
from jax import lax
from jax.experimental import pallas as pl
from jax.experimental.pallas import tpu as pltpu
from jax.sharding import Mesh, PartitionSpec as P

ADAPTERS = 8
RANK = 16
EPSILON = 1e-05
GELU_SCALE = 0.7978845608028654
NEGATIVE = -1e30
SCALE = 64 ** -0.5
BF = jnp.bfloat16
F32 = jnp.float32
WSH = ("y", "xh")
TP = ("xl", "z")
CTX = ("xl", "z", "c")
VMEM_LIMIT = 58 * 1024 * 1024


def nn(a, b):
    return lax.dot_general(a, b, (((1,), (0,)), ((), ())), preferred_element_type=F32)


def nt(a, b):
    return lax.dot_general(a, b, (((1,), (1,)), ((), ())), preferred_element_type=F32)


def tn(a, b):
    return lax.dot_general(a, b, (((0,), (0,)), ((), ())), preferred_element_type=F32)


def adapter_mask(aid, columns):
    col = lax.broadcasted_iota(jnp.int32, (aid.shape[0], columns), 1)
    return (lax.shift_right_logical(col, 4) & 7) == aid.astype(jnp.int32)


def turn(values, cosine, sine):
    width = values.shape[1]
    lane = lax.broadcasted_iota(jnp.int32, values.shape, 1) & 63
    partner = jnp.where(
        lane < 16, pltpu.roll(values, width - 16, 1), pltpu.roll(values, 16, 1)
    )
    return values * cosine + partner * sine


ANY = pl.BlockSpec(memory_space=pl.ANY)
SMEM = pl.BlockSpec(memory_space=pltpu.SMEM)
VM = pl.BlockSpec(memory_space=pltpu.VMEM)
PARAMS = pltpu.CompilerParams(vmem_limit_bytes=VMEM_LIMIT)
MAIN = 208
SECOND = 288
NEAR = 1280


def whole(shape):
    return pl.BlockSpec(shape, lambda t: (0,) * len(shape), pipeline_mode=pl.Buffered(1))


def start_all(pairs, sem):
    for source, target in pairs:
        pltpu.make_async_copy(source, target, sem).start()


def wait_all(target, sem):
    pltpu.make_async_copy(target, target, sem).wait()


def token_copies(blocks, target):
    pairs = [(blocks[i], target.at[i // 2, i % 2], i) for i in range(6)]
    for i in range(4):
        pairs.append((blocks[6 + i], target.at[3, i // 2, pl.ds(64 * (i % 2), 64)], 6 + i // 2))
    return pairs


def start_tokens(blocks, target, sem, first, last):
    for source, part, i in token_copies(blocks, target):
        if first <= i < last:
            pltpu.make_async_copy(source, part, sem.at[i]).start()


def wait_tokens(target, sem, step):
    for i in range(2):
        part = target.at[step, i]
        pltpu.make_async_copy(part, part, sem.at[2 * step + i]).wait()


def pieces_qkv(g1, target):
    return [
        (
            g1.at[y, c, pl.ds(MAIN * xh, 128), pl.ds(0, 768)],
            target.at[pl.ds((2 * y + xh) * 256 + c * 128, 128), :],
        )
        for y in range(4)
        for xh in range(2)
        for c in range(2)
    ]


def pieces_downs(g1, target):
    return [
        (
            g1.at[:, c, pl.ds(MAIN * xh + 128 + 32 * i + 16 * b, 16), :],
            target.at[c, i, :, xh, :, pl.ds(1024 * b, 1024)],
        )
        for c in range(2)
        for i in range(2)
        for xh in range(2)
        for b in range(2)
    ]


def pieces_rank(g, base, stride, target, row):
    return [
        (
            g.at[y, c, pl.ds(stride * xh + base, 16), :],
            target.at[pl.ds(row + (2 * y + xh) * 16, 16), pl.ds(1024 * c, 1024)],
        )
        for y in range(4)
        for xh in range(2)
        for c in range(2)
    ]


def pieces_dense(g1, target, row):
    return [
        (
            g1.at[y, c, pl.ds(2 * MAIN + 32 * b, 32), :],
            target.at[pl.ds(row + 64 * y + 32 * c, 32), pl.ds(1024 * b, 1024)],
        )
        for y in range(4)
        for c in range(2)
        for b in range(2)
    ]


def pieces_w1(g2, target):
    return [
        (
            g2.at[y, c, pl.ds(SECOND * xh, 128), :],
            target.at[pl.ds((2 * y + xh) * 256 + c * 128, 128), :],
        )
        for y in range(4)
        for xh in range(2)
        for c in range(2)
    ]


def pieces_sixteen(g2, c, target, row):
    return [
        (
            g2.at[y, c, pl.ds(SECOND * xh + 128, 16), :],
            target.at[pl.ds(row + (2 * y + xh) * 16, 16), :],
        )
        for y in range(4)
        for xh in range(2)
    ]


def pieces_w2(g2, target):
    return [
        (
            g2.at[y, c, pl.ds(SECOND * xh + 144 + 64 * b, 64), :],
            target.at[pl.ds((2 * y + xh) * 128 + c * 64, 64), pl.ds(1024 * b, 1024)],
        )
        for y in range(4)
        for xh in range(2)
        for c in range(2)
        for b in range(2)
    ]


def block_diagonal(source, target):
    target[...] = jnp.zeros_like(target)
    for p in range(3):
        cols = slice(256 * p, 256 * p + 256)
        target[128 * p : 128 * p + 128, cols] = source[:, cols]


def k1_body(*refs):
    blocks, refs = refs[:10], refs[10:]
    (scal_ref, g1_ref, up_ref, misc_ref, bias_ref, cos_ref, sin_ref,
     hb_ref, inner_ref, keep_ref, send_ref, aid_ref, x_s, w_s, down_s, up_s, x_sem, w_sem) = refs
    step = pl.program_id(0)

    @pl.when(step == 0)
    def _():
        start_tokens(blocks, x_s, x_sem, 0, 2)
        start_all(pieces_downs(g1_ref, down_s), w_sem.at[0])
        start_all(pieces_qkv(g1_ref, w_s.at[:, pl.ds(0, 768)]), w_sem.at[1])
        start_tokens(blocks, x_s, x_sem, 2, 8)

    wait_tokens(x_s, x_sem, step)
    tile = x_s[step].reshape(256, 2176)
    x = tile[:, :2048].astype(F32)
    aid_ref[...] = tile[:, 2048:]
    aid = tile[:, 2048:2049].astype(F32)
    mean = jnp.mean(x, axis=1, keepdims=True)
    center = x - mean
    spread = jnp.mean(center * center, axis=1, keepdims=True)
    h = center * lax.rsqrt(spread + EPSILON) * misc_ref[0:1, :] + misc_ref[1:2, :]
    hb = h.astype(BF)
    hb_ref[...] = hb

    @pl.when(step == 0)
    def _():
        block_diagonal(up_ref, up_s)
        wait_all(down_s, w_sem.at[0])
        w_s[:, 768:] = down_s[...].reshape(512, 2048).T
        wait_all(w_s.at[:, pl.ds(0, 768)], w_sem.at[1])

    pre_all = nn(hb, w_s[...])
    inner = jnp.where(adapter_mask(aid, 512), pre_all[:, 768:], 0.0).astype(BF)
    inner_ref[...] = inner
    pre_all = pre_all[:, :768] + nn(inner[:, :384], up_s[...]) + bias_ref[...]
    first_core = scal_ref[8] == 0
    cosine = jnp.concatenate([cos_ref[...]] * 2, axis=1)
    sine = jnp.concatenate([sin_ref[...]] * 2, axis=1)
    for p in range(3):
        cols = slice(256 * p, 256 * p + 256)
        pre = pre_all[:, cols]
        if p < 2:
            pre = turn(pre, cosine, sine)
        low = pre.astype(BF)
        keep_ref[p] = jnp.where(first_core, low[:, :128], low[:, 128:])
        send_ref[p] = jnp.where(first_core, low[:, 128:], low[:, :128])


def k1(blocks, scal, g1, ups, misc, bias, cosine, sine):
    rows = 256
    return pl.pallas_call(
        k1_body,
        grid=(4,),
        in_specs=[ANY] * 10
        + [
            SMEM,
            ANY,
            whole((128, 768)),
            whole((2, 2048)),
            whole((1, 768)),
            pl.BlockSpec((rows, 128), lambda t: (t, 0)),
            pl.BlockSpec((rows, 128), lambda t: (t, 0)),
        ],
        out_specs=[
            pl.BlockSpec((rows, 2048), lambda t: (t, 0)),
            pl.BlockSpec((rows, 512), lambda t: (t, 0)),
            pl.BlockSpec((3, rows, 128), lambda t: (0, t, 0)),
            pl.BlockSpec((3, rows, 128), lambda t: (0, t, 0)),
            pl.BlockSpec((rows, 128), lambda t: (t, 0)),
        ],
        out_shape=[
            jax.ShapeDtypeStruct((1024, 2048), BF),
            jax.ShapeDtypeStruct((1024, 512), BF),
            jax.ShapeDtypeStruct((3, 1024, 128), BF),
            jax.ShapeDtypeStruct((3, 1024, 128), BF),
            jax.ShapeDtypeStruct((1024, 128), BF),
        ],
        scratch_shapes=[
            pltpu.VMEM((4, 2, 128, 2176), BF),
            pltpu.VMEM((2048, 1280), BF),
            pltpu.VMEM((2, 2, 4, 2, 16, 2048), BF),
            pltpu.VMEM((384, 768), BF),
            pltpu.SemaphoreType.DMA((8,)),
            pltpu.SemaphoreType.DMA((2,)),
        ],
        compiler_params=PARAMS,
        cost_estimate=pl.CostEstimate(flops=6_000_000_000, bytes_accessed=20_000_000, transcendentals=0),
        name="norm_qkv",
    )(*blocks, scal, g1, ups, misc, bias, cosine, sine)


def k1b_body(*refs):
    blocks, refs = refs[:10], refs[10:]
    scal_ref, aid_ref, g1_ref, dd_ref, keep_ref, send_ref, ginner_ref, dy_s, w_s, dy_sem, w_sem = refs
    start_all(pieces_dense(g1_ref, w_s, 0) + pieces_rank(g1_ref, 192, MAIN, w_s, 256), w_sem)
    start_tokens(blocks, dy_s, dy_sem, 0, 8)
    wait_all(w_s, w_sem)
    for step in range(4):
        wait_tokens(dy_s, dy_sem, step)
    first_core = scal_ref[8] == 0
    both = nt(dy_s[...].reshape(1024, 2048), w_s[...])
    aid = aid_ref[:, 0:1].astype(F32)
    ginner = jnp.where(adapter_mask(aid, 128), both[:, 256:], 0.0).astype(BF)
    ginner_ref[...] = ginner
    dob = (both[:, :256] + nn(ginner, dd_ref[...])).astype(BF)
    keep_ref[...] = jnp.where(first_core, dob[:, :128], dob[:, 128:])
    send_ref[...] = jnp.where(first_core, dob[:, 128:], dob[:, :128])


def k1b(blocks, scal, aid, g1, dd):
    return pl.pallas_call(
        k1b_body,
        in_specs=[ANY] * 10 + [SMEM, VM, ANY, VM],
        out_specs=[VM, VM, VM],
        out_shape=[jax.ShapeDtypeStruct((1024, 128), BF)] * 3,
        scratch_shapes=[
            pltpu.VMEM((4, 2, 128, 2048), BF),
            pltpu.VMEM((384, 2048), BF),
            pltpu.SemaphoreType.DMA((8,)),
            pltpu.SemaphoreType.DMA,
        ],
        compiler_params=PARAMS,
        cost_estimate=pl.CostEstimate(flops=2_000_000_000, bytes_accessed=8_000_000, transcendentals=0),
        name="attention_output_grad",
    )(*blocks, scal, aid, g1, dd)


def k3_body(
    scal_ref, qkv_keep, qkv_recv, dob_keep, dob_recv, idrow_ref, idcol_ref, cos_ref, sin_ref,
    keep_out, send_out, x_s, out_s, kt_s, vt_s, dk_s, dv_s, sem, sem_out,
):
    core = scal_ref[8]
    copies = []
    for b in range(8):
        rows = pl.ds(128 * b, 128)
        spot = scal_ref[b]
        for side, (qkv, dob) in enumerate(((qkv_keep, dob_keep), (qkv_recv, dob_recv))):
            parity = core if side == 0 else 1 - core
            copies.append((qkv.at[:, rows, :], x_s.at[pl.ds(0, 3), spot, parity]))
            copies.append((dob.at[rows, :], x_s.at[3, spot, parity]))
    start_all(copies, sem)
    dk_s[...] = jnp.zeros_like(dk_s)
    dv_s[...] = jnp.zeros_like(dv_s)
    wait_all(x_s, sem)
    kt_s[...] = x_s[1].reshape(2048, 128).T
    vt_s[...] = x_s[2].reshape(2048, 128).T
    tile = 256
    lane = lax.broadcasted_iota(jnp.int32, (tile, 128), 1)

    def span(i, start, stop):
        return x_s[i, start // 256 : stop // 256].reshape(stop - start, 128)

    for t in range(8):
        start, stop = tile * t, tile * t + tile
        length = min(stop + tile, 2048)
        q = span(0, start, stop)
        dob = span(3, start, stop)
        zero = jnp.zeros_like(q)
        q2 = jnp.concatenate([jnp.where(lane < 64, q, zero), jnp.where(lane < 64, zero, q)], axis=0)
        d2 = jnp.concatenate([jnp.where(lane < 64, dob, zero), jnp.where(lane < 64, zero, dob)], axis=0)
        query_ids = idrow_ref[0:1, start:stop]
        query_ids = jnp.concatenate([query_ids, query_ids], axis=1)
        allowed = idcol_ref[start:length, 0:1] <= query_ids
        s = jnp.where(allowed, nt(span(1, start, length), q2), NEGATIVE)
        largest = jnp.max(s, axis=0, keepdims=True)
        if start:
            s_head = nt(span(1, 0, start), q2)
            largest = jnp.maximum(largest, jnp.max(s_head, axis=0, keepdims=True))
            s = jnp.concatenate([s_head, s], axis=0)
        e = jnp.exp((s - largest) * SCALE)
        recip = 1.0 / jnp.sum(e, axis=0, keepdims=True)
        p = e * recip
        pb = p.astype(BF)
        dp = nt(span(2, 0, length), d2)
        delta = jnp.sum(p * dp, axis=0, keepdims=True)
        ds = (p * (dp - delta)).astype(BF)
        dk_s[:length] += nn(ds, q2)
        dv_s[:length] += nn(pb, d2)
        ot = nn(vt_s[:, :length], pb)
        dqt = nn(kt_s[:, :length], ds)
        o_parts = [ot[:64, :256], ot[64:, 256:]]
        dq_parts = [dqt[:64, :256], dqt[64:, 256:]]
        o = jnp.concatenate(o_parts, axis=0).T
        dq = jnp.concatenate(dq_parts, axis=0).T * SCALE
        rows = slice(start, stop)
        out_s[0, t] = o.astype(BF).reshape(2, 128, 128)
        out_s[1, t] = turn(dq, cos_ref[rows], -sin_ref[rows]).astype(BF).reshape(2, 128, 128)
    out_s[2] = turn(dk_s[...] * SCALE, cos_ref[...], -sin_ref[...]).astype(BF).reshape(8, 2, 128, 128)
    out_s[3] = dv_s[...].astype(BF).reshape(8, 2, 128, 128)
    copies = []
    for b in range(8):
        rows = pl.ds(128 * b, 128)
        spot = scal_ref[b]
        copies.append((out_s.at[:, spot, core], keep_out.at[:, rows, :]))
        copies.append((out_s.at[:, spot, 1 - core], send_out.at[:, rows, :]))
    start_all(copies, sem_out)
    wait_all(out_s, sem_out)


def k3(scal, qkv_keep, qkv_recv, dob_keep, dob_recv, idrow, idcol, cosine, sine):
    vm = pl.BlockSpec(memory_space=pltpu.VMEM)
    return pl.pallas_call(
        k3_body,
        in_specs=[SMEM] + [ANY] * 4 + [vm] * 4,
        out_specs=[ANY, ANY],
        out_shape=[jax.ShapeDtypeStruct((4, 1024, 128), BF)] * 2,
        scratch_shapes=[
            pltpu.VMEM((4, 8, 2, 128, 128), BF),
            pltpu.VMEM((4, 8, 2, 128, 128), BF),
            pltpu.VMEM((128, 2048), BF),
            pltpu.VMEM((128, 2048), BF),
            pltpu.VMEM((2048, 128), F32),
            pltpu.VMEM((2048, 128), F32),
            pltpu.SemaphoreType.DMA,
            pltpu.SemaphoreType.DMA,
        ],
        compiler_params=PARAMS,
        cost_estimate=pl.CostEstimate(flops=15_000_000_000, bytes_accessed=8_000_000, transcendentals=5_000_000),
        name="attention",
    )(scal, qkv_keep, qkv_recv, dob_keep, dob_recv, idrow, idcol, cosine, sine)


def heads_of(keep_ref, recv_ref, i, first_core):
    a, b = keep_ref[i], recv_ref[i]
    return jnp.concatenate([jnp.where(first_core, a, b), jnp.where(first_core, b, a)], axis=1)


def tile_spec(width, rows=256):
    return pl.BlockSpec((rows, width), lambda t, s: (t, 0))


def const_spec(shape):
    return pl.BlockSpec(shape, lambda t, s: (0,) * len(shape), pipeline_mode=pl.Buffered(1))


def placed_spec(width):
    return pl.BlockSpec((2, 1, 128, width), lambda t, s: (0, s[12 + t], 0, 0))


def place(ref, xl, value):
    ref[xl, 0] = value[:128]
    ref[1 - xl, 0] = value[128:]


def accumulate(step, pairs):
    @pl.when(step == 0)
    def _():
        for ref, value in pairs:
            ref[...] = value

    @pl.when(step > 0)
    def _():
        for ref, value in pairs:
            ref[...] += value


def att_spec(first, count):
    return pl.BlockSpec((count, 256, 128), lambda t, s: (first, t, 0))


def k2f_body(
    scal_ref, hb_ref, aid_ref, inner_ref, gdense_ref, keep_ref, recv_ref, g1_ref, g2_ref, dd_ref, b1_ref,
    out_ref, gb_ref, slope_ref, low_ref, gdd_ref,
    w1_s, wout_s, d2_s, rest_s, sems,
):
    step = pl.program_id(0)

    @pl.when(step == 0)
    def _():
        start_all(pieces_w1(g2_ref, w1_s) + pieces_sixteen(g2_ref, 0, w1_s, 2048), sems.at[0])
        start_all(pieces_sixteen(g2_ref, 1, d2_s, 0), sems.at[1])
        start_all(pieces_w2(g2_ref, wout_s) + pieces_dense(g1_ref, wout_s, 1024), sems.at[2])
        start_all(
            pieces_rank(g1_ref, 192, MAIN, rest_s, 0) + pieces_rank(g2_ref, 272, SECOND, rest_s, 128), sems.at[3]
        )
        wout_s[:, 2048:] = jnp.zeros((1280, 256), BF)
        wout_s[1024:, 2048:2176] = dd_ref[...].T
        wait_all(d2_s, sems.at[1])
        wout_s[:1024, 2176:] = d2_s[...].T
        wait_all(w1_s, sems.at[0])

    keep = adapter_mask(aid_ref[:, 0:1].astype(F32), 256)
    f = nn(jnp.concatenate([hb_ref[...], inner_ref[...]], axis=1), w1_s[...]) + b1_ref[...]
    square = f * f
    th = jnp.tanh(GELU_SCALE * f * (1.0 + 0.044715 * square))
    half = 0.5 * (1.0 + th)
    gb = (f * half).astype(BF)
    gb_ref[...] = gb
    slope = half + (0.5 * GELU_SCALE) * f * (1.0 - th * th) * (1.0 + 3 * 0.044715 * square)
    slope_ref[...] = slope.astype(BF)
    ob = heads_of(keep_ref, recv_ref, 0, scal_ref[8] == 0)

    @pl.when(step == 0)
    def _():
        wait_all(wout_s.at[:, pl.ds(0, 2048)], sems.at[2])
        wait_all(rest_s, sems.at[3])

    total = nn(jnp.concatenate([gb, ob], axis=1), wout_s[...])
    low = jnp.where(keep, total[:, 2048:], 0.0).astype(BF)
    low_ref[...] = low
    out = (total[:, :2048] + nn(low, rest_s[...])).astype(BF)
    place(out_ref, scal_ref[10], out)
    accumulate(step, [(gdd_ref, tn(gdense_ref[...], ob))])


def k2f(scal, hb, aid, inner, gdense, keep, recv, g1, g2, dd, b1):
    return pl.pallas_call(
        k2f_body,
        grid_spec=pltpu.PrefetchScalarGridSpec(
            num_scalar_prefetch=1,
            grid=(4,),
            in_specs=[
                tile_spec(2048),
                tile_spec(128),
                pl.BlockSpec((256, 128), lambda t, s: (t, 3)),
                tile_spec(128),
                att_spec(0, 1),
                att_spec(0, 1),
                ANY,
                ANY,
                const_spec((128, 256)),
                const_spec((1, 1024)),
            ],
            out_specs=[
                placed_spec(2048),
                tile_spec(1024),
                tile_spec(1024),
                tile_spec(256),
                const_spec((128, 256)),
            ],
            scratch_shapes=[
                pltpu.VMEM((2176, 1024), BF),
                pltpu.VMEM((1280, 2304), BF),
                pltpu.VMEM((128, 1024), BF),
                pltpu.VMEM((256, 2048), BF),
                pltpu.SemaphoreType.DMA((4,)),
            ],
        ),
        out_shape=[
            jax.ShapeDtypeStruct((2, 4, 128, 2048), BF),
            jax.ShapeDtypeStruct((1024, 1024), BF),
            jax.ShapeDtypeStruct((1024, 1024), BF),
            jax.ShapeDtypeStruct((1024, 256), BF),
            jax.ShapeDtypeStruct((128, 256), F32),
        ],
        compiler_params=PARAMS,
        cost_estimate=pl.CostEstimate(flops=14_000_000_000, bytes_accessed=24_000_000, transcendentals=1_000_000),
        name="out_rows",
    )(scal, hb, aid, inner, gdense, keep, recv, g1, g2, dd, b1)


def k2g_body(scal_ref, *refs):
    blocks, refs = refs[:10], refs[10:]
    (aid_ref, inner_ref, keep_ref, recv_ref, gb_ref, slope_ref, low_out_ref, g2_ref, up_ref, fold_ref,
     df_ref, low_ref, small_ref, gup1_ref, gd2_ref,
     dy_s, w2_s, up1_s, d2_s, up_s, dy_sem, sems) = refs
    step = pl.program_id(0)

    @pl.when(step == 0)
    def _():
        start_tokens(blocks, dy_s, dy_sem, 0, 2)
        start_all(pieces_w2(g2_ref, w2_s) + pieces_rank(g2_ref, 272, SECOND, w2_s, 1024), sems.at[0])
        start_all(pieces_sixteen(g2_ref, 1, d2_s, 0), sems.at[1])
        start_all(pieces_sixteen(g2_ref, 0, up1_s, 0), sems.at[2])
        start_tokens(blocks, dy_s, dy_sem, 2, 8)
        block_diagonal(up_ref, up_s)
        wait_all(w2_s, sems.at[0])
        wait_all(d2_s, sems.at[1])
        wait_all(up1_s, sems.at[2])

    wait_tokens(dy_s, dy_sem, step)
    aid = aid_ref[:, 0:1].astype(F32)
    first_core = scal_ref[8] == 0
    wide = nt(dy_s[step].reshape(256, 2048), w2_s[...])
    ginner2 = jnp.where(adapter_mask(aid, 128), wide[:, 1024:], 0.0).astype(BF)
    dpre = jnp.concatenate([heads_of(keep_ref, recv_ref, p, first_core) for p in (1, 2, 3)], axis=1)
    ginner = nt(dpre, up_s[...])
    df = ((wide[:, :1024] + nn(ginner2, d2_s[...])) * slope_ref[...].astype(F32)).astype(BF)
    df_ref[...] = df
    ginner1 = nt(df, up1_s[...])
    low = jnp.concatenate([ginner, ginner1], axis=1)
    low = jnp.where(adapter_mask(aid, 512), low, 0.0).astype(BF)
    low_ref[...] = low
    folded = nn(jnp.concatenate([low, low_out_ref[...]], axis=1), fold_ref[...])
    place(small_ref, scal_ref[10], folded.astype(BF))
    accumulate(step, [(gup1_ref, tn(inner_ref[...], df)), (gd2_ref, tn(ginner2, gb_ref[...]))])


def k2g(blocks, scal, aid, inner, keep, recv, gb, slope, low_out, g2, ups, fold):
    return pl.pallas_call(
        k2g_body,
        grid_spec=pltpu.PrefetchScalarGridSpec(
            num_scalar_prefetch=1,
            grid=(4,),
            in_specs=[ANY] * 10
            + [
                tile_spec(128),
                pl.BlockSpec((256, 128), lambda t, s: (t, 3)),
                att_spec(0, 4),
                att_spec(0, 4),
                tile_spec(1024),
                tile_spec(1024),
                tile_spec(256),
                ANY,
                const_spec((128, 768)),
                const_spec((768, 128)),
            ],
            out_specs=[
                tile_spec(1024),
                tile_spec(512),
                placed_spec(128),
                const_spec((128, 1024)),
                const_spec((128, 1024)),
            ],
            scratch_shapes=[
                pltpu.VMEM((4, 2, 128, 2048), BF),
                pltpu.VMEM((1152, 2048), BF),
                pltpu.VMEM((128, 1024), BF),
                pltpu.VMEM((128, 1024), BF),
                pltpu.VMEM((384, 768), BF),
                pltpu.SemaphoreType.DMA((8,)),
                pltpu.SemaphoreType.DMA((3,)),
            ],
        ),
        out_shape=[
            jax.ShapeDtypeStruct((1024, 1024), BF),
            jax.ShapeDtypeStruct((1024, 512), BF),
            jax.ShapeDtypeStruct((2, 4, 128, 128), BF),
            jax.ShapeDtypeStruct((128, 1024), F32),
            jax.ShapeDtypeStruct((128, 1024), F32),
        ],
        compiler_params=PARAMS,
        cost_estimate=pl.CostEstimate(flops=8_000_000_000, bytes_accessed=20_000_000, transcendentals=0),
        name="feed_forward_grad",
    )(scal, *blocks, aid, inner, keep, recv, gb, slope, low_out, g2, ups, fold)


def k2h_body(
    scal_ref, df_ref, keep_ref, recv_ref, low_ref, inner_ref, g1_ref, g2_ref,
    near_ref, owns_ref, sides_ref, gqkv_ref, w_s, down_s, sems,
):
    step = pl.program_id(0)

    @pl.when(step == 0)
    def _():
        start_all(
            pieces_w1(g2_ref, w_s.at[:, pl.ds(0, 1024)]) + pieces_qkv(g1_ref, w_s.at[:, pl.ds(1024, 768)]), sems.at[0]
        )
        start_all(pieces_downs(g1_ref, down_s), sems.at[1])
        wait_all(w_s, sems.at[0])
        wait_all(down_s, sems.at[1])

    first_core = scal_ref[8] == 0
    dpre = [heads_of(keep_ref, recv_ref, p, first_core) for p in (1, 2, 3)]
    dh = nt(jnp.concatenate([df_ref[...]] + dpre, axis=1), w_s[...])
    dh = (dh + nn(low_ref[...], down_s[...].reshape(512, 2048))).astype(BF)
    near_ref[0] = dh[:128, :NEAR]
    near_ref[1] = dh[128:, :NEAR]
    owns_ref[0] = dh[:128, NEAR:]
    sides_ref[0] = dh[128:, NEAR:]
    gqkv = [tn(inner_ref[:, 128 * p : 128 * p + 128], dpre[p]) for p in range(3)]
    accumulate(step, [(gqkv_ref, jnp.concatenate(gqkv, axis=1))])


def k2h(scal, df, keep, recv, low_in, inner, g1, g2):
    return pl.pallas_call(
        k2h_body,
        grid_spec=pltpu.PrefetchScalarGridSpec(
            num_scalar_prefetch=1,
            grid=(4,),
            in_specs=[tile_spec(1024), att_spec(0, 4), att_spec(0, 4), tile_spec(512), tile_spec(512), ANY, ANY],
            out_specs=[
                pl.BlockSpec((2, 128, NEAR), lambda t, s: (t, 0, 0)),
                pl.BlockSpec((1, 128, 2048 - NEAR), lambda t, s: (t, 0, 0)),
                pl.BlockSpec((1, 128, 2048 - NEAR), lambda t, s: (t, 0, 0)),
                const_spec((128, 768)),
            ],
            scratch_shapes=[
                pltpu.VMEM((2048, 1792), BF),
                pltpu.VMEM((2, 2, 4, 2, 16, 2048), BF),
                pltpu.SemaphoreType.DMA((2,)),
            ],
        ),
        out_shape=[
            jax.ShapeDtypeStruct((8, 128, NEAR), BF),
            jax.ShapeDtypeStruct((4, 128, 2048 - NEAR), BF),
            jax.ShapeDtypeStruct((4, 128, 2048 - NEAR), BF),
            jax.ShapeDtypeStruct((128, 768), F32),
        ],
        compiler_params=PARAMS,
        cost_estimate=pl.CostEstimate(flops=10_000_000_000, bytes_accessed=18_000_000, transcendentals=0),
        name="hidden_grad",
    )(scal, df, keep, recv, low_in, inner, g1, g2)


def k5_body(scal_ref, small_ref, aid_ref, hb_ref, spread_ref, gup1_ref, gd2_ref, gqkv_ref, gdd_ref, *refs):
    blocks, refs = refs[:10], refs[10:]
    keep_ref, send_ref, dy_s, sem = refs
    column = pl.multiple_of(256 * scal_ref[9], 256)
    start_all(
        [(source.at[:, pl.ds(column, 256)], part) for source, part, _ in token_copies(blocks, dy_s)], sem
    )
    first_core = scal_ref[8] == 0

    def store(section, left, right):
        kept = jnp.where(first_core, left, right)
        sent = jnp.where(first_core, right, left)
        keep_ref[:, 16 * section : 16 * section + 16] = kept.reshape(8, 16, 512)
        send_ref[:, 16 * section : 16 * section + 16] = sent.astype(BF).reshape(8, 16, 512)

    small = jnp.concatenate([small_ref[scal_ref[b]] for b in range(8)], axis=0)
    aid = aid_ref[:, 0:1].astype(F32)
    wide = jnp.where(adapter_mask(aid, 768), nn(small, spread_ref[...]), 0.0).astype(BF)
    down = tn(wide[:, :512], hb_ref[...])
    store(
        0,
        jnp.concatenate([down[:128], down[128:256]], axis=1),
        jnp.concatenate([down[256:384], down[384:]], axis=1),
    )
    store(1, gqkv_ref[:, :512], jnp.concatenate([gqkv_ref[:, 512:], gdd_ref[...]], axis=1))
    store(2, gup1_ref[:, :512], gup1_ref[:, 512:])
    store(3, gd2_ref[:, :512], gd2_ref[:, 512:])
    wait_all(dy_s, sem)
    up = tn(wide[:, 512:], dy_s[...].reshape(1024, 256))
    left = jnp.concatenate([up[:128], up[128:]], axis=1)
    store(4, left, jnp.zeros_like(left))


def k5(scal, small, aid, hb, spread, gup1, gd2, gqkv, gdd, blocks):
    def const(shape):
        return pl.BlockSpec(shape, lambda t, s: (0,) * len(shape))

    return pl.pallas_call(
        k5_body,
        grid_spec=pltpu.PrefetchScalarGridSpec(
            num_scalar_prefetch=1,
            grid=(1,),
            in_specs=[
                const((8, 128, 128)),
                const((1024, 128)),
                pl.BlockSpec((1024, 256), lambda t, s: (0, s[9])),
                const((128, 768)),
                const((128, 1024)),
                const((128, 1024)),
                const((128, 768)),
                const((128, 256)),
            ]
            + [ANY] * 10,
            out_specs=[const((8, 80, 512)), const((8, 80, 512))],
            scratch_shapes=[pltpu.VMEM((4, 2, 128, 256), BF), pltpu.SemaphoreType.DMA],
        ),
        out_shape=[jax.ShapeDtypeStruct((8, 80, 512), F32), jax.ShapeDtypeStruct((8, 80, 512), BF)],
        compiler_params=PARAMS,
        cost_estimate=pl.CostEstimate(flops=1_500_000_000, bytes_accessed=6_000_000, transcendentals=0),
        name="adapter_grads",
    )(scal, small, aid, hb, spread, gup1, gd2, gqkv, gdd, *blocks)


def kf_body(scal_ref, mine_ref, theirs_ref, down_ref, up_ref, dd_ref, ud_ref, f1d_ref, f1u_ref, f2d_ref, f2u_ref):
    lane = lax.broadcasted_iota(jnp.int32, (16, 128), 1)

    core = scal_ref[8]

    def part(j, half, section, start, width):
        rows, cols = slice(16 * section, 16 * section + 16), slice(start, start + width)
        return jnp.where(core == half, mine_ref[j, rows, cols], theirs_ref[j, rows, cols]).astype(F32)

    for j in range(8):
        block = slice(256 * j, 256 * j + 256)
        down_ref[0, :, block] = part(j, 0, 0, 0, 256)
        down_ref[1, :, block] = part(j, 0, 0, 256, 256)
        down_ref[2, :, block] = part(j, 1, 0, 0, 256)
        f1d_ref[:, block] = part(j, 1, 0, 256, 256)
        ud_ref[:, block] = part(j, 0, 4, 0, 256)
        f2u_ref[:, block] = part(j, 0, 4, 256, 256)
        for w in range(8):
            spot = slice(1024 * w + 128 * j, 1024 * w + 128 * j + 128)
            f1u_ref[:, spot] = part(j, w // 4, 2, 128 * (w % 4), 128)
            f2d_ref[:, spot] = part(j, w // 4, 3, 128 * (w % 4), 128)
    for i in range(4):
        for x in range(2):
            for y in range(4):
                for h in range(2):
                    start = 256 * (i % 2) + 128 * (y // 2)
                    a = part(4 * x + 2 * h, i // 2, 1, start, 128)
                    b = part(4 * x + 2 * h + 1, i // 2, 1, start, 128)
                    if y % 2:
                        a = pltpu.roll(a, 64, 1)
                    else:
                        b = pltpu.roll(b, 64, 1)
                    value = jnp.where(lane < 64, a, b)
                    spot = slice(256 * (2 * y + x) + 128 * h, 256 * (2 * y + x) + 128 * h + 128)
                    if i < 3:
                        up_ref[i, :, spot] = value
                    else:
                        dd_ref[:, spot] = value


def kf(scal, mine, theirs):
    return pl.pallas_call(
        kf_body,
        in_specs=[SMEM, VM, VM],
        out_specs=[VM] * 8,
        out_shape=[
            jax.ShapeDtypeStruct((3, 16, 2048), F32),
            jax.ShapeDtypeStruct((3, 16, 2048), F32),
            jax.ShapeDtypeStruct((16, 2048), F32),
            jax.ShapeDtypeStruct((16, 2048), F32),
            jax.ShapeDtypeStruct((16, 2048), F32),
            jax.ShapeDtypeStruct((16, 8192), F32),
            jax.ShapeDtypeStruct((16, 8192), F32),
            jax.ShapeDtypeStruct((16, 2048), F32),
        ],
        compiler_params=PARAMS,
        name="finish",
    )(scal, mine, theirs)


def pack1_body(
    scal_ref, wq, wk, wv, wd, ad_ref, fd_ref, au_ref, dd_ref, du_ref, misc_ref, b1_ref,
    own_ref, other_ref, w_s, d_s, sem, d_sem,
):
    c, z = scal_ref[8], scal_ref[11]
    start_all([(w.at[pl.ds(128 * c, 128), :], w_s.at[i]) for i, w in enumerate((wq, wk, wv))], sem)
    start_all([(wd.at[pl.ds(64 * z + 32 * c, 32), :], d_s)], d_sem)
    first_core = c == 0
    odd = lax.rem(z, 2) == 1
    targets = ((own_ref, scal_ref[10]), (other_ref, 1 - scal_ref[10]))

    def head_pair(read, rows, i, xl):
        lane = lax.broadcasted_iota(jnp.int32, (rows, 128), 1)
        parts = []
        for k in range(2):
            start = (2 * (i + k) + xl) * 256 + (z // 2) * 128
            v = read(pl.ds(pl.multiple_of(start, 128), 128)).astype(F32)
            turned = pltpu.roll(v, 64, 1)
            parts.append(jnp.where(odd, turned, v) if k == 0 else jnp.where(odd, v, turned))
        return jnp.where(lane < 64, parts[0], parts[1]).astype(BF)

    half = pl.ds(pl.multiple_of((z // 2) * 128, 128), 128)
    row = lax.broadcasted_iota(jnp.int32, (16, 128), 0)
    lane = lax.broadcasted_iota(jnp.int32, (16, 128), 1)

    def biases(xl):
        plain = misc_ref[:, :128].astype(F32), misc_ref[:, 128:256].astype(F32)
        mine = misc_ref[:, half].astype(F32)
        turned = pltpu.roll(mine, 64, 1)
        low = jnp.where(odd, turned, mine)
        high = jnp.where(odd, mine, turned)
        query_key = jnp.where(lane[:1] < 64, low[4:5], high[5:6])
        value = jnp.where(lane[:1] < 64, low[6:7], 0.0)
        hidden = jnp.where(row[:8] == xl * 4 + z, b1_ref[...].astype(F32), 0.0)
        hidden = jnp.sum(hidden, axis=0, keepdims=True)
        left = jnp.where(row < 4, plain[0], jnp.where(row == 4, query_key, hidden))
        right = jnp.where(row < 4, plain[1], value)
        return left.astype(BF), right.astype(BF)

    a = jnp.where(first_core, ad_ref[0], ad_ref[2])
    b = jnp.where(first_core, ad_ref[1], fd_ref[...])
    du = jnp.where(first_core, du_ref[:, :1024], du_ref[:, 1024:])
    for out_ref, xl in targets:
        rows_of = biases(xl)
        for p in range(4):
            for i in (0, 2):
                read = (lambda s, p=p: au_ref[p, :, s]) if p < 3 else (lambda s: dd_ref[:, s])
                value = head_pair(read, 16, i, xl)
                rows = slice(16 * p, 16 * p + 16)
                if p == 0:
                    value = jnp.where(first_core, value, rows_of[i // 2])
                out_ref[rows, 768 + 64 * i : 768 + 64 * i + 128] = value
        out_ref[64:128, 768:] = jnp.zeros((64, 256), BF)
        out_ref[128:144] = a[:, :1024]
        out_ref[144:160] = a[:, 1024:]
        out_ref[160:176] = b[:, :1024]
        out_ref[176:192] = b[:, 1024:]
        out_ref[192:208] = du
    wait_all(d_s, d_sem)
    for out_ref, _ in targets:
        out_ref[208:240] = d_s[:, :1024]
        out_ref[240:272] = d_s[:, 1024:]
    wait_all(w_s, sem)
    for p in range(3):
        for i in (0, 2):
            start = 256 * p + 64 * i
            for out_ref, xl in targets:
                out_ref[:128, start : start + 128] = head_pair(lambda s, p=p: w_s[p, :, s], 128, i, xl)


def pack1(scal, wq, wk, wv, wd, ad, fd, au, dd, du, misc, b1):
    return pl.pallas_call(
        pack1_body,
        in_specs=[SMEM] + [ANY] * 4 + [VM] * 7,
        out_specs=[VM, VM],
        out_shape=[jax.ShapeDtypeStruct((272, 1024), BF)] * 2,
        scratch_shapes=[
            pltpu.VMEM((3, 128, 2048), BF),
            pltpu.VMEM((32, 2048), BF),
            pltpu.SemaphoreType.DMA,
            pltpu.SemaphoreType.DMA,
        ],
        compiler_params=PARAMS,
        cost_estimate=pl.CostEstimate(flops=1_000_000, bytes_accessed=4_000_000, transcendentals=0),
        name="pack_qkv",
    )(scal, wq, wk, wv, wd, ad, fd, au, dd, du, misc, b1)


def pack2_body(scal_ref, w1, w2, up_ref, down_ref, up2_ref, own_ref, w1_s, w2_s, sem, sem2):
    c, j = scal_ref[8], scal_ref[9]
    start_all([(w1.at[pl.ds(128 * c, 128), :], w1_s)], sem)
    start_all([(w2.at[pl.ds(128 * j + 64 * c, 64), :], w2_s)], sem2)
    first_core = c == 0
    own_ref[272:288] = jnp.where(first_core, up2_ref[:, :1024], up2_ref[:, 1024:])

    def column(w):
        return pl.ds(pl.multiple_of(1024 * w + 128 * j, 128), 128)

    for w in range(8):
        own_ref[128:144, 128 * w : 128 * w + 128] = jnp.where(first_core, up_ref[:, column(w)], down_ref[:, column(w)])
    wait_all(w2_s, sem2)
    own_ref[144:208] = w2_s[:, :1024]
    own_ref[208:272] = w2_s[:, 1024:]
    wait_all(w1_s, sem)
    for w in range(8):
        own_ref[:128, 128 * w : 128 * w + 128] = w1_s[:, column(w)]


def pack2(scal, w1, w2, up, down, up2):
    return pl.pallas_call(
        pack2_body,
        in_specs=[SMEM, ANY, ANY, VM, VM, VM],
        out_specs=VM,
        out_shape=jax.ShapeDtypeStruct((288, 1024), BF),
        scratch_shapes=[
            pltpu.VMEM((128, 8192), BF),
            pltpu.VMEM((64, 2048), BF),
            pltpu.SemaphoreType.DMA,
            pltpu.SemaphoreType.DMA,
        ],
        compiler_params=PARAMS,
        cost_estimate=pl.CostEstimate(flops=1_000_000, bytes_accessed=4_000_000, transcendentals=0),
        name="pack_hidden",
    )(scal, w1, w2, up, down, up2)


def rotary_tables(positions):
    lane = np.arange(128) % 64
    rate = np.where(lane < 32, 10000.0 ** (-2.0 * (lane % 16) / 32.0), 0.0).astype(np.float32)
    sign = np.where(lane < 16, -1.0, 1.0).astype(np.float32)
    angles = positions.astype(F32)[:, None] * jnp.asarray(rate)[None, :]
    return jnp.cos(angles), jnp.sin(angles) * jnp.asarray(sign)[None, :]


def fold_matrix():
    row = np.arange(768)
    target = (row // 128) * 16 + row % 16
    return jnp.asarray((target[:, None] == np.arange(128)[None, :]).astype(np.float32)).astype(BF)


def halves(a):
    m = a.shape[1] // 2
    return jnp.concatenate([a[:, :m], a[:, m:]], axis=0)


SWAP = [(0, 1), (1, 0)]
FLIP = [(i, 3 - i) for i in range(4)]
UP = [(i, (i + 1) % 4) for i in range(4)]
DOWN = [(i, (i + 3) % 4) for i in range(4)]
Z_OFFSETS = (0, -1, 1, 2)


def together(*values):
    return lax.optimization_barrier(values)


def up(a):
    return lax.ppermute(a, "z", UP)


def down(a):
    return lax.ppermute(a, "z", DOWN)


def across(a):
    return lax.ppermute(a, "xl", SWAP)


def gather_pair(own, other, single):
    xh = lax.axis_index("xh")
    parts = [jnp.where(xh == 0, own, other), jnp.where(xh == 0, other, own)]
    if single is not None:
        parts.append(single)
    packed = jnp.concatenate(parts, axis=0)
    g = lax.all_gather(packed, ("y", "c"), axis=0, tiled=False)
    return g.reshape((4, 2) + packed.shape)


def add(*terms):
    return sum(t.astype(F32) for t in terms)


def scatter_sum(near, owns, sides):
    own, side, down_own, down_side, up_own, up_side, far_own, far_side = [near[b] for b in range(8)]
    from_side = lax.ppermute(sides, "xl", SWAP)
    via_below = lax.ppermute(far_own, "z", UP)
    via_above = lax.ppermute(far_side, "z", DOWN)
    up_side = lax.ppermute(up_side, "z", UP)
    down_own = lax.ppermute(down_own, "z", DOWN)
    up_own = lax.ppermute(add(up_own, via_below).astype(BF), "z", UP)
    down_side = lax.ppermute(add(down_side, via_above).astype(BF), "z", DOWN)
    side = lax.ppermute(add(side, up_side, down_side).astype(BF), "xl", SWAP)
    first = add(own, up_own, down_own, side)
    t = add(owns, from_side)
    far = t[3].astype(BF)
    half_up = lax.ppermute(far[:64], "z", UP)
    half_down = lax.ppermute(far[64:], "z", DOWN)
    up = jnp.concatenate([t[2, :64] + half_up.astype(F32), t[2, 64:]], axis=0).astype(BF)
    down = jnp.concatenate([t[1, :64], t[1, 64:] + half_down.astype(F32)], axis=0).astype(BF)
    second = add(t[0], lax.ppermute(up, "z", UP), lax.ppermute(down, "z", DOWN))
    return jnp.concatenate([first, second], axis=1)


def local(
    inputs,
    output_cotangent,
    block_index_per_position,
    adapter_index_per_run,
    norm_gain,
    norm_bias,
    query_weight,
    key_weight,
    value_weight,
    dense_weight,
    query_bias,
    key_bias,
    value_bias,
    dense_bias,
    feedforward_in_weight,
    feedforward_in_bias,
    feedforward_out_weight,
    feedforward_out_bias,
    adapter_attention_down,
    adapter_attention_up,
    adapter_dense_down,
    adapter_dense_up,
    adapter_feedforward_in_down,
    adapter_feedforward_in_up,
    adapter_feedforward_out_down,
    adapter_feedforward_out_up,
):
    xl, z, c = lax.axis_index("xl"), lax.axis_index("z"), lax.axis_index("c")
    xh = lax.axis_index("xh")
    j = xl * 4 + z
    x_own = inputs[0]
    dy_own = output_cotangent[0]
    run_adapter = adapter_index_per_run[0, 0].astype(F32).astype(BF)
    block_row = block_index_per_position[0]
    z_of = [lax.rem(z + o + 4, 4) for o in Z_OFFSETS]
    spots = [(xl if side == 0 else 1 - xl) * 4 + zz for zz in z_of for side in range(2)]
    scal = jnp.stack(spots + [c, j, xl, z] + z_of).astype(jnp.int32)

    zero = jnp.zeros((256,), BF)
    misc_own = jnp.stack(
        [norm_gain, norm_bias, dense_bias, feedforward_out_bias, query_bias, key_bias, value_bias] + [zero] * 9
    )
    sent1, for_other = pack1(
        scal,
        query_weight,
        key_weight,
        value_weight,
        dense_weight,
        adapter_attention_down[0],
        adapter_feedforward_in_down[0],
        adapter_attention_up[0],
        adapter_dense_down[0],
        adapter_dense_up[0],
        misc_own,
        feedforward_in_bias.reshape(8, 128),
    )
    own2 = pack2(
        scal,
        feedforward_in_weight,
        feedforward_out_weight,
        adapter_feedforward_in_up[0],
        adapter_feedforward_out_down[0],
        adapter_feedforward_out_up[0],
    )
    spread = jnp.stack(spots)
    my_positions = ((spread * 2 + c) * 128)[:, None] + jnp.arange(128, dtype=jnp.int32)[None, :]
    tables = rotary_tables(my_positions.reshape(1024)) + rotary_tables(jnp.arange(2048, dtype=jnp.int32))
    tables = tables + (jnp.broadcast_to(block_row[:, None], (2048, 128)),)
    x_send = jnp.concatenate([x_own, jnp.full((128, 128), run_adapter, BF)], axis=1)

    x_up, x_down, x_side, other1, own2, tables = together(
        up(x_send), down(x_send), across(x_send), lax.ppermute(for_other, ("xl", "xh"), FLIP), own2, tables
    )
    g1 = gather_pair(sent1[:MAIN], other1[:MAIN], jnp.where(xh == xl, sent1[MAIN:], other1[MAIN:]))
    x_up, x_down, x_side, dy_own = together(x_up, x_down, x_side, dy_own)
    x_up_side, x_down_side, x_far_a, x_far_b, dy_side = together(
        up(x_side), down(x_side), up(x_up[:64]), down(x_down[64:]), across(dy_own)
    )
    x_far_side_a, x_far_side_b, dy_up, dy_down, other2 = together(
        across(x_far_a), across(x_far_b), up(dy_own), down(dy_own), lax.ppermute(own2, "xh", SWAP)
    )
    g2 = gather_pair(own2, other2, None)
    dy_side, dy_up, dy_down = together(dy_side, dy_up, dy_down)
    dy_far_a, dy_far_b, dy_up_side, dy_down_side = together(
        up(dy_up[:64]), down(dy_down[64:]), up(dy_side), down(dy_side)
    )
    dy_far_side_a, dy_far_side_b = across(dy_far_a), across(dy_far_b)
    x_blocks = [x_send, x_side, x_up, x_up_side, x_down, x_down_side, x_far_a, x_far_b, x_far_side_a, x_far_side_b]
    dy_blocks = [dy_own, dy_side, dy_up, dy_up_side, dy_down, dy_down_side]
    dy_blocks = dy_blocks + [dy_far_a, dy_far_b, dy_far_side_a, dy_far_side_b]

    def side_of(core):
        return jnp.stack(
            [g1[:, core, MAIN * h : MAIN * h + 64, 768:] for h in range(2)], axis=1
        ).reshape(8, 64, 256)

    ups_all = side_of(0).reshape(8, 4, 16, 256).transpose(1, 0, 2, 3).reshape(4, 128, 256)
    ups = jnp.concatenate([ups_all[0], ups_all[1], ups_all[2]], axis=1)
    dd = ups_all[3]
    small_all = side_of(1)[:, :6].astype(F32)
    misc = small_all[:, :4].transpose(1, 0, 2).reshape(4, 2048)
    head_b = lax.dynamic_index_in_dim(small_all[:, 4, :192].reshape(4, 2, 3, 64), xl, 1, keepdims=False)
    bias_qkv = head_b.transpose(1, 0, 2).reshape(1, 768)
    b1 = small_all[:, 5, :128].reshape(1, 1024)

    cos_mine, sin_mine, cos_all, sin_all, idcol = tables

    hb, inner, qkv_keep, qkv_send, aid = k1(x_blocks, scal, g1, ups, misc[:2], bias_qkv, cos_mine, sin_mine)
    qkv_recv = lax.ppermute(qkv_send, "c", SWAP)
    dob_keep, dob_send, gdense = k1b(dy_blocks, scal, aid, g1, dd)
    dob_recv = lax.ppermute(dob_send, "c", SWAP)

    idrow = jnp.broadcast_to(block_row[None, :], (8, 2048))
    att_keep, att_send = k3(scal, qkv_keep, qkv_recv, dob_keep, dob_recv, idrow, idcol, cos_all, sin_all)
    att_recv = lax.ppermute(att_send, "c", SWAP)

    fold = fold_matrix()
    out_part, gb, slope, low_out, gdd = k2f(scal, hb, aid, inner, gdense, att_keep, att_recv, g1, g2, dd, b1)
    out_sum = lax.psum_scatter(out_part.reshape(1024, 2048), TP, scatter_dimension=0, tiled=True)
    df, low_in, small, gup1, gd2 = k2g(
        dy_blocks, scal, aid, inner, att_keep, att_recv, gb, slope, low_out, g2, ups, fold
    )
    small = lax.all_to_all(small.reshape(8, 128, 128), TP, 0, 0, tiled=True)
    small = jnp.sum(small.astype(F32), axis=0).astype(BF)
    small = lax.all_to_all(jnp.broadcast_to(small[None], (8, 128, 128)), TP, 0, 0, tiled=True)
    near, owns, sides, gqkv = k2h(scal, df, att_keep, att_recv, low_in, inner, g1, g2)
    dh_sum = scatter_sum(near, owns, sides)

    keep, send = k5(scal, small, aid, hb, fold.T, gup1, gd2, gqkv, gdd, dy_blocks)
    grads = (keep + lax.ppermute(send, "c", SWAP).astype(F32)).astype(BF)
    grads = lax.all_to_all(grads, WSH, 0, 0, tiled=True)
    grads = jnp.sum(grads.astype(F32), axis=0).astype(BF)
    grads = lax.all_to_all(jnp.broadcast_to(grads[None], (8, 80, 512)), TP, 0, 0, tiled=True)
    down_qkv, up_qkv, gdd, gud, gf1d, gf1u, gf2d, gf2u = kf(scal, grads, lax.ppermute(grads, "c", SWAP))

    source = x_own.astype(F32)
    outputs = (source + out_sum.astype(F32) + misc[2:3] + misc[3:4]).astype(BF)[None]
    mean = jnp.mean(source, axis=1, keepdims=True)
    center = source - mean
    inv = lax.rsqrt(jnp.mean(center * center, axis=1, keepdims=True) + EPSILON)
    hn = center * inv
    e = dh_sum.astype(F32) * misc[0:1]
    dx = (e - jnp.mean(e, axis=1, keepdims=True) - hn * jnp.mean(e * hn, axis=1, keepdims=True)) * inv
    grad_inputs = (dy_own.astype(F32) + dx).astype(BF)[None]
    return (
        outputs,
        grad_inputs,
        down_qkv[None],
        up_qkv[None],
        gdd[None],
        gud[None],
        gf1d[None],
        gf1u[None],
        gf2d[None],
        gf2u[None],
    )


def solution(mesh):
    fine = Mesh(np.asarray(mesh.devices).reshape(2, 4, 2, 4, 2), ("xl", "z", "c", "y", "xh"))
    tokens = P(WSH, CTX, None)
    w1 = P(WSH)
    w2 = P(WSH, None)
    w3 = P(WSH, None, None)
    w4 = P(WSH, None, None, None)
    placed = (tokens, tokens, w2, P(WSH, CTX)) + (w1, w1, w2, w2, w2, w2, w1, w1, w1, w1, w2, w1, w2, w1)
    placed = placed + (w4, w4, w3, w3, w3, w3, w3, w3)
    return jax.shard_map(
        local,
        mesh=fine,
        in_specs=placed,
        out_specs=(tokens, tokens, w4, w4, w3, w3, w3, w3, w3, w3),
        check_vma=False,
    )
```

```python
import functools

import jax
import jax.numpy as jnp
import numpy as np
from jax import lax
from jax.experimental import pallas as pl
from jax.experimental.pallas import tpu as pltpu
from jax.sharding import Mesh, PartitionSpec as P

ADAPTERS = 8
RANK = 16
EPSILON = 1e-05
GELU_SCALE = 0.7978845608028654
NEGATIVE = -1e30
SCALE = 64 ** -0.5
BF = jnp.bfloat16
F32 = jnp.float32
WSH = ("y", "xh")
TP = ("xl", "z")
CTX = ("xl", "z", "c")
VMEM_LIMIT = 58 * 1024 * 1024


def nn(a, b):
    return lax.dot_general(a, b, (((1,), (0,)), ((), ())), preferred_element_type=F32)


def nt(a, b):
    return lax.dot_general(a, b, (((1,), (1,)), ((), ())), preferred_element_type=F32)


def tn(a, b):
    return lax.dot_general(a, b, (((0,), (0,)), ((), ())), preferred_element_type=F32)


def adapter_mask(aid, columns):
    col = lax.broadcasted_iota(jnp.int32, (aid.shape[0], columns), 1)
    return (lax.shift_right_logical(col, 4) & 7) == aid.astype(jnp.int32)


def turn(values, cosine, sine):
    width = values.shape[1]
    lane = lax.broadcasted_iota(jnp.int32, values.shape, 1) & 63
    partner = jnp.where(
        lane < 16, pltpu.roll(values, width - 16, 1), pltpu.roll(values, 16, 1)
    )
    return values * cosine + partner * sine


ANY = pl.BlockSpec(memory_space=pl.ANY)
SMEM = pl.BlockSpec(memory_space=pltpu.SMEM)
VM = pl.BlockSpec(memory_space=pltpu.VMEM)
PARAMS = pltpu.CompilerParams(vmem_limit_bytes=VMEM_LIMIT)
MAIN = 208
SECOND = 288
NEAR = 1280


def whole(shape):
    return pl.BlockSpec(shape, lambda t: (0,) * len(shape), pipeline_mode=pl.Buffered(1))


def start_all(pairs, sem):
    for source, target in pairs:
        pltpu.make_async_copy(source, target, sem).start()


def wait_all(target, sem):
    pltpu.make_async_copy(target, target, sem).wait()


def token_copies(blocks, target):
    pairs = [(blocks[i], target.at[i // 2, i % 2], i) for i in range(6)]
    for i in range(4):
        pairs.append((blocks[6 + i], target.at[3, i // 2, pl.ds(64 * (i % 2), 64)], 6 + i // 2))
    return pairs


def start_tokens(blocks, target, sem, first, last):
    for source, part, i in token_copies(blocks, target):
        if first <= i < last:
            pltpu.make_async_copy(source, part, sem.at[i]).start()


def wait_tokens(target, sem, step):
    for i in range(2):
        part = target.at[step, i]
        pltpu.make_async_copy(part, part, sem.at[2 * step + i]).wait()


def pieces_qkv(g1, target):
    return [
        (
            g1.at[y, c, pl.ds(MAIN * xh, 128), pl.ds(0, 768)],
            target.at[pl.ds((2 * y + xh) * 256 + c * 128, 128), :],
        )
        for y in range(4)
        for xh in range(2)
        for c in range(2)
    ]


def pieces_downs(g1, target):
    return [
        (
            g1.at[:, c, pl.ds(MAIN * xh + 128 + 32 * i + 16 * b, 16), :],
            target.at[c, i, :, xh, :, pl.ds(1024 * b, 1024)],
        )
        for c in range(2)
        for i in range(2)
        for xh in range(2)
        for b in range(2)
    ]


def pieces_rank(g, base, stride, target, row):
    return [
        (
            g.at[y, c, pl.ds(stride * xh + base, 16), :],
            target.at[pl.ds(row + (2 * y + xh) * 16, 16), pl.ds(1024 * c, 1024)],
        )
        for y in range(4)
        for xh in range(2)
        for c in range(2)
    ]


def pieces_dense(g1, target, row):
    return [
        (
            g1.at[y, c, pl.ds(2 * MAIN + 32 * b, 32), :],
            target.at[pl.ds(row + 64 * y + 32 * c, 32), pl.ds(1024 * b, 1024)],
        )
        for y in range(4)
        for c in range(2)
        for b in range(2)
    ]


def pieces_w1(g2, target):
    return [
        (
            g2.at[y, c, pl.ds(SECOND * xh, 128), :],
            target.at[pl.ds((2 * y + xh) * 256 + c * 128, 128), :],
        )
        for y in range(4)
        for xh in range(2)
        for c in range(2)
    ]


def pieces_sixteen(g2, c, target, row):
    return [
        (
            g2.at[y, c, pl.ds(SECOND * xh + 128, 16), :],
            target.at[pl.ds(row + (2 * y + xh) * 16, 16), :],
        )
        for y in range(4)
        for xh in range(2)
    ]


def pieces_w2(g2, target):
    return [
        (
            g2.at[y, c, pl.ds(SECOND * xh + 144 + 64 * b, 64), :],
            target.at[pl.ds((2 * y + xh) * 128 + c * 64, 64), pl.ds(1024 * b, 1024)],
        )
        for y in range(4)
        for xh in range(2)
        for c in range(2)
        for b in range(2)
    ]


def block_diagonal(source, target):
    target[...] = jnp.zeros_like(target)
    for p in range(3):
        cols = slice(256 * p, 256 * p + 256)
        target[128 * p : 128 * p + 128, cols] = source[:, cols]


def k0_body(*refs):
    blocks, (stat_ref, x_s, x_sem) = refs[:10], refs[10:]
    start_tokens(blocks, x_s, x_sem, 0, 8)
    lane = lax.broadcasted_iota(jnp.int32, (256, 128), 1)
    for step in range(4):
        wait_tokens(x_s, x_sem, step)
        x = x_s[step].reshape(256, 2176)[:, :2048].astype(F32)
        mean = jnp.mean(x, axis=1, keepdims=True)
        center = x - mean
        spread = jnp.mean(center * center, axis=1, keepdims=True)
        stat_ref[256 * step : 256 * step + 256] = jnp.where(lane == 0, mean, lax.rsqrt(spread + EPSILON))


def k0(blocks):
    return pl.pallas_call(
        k0_body,
        in_specs=[ANY] * 10,
        out_specs=VM,
        out_shape=jax.ShapeDtypeStruct((1024, 128), F32),
        scratch_shapes=[pltpu.VMEM((4, 2, 128, 2176), BF), pltpu.SemaphoreType.DMA((8,))],
        compiler_params=PARAMS,
        cost_estimate=pl.CostEstimate(flops=20_000_000, bytes_accessed=5_000_000, transcendentals=0),
        name="norm_statistics",
    )(*blocks)


def k1_body(*refs):
    blocks, refs = refs[:10], refs[10:]
    (scal_ref, g1_ref, up_ref, misc_ref, bias_ref, cos_ref, sin_ref, stat_ref,
     hb_ref, inner_ref, keep_ref, send_ref, aid_ref, x_s, w_s, down_s, up_s, x_sem, w_sem) = refs
    step = pl.program_id(0)

    @pl.when(step == 0)
    def _():
        start_tokens(blocks, x_s, x_sem, 0, 2)
        start_all(pieces_downs(g1_ref, down_s), w_sem.at[0])
        start_all(pieces_qkv(g1_ref, w_s.at[:, pl.ds(0, 768)]), w_sem.at[1])
        start_tokens(blocks, x_s, x_sem, 2, 8)

    wait_tokens(x_s, x_sem, step)
    tile = x_s[step].reshape(256, 2176)
    x = tile[:, :2048].astype(F32)
    aid_ref[...] = tile[:, 2048:]
    aid = tile[:, 2048:2049].astype(F32)
    h = (x - stat_ref[:, 0:1]) * stat_ref[:, 1:2] * misc_ref[0:1, :] + misc_ref[1:2, :]
    hb = h.astype(BF)
    hb_ref[...] = hb

    @pl.when(step == 0)
    def _():
        block_diagonal(up_ref, up_s)
        wait_all(down_s, w_sem.at[0])
        w_s[:, 768:] = down_s[...].reshape(512, 2048).T
        wait_all(w_s.at[:, pl.ds(0, 768)], w_sem.at[1])

    pre_all = nn(hb, w_s[...])
    inner = jnp.where(adapter_mask(aid, 512), pre_all[:, 768:], 0.0).astype(BF)
    inner_ref[...] = inner
    pre_all = pre_all[:, :768] + nn(inner[:, :384], up_s[...]) + bias_ref[...]
    first_core = scal_ref[8] == 0
    cosine = jnp.concatenate([cos_ref[...]] * 2, axis=1)
    sine = jnp.concatenate([sin_ref[...]] * 2, axis=1)
    for p in range(3):
        cols = slice(256 * p, 256 * p + 256)
        pre = pre_all[:, cols]
        if p < 2:
            pre = turn(pre, cosine, sine)
        low = pre.astype(BF)
        keep_ref[p] = jnp.where(first_core, low[:, :128], low[:, 128:])
        send_ref[p] = jnp.where(first_core, low[:, 128:], low[:, :128])


def k1(blocks, scal, g1, ups, misc, bias, cosine, sine, stats):
    rows = 256
    return pl.pallas_call(
        k1_body,
        grid=(4,),
        in_specs=[ANY] * 10
        + [
            SMEM,
            ANY,
            whole((128, 768)),
            whole((2, 2048)),
            whole((1, 768)),
            pl.BlockSpec((rows, 128), lambda t: (t, 0)),
            pl.BlockSpec((rows, 128), lambda t: (t, 0)),
            pl.BlockSpec((rows, 128), lambda t: (t, 0)),
        ],
        out_specs=[
            pl.BlockSpec((rows, 2048), lambda t: (t, 0)),
            pl.BlockSpec((rows, 512), lambda t: (t, 0)),
            pl.BlockSpec((3, rows, 128), lambda t: (0, t, 0)),
            pl.BlockSpec((3, rows, 128), lambda t: (0, t, 0)),
            pl.BlockSpec((rows, 128), lambda t: (t, 0)),
        ],
        out_shape=[
            jax.ShapeDtypeStruct((1024, 2048), BF),
            jax.ShapeDtypeStruct((1024, 512), BF),
            jax.ShapeDtypeStruct((3, 1024, 128), BF),
            jax.ShapeDtypeStruct((3, 1024, 128), BF),
            jax.ShapeDtypeStruct((1024, 128), BF),
        ],
        scratch_shapes=[
            pltpu.VMEM((4, 2, 128, 2176), BF),
            pltpu.VMEM((2048, 1280), BF),
            pltpu.VMEM((2, 2, 4, 2, 16, 2048), BF),
            pltpu.VMEM((384, 768), BF),
            pltpu.SemaphoreType.DMA((8,)),
            pltpu.SemaphoreType.DMA((2,)),
        ],
        compiler_params=PARAMS,
        cost_estimate=pl.CostEstimate(flops=6_000_000_000, bytes_accessed=20_000_000, transcendentals=0),
        name="norm_qkv",
    )(*blocks, scal, g1, ups, misc, bias, cosine, sine, stats)


def k1b_body(*refs):
    blocks, refs = refs[:10], refs[10:]
    scal_ref, aid_ref, g1_ref, dd_ref, keep_ref, send_ref, ginner_ref, dy_s, w_s, dy_sem, w_sem = refs
    start_all(pieces_dense(g1_ref, w_s, 0) + pieces_rank(g1_ref, 192, MAIN, w_s, 256), w_sem)
    start_tokens(blocks, dy_s, dy_sem, 0, 8)
    wait_all(w_s, w_sem)
    for step in range(4):
        wait_tokens(dy_s, dy_sem, step)
    first_core = scal_ref[8] == 0
    both = nt(dy_s[...].reshape(1024, 2048), w_s[...])
    aid = aid_ref[:, 0:1].astype(F32)
    ginner = jnp.where(adapter_mask(aid, 128), both[:, 256:], 0.0).astype(BF)
    ginner_ref[...] = ginner
    dob = (both[:, :256] + nn(ginner, dd_ref[...])).astype(BF)
    keep_ref[...] = jnp.where(first_core, dob[:, :128], dob[:, 128:])
    send_ref[...] = jnp.where(first_core, dob[:, 128:], dob[:, :128])


def k1b(blocks, scal, aid, g1, dd):
    return pl.pallas_call(
        k1b_body,
        in_specs=[ANY] * 10 + [SMEM, VM, ANY, VM],
        out_specs=[VM, VM, VM],
        out_shape=[jax.ShapeDtypeStruct((1024, 128), BF)] * 3,
        scratch_shapes=[
            pltpu.VMEM((4, 2, 128, 2048), BF),
            pltpu.VMEM((384, 2048), BF),
            pltpu.SemaphoreType.DMA((8,)),
            pltpu.SemaphoreType.DMA,
        ],
        compiler_params=PARAMS,
        cost_estimate=pl.CostEstimate(flops=2_000_000_000, bytes_accessed=8_000_000, transcendentals=0),
        name="attention_output_grad",
    )(*blocks, scal, aid, g1, dd)


def k3_body(
    scal_ref, qkv_keep, qkv_recv, dob_keep, dob_recv, idrow_ref, idcol_ref, cos_ref, sin_ref,
    keep_out, send_out, x_s, out_s, kt_s, vt_s, dk_s, dv_s, sem, sem_out,
):
    core = scal_ref[8]
    copies = []
    for b in range(8):
        rows = pl.ds(128 * b, 128)
        spot = scal_ref[b]
        for side, (qkv, dob) in enumerate(((qkv_keep, dob_keep), (qkv_recv, dob_recv))):
            parity = core if side == 0 else 1 - core
            copies.append((qkv.at[:, rows, :], x_s.at[pl.ds(0, 3), spot, parity]))
            copies.append((dob.at[rows, :], x_s.at[3, spot, parity]))
    start_all(copies, sem)
    dk_s[...] = jnp.zeros_like(dk_s)
    dv_s[...] = jnp.zeros_like(dv_s)
    wait_all(x_s, sem)
    kt_s[...] = x_s[1].reshape(2048, 128).T
    vt_s[...] = x_s[2].reshape(2048, 128).T
    tile = 256
    lane = lax.broadcasted_iota(jnp.int32, (tile, 128), 1)

    def span(i, start, stop):
        return x_s[i, start // 256 : stop // 256].reshape(stop - start, 128)

    for t in range(8):
        start, stop = tile * t, tile * t + tile
        length = min(stop + tile, 2048)
        q = span(0, start, stop)
        dob = span(3, start, stop)
        zero = jnp.zeros_like(q)
        q = q * jnp.asarray(SCALE, BF)
        q2 = jnp.concatenate([jnp.where(lane < 64, q, zero), jnp.where(lane < 64, zero, q)], axis=0)
        d2 = jnp.concatenate([jnp.where(lane < 64, dob, zero), jnp.where(lane < 64, zero, dob)], axis=0)
        query_ids = idrow_ref[0:1, start:stop]
        query_ids = jnp.concatenate([query_ids, query_ids], axis=1)
        allowed = idcol_ref[start:length, 0:1] <= query_ids
        s = jnp.where(allowed, nt(span(1, start, length), q2), NEGATIVE)
        largest = jnp.max(s, axis=0, keepdims=True)
        if start:
            s_head = nt(span(1, 0, start), q2)
            largest = jnp.maximum(largest, jnp.max(s_head, axis=0, keepdims=True))
            s = jnp.concatenate([s_head, s], axis=0)
        e = jnp.exp(s - largest)
        recip = 1.0 / jnp.sum(e, axis=0, keepdims=True)
        p = e * recip
        pb = p.astype(BF)
        ot = nn(vt_s[:, :length], pb)
        dp = nt(span(2, 0, length), d2)
        o_parts = [ot[:64, :256], ot[64:, 256:]]
        dobt = dob.astype(F32).T
        delta = jnp.concatenate(
            [
                jnp.sum(o_parts[0] * dobt[:64], axis=0, keepdims=True),
                jnp.sum(o_parts[1] * dobt[64:], axis=0, keepdims=True),
            ],
            axis=1,
        )
        ds = (p * (dp - delta)).astype(BF)
        dk_s[:length] += nn(ds, q2)
        dv_s[:length] += nn(pb, d2)
        dqt = nn(kt_s[:, :length], ds)
        dq_parts = [dqt[:64, :256], dqt[64:, 256:]]
        o = jnp.concatenate(o_parts, axis=0).T
        dq = jnp.concatenate(dq_parts, axis=0).T * SCALE
        rows = slice(start, stop)
        out_s[0, t] = o.astype(BF).reshape(2, 128, 128)
        out_s[1, t] = turn(dq, cos_ref[rows], -sin_ref[rows]).astype(BF).reshape(2, 128, 128)
    out_s[2] = turn(dk_s[...], cos_ref[...], -sin_ref[...]).astype(BF).reshape(8, 2, 128, 128)
    out_s[3] = dv_s[...].astype(BF).reshape(8, 2, 128, 128)
    copies = []
    for b in range(8):
        rows = pl.ds(128 * b, 128)
        spot = scal_ref[b]
        copies.append((out_s.at[:, spot, core], keep_out.at[:, rows, :]))
        copies.append((out_s.at[:, spot, 1 - core], send_out.at[:, rows, :]))
    start_all(copies, sem_out)
    wait_all(out_s, sem_out)


def k3(scal, qkv_keep, qkv_recv, dob_keep, dob_recv, idrow, idcol, cosine, sine):
    vm = pl.BlockSpec(memory_space=pltpu.VMEM)
    return pl.pallas_call(
        k3_body,
        in_specs=[SMEM] + [ANY] * 4 + [vm] * 4,
        out_specs=[ANY, ANY],
        out_shape=[jax.ShapeDtypeStruct((4, 1024, 128), BF)] * 2,
        scratch_shapes=[
            pltpu.VMEM((4, 8, 2, 128, 128), BF),
            pltpu.VMEM((4, 8, 2, 128, 128), BF),
            pltpu.VMEM((128, 2048), BF),
            pltpu.VMEM((128, 2048), BF),
            pltpu.VMEM((2048, 128), F32),
            pltpu.VMEM((2048, 128), F32),
            pltpu.SemaphoreType.DMA,
            pltpu.SemaphoreType.DMA,
        ],
        compiler_params=PARAMS,
        cost_estimate=pl.CostEstimate(flops=15_000_000_000, bytes_accessed=8_000_000, transcendentals=5_000_000),
        name="attention",
    )(scal, qkv_keep, qkv_recv, dob_keep, dob_recv, idrow, idcol, cosine, sine)


def heads_of(keep_ref, recv_ref, i, first_core):
    a, b = keep_ref[i], recv_ref[i]
    return jnp.concatenate([jnp.where(first_core, a, b), jnp.where(first_core, b, a)], axis=1)


def tile_spec(width, rows=256):
    return pl.BlockSpec((rows, width), lambda t, s: (t, 0))


def const_spec(shape):
    return pl.BlockSpec(shape, lambda t, s: (0,) * len(shape), pipeline_mode=pl.Buffered(1))


def placed_spec(width):
    return pl.BlockSpec((2, 1, 128, width), lambda t, s: (0, s[12 + t], 0, 0))


def place(ref, xl, value):
    ref[xl, 0] = value[:128]
    ref[1 - xl, 0] = value[128:]


def accumulate(step, pairs):
    @pl.when(step == 0)
    def _():
        for ref, value in pairs:
            ref[...] = value

    @pl.when(step > 0)
    def _():
        for ref, value in pairs:
            ref[...] += value


def att_spec(first, count):
    return pl.BlockSpec((count, 256, 128), lambda t, s: (first, t, 0))


def k2f_body(
    scal_ref, hb_ref, aid_ref, inner_ref, gdense_ref, keep_ref, recv_ref, g1_ref, g2_ref, dd_ref, b1_ref,
    out_ref, gb_ref, slope_ref, low_ref, gdd_ref,
    w1_s, wout_s, d2_s, rest_s, sems,
):
    step = pl.program_id(0)

    @pl.when(step == 0)
    def _():
        start_all(pieces_w1(g2_ref, w1_s) + pieces_sixteen(g2_ref, 0, w1_s, 2048), sems.at[0])
        start_all(pieces_sixteen(g2_ref, 1, d2_s, 0), sems.at[1])
        start_all(pieces_w2(g2_ref, wout_s) + pieces_dense(g1_ref, wout_s, 1024), sems.at[2])
        start_all(
            pieces_rank(g1_ref, 192, MAIN, rest_s, 0) + pieces_rank(g2_ref, 272, SECOND, rest_s, 128), sems.at[3]
        )
        wout_s[:, 2048:] = jnp.zeros((1280, 256), BF)
        wout_s[1024:, 2048:2176] = dd_ref[...].T
        wait_all(d2_s, sems.at[1])
        wout_s[:1024, 2176:] = d2_s[...].T
        wait_all(w1_s, sems.at[0])

    keep = adapter_mask(aid_ref[:, 0:1].astype(F32), 256)
    f = nn(jnp.concatenate([hb_ref[...], inner_ref[...]], axis=1), w1_s[...]) + b1_ref[...]
    square = f * f
    th = jnp.tanh(GELU_SCALE * f * (1.0 + 0.044715 * square))
    half = 0.5 * (1.0 + th)
    gb = (f * half).astype(BF)
    gb_ref[...] = gb
    slope = half + (0.5 * GELU_SCALE) * f * (1.0 - th * th) * (1.0 + 3 * 0.044715 * square)
    slope_ref[...] = slope.astype(BF)
    ob = heads_of(keep_ref, recv_ref, 0, scal_ref[8] == 0)

    @pl.when(step == 0)
    def _():
        wait_all(wout_s.at[:, pl.ds(0, 2048)], sems.at[2])
        wait_all(rest_s, sems.at[3])

    total = nn(jnp.concatenate([gb, ob], axis=1), wout_s[...])
    low = jnp.where(keep, total[:, 2048:], 0.0).astype(BF)
    low_ref[...] = low
    out = (total[:, :2048] + nn(low, rest_s[...])).astype(BF)
    place(out_ref, scal_ref[10], out)
    accumulate(step, [(gdd_ref, tn(gdense_ref[...], ob))])


def k2f(scal, hb, aid, inner, gdense, keep, recv, g1, g2, dd, b1):
    return pl.pallas_call(
        k2f_body,
        grid_spec=pltpu.PrefetchScalarGridSpec(
            num_scalar_prefetch=1,
            grid=(4,),
            in_specs=[
                tile_spec(2048),
                tile_spec(128),
                pl.BlockSpec((256, 128), lambda t, s: (t, 3)),
                tile_spec(128),
                att_spec(0, 1),
                att_spec(0, 1),
                ANY,
                ANY,
                const_spec((128, 256)),
                const_spec((1, 1024)),
            ],
            out_specs=[
                placed_spec(2048),
                tile_spec(1024),
                tile_spec(1024),
                tile_spec(256),
                const_spec((128, 256)),
            ],
            scratch_shapes=[
                pltpu.VMEM((2176, 1024), BF),
                pltpu.VMEM((1280, 2304), BF),
                pltpu.VMEM((128, 1024), BF),
                pltpu.VMEM((256, 2048), BF),
                pltpu.SemaphoreType.DMA((4,)),
            ],
        ),
        out_shape=[
            jax.ShapeDtypeStruct((2, 4, 128, 2048), BF),
            jax.ShapeDtypeStruct((1024, 1024), BF),
            jax.ShapeDtypeStruct((1024, 1024), BF),
            jax.ShapeDtypeStruct((1024, 256), BF),
            jax.ShapeDtypeStruct((128, 256), F32),
        ],
        compiler_params=PARAMS,
        cost_estimate=pl.CostEstimate(flops=14_000_000_000, bytes_accessed=24_000_000, transcendentals=1_000_000),
        name="out_rows",
    )(scal, hb, aid, inner, gdense, keep, recv, g1, g2, dd, b1)


def k2g_body(scal_ref, *refs):
    blocks, refs = refs[:10], refs[10:]
    (aid_ref, inner_ref, keep_ref, recv_ref, gb_ref, slope_ref, low_out_ref, g2_ref, up_ref, fold_ref,
     df_ref, low_ref, small_ref, gup1_ref, gd2_ref,
     dy_s, w2_s, up1_s, d2_s, up_s, dy_sem, sems) = refs
    step = pl.program_id(0)

    @pl.when(step == 0)
    def _():
        start_tokens(blocks, dy_s, dy_sem, 0, 2)
        start_all(pieces_w2(g2_ref, w2_s) + pieces_rank(g2_ref, 272, SECOND, w2_s, 1024), sems.at[0])
        start_all(pieces_sixteen(g2_ref, 1, d2_s, 0), sems.at[1])
        start_all(pieces_sixteen(g2_ref, 0, up1_s, 0), sems.at[2])
        start_tokens(blocks, dy_s, dy_sem, 2, 8)
        block_diagonal(up_ref, up_s)
        wait_all(w2_s, sems.at[0])
        wait_all(d2_s, sems.at[1])
        wait_all(up1_s, sems.at[2])

    wait_tokens(dy_s, dy_sem, step)
    aid = aid_ref[:, 0:1].astype(F32)
    first_core = scal_ref[8] == 0
    wide = nt(dy_s[step].reshape(256, 2048), w2_s[...])
    ginner2 = jnp.where(adapter_mask(aid, 128), wide[:, 1024:], 0.0).astype(BF)
    dpre = jnp.concatenate([heads_of(keep_ref, recv_ref, p, first_core) for p in (1, 2, 3)], axis=1)
    ginner = nt(dpre, up_s[...])
    df = ((wide[:, :1024] + nn(ginner2, d2_s[...])) * slope_ref[...].astype(F32)).astype(BF)
    df_ref[...] = df
    ginner1 = nt(df, up1_s[...])
    low = jnp.concatenate([ginner, ginner1], axis=1)
    low = jnp.where(adapter_mask(aid, 512), low, 0.0).astype(BF)
    low_ref[...] = low
    folded = nn(jnp.concatenate([low, low_out_ref[...]], axis=1), fold_ref[...])
    place(small_ref, scal_ref[10], folded.astype(BF))
    accumulate(step, [(gup1_ref, tn(inner_ref[...], df)), (gd2_ref, tn(ginner2, gb_ref[...]))])


def k2g(blocks, scal, aid, inner, keep, recv, gb, slope, low_out, g2, ups, fold):
    return pl.pallas_call(
        k2g_body,
        grid_spec=pltpu.PrefetchScalarGridSpec(
            num_scalar_prefetch=1,
            grid=(4,),
            in_specs=[ANY] * 10
            + [
                tile_spec(128),
                pl.BlockSpec((256, 128), lambda t, s: (t, 3)),
                att_spec(0, 4),
                att_spec(0, 4),
                tile_spec(1024),
                tile_spec(1024),
                tile_spec(256),
                ANY,
                const_spec((128, 768)),
                const_spec((768, 128)),
            ],
            out_specs=[
                tile_spec(1024),
                tile_spec(512),
                placed_spec(128),
                const_spec((128, 1024)),
                const_spec((128, 1024)),
            ],
            scratch_shapes=[
                pltpu.VMEM((4, 2, 128, 2048), BF),
                pltpu.VMEM((1152, 2048), BF),
                pltpu.VMEM((128, 1024), BF),
                pltpu.VMEM((128, 1024), BF),
                pltpu.VMEM((384, 768), BF),
                pltpu.SemaphoreType.DMA((8,)),
                pltpu.SemaphoreType.DMA((3,)),
            ],
        ),
        out_shape=[
            jax.ShapeDtypeStruct((1024, 1024), BF),
            jax.ShapeDtypeStruct((1024, 512), BF),
            jax.ShapeDtypeStruct((2, 4, 128, 128), BF),
            jax.ShapeDtypeStruct((128, 1024), F32),
            jax.ShapeDtypeStruct((128, 1024), F32),
        ],
        compiler_params=PARAMS,
        cost_estimate=pl.CostEstimate(flops=8_000_000_000, bytes_accessed=20_000_000, transcendentals=0),
        name="feed_forward_grad",
    )(scal, *blocks, aid, inner, keep, recv, gb, slope, low_out, g2, ups, fold)


def k2h_body(
    scal_ref, df_ref, keep_ref, recv_ref, low_ref, inner_ref, g1_ref, g2_ref,
    near_ref, owns_ref, sides_ref, gqkv_ref, w_s, down_s, sems,
):
    step = pl.program_id(0)

    @pl.when(step == 0)
    def _():
        start_all(
            pieces_w1(g2_ref, w_s.at[:, pl.ds(0, 1024)]) + pieces_qkv(g1_ref, w_s.at[:, pl.ds(1024, 768)]), sems.at[0]
        )
        start_all(pieces_downs(g1_ref, down_s), sems.at[1])
        wait_all(w_s, sems.at[0])
        wait_all(down_s, sems.at[1])

    first_core = scal_ref[8] == 0
    dpre = [heads_of(keep_ref, recv_ref, p, first_core) for p in (1, 2, 3)]
    dh = nt(jnp.concatenate([df_ref[...]] + dpre, axis=1), w_s[...])
    dh = (dh + nn(low_ref[...], down_s[...].reshape(512, 2048))).astype(BF)
    near_ref[0] = dh[:128, :NEAR]
    near_ref[1] = dh[128:, :NEAR]
    owns_ref[0] = dh[:128, NEAR:]
    sides_ref[0] = dh[128:, NEAR:]
    gqkv = [tn(inner_ref[:, 128 * p : 128 * p + 128], dpre[p]) for p in range(3)]
    accumulate(step, [(gqkv_ref, jnp.concatenate(gqkv, axis=1))])


def k2h(scal, df, keep, recv, low_in, inner, g1, g2):
    return pl.pallas_call(
        k2h_body,
        grid_spec=pltpu.PrefetchScalarGridSpec(
            num_scalar_prefetch=1,
            grid=(4,),
            in_specs=[tile_spec(1024), att_spec(0, 4), att_spec(0, 4), tile_spec(512), tile_spec(512), ANY, ANY],
            out_specs=[
                pl.BlockSpec((2, 128, NEAR), lambda t, s: (t, 0, 0)),
                pl.BlockSpec((1, 128, 2048 - NEAR), lambda t, s: (t, 0, 0)),
                pl.BlockSpec((1, 128, 2048 - NEAR), lambda t, s: (t, 0, 0)),
                const_spec((128, 768)),
            ],
            scratch_shapes=[
                pltpu.VMEM((2048, 1792), BF),
                pltpu.VMEM((2, 2, 4, 2, 16, 2048), BF),
                pltpu.SemaphoreType.DMA((2,)),
            ],
        ),
        out_shape=[
            jax.ShapeDtypeStruct((8, 128, NEAR), BF),
            jax.ShapeDtypeStruct((4, 128, 2048 - NEAR), BF),
            jax.ShapeDtypeStruct((4, 128, 2048 - NEAR), BF),
            jax.ShapeDtypeStruct((128, 768), F32),
        ],
        compiler_params=PARAMS,
        cost_estimate=pl.CostEstimate(flops=10_000_000_000, bytes_accessed=18_000_000, transcendentals=0),
        name="hidden_grad",
    )(scal, df, keep, recv, low_in, inner, g1, g2)


def k5_body(scal_ref, small_ref, aid_ref, hb_ref, spread_ref, gup1_ref, gd2_ref, gqkv_ref, gdd_ref, *refs):
    blocks, refs = refs[:10], refs[10:]
    keep_ref, send_ref, dy_s, sem = refs
    column = pl.multiple_of(256 * scal_ref[9], 256)
    start_all(
        [(source.at[:, pl.ds(column, 256)], part) for source, part, _ in token_copies(blocks, dy_s)], sem
    )
    first_core = scal_ref[8] == 0

    def store(section, left, right):
        kept = jnp.where(first_core, left, right)
        sent = jnp.where(first_core, right, left)
        keep_ref[:, 16 * section : 16 * section + 16] = kept.reshape(8, 16, 512)
        send_ref[:, 16 * section : 16 * section + 16] = sent.astype(BF).reshape(8, 16, 512)

    small = jnp.concatenate([small_ref[scal_ref[b]] for b in range(8)], axis=0)
    aid = aid_ref[:, 0:1].astype(F32)
    wide = jnp.where(adapter_mask(aid, 768), nn(small, spread_ref[...]), 0.0).astype(BF)
    down = tn(wide[:, :512], hb_ref[...])
    store(
        0,
        jnp.concatenate([down[:128], down[128:256]], axis=1),
        jnp.concatenate([down[256:384], down[384:]], axis=1),
    )
    store(1, gqkv_ref[:, :512], jnp.concatenate([gqkv_ref[:, 512:], gdd_ref[...]], axis=1))
    store(2, gup1_ref[:, :512], gup1_ref[:, 512:])
    store(3, gd2_ref[:, :512], gd2_ref[:, 512:])
    wait_all(dy_s, sem)
    up = tn(wide[:, 512:], dy_s[...].reshape(1024, 256))
    left = jnp.concatenate([up[:128], up[128:]], axis=1)
    store(4, left, jnp.zeros_like(left))


def k5(scal, small, aid, hb, spread, gup1, gd2, gqkv, gdd, blocks):
    def const(shape):
        return pl.BlockSpec(shape, lambda t, s: (0,) * len(shape))

    return pl.pallas_call(
        k5_body,
        grid_spec=pltpu.PrefetchScalarGridSpec(
            num_scalar_prefetch=1,
            grid=(1,),
            in_specs=[
                const((8, 128, 128)),
                const((1024, 128)),
                pl.BlockSpec((1024, 256), lambda t, s: (0, s[9])),
                const((128, 768)),
                const((128, 1024)),
                const((128, 1024)),
                const((128, 768)),
                const((128, 256)),
            ]
            + [ANY] * 10,
            out_specs=[const((8, 80, 512)), const((8, 80, 512))],
            scratch_shapes=[pltpu.VMEM((4, 2, 128, 256), BF), pltpu.SemaphoreType.DMA],
        ),
        out_shape=[jax.ShapeDtypeStruct((8, 80, 512), F32), jax.ShapeDtypeStruct((8, 80, 512), BF)],
        compiler_params=PARAMS,
        cost_estimate=pl.CostEstimate(flops=1_500_000_000, bytes_accessed=6_000_000, transcendentals=0),
        name="adapter_grads",
    )(scal, small, aid, hb, spread, gup1, gd2, gqkv, gdd, *blocks)


def kf_body(scal_ref, mine_ref, theirs_ref, down_ref, up_ref, dd_ref, ud_ref, f1d_ref, f1u_ref, f2d_ref, f2u_ref):
    lane = lax.broadcasted_iota(jnp.int32, (16, 128), 1)

    core = scal_ref[8]

    def part(j, half, section, start, width):
        rows, cols = slice(16 * section, 16 * section + 16), slice(start, start + width)
        return jnp.where(core == half, mine_ref[j, rows, cols], theirs_ref[j, rows, cols]).astype(F32)

    for j in range(8):
        block = slice(256 * j, 256 * j + 256)
        down_ref[0, :, block] = part(j, 0, 0, 0, 256)
        down_ref[1, :, block] = part(j, 0, 0, 256, 256)
        down_ref[2, :, block] = part(j, 1, 0, 0, 256)
        f1d_ref[:, block] = part(j, 1, 0, 256, 256)
        ud_ref[:, block] = part(j, 0, 4, 0, 256)
        f2u_ref[:, block] = part(j, 0, 4, 256, 256)
        for w in range(8):
            spot = slice(1024 * w + 128 * j, 1024 * w + 128 * j + 128)
            f1u_ref[:, spot] = part(j, w // 4, 2, 128 * (w % 4), 128)
            f2d_ref[:, spot] = part(j, w // 4, 3, 128 * (w % 4), 128)
    for i in range(4):
        for x in range(2):
            for y in range(4):
                for h in range(2):
                    start = 256 * (i % 2) + 128 * (y // 2)
                    a = part(4 * x + 2 * h, i // 2, 1, start, 128)
                    b = part(4 * x + 2 * h + 1, i // 2, 1, start, 128)
                    if y % 2:
                        a = pltpu.roll(a, 64, 1)
                    else:
                        b = pltpu.roll(b, 64, 1)
                    value = jnp.where(lane < 64, a, b)
                    spot = slice(256 * (2 * y + x) + 128 * h, 256 * (2 * y + x) + 128 * h + 128)
                    if i < 3:
                        up_ref[i, :, spot] = value
                    else:
                        dd_ref[:, spot] = value


def kf(scal, mine, theirs):
    return pl.pallas_call(
        kf_body,
        in_specs=[SMEM, VM, VM],
        out_specs=[VM] * 8,
        out_shape=[
            jax.ShapeDtypeStruct((3, 16, 2048), F32),
            jax.ShapeDtypeStruct((3, 16, 2048), F32),
            jax.ShapeDtypeStruct((16, 2048), F32),
            jax.ShapeDtypeStruct((16, 2048), F32),
            jax.ShapeDtypeStruct((16, 2048), F32),
            jax.ShapeDtypeStruct((16, 8192), F32),
            jax.ShapeDtypeStruct((16, 8192), F32),
            jax.ShapeDtypeStruct((16, 2048), F32),
        ],
        compiler_params=PARAMS,
        name="finish",
    )(scal, mine, theirs)


def kn_body(x_ref, dy_ref, gain_ref, own_ref, up_ref, down_ref, side_ref, t_ref, up2_ref, down2_ref, out_ref):
    def total(*parts):
        return sum(p[...].astype(F32) for p in parts)

    dh = jnp.concatenate([total(own_ref, up_ref, down_ref, side_ref), total(t_ref, up2_ref, down2_ref)], axis=1)
    x = x_ref[...].astype(F32)
    center = x - jnp.mean(x, axis=1, keepdims=True)
    inv = lax.rsqrt(jnp.mean(center * center, axis=1, keepdims=True) + EPSILON)
    hn = center * inv
    e = dh * gain_ref[...]
    dx = (e - jnp.mean(e, axis=1, keepdims=True) - hn * jnp.mean(e * hn, axis=1, keepdims=True)) * inv
    out_ref[...] = (dy_ref[...].astype(F32) + dx).astype(BF)


def kn(*args):
    return pl.pallas_call(
        kn_body,
        in_specs=[VM] * 10,
        out_specs=VM,
        out_shape=jax.ShapeDtypeStruct((128, 2048), BF),
        compiler_params=PARAMS,
        name="norm_grad",
    )(*args)


def pack1_body(
    scal_ref, wq, wk, wv, wd, ad_ref, fd_ref, au_ref, dd_ref, du_ref, misc_ref, b1_ref,
    own_ref, other_ref, w_s, d_s, sem, d_sem,
):
    c, z = scal_ref[8], scal_ref[11]
    start_all([(w.at[pl.ds(128 * c, 128), :], w_s.at[i]) for i, w in enumerate((wq, wk, wv))], sem)
    start_all([(wd.at[pl.ds(64 * z + 32 * c, 32), :], d_s)], d_sem)
    first_core = c == 0
    odd = lax.rem(z, 2) == 1
    targets = ((own_ref, scal_ref[10]), (other_ref, 1 - scal_ref[10]))

    def head_pair(read, rows, i, xl):
        lane = lax.broadcasted_iota(jnp.int32, (rows, 128), 1)
        parts = []
        for k in range(2):
            start = (2 * (i + k) + xl) * 256 + (z // 2) * 128
            v = read(pl.ds(pl.multiple_of(start, 128), 128)).astype(F32)
            turned = pltpu.roll(v, 64, 1)
            parts.append(jnp.where(odd, turned, v) if k == 0 else jnp.where(odd, v, turned))
        return jnp.where(lane < 64, parts[0], parts[1]).astype(BF)

    half = pl.ds(pl.multiple_of((z // 2) * 128, 128), 128)
    row = lax.broadcasted_iota(jnp.int32, (16, 128), 0)
    lane = lax.broadcasted_iota(jnp.int32, (16, 128), 1)

    def biases(xl):
        plain = misc_ref[:, :128].astype(F32), misc_ref[:, 128:256].astype(F32)
        mine = misc_ref[:, half].astype(F32)
        turned = pltpu.roll(mine, 64, 1)
        low = jnp.where(odd, turned, mine)
        high = jnp.where(odd, mine, turned)
        query_key = jnp.where(lane[:1] < 64, low[4:5], high[5:6])
        value = jnp.where(lane[:1] < 64, low[6:7], 0.0)
        hidden = jnp.where(row[:8] == xl * 4 + z, b1_ref[...].astype(F32), 0.0)
        hidden = jnp.sum(hidden, axis=0, keepdims=True)
        left = jnp.where(row < 4, plain[0], jnp.where(row == 4, query_key, hidden))
        right = jnp.where(row < 4, plain[1], value)
        return left.astype(BF), right.astype(BF)

    a = jnp.where(first_core, ad_ref[0], ad_ref[2])
    b = jnp.where(first_core, ad_ref[1], fd_ref[...])
    du = jnp.where(first_core, du_ref[:, :1024], du_ref[:, 1024:])
    for out_ref, xl in targets:
        rows_of = biases(xl)
        for p in range(4):
            for i in (0, 2):
                read = (lambda s, p=p: au_ref[p, :, s]) if p < 3 else (lambda s: dd_ref[:, s])
                value = head_pair(read, 16, i, xl)
                rows = slice(16 * p, 16 * p + 16)
                if p == 0:
                    value = jnp.where(first_core, value, rows_of[i // 2])
                out_ref[rows, 768 + 64 * i : 768 + 64 * i + 128] = value
        out_ref[64:128, 768:] = jnp.zeros((64, 256), BF)
        out_ref[128:144] = a[:, :1024]
        out_ref[144:160] = a[:, 1024:]
        out_ref[160:176] = b[:, :1024]
        out_ref[176:192] = b[:, 1024:]
        out_ref[192:208] = du
    wait_all(d_s, d_sem)
    for out_ref, _ in targets:
        out_ref[208:240] = d_s[:, :1024]
        out_ref[240:272] = d_s[:, 1024:]
    wait_all(w_s, sem)
    for p in range(3):
        for i in (0, 2):
            start = 256 * p + 64 * i
            for out_ref, xl in targets:
                out_ref[:128, start : start + 128] = head_pair(lambda s, p=p: w_s[p, :, s], 128, i, xl)


def pack1(scal, wq, wk, wv, wd, ad, fd, au, dd, du, misc, b1):
    return pl.pallas_call(
        pack1_body,
        in_specs=[SMEM] + [ANY] * 4 + [VM] * 7,
        out_specs=[VM, VM],
        out_shape=[jax.ShapeDtypeStruct((272, 1024), BF)] * 2,
        scratch_shapes=[
            pltpu.VMEM((3, 128, 2048), BF),
            pltpu.VMEM((32, 2048), BF),
            pltpu.SemaphoreType.DMA,
            pltpu.SemaphoreType.DMA,
        ],
        compiler_params=PARAMS,
        cost_estimate=pl.CostEstimate(flops=1_000_000, bytes_accessed=4_000_000, transcendentals=0),
        name="pack_qkv",
    )(scal, wq, wk, wv, wd, ad, fd, au, dd, du, misc, b1)


def pack2_body(scal_ref, w1, w2, up_ref, down_ref, up2_ref, own_ref, w1_s, w2_s, sem, sem2):
    c, j = scal_ref[8], scal_ref[9]
    start_all([(w1.at[pl.ds(128 * c, 128), :], w1_s)], sem)
    start_all([(w2.at[pl.ds(128 * j + 64 * c, 64), :], w2_s)], sem2)
    first_core = c == 0
    own_ref[272:288] = jnp.where(first_core, up2_ref[:, :1024], up2_ref[:, 1024:])

    def column(w):
        return pl.ds(pl.multiple_of(1024 * w + 128 * j, 128), 128)

    for w in range(8):
        own_ref[128:144, 128 * w : 128 * w + 128] = jnp.where(first_core, up_ref[:, column(w)], down_ref[:, column(w)])
    wait_all(w2_s, sem2)
    own_ref[144:208] = w2_s[:, :1024]
    own_ref[208:272] = w2_s[:, 1024:]
    wait_all(w1_s, sem)
    for w in range(8):
        own_ref[:128, 128 * w : 128 * w + 128] = w1_s[:, column(w)]


def pack2(scal, w1, w2, up, down, up2):
    return pl.pallas_call(
        pack2_body,
        in_specs=[SMEM, ANY, ANY, VM, VM, VM],
        out_specs=VM,
        out_shape=jax.ShapeDtypeStruct((288, 1024), BF),
        scratch_shapes=[
            pltpu.VMEM((128, 8192), BF),
            pltpu.VMEM((64, 2048), BF),
            pltpu.SemaphoreType.DMA,
            pltpu.SemaphoreType.DMA,
        ],
        compiler_params=PARAMS,
        cost_estimate=pl.CostEstimate(flops=1_000_000, bytes_accessed=4_000_000, transcendentals=0),
        name="pack_hidden",
    )(scal, w1, w2, up, down, up2)


def rotary_tables(positions):
    lane = np.arange(128) % 64
    rate = np.where(lane < 32, 10000.0 ** (-2.0 * (lane % 16) / 32.0), 0.0).astype(np.float32)
    sign = np.where(lane < 16, -1.0, 1.0).astype(np.float32)
    angles = positions.astype(F32)[:, None] * jnp.asarray(rate)[None, :]
    return jnp.cos(angles), jnp.sin(angles) * jnp.asarray(sign)[None, :]


def fold_matrix():
    row = np.arange(768)
    target = (row // 128) * 16 + row % 16
    return jnp.asarray((target[:, None] == np.arange(128)[None, :]).astype(np.float32)).astype(BF)


def halves(a):
    m = a.shape[1] // 2
    return jnp.concatenate([a[:, :m], a[:, m:]], axis=0)


SWAP = [(0, 1), (1, 0)]
FLIP = [(i, 3 - i) for i in range(4)]
UP = [(i, (i + 1) % 4) for i in range(4)]
DOWN = [(i, (i + 3) % 4) for i in range(4)]
Z_OFFSETS = (0, -1, 1, 2)


def together(*values):
    return lax.optimization_barrier(values)


def up(a):
    return lax.ppermute(a, "z", UP)


def down(a):
    return lax.ppermute(a, "z", DOWN)


def across(a):
    return lax.ppermute(a, "xl", SWAP)


def gather_pair(own, other, single):
    xh = lax.axis_index("xh")
    parts = [jnp.where(xh == 0, own, other), jnp.where(xh == 0, other, own)]
    if single is not None:
        parts.append(single)
    packed = jnp.concatenate(parts, axis=0)
    g = lax.all_gather(packed, ("y", "c"), axis=0, tiled=False)
    return g.reshape((4, 2) + packed.shape)


def add(*terms):
    return sum(t.astype(F32) for t in terms)


def scatter_sum(near, owns, sides):
    own, side, down_own, down_side, up_own, up_side, far_own, far_side = [near[b] for b in range(8)]
    from_side = lax.ppermute(sides, "xl", SWAP)
    via_below = lax.ppermute(far_own, "z", UP)
    via_above = lax.ppermute(far_side, "z", DOWN)
    up_side = lax.ppermute(up_side, "z", UP)
    down_own = lax.ppermute(down_own, "z", DOWN)
    up_own = lax.ppermute(add(up_own, via_below).astype(BF), "z", UP)
    down_side = lax.ppermute(add(down_side, via_above).astype(BF), "z", DOWN)
    side = lax.ppermute(add(side, up_side, down_side).astype(BF), "xl", SWAP)
    t = add(owns, from_side)
    far = t[3].astype(BF)
    half_up = lax.ppermute(far[:64], "z", UP)
    half_down = lax.ppermute(far[64:], "z", DOWN)
    up = jnp.concatenate([t[2, :64] + half_up.astype(F32), t[2, 64:]], axis=0).astype(BF)
    down = jnp.concatenate([t[1, :64], t[1, 64:] + half_down.astype(F32)], axis=0).astype(BF)
    return own, up_own, down_own, side, t[0], lax.ppermute(up, "z", UP), lax.ppermute(down, "z", DOWN)


def local(
    inputs,
    output_cotangent,
    block_index_per_position,
    adapter_index_per_run,
    norm_gain,
    norm_bias,
    query_weight,
    key_weight,
    value_weight,
    dense_weight,
    query_bias,
    key_bias,
    value_bias,
    dense_bias,
    feedforward_in_weight,
    feedforward_in_bias,
    feedforward_out_weight,
    feedforward_out_bias,
    adapter_attention_down,
    adapter_attention_up,
    adapter_dense_down,
    adapter_dense_up,
    adapter_feedforward_in_down,
    adapter_feedforward_in_up,
    adapter_feedforward_out_down,
    adapter_feedforward_out_up,
):
    xl, z, c = lax.axis_index("xl"), lax.axis_index("z"), lax.axis_index("c")
    xh = lax.axis_index("xh")
    j = xl * 4 + z
    x_own = inputs[0]
    dy_own = output_cotangent[0]
    run_adapter = adapter_index_per_run[0, 0].astype(F32).astype(BF)
    block_row = block_index_per_position[0]
    z_of = [lax.rem(z + o + 4, 4) for o in Z_OFFSETS]
    spots = [(xl if side == 0 else 1 - xl) * 4 + zz for zz in z_of for side in range(2)]
    scal = jnp.stack(spots + [c, j, xl, z] + z_of).astype(jnp.int32)

    zero = jnp.zeros((256,), BF)
    misc_own = jnp.stack(
        [norm_gain, norm_bias, dense_bias, feedforward_out_bias, query_bias, key_bias, value_bias] + [zero] * 9
    )
    sent1, for_other = pack1(
        scal,
        query_weight,
        key_weight,
        value_weight,
        dense_weight,
        adapter_attention_down[0],
        adapter_feedforward_in_down[0],
        adapter_attention_up[0],
        adapter_dense_down[0],
        adapter_dense_up[0],
        misc_own,
        feedforward_in_bias.reshape(8, 128),
    )
    own2 = pack2(
        scal,
        feedforward_in_weight,
        feedforward_out_weight,
        adapter_feedforward_in_up[0],
        adapter_feedforward_out_down[0],
        adapter_feedforward_out_up[0],
    )
    spread = jnp.stack(spots)
    my_positions = ((spread * 2 + c) * 128)[:, None] + jnp.arange(128, dtype=jnp.int32)[None, :]
    tables = rotary_tables(my_positions.reshape(1024)) + rotary_tables(jnp.arange(2048, dtype=jnp.int32))
    tables = tables + (jnp.broadcast_to(block_row[:, None], (2048, 128)),)
    x_send = jnp.concatenate([x_own, jnp.full((128, 128), run_adapter, BF)], axis=1)

    x_up, x_down, x_side = together(up(x_send), down(x_send), across(x_send))
    other1, own2, tables = together(lax.ppermute(for_other, ("xl", "xh"), FLIP), own2, tables, x_side)[:3]
    g1 = gather_pair(sent1[:MAIN], other1[:MAIN], jnp.where(xh == xl, sent1[MAIN:], other1[MAIN:]))
    x_up, x_down, x_side, dy_own = together(x_up, x_down, x_side, dy_own)
    x_up_side, x_down_side, x_far_a, x_far_b, dy_side = together(
        up(x_side), down(x_side), up(x_up[:64]), down(x_down[64:]), across(dy_own)
    )
    x_far_side_a, x_far_side_b, dy_up, dy_down, other2 = together(
        across(x_far_a), across(x_far_b), up(dy_own), down(dy_own), lax.ppermute(own2, "xh", SWAP)
    )
    g2 = gather_pair(own2, other2, None)
    dy_side, dy_up, dy_down = together(dy_side, dy_up, dy_down)
    dy_far_a, dy_far_b, dy_up_side, dy_down_side = together(
        up(dy_up[:64]), down(dy_down[64:]), up(dy_side), down(dy_side)
    )
    dy_far_side_a, dy_far_side_b = across(dy_far_a), across(dy_far_b)
    x_blocks = [x_send, x_side, x_up, x_up_side, x_down, x_down_side, x_far_a, x_far_b, x_far_side_a, x_far_side_b]
    dy_blocks = [dy_own, dy_side, dy_up, dy_up_side, dy_down, dy_down_side]
    dy_blocks = dy_blocks + [dy_far_a, dy_far_b, dy_far_side_a, dy_far_side_b]

    def side_of(core):
        return jnp.stack(
            [g1[:, core, MAIN * h : MAIN * h + 64, 768:] for h in range(2)], axis=1
        ).reshape(8, 64, 256)

    ups_all = side_of(0).reshape(8, 4, 16, 256).transpose(1, 0, 2, 3).reshape(4, 128, 256)
    ups = jnp.concatenate([ups_all[0], ups_all[1], ups_all[2]], axis=1)
    dd = ups_all[3]
    small_all = side_of(1)[:, :6].astype(F32)
    misc = small_all[:, :4].transpose(1, 0, 2).reshape(4, 2048)
    head_b = lax.dynamic_index_in_dim(small_all[:, 4, :192].reshape(4, 2, 3, 64), xl, 1, keepdims=False)
    bias_qkv = head_b.transpose(1, 0, 2).reshape(1, 768)
    b1 = small_all[:, 5, :128].reshape(1, 1024)

    cos_mine, sin_mine, cos_all, sin_all, idcol = tables

    hb, inner, qkv_keep, qkv_send, aid = k1(
        x_blocks, scal, g1, ups, misc[:2], bias_qkv, cos_mine, sin_mine, k0(x_blocks)
    )
    qkv_recv = lax.ppermute(qkv_send, "c", SWAP)
    dob_keep, dob_send, gdense = k1b(dy_blocks, scal, aid, g1, dd)
    dob_recv = lax.ppermute(dob_send, "c", SWAP)

    idrow = jnp.broadcast_to(block_row[None, :], (8, 2048))
    att_keep, att_send = k3(scal, qkv_keep, qkv_recv, dob_keep, dob_recv, idrow, idcol, cos_all, sin_all)
    att_recv = lax.ppermute(att_send, "c", SWAP)

    fold = fold_matrix()
    out_part, gb, slope, low_out, gdd = k2f(scal, hb, aid, inner, gdense, att_keep, att_recv, g1, g2, dd, b1)
    out_sum = lax.psum_scatter(out_part.reshape(1024, 2048), TP, scatter_dimension=0, tiled=True)
    df, low_in, small, gup1, gd2 = k2g(
        dy_blocks, scal, aid, inner, att_keep, att_recv, gb, slope, low_out, g2, ups, fold
    )
    small = lax.all_to_all(small.reshape(8, 128, 128), TP, 0, 0, tiled=True)
    small = jnp.sum(small.astype(F32), axis=0).astype(BF)
    small = lax.all_to_all(jnp.broadcast_to(small[None], (8, 128, 128)), TP, 0, 0, tiled=True)
    near, owns, sides, gqkv = k2h(scal, df, att_keep, att_recv, low_in, inner, g1, g2)
    near, owns, sides, small = together(near, owns, sides, small)
    shares = scatter_sum(near, owns, sides)

    keep, send = k5(scal, small, aid, hb, fold.T, gup1, gd2, gqkv, gdd, dy_blocks)
    grads = (keep + lax.ppermute(send, "c", SWAP).astype(F32)).astype(BF)
    grads = lax.all_to_all(grads, WSH, 0, 0, tiled=True)
    grads = jnp.sum(grads.astype(F32), axis=0).astype(BF)
    grads = lax.all_to_all(jnp.broadcast_to(grads[None], (8, 80, 512)), TP, 0, 0, tiled=True)
    down_qkv, up_qkv, gdd, gud, gf1d, gf1u, gf2d, gf2u = kf(scal, grads, lax.ppermute(grads, "c", SWAP))

    source = x_own.astype(F32)
    outputs = (source + out_sum.astype(F32) + misc[2:3] + misc[3:4]).astype(BF)[None]
    grad_inputs = kn(x_own, output_cotangent[0], misc[0:1], *shares)[None]
    return (
        outputs,
        grad_inputs,
        down_qkv[None],
        up_qkv[None],
        gdd[None],
        gud[None],
        gf1d[None],
        gf1u[None],
        gf2d[None],
        gf2u[None],
    )


def solution(mesh):
    fine = Mesh(np.asarray(mesh.devices).reshape(2, 4, 2, 4, 2), ("xl", "z", "c", "y", "xh"))
    tokens = P(WSH, CTX, None)
    w1 = P(WSH)
    w2 = P(WSH, None)
    w3 = P(WSH, None, None)
    w4 = P(WSH, None, None, None)
    placed = (tokens, tokens, w2, P(WSH, CTX)) + (w1, w1, w2, w2, w2, w2, w1, w1, w1, w1, w2, w1, w2, w1)
    placed = placed + (w4, w4, w3, w3, w3, w3, w3, w3)
    return jax.shard_map(
        local,
        mesh=fine,
        in_specs=placed,
        out_specs=(tokens, tokens, w4, w4, w3, w3, w3, w3, w3, w3),
        check_vma=False,
    )
```

```python
import functools

import jax
import jax.numpy as jnp
import numpy as np
from jax import lax
from jax.experimental import pallas as pl
from jax.experimental.pallas import tpu as pltpu
from jax.sharding import Mesh, PartitionSpec as P

ADAPTERS = 8
RANK = 16
EPSILON = 1e-05
GELU_SCALE = 0.7978845608028654
NEGATIVE = -1e30
SCALE = 64 ** -0.5
BF = jnp.bfloat16
F32 = jnp.float32
WSH = ("y", "xh")
TP = ("xl", "z")
CTX = ("xl", "z", "c")
VMEM_LIMIT = 58 * 1024 * 1024


def nn(a, b):
    return lax.dot_general(a, b, (((1,), (0,)), ((), ())), preferred_element_type=F32)


def nt(a, b):
    return lax.dot_general(a, b, (((1,), (1,)), ((), ())), preferred_element_type=F32)


def tn(a, b):
    return lax.dot_general(a, b, (((0,), (0,)), ((), ())), preferred_element_type=F32)


def adapter_mask(aid, columns):
    col = lax.broadcasted_iota(jnp.int32, (aid.shape[0], columns), 1)
    return (lax.shift_right_logical(col, 4) & 7) == aid.astype(jnp.int32)


def turn(values, cosine, sine):
    width = values.shape[1]
    lane = lax.broadcasted_iota(jnp.int32, values.shape, 1) & 63
    partner = jnp.where(
        lane < 16, pltpu.roll(values, width - 16, 1), pltpu.roll(values, 16, 1)
    )
    return values * cosine + partner * sine


ANY = pl.BlockSpec(memory_space=pl.ANY)
SMEM = pl.BlockSpec(memory_space=pltpu.SMEM)
VM = pl.BlockSpec(memory_space=pltpu.VMEM)
PARAMS = pltpu.CompilerParams(vmem_limit_bytes=VMEM_LIMIT)
MAIN = 208
SECOND = 288
NEAR = 1280


def whole(shape):
    return pl.BlockSpec(shape, lambda t: (0,) * len(shape), pipeline_mode=pl.Buffered(1))


def start_all(pairs, sem):
    for source, target in pairs:
        pltpu.make_async_copy(source, target, sem).start()


def wait_all(target, sem):
    pltpu.make_async_copy(target, target, sem).wait()


def token_copies(blocks, target):
    own, side, above, below, up_more, down_more, far_side = blocks
    return [
        (own, target.at[0, 0], 0),
        (side, target.at[0, 1], 1),
        (above, target.at[1, 0], 2),
        (up_more.at[pl.ds(0, 128), :], target.at[1, 1], 3),
        (below, target.at[2, 0], 4),
        (down_more.at[pl.ds(0, 128), :], target.at[2, 1], 5),
        (up_more.at[pl.ds(128, 64), :], target.at[3, 0, pl.ds(0, 64)], 6),
        (down_more.at[pl.ds(128, 64), :], target.at[3, 0, pl.ds(64, 64)], 6),
        (far_side, target.at[3, 1], 7),
    ]


def start_tokens(blocks, target, sem, first, last):
    for source, part, i in token_copies(blocks, target):
        if first <= i < last:
            pltpu.make_async_copy(source, part, sem.at[i]).start()


def wait_tokens(target, sem, step):
    for i in range(2):
        part = target.at[step, i]
        pltpu.make_async_copy(part, part, sem.at[2 * step + i]).wait()


def pieces_qkv(g1, target):
    return [
        (
            g1.at[y, c, pl.ds(MAIN * xh, 128), pl.ds(0, 768)],
            target.at[pl.ds((2 * y + xh) * 256 + c * 128, 128), :],
        )
        for y in range(4)
        for xh in range(2)
        for c in range(2)
    ]


def pieces_downs(g1, target):
    return [
        (
            g1.at[:, c, pl.ds(MAIN * xh + 128 + 32 * i + 16 * b, 16), :],
            target.at[c, i, :, xh, :, pl.ds(1024 * b, 1024)],
        )
        for c in range(2)
        for i in range(2)
        for xh in range(2)
        for b in range(2)
    ]


def pieces_rank(g, base, stride, target, row):
    return [
        (
            g.at[y, c, pl.ds(stride * xh + base, 16), :],
            target.at[pl.ds(row + (2 * y + xh) * 16, 16), pl.ds(1024 * c, 1024)],
        )
        for y in range(4)
        for xh in range(2)
        for c in range(2)
    ]


def pieces_dense(g1, target, row):
    return [
        (
            g1.at[y, c, pl.ds(2 * MAIN + 32 * b, 32), :],
            target.at[pl.ds(row + 64 * y + 32 * c, 32), pl.ds(1024 * b, 1024)],
        )
        for y in range(4)
        for c in range(2)
        for b in range(2)
    ]


def pieces_w1(g2, target):
    return [
        (
            g2.at[y, c, pl.ds(SECOND * xh, 128), :],
            target.at[pl.ds((2 * y + xh) * 256 + c * 128, 128), :],
        )
        for y in range(4)
        for xh in range(2)
        for c in range(2)
    ]


def pieces_sixteen(g2, c, target, row):
    return [
        (
            g2.at[y, c, pl.ds(SECOND * xh + 128, 16), :],
            target.at[pl.ds(row + (2 * y + xh) * 16, 16), :],
        )
        for y in range(4)
        for xh in range(2)
    ]


def pieces_w2(g2, target):
    return [
        (
            g2.at[y, c, pl.ds(SECOND * xh + 144 + 64 * b, 64), :],
            target.at[pl.ds((2 * y + xh) * 128 + c * 64, 64), pl.ds(1024 * b, 1024)],
        )
        for y in range(4)
        for xh in range(2)
        for c in range(2)
        for b in range(2)
    ]


def block_diagonal(source, target):
    target[...] = jnp.zeros_like(target)
    for p in range(3):
        cols = slice(256 * p, 256 * p + 256)
        target[128 * p : 128 * p + 128, cols] = source[:, cols]


def k1_body(*refs):
    blocks, refs = refs[:7], refs[7:]
    (scal_ref, g1_ref, up_ref, misc_ref, bias_ref, cos_ref, sin_ref,
     hb_ref, inner_ref, keep_ref, send_ref, aid_ref, x_s, w_s, down_s, up_s, x_sem, w_sem) = refs
    step = pl.program_id(0)

    @pl.when(step == 0)
    def _():
        start_tokens(blocks, x_s, x_sem, 0, 2)
        start_all(pieces_downs(g1_ref, down_s), w_sem.at[0])
        start_all(pieces_qkv(g1_ref, w_s.at[:, pl.ds(0, 768)]), w_sem.at[1])
        start_tokens(blocks, x_s, x_sem, 2, 8)

    wait_tokens(x_s, x_sem, step)
    tile = x_s[step].reshape(256, 2176)
    x = tile[:, :2048].astype(F32)
    aid_ref[...] = tile[:, 2048:]
    aid = tile[:, 2048:2049].astype(F32)
    mean = jnp.mean(x, axis=1, keepdims=True)
    center = x - mean
    spread = jnp.mean(center * center, axis=1, keepdims=True)
    h = center * lax.rsqrt(spread + EPSILON) * misc_ref[0:1, :] + misc_ref[1:2, :]
    hb = h.astype(BF)
    hb_ref[...] = hb

    @pl.when(step == 0)
    def _():
        block_diagonal(up_ref, up_s)
        wait_all(down_s, w_sem.at[0])
        w_s[:, 768:] = down_s[...].reshape(512, 2048).T
        wait_all(w_s.at[:, pl.ds(0, 768)], w_sem.at[1])

    pre_all = nn(hb, w_s[...])
    inner = jnp.where(adapter_mask(aid, 512), pre_all[:, 768:], 0.0).astype(BF)
    inner_ref[...] = inner
    pre_all = pre_all[:, :768] + nn(inner[:, :384], up_s[...]) + bias_ref[...]
    first_core = scal_ref[8] == 0
    cosine = jnp.concatenate([cos_ref[...]] * 2, axis=1)
    sine = jnp.concatenate([sin_ref[...]] * 2, axis=1)
    for p in range(3):
        cols = slice(256 * p, 256 * p + 256)
        pre = pre_all[:, cols]
        if p < 2:
            pre = turn(pre, cosine, sine)
        low = pre.astype(BF)
        keep_ref[p] = jnp.where(first_core, low[:, :128], low[:, 128:])
        send_ref[p] = jnp.where(first_core, low[:, 128:], low[:, :128])


def k1(blocks, scal, g1, ups, misc, bias, cosine, sine):
    rows = 256
    return pl.pallas_call(
        k1_body,
        grid=(4,),
        in_specs=[ANY] * 7
        + [
            SMEM,
            ANY,
            whole((128, 768)),
            whole((2, 2048)),
            whole((1, 768)),
            pl.BlockSpec((rows, 128), lambda t: (t, 0)),
            pl.BlockSpec((rows, 128), lambda t: (t, 0)),
        ],
        out_specs=[
            pl.BlockSpec((rows, 2048), lambda t: (t, 0)),
            pl.BlockSpec((rows, 512), lambda t: (t, 0)),
            pl.BlockSpec((3, rows, 128), lambda t: (0, t, 0)),
            pl.BlockSpec((3, rows, 128), lambda t: (0, t, 0)),
            pl.BlockSpec((rows, 128), lambda t: (t, 0)),
        ],
        out_shape=[
            jax.ShapeDtypeStruct((1024, 2048), BF),
            jax.ShapeDtypeStruct((1024, 512), BF),
            jax.ShapeDtypeStruct((3, 1024, 128), BF),
            jax.ShapeDtypeStruct((3, 1024, 128), BF),
            jax.ShapeDtypeStruct((1024, 128), BF),
        ],
        scratch_shapes=[
            pltpu.VMEM((4, 2, 128, 2176), BF),
            pltpu.VMEM((2048, 1280), BF),
            pltpu.VMEM((2, 2, 4, 2, 16, 2048), BF),
            pltpu.VMEM((384, 768), BF),
            pltpu.SemaphoreType.DMA((8,)),
            pltpu.SemaphoreType.DMA((2,)),
        ],
        compiler_params=PARAMS,
        cost_estimate=pl.CostEstimate(flops=6_000_000_000, bytes_accessed=20_000_000, transcendentals=0),
        name="norm_qkv",
    )(*blocks, scal, g1, ups, misc, bias, cosine, sine)


def k1b_body(*refs):
    blocks, refs = refs[:7], refs[7:]
    scal_ref, aid_ref, g1_ref, dd_ref, keep_ref, send_ref, ginner_ref, dy_s, w_s, dy_sem, w_sem = refs
    start_all(pieces_dense(g1_ref, w_s, 0) + pieces_rank(g1_ref, 192, MAIN, w_s, 256), w_sem)
    start_tokens(blocks, dy_s, dy_sem, 0, 8)
    wait_all(w_s, w_sem)
    for step in range(4):
        wait_tokens(dy_s, dy_sem, step)
    first_core = scal_ref[8] == 0
    both = nt(dy_s[...].reshape(1024, 2048), w_s[...])
    aid = aid_ref[:, 0:1].astype(F32)
    ginner = jnp.where(adapter_mask(aid, 128), both[:, 256:], 0.0).astype(BF)
    ginner_ref[...] = ginner
    dob = (both[:, :256] + nn(ginner, dd_ref[...])).astype(BF)
    keep_ref[...] = jnp.where(first_core, dob[:, :128], dob[:, 128:])
    send_ref[...] = jnp.where(first_core, dob[:, 128:], dob[:, :128])


def k1b(blocks, scal, aid, g1, dd):
    return pl.pallas_call(
        k1b_body,
        in_specs=[ANY] * 7 + [SMEM, VM, ANY, VM],
        out_specs=[VM, VM, VM],
        out_shape=[jax.ShapeDtypeStruct((1024, 128), BF)] * 3,
        scratch_shapes=[
            pltpu.VMEM((4, 2, 128, 2048), BF),
            pltpu.VMEM((384, 2048), BF),
            pltpu.SemaphoreType.DMA((8,)),
            pltpu.SemaphoreType.DMA,
        ],
        compiler_params=PARAMS,
        cost_estimate=pl.CostEstimate(flops=2_000_000_000, bytes_accessed=8_000_000, transcendentals=0),
        name="attention_output_grad",
    )(*blocks, scal, aid, g1, dd)


def k3_body(
    scal_ref, qkv_keep, qkv_recv, dob_keep, dob_recv, idrow_ref, idcol_ref, cos_ref, sin_ref,
    keep_out, send_out, x_s, out_s, kt_s, vt_s, dk_s, dv_s, sem, sem_out,
):
    core = scal_ref[8]
    copies = []
    for b in range(8):
        rows = pl.ds(128 * b, 128)
        spot = scal_ref[b]
        for side, (qkv, dob) in enumerate(((qkv_keep, dob_keep), (qkv_recv, dob_recv))):
            parity = core if side == 0 else 1 - core
            copies.append((qkv.at[:, rows, :], x_s.at[pl.ds(0, 3), spot, parity]))
            copies.append((dob.at[rows, :], x_s.at[3, spot, parity]))
    start_all(copies, sem)
    dk_s[...] = jnp.zeros_like(dk_s)
    dv_s[...] = jnp.zeros_like(dv_s)
    wait_all(x_s, sem)
    kt_s[...] = x_s[1].reshape(2048, 128).T
    vt_s[...] = x_s[2].reshape(2048, 128).T
    tile = 256
    lane = lax.broadcasted_iota(jnp.int32, (tile, 128), 1)

    def span(i, start, stop):
        return x_s[i, start // 256 : stop // 256].reshape(stop - start, 128)

    for t in range(8):
        start, stop = tile * t, tile * t + tile
        length = min(stop + tile, 2048)
        q = span(0, start, stop)
        dob = span(3, start, stop)
        zero = jnp.zeros_like(q)
        q = q * jnp.asarray(SCALE, BF)
        q2 = jnp.concatenate([jnp.where(lane < 64, q, zero), jnp.where(lane < 64, zero, q)], axis=0)
        d2 = jnp.concatenate([jnp.where(lane < 64, dob, zero), jnp.where(lane < 64, zero, dob)], axis=0)
        query_ids = idrow_ref[0:1, start:stop]
        query_ids = jnp.concatenate([query_ids, query_ids], axis=1)
        allowed = idcol_ref[start:length, 0:1] <= query_ids
        s = jnp.where(allowed, nt(span(1, start, length), q2), NEGATIVE)
        largest = jnp.max(s, axis=0, keepdims=True)
        if start:
            s_head = nt(span(1, 0, start), q2)
            largest = jnp.maximum(largest, jnp.max(s_head, axis=0, keepdims=True))
            s = jnp.concatenate([s_head, s], axis=0)
        e = jnp.exp(s - largest)
        recip = 1.0 / jnp.sum(e, axis=0, keepdims=True)
        p = e * recip
        pb = p.astype(BF)
        ot = nn(vt_s[:, :length], pb)
        dp = nt(span(2, 0, length), d2)
        o_parts = [ot[:64, :256], ot[64:, 256:]]
        dobt = dob.astype(F32).T
        delta = jnp.concatenate(
            [
                jnp.sum(o_parts[0] * dobt[:64], axis=0, keepdims=True),
                jnp.sum(o_parts[1] * dobt[64:], axis=0, keepdims=True),
            ],
            axis=1,
        )
        ds = (p * (dp - delta)).astype(BF)
        dk_s[:length] += nn(ds, q2)
        dv_s[:length] += nn(pb, d2)
        dqt = nn(kt_s[:, :length], ds)
        dq_parts = [dqt[:64, :256], dqt[64:, 256:]]
        o = jnp.concatenate(o_parts, axis=0).T
        dq = jnp.concatenate(dq_parts, axis=0).T * SCALE
        rows = slice(start, stop)
        out_s[0, t] = o.astype(BF).reshape(2, 128, 128)
        out_s[1, t] = turn(dq, cos_ref[rows], -sin_ref[rows]).astype(BF).reshape(2, 128, 128)
    out_s[2] = turn(dk_s[...], cos_ref[...], -sin_ref[...]).astype(BF).reshape(8, 2, 128, 128)
    out_s[3] = dv_s[...].astype(BF).reshape(8, 2, 128, 128)
    copies = []
    for b in range(8):
        rows = pl.ds(128 * b, 128)
        spot = scal_ref[b]
        copies.append((out_s.at[:, spot, core], keep_out.at[:, rows, :]))
        copies.append((out_s.at[:, spot, 1 - core], send_out.at[:, rows, :]))
    start_all(copies, sem_out)
    wait_all(out_s, sem_out)


def k3(scal, qkv_keep, qkv_recv, dob_keep, dob_recv, idrow, idcol, cosine, sine):
    vm = pl.BlockSpec(memory_space=pltpu.VMEM)
    return pl.pallas_call(
        k3_body,
        in_specs=[SMEM] + [ANY] * 4 + [vm] * 4,
        out_specs=[ANY, ANY],
        out_shape=[jax.ShapeDtypeStruct((4, 1024, 128), BF)] * 2,
        scratch_shapes=[
            pltpu.VMEM((4, 8, 2, 128, 128), BF),
            pltpu.VMEM((4, 8, 2, 128, 128), BF),
            pltpu.VMEM((128, 2048), BF),
            pltpu.VMEM((128, 2048), BF),
            pltpu.VMEM((2048, 128), F32),
            pltpu.VMEM((2048, 128), F32),
            pltpu.SemaphoreType.DMA,
            pltpu.SemaphoreType.DMA,
        ],
        compiler_params=PARAMS,
        cost_estimate=pl.CostEstimate(flops=15_000_000_000, bytes_accessed=8_000_000, transcendentals=5_000_000),
        name="attention",
    )(scal, qkv_keep, qkv_recv, dob_keep, dob_recv, idrow, idcol, cosine, sine)


def heads_of(keep_ref, recv_ref, i, first_core):
    a, b = keep_ref[i], recv_ref[i]
    return jnp.concatenate([jnp.where(first_core, a, b), jnp.where(first_core, b, a)], axis=1)


def tile_spec(width, rows=256):
    return pl.BlockSpec((rows, width), lambda t, s: (t, 0))


def const_spec(shape):
    return pl.BlockSpec(shape, lambda t, s: (0,) * len(shape), pipeline_mode=pl.Buffered(1))


def placed_spec(width):
    return pl.BlockSpec((2, 1, 128, width), lambda t, s: (0, s[12 + t], 0, 0))


def place(ref, xl, value):
    ref[xl, 0] = value[:128]
    ref[1 - xl, 0] = value[128:]


def accumulate(step, pairs):
    @pl.when(step == 0)
    def _():
        for ref, value in pairs:
            ref[...] = value

    @pl.when(step > 0)
    def _():
        for ref, value in pairs:
            ref[...] += value


def k2m_body(scal_ref, *refs):
    blocks, refs = refs[:7], refs[7:]
    (hb_ref, aid_ref, inner_ref, gdense_ref, keep_ref, recv_ref, g2_ref, up_ref, dd_ref, b1_ref, fold_ref,
     gb_ref, df_ref, low_out_ref, low_in_ref, small_ref, gup1_ref, gd2_ref, gdd_ref,
     dy_s, w1_s, w2_s, d2_s, up_s, dy_sem, sems) = refs
    step = pl.program_id(0)

    @pl.when(step == 0)
    def _():
        start_all(pieces_w1(g2_ref, w1_s) + pieces_sixteen(g2_ref, 0, w1_s, 2048), sems.at[0])
        start_all(pieces_sixteen(g2_ref, 1, d2_s, 0), sems.at[1])
        start_tokens(blocks, dy_s, dy_sem, 0, 2)
        start_all(pieces_w2(g2_ref, w2_s) + pieces_rank(g2_ref, 272, SECOND, w2_s, 1024), sems.at[2])
        start_tokens(blocks, dy_s, dy_sem, 2, 8)
        block_diagonal(up_ref, up_s)
        wait_all(w1_s, sems.at[0])

    aid = aid_ref[:, 0:1].astype(F32)
    first_core = scal_ref[8] == 0
    f = nn(jnp.concatenate([hb_ref[...], inner_ref[...]], axis=1), w1_s[...]) + b1_ref[...]

    @pl.when(step == 0)
    def _():
        wait_all(w2_s, sems.at[2])
        wait_all(d2_s, sems.at[1])

    wait_tokens(dy_s, dy_sem, step)
    wide = nt(dy_s[step].reshape(256, 2048), w2_s[...])
    square = f * f
    th = jnp.tanh(GELU_SCALE * f * (1.0 + 0.044715 * square))
    half = 0.5 * (1.0 + th)
    gb = (f * half).astype(BF)
    gb_ref[...] = gb
    slope = half + (0.5 * GELU_SCALE) * f * (1.0 - th * th) * (1.0 + 3 * 0.044715 * square)
    ginner2 = jnp.where(adapter_mask(aid, 128), wide[:, 1024:], 0.0).astype(BF)
    ob = heads_of(keep_ref, recv_ref, 0, first_core)
    dpre = jnp.concatenate([heads_of(keep_ref, recv_ref, p, first_core) for p in (1, 2, 3)], axis=1)
    inner2 = nt(gb, d2_s[...])
    innerd = nt(ob, dd_ref[...])
    ginner = nt(dpre, up_s[...])
    df = ((wide[:, :1024] + nn(ginner2, d2_s[...])) * slope).astype(BF)
    df_ref[...] = df
    ginner1 = nt(df, w1_s[2048:])
    low = jnp.concatenate([ginner, ginner1, innerd, inner2], axis=1)
    low = jnp.where(adapter_mask(aid, 768), low, 0.0).astype(BF)
    low_in_ref[...] = low[:, :512]
    low_out_ref[...] = low[:, 512:]
    place(small_ref, scal_ref[10], nn(low, fold_ref[...]).astype(BF))
    accumulate(
        step,
        [
            (gup1_ref, tn(inner_ref[...], df)),
            (gd2_ref, tn(ginner2, gb)),
            (gdd_ref, tn(gdense_ref[...], ob)),
        ],
    )


def att_spec(first, count):
    return pl.BlockSpec((count, 256, 128), lambda t, s: (first, t, 0))


def k2m(blocks, scal, hb, aid, inner, gdense, keep, recv, g2, ups, dd, b1, fold):
    return pl.pallas_call(
        k2m_body,
        grid_spec=pltpu.PrefetchScalarGridSpec(
            num_scalar_prefetch=1,
            grid=(4,),
            in_specs=[ANY] * 7
            + [
                tile_spec(2048),
                tile_spec(128),
                pl.BlockSpec((256, 128), lambda t, s: (t, 3)),
                tile_spec(128),
                att_spec(0, 4),
                att_spec(0, 4),
                ANY,
                const_spec((128, 768)),
                const_spec((128, 256)),
                const_spec((1, 1024)),
                const_spec((768, 128)),
            ],
            out_specs=[
                tile_spec(1024),
                tile_spec(1024),
                tile_spec(256),
                tile_spec(512),
                placed_spec(128),
                const_spec((128, 1024)),
                const_spec((128, 1024)),
                const_spec((128, 256)),
            ],
            scratch_shapes=[
                pltpu.VMEM((4, 2, 128, 2048), BF),
                pltpu.VMEM((2176, 1024), BF),
                pltpu.VMEM((1152, 2048), BF),
                pltpu.VMEM((128, 1024), BF),
                pltpu.VMEM((384, 768), BF),
                pltpu.SemaphoreType.DMA((8,)),
                pltpu.SemaphoreType.DMA((3,)),
            ],
        ),
        out_shape=[
            jax.ShapeDtypeStruct((1024, 1024), BF),
            jax.ShapeDtypeStruct((1024, 1024), BF),
            jax.ShapeDtypeStruct((1024, 256), BF),
            jax.ShapeDtypeStruct((1024, 512), BF),
            jax.ShapeDtypeStruct((2, 4, 128, 128), BF),
            jax.ShapeDtypeStruct((128, 1024), F32),
            jax.ShapeDtypeStruct((128, 1024), F32),
            jax.ShapeDtypeStruct((128, 256), F32),
        ],
        compiler_params=PARAMS,
        cost_estimate=pl.CostEstimate(flops=14_000_000_000, bytes_accessed=30_000_000, transcendentals=1_000_000),
        name="feed_forward",
    )(scal, *blocks, hb, aid, inner, gdense, keep, recv, g2, ups, dd, b1, fold)


def k2o_body(scal_ref, gb_ref, keep_ref, recv_ref, low_ref, g1_ref, g2_ref, out_ref, w_s, sem):
    step = pl.program_id(0)

    @pl.when(step == 0)
    def _():
        start_all(
            pieces_w2(g2_ref, w_s)
            + pieces_dense(g1_ref, w_s, 1024)
            + pieces_rank(g1_ref, 192, MAIN, w_s, 1280)
            + pieces_rank(g2_ref, 272, SECOND, w_s, 1408),
            sem,
        )
        wait_all(w_s, sem)

    ob = heads_of(keep_ref, recv_ref, 0, scal_ref[8] == 0)
    out = nn(jnp.concatenate([gb_ref[...], ob, low_ref[...]], axis=1), w_s[...]).astype(BF)
    place(out_ref, scal_ref[10], out)


def k2o(scal, gb, keep, recv, low_out, g1, g2):
    return pl.pallas_call(
        k2o_body,
        grid_spec=pltpu.PrefetchScalarGridSpec(
            num_scalar_prefetch=1,
            grid=(4,),
            in_specs=[tile_spec(1024), att_spec(0, 1), att_spec(0, 1), tile_spec(256), ANY, ANY],
            out_specs=[placed_spec(2048)],
            scratch_shapes=[pltpu.VMEM((1536, 2048), BF), pltpu.SemaphoreType.DMA],
        ),
        out_shape=[jax.ShapeDtypeStruct((2, 4, 128, 2048), BF)],
        compiler_params=PARAMS,
        cost_estimate=pl.CostEstimate(flops=7_000_000_000, bytes_accessed=14_000_000, transcendentals=0),
        name="out_rows",
    )(scal, gb, keep, recv, low_out, g1, g2)[0]


def k2h_body(
    scal_ref, df_ref, keep_ref, recv_ref, low_ref, inner_ref, g1_ref, g2_ref,
    near_ref, owns_ref, sides_ref, gqkv_ref, w_s, down_s, sems,
):
    step = pl.program_id(0)

    @pl.when(step == 0)
    def _():
        start_all(
            pieces_w1(g2_ref, w_s.at[:, pl.ds(0, 1024)]) + pieces_qkv(g1_ref, w_s.at[:, pl.ds(1024, 768)]), sems.at[0]
        )
        start_all(pieces_downs(g1_ref, down_s), sems.at[1])
        wait_all(w_s, sems.at[0])
        wait_all(down_s, sems.at[1])

    first_core = scal_ref[8] == 0
    dpre = [heads_of(keep_ref, recv_ref, p, first_core) for p in (1, 2, 3)]
    dh = nt(jnp.concatenate([df_ref[...]] + dpre, axis=1), w_s[...])
    dh = (dh + nn(low_ref[...], down_s[...].reshape(512, 2048))).astype(BF)
    near_ref[0] = dh[:128, :NEAR]
    near_ref[1] = dh[128:, :NEAR]
    owns_ref[0] = dh[:128, NEAR:]
    sides_ref[0] = dh[128:, NEAR:]
    gqkv = [tn(inner_ref[:, 128 * p : 128 * p + 128], dpre[p]) for p in range(3)]
    accumulate(step, [(gqkv_ref, jnp.concatenate(gqkv, axis=1))])


def k2h(scal, df, keep, recv, low_in, inner, g1, g2):
    return pl.pallas_call(
        k2h_body,
        grid_spec=pltpu.PrefetchScalarGridSpec(
            num_scalar_prefetch=1,
            grid=(4,),
            in_specs=[tile_spec(1024), att_spec(0, 4), att_spec(0, 4), tile_spec(512), tile_spec(512), ANY, ANY],
            out_specs=[
                pl.BlockSpec((2, 128, NEAR), lambda t, s: (t, 0, 0)),
                pl.BlockSpec((1, 128, 2048 - NEAR), lambda t, s: (t, 0, 0)),
                pl.BlockSpec((1, 128, 2048 - NEAR), lambda t, s: (t, 0, 0)),
                const_spec((128, 768)),
            ],
            scratch_shapes=[
                pltpu.VMEM((2048, 1792), BF),
                pltpu.VMEM((2, 2, 4, 2, 16, 2048), BF),
                pltpu.SemaphoreType.DMA((2,)),
            ],
        ),
        out_shape=[
            jax.ShapeDtypeStruct((8, 128, NEAR), BF),
            jax.ShapeDtypeStruct((4, 128, 2048 - NEAR), BF),
            jax.ShapeDtypeStruct((4, 128, 2048 - NEAR), BF),
            jax.ShapeDtypeStruct((128, 768), F32),
        ],
        compiler_params=PARAMS,
        cost_estimate=pl.CostEstimate(flops=10_000_000_000, bytes_accessed=18_000_000, transcendentals=0),
        name="hidden_grad",
    )(scal, df, keep, recv, low_in, inner, g1, g2)


def k5_body(scal_ref, small_ref, aid_ref, hb_ref, spread_ref, gup1_ref, gd2_ref, gqkv_ref, gdd_ref, *refs):
    blocks, refs = refs[:7], refs[7:]
    keep_ref, send_ref, dy_s, sem = refs
    column = pl.multiple_of(256 * scal_ref[9], 256)
    start_all(
        [(source.at[:, pl.ds(column, 256)], part) for source, part, _ in token_copies(blocks, dy_s)], sem
    )
    first_core = scal_ref[8] == 0

    def store(section, left, right):
        kept = jnp.where(first_core, left, right)
        sent = jnp.where(first_core, right, left)
        keep_ref[:, 16 * section : 16 * section + 16] = kept.reshape(8, 16, 512)
        send_ref[:, 16 * section : 16 * section + 16] = sent.astype(BF).reshape(8, 16, 512)

    small = jnp.concatenate([small_ref[scal_ref[b]] for b in range(8)], axis=0)
    aid = aid_ref[:, 0:1].astype(F32)
    wide = jnp.where(adapter_mask(aid, 768), nn(small, spread_ref[...]), 0.0).astype(BF)
    down = tn(wide[:, :512], hb_ref[...])
    store(
        0,
        jnp.concatenate([down[:128], down[128:256]], axis=1),
        jnp.concatenate([down[256:384], down[384:]], axis=1),
    )
    store(1, gqkv_ref[:, :512], jnp.concatenate([gqkv_ref[:, 512:], gdd_ref[...]], axis=1))
    store(2, gup1_ref[:, :512], gup1_ref[:, 512:])
    store(3, gd2_ref[:, :512], gd2_ref[:, 512:])
    wait_all(dy_s, sem)
    up = tn(wide[:, 512:], dy_s[...].reshape(1024, 256))
    left = jnp.concatenate([up[:128], up[128:]], axis=1)
    store(4, left, jnp.zeros_like(left))


def k5(scal, small, aid, hb, spread, gup1, gd2, gqkv, gdd, blocks):
    def const(shape):
        return pl.BlockSpec(shape, lambda t, s: (0,) * len(shape))

    return pl.pallas_call(
        k5_body,
        grid_spec=pltpu.PrefetchScalarGridSpec(
            num_scalar_prefetch=1,
            grid=(1,),
            in_specs=[
                const((8, 128, 128)),
                const((1024, 128)),
                pl.BlockSpec((1024, 256), lambda t, s: (0, s[9])),
                const((128, 768)),
                const((128, 1024)),
                const((128, 1024)),
                const((128, 768)),
                const((128, 256)),
            ]
            + [ANY] * 7,
            out_specs=[const((8, 80, 512)), const((8, 80, 512))],
            scratch_shapes=[pltpu.VMEM((4, 2, 128, 256), BF), pltpu.SemaphoreType.DMA],
        ),
        out_shape=[jax.ShapeDtypeStruct((8, 80, 512), F32), jax.ShapeDtypeStruct((8, 80, 512), BF)],
        compiler_params=PARAMS,
        cost_estimate=pl.CostEstimate(flops=1_500_000_000, bytes_accessed=6_000_000, transcendentals=0),
        name="adapter_grads",
    )(scal, small, aid, hb, spread, gup1, gd2, gqkv, gdd, *blocks)


def kf_body(scal_ref, mine_ref, theirs_ref, down_ref, up_ref, dd_ref, ud_ref, f1d_ref, f1u_ref, f2d_ref, f2u_ref):
    lane = lax.broadcasted_iota(jnp.int32, (16, 128), 1)

    core = scal_ref[8]

    def part(j, half, section, start, width):
        rows, cols = slice(16 * section, 16 * section + 16), slice(start, start + width)
        return jnp.where(core == half, mine_ref[j, rows, cols], theirs_ref[j, rows, cols]).astype(F32)

    for j in range(8):
        block = slice(256 * j, 256 * j + 256)
        down_ref[0, :, block] = part(j, 0, 0, 0, 256)
        down_ref[1, :, block] = part(j, 0, 0, 256, 256)
        down_ref[2, :, block] = part(j, 1, 0, 0, 256)
        f1d_ref[:, block] = part(j, 1, 0, 256, 256)
        ud_ref[:, block] = part(j, 0, 4, 0, 256)
        f2u_ref[:, block] = part(j, 0, 4, 256, 256)
        for w in range(8):
            spot = slice(1024 * w + 128 * j, 1024 * w + 128 * j + 128)
            f1u_ref[:, spot] = part(j, w // 4, 2, 128 * (w % 4), 128)
            f2d_ref[:, spot] = part(j, w // 4, 3, 128 * (w % 4), 128)
    for i in range(4):
        for x in range(2):
            for y in range(4):
                for h in range(2):
                    start = 256 * (i % 2) + 128 * (y // 2)
                    a = part(4 * x + 2 * h, i // 2, 1, start, 128)
                    b = part(4 * x + 2 * h + 1, i // 2, 1, start, 128)
                    if y % 2:
                        a = pltpu.roll(a, 64, 1)
                    else:
                        b = pltpu.roll(b, 64, 1)
                    value = jnp.where(lane < 64, a, b)
                    spot = slice(256 * (2 * y + x) + 128 * h, 256 * (2 * y + x) + 128 * h + 128)
                    if i < 3:
                        up_ref[i, :, spot] = value
                    else:
                        dd_ref[:, spot] = value


def kf(scal, mine, theirs):
    return pl.pallas_call(
        kf_body,
        in_specs=[SMEM, VM, VM],
        out_specs=[VM] * 8,
        out_shape=[
            jax.ShapeDtypeStruct((3, 16, 2048), F32),
            jax.ShapeDtypeStruct((3, 16, 2048), F32),
            jax.ShapeDtypeStruct((16, 2048), F32),
            jax.ShapeDtypeStruct((16, 2048), F32),
            jax.ShapeDtypeStruct((16, 2048), F32),
            jax.ShapeDtypeStruct((16, 8192), F32),
            jax.ShapeDtypeStruct((16, 8192), F32),
            jax.ShapeDtypeStruct((16, 2048), F32),
        ],
        compiler_params=PARAMS,
        name="finish",
    )(scal, mine, theirs)


def kn_body(x_ref, dy_ref, gain_ref, own_ref, up_ref, down_ref, side_ref, t_ref, up2_ref, down2_ref, out_ref):
    def total(*parts):
        return sum(p[...].astype(F32) for p in parts)

    dh = jnp.concatenate([total(own_ref, up_ref, down_ref, side_ref), total(t_ref, up2_ref, down2_ref)], axis=1)
    x = x_ref[...].astype(F32)
    center = x - jnp.mean(x, axis=1, keepdims=True)
    inv = lax.rsqrt(jnp.mean(center * center, axis=1, keepdims=True) + EPSILON)
    hn = center * inv
    e = dh * gain_ref[...]
    dx = (e - jnp.mean(e, axis=1, keepdims=True) - hn * jnp.mean(e * hn, axis=1, keepdims=True)) * inv
    out_ref[...] = (dy_ref[...].astype(F32) + dx).astype(BF)


def kn(*args):
    return pl.pallas_call(
        kn_body,
        in_specs=[VM] * 10,
        out_specs=VM,
        out_shape=jax.ShapeDtypeStruct((128, 2048), BF),
        compiler_params=PARAMS,
        name="norm_grad",
    )(*args)


def pack1_body(
    scal_ref, wq, wk, wv, wd, ad_ref, fd_ref, au_ref, dd_ref, du_ref, misc_ref, b1_ref,
    own_ref, other_ref, w_s, d_s, sem, d_sem,
):
    c, z = scal_ref[8], scal_ref[11]
    start_all([(w.at[pl.ds(128 * c, 128), :], w_s.at[i]) for i, w in enumerate((wq, wk, wv))], sem)
    start_all([(wd.at[pl.ds(64 * z + 32 * c, 32), :], d_s)], d_sem)
    first_core = c == 0
    odd = lax.rem(z, 2) == 1
    targets = ((own_ref, scal_ref[10]), (other_ref, 1 - scal_ref[10]))

    def head_pair(read, rows, i, xl):
        lane = lax.broadcasted_iota(jnp.int32, (rows, 128), 1)
        parts = []
        for k in range(2):
            start = (2 * (i + k) + xl) * 256 + (z // 2) * 128
            v = read(pl.ds(pl.multiple_of(start, 128), 128)).astype(F32)
            turned = pltpu.roll(v, 64, 1)
            parts.append(jnp.where(odd, turned, v) if k == 0 else jnp.where(odd, v, turned))
        return jnp.where(lane < 64, parts[0], parts[1]).astype(BF)

    half = pl.ds(pl.multiple_of((z // 2) * 128, 128), 128)
    row = lax.broadcasted_iota(jnp.int32, (16, 128), 0)
    lane = lax.broadcasted_iota(jnp.int32, (16, 128), 1)

    def biases(xl):
        plain = misc_ref[:, :128].astype(F32), misc_ref[:, 128:256].astype(F32)
        mine = misc_ref[:, half].astype(F32)
        turned = pltpu.roll(mine, 64, 1)
        low = jnp.where(odd, turned, mine)
        high = jnp.where(odd, mine, turned)
        query_key = jnp.where(lane[:1] < 64, low[4:5], high[5:6])
        value = jnp.where(lane[:1] < 64, low[6:7], 0.0)
        hidden = jnp.where(row[:8] == xl * 4 + z, b1_ref[...].astype(F32), 0.0)
        hidden = jnp.sum(hidden, axis=0, keepdims=True)
        left = jnp.where(row < 4, plain[0], jnp.where(row == 4, query_key, hidden))
        right = jnp.where(row < 4, plain[1], value)
        return left.astype(BF), right.astype(BF)

    a = jnp.where(first_core, ad_ref[0], ad_ref[2])
    b = jnp.where(first_core, ad_ref[1], fd_ref[...])
    du = jnp.where(first_core, du_ref[:, :1024], du_ref[:, 1024:])
    for out_ref, xl in targets:
        rows_of = biases(xl)
        for p in range(4):
            for i in (0, 2):
                read = (lambda s, p=p: au_ref[p, :, s]) if p < 3 else (lambda s: dd_ref[:, s])
                value = head_pair(read, 16, i, xl)
                rows = slice(16 * p, 16 * p + 16)
                if p == 0:
                    value = jnp.where(first_core, value, rows_of[i // 2])
                out_ref[rows, 768 + 64 * i : 768 + 64 * i + 128] = value
        out_ref[64:128, 768:] = jnp.zeros((64, 256), BF)
        out_ref[128:144] = a[:, :1024]
        out_ref[144:160] = a[:, 1024:]
        out_ref[160:176] = b[:, :1024]
        out_ref[176:192] = b[:, 1024:]
        out_ref[192:208] = du
    wait_all(d_s, d_sem)
    for out_ref, _ in targets:
        out_ref[208:240] = d_s[:, :1024]
        out_ref[240:272] = d_s[:, 1024:]
    wait_all(w_s, sem)
    for p in range(3):
        for i in (0, 2):
            start = 256 * p + 64 * i
            for out_ref, xl in targets:
                out_ref[:128, start : start + 128] = head_pair(lambda s, p=p: w_s[p, :, s], 128, i, xl)


def pack1(scal, wq, wk, wv, wd, ad, fd, au, dd, du, misc, b1):
    return pl.pallas_call(
        pack1_body,
        in_specs=[SMEM] + [ANY] * 4 + [VM] * 7,
        out_specs=[VM, VM],
        out_shape=[jax.ShapeDtypeStruct((272, 1024), BF)] * 2,
        scratch_shapes=[
            pltpu.VMEM((3, 128, 2048), BF),
            pltpu.VMEM((32, 2048), BF),
            pltpu.SemaphoreType.DMA,
            pltpu.SemaphoreType.DMA,
        ],
        compiler_params=PARAMS,
        cost_estimate=pl.CostEstimate(flops=1_000_000, bytes_accessed=4_000_000, transcendentals=0),
        name="pack_qkv",
    )(scal, wq, wk, wv, wd, ad, fd, au, dd, du, misc, b1)


def pack2_body(scal_ref, w1, w2, up_ref, down_ref, up2_ref, own_ref, w1_s, w2_s, sem, sem2):
    c, j = scal_ref[8], scal_ref[9]
    start_all([(w1.at[pl.ds(128 * c, 128), :], w1_s)], sem)
    start_all([(w2.at[pl.ds(128 * j + 64 * c, 64), :], w2_s)], sem2)
    first_core = c == 0
    own_ref[272:288] = jnp.where(first_core, up2_ref[:, :1024], up2_ref[:, 1024:])

    def column(w):
        return pl.ds(pl.multiple_of(1024 * w + 128 * j, 128), 128)

    for w in range(8):
        own_ref[128:144, 128 * w : 128 * w + 128] = jnp.where(first_core, up_ref[:, column(w)], down_ref[:, column(w)])
    wait_all(w2_s, sem2)
    own_ref[144:208] = w2_s[:, :1024]
    own_ref[208:272] = w2_s[:, 1024:]
    wait_all(w1_s, sem)
    for w in range(8):
        own_ref[:128, 128 * w : 128 * w + 128] = w1_s[:, column(w)]


def pack2(scal, w1, w2, up, down, up2):
    return pl.pallas_call(
        pack2_body,
        in_specs=[SMEM, ANY, ANY, VM, VM, VM],
        out_specs=VM,
        out_shape=jax.ShapeDtypeStruct((288, 1024), BF),
        scratch_shapes=[
            pltpu.VMEM((128, 8192), BF),
            pltpu.VMEM((64, 2048), BF),
            pltpu.SemaphoreType.DMA,
            pltpu.SemaphoreType.DMA,
        ],
        compiler_params=PARAMS,
        cost_estimate=pl.CostEstimate(flops=1_000_000, bytes_accessed=4_000_000, transcendentals=0),
        name="pack_hidden",
    )(scal, w1, w2, up, down, up2)


def rotary_tables(positions):
    lane = np.arange(128) % 64
    rate = np.where(lane < 32, 10000.0 ** (-2.0 * (lane % 16) / 32.0), 0.0).astype(np.float32)
    sign = np.where(lane < 16, -1.0, 1.0).astype(np.float32)
    angles = positions.astype(F32)[:, None] * jnp.asarray(rate)[None, :]
    return jnp.cos(angles), jnp.sin(angles) * jnp.asarray(sign)[None, :]


def fold_matrix():
    row = np.arange(768)
    target = (row // 128) * 16 + row % 16
    return jnp.asarray((target[:, None] == np.arange(128)[None, :]).astype(np.float32)).astype(BF)


def halves(a):
    m = a.shape[1] // 2
    return jnp.concatenate([a[:, :m], a[:, m:]], axis=0)


SWAP = [(0, 1), (1, 0)]
FLIP = [(i, 3 - i) for i in range(4)]
UP = [(i, (i + 1) % 4) for i in range(4)]
DOWN = [(i, (i + 3) % 4) for i in range(4)]
Z_OFFSETS = (0, -1, 1, 2)


def together(*values):
    return lax.optimization_barrier(values)


def up(a):
    return lax.ppermute(a, "z", UP)


def down(a):
    return lax.ppermute(a, "z", DOWN)


def across(a):
    return lax.ppermute(a, "xl", SWAP)


def gather_pair(own, other, single):
    xh = lax.axis_index("xh")
    parts = [jnp.where(xh == 0, own, other), jnp.where(xh == 0, other, own)]
    if single is not None:
        parts.append(single)
    packed = jnp.concatenate(parts, axis=0)
    g = lax.all_gather(packed, ("y", "c"), axis=0, tiled=False)
    return g.reshape((4, 2) + packed.shape)


def add(*terms):
    return sum(t.astype(F32) for t in terms)


def scatter_sum(near, owns, sides):
    own, side, down_own, down_side, up_own, up_side, far_own, far_side = [near[b] for b in range(8)]
    from_side = lax.ppermute(sides, "xl", SWAP)
    via_below = lax.ppermute(far_own, "z", UP)
    via_above = lax.ppermute(far_side, "z", DOWN)
    up_side = lax.ppermute(up_side, "z", UP)
    down_own = lax.ppermute(down_own, "z", DOWN)
    up_own = lax.ppermute(add(up_own, via_below).astype(BF), "z", UP)
    down_side = lax.ppermute(add(down_side, via_above).astype(BF), "z", DOWN)
    side = lax.ppermute(add(side, up_side, down_side).astype(BF), "xl", SWAP)
    t = add(owns, from_side)
    far = t[3].astype(BF)
    half_up = lax.ppermute(far[:64], "z", UP)
    half_down = lax.ppermute(far[64:], "z", DOWN)
    up = jnp.concatenate([t[2, :64] + half_up.astype(F32), t[2, 64:]], axis=0).astype(BF)
    down = jnp.concatenate([t[1, :64], t[1, 64:] + half_down.astype(F32)], axis=0).astype(BF)
    return own, up_own, down_own, side, t[0], lax.ppermute(up, "z", UP), lax.ppermute(down, "z", DOWN)


def local(
    inputs,
    output_cotangent,
    block_index_per_position,
    adapter_index_per_run,
    norm_gain,
    norm_bias,
    query_weight,
    key_weight,
    value_weight,
    dense_weight,
    query_bias,
    key_bias,
    value_bias,
    dense_bias,
    feedforward_in_weight,
    feedforward_in_bias,
    feedforward_out_weight,
    feedforward_out_bias,
    adapter_attention_down,
    adapter_attention_up,
    adapter_dense_down,
    adapter_dense_up,
    adapter_feedforward_in_down,
    adapter_feedforward_in_up,
    adapter_feedforward_out_down,
    adapter_feedforward_out_up,
):
    xl, z, c = lax.axis_index("xl"), lax.axis_index("z"), lax.axis_index("c")
    xh = lax.axis_index("xh")
    j = xl * 4 + z
    x_own = inputs[0]
    dy_own = output_cotangent[0]
    run_adapter = adapter_index_per_run[0, 0].astype(F32).astype(BF)
    block_row = block_index_per_position[0]
    z_of = [lax.rem(z + o + 4, 4) for o in Z_OFFSETS]
    spots = [(xl if side == 0 else 1 - xl) * 4 + zz for zz in z_of for side in range(2)]
    scal = jnp.stack(spots + [c, j, xl, z] + z_of).astype(jnp.int32)

    zero = jnp.zeros((256,), BF)
    misc_own = jnp.stack(
        [norm_gain, norm_bias, dense_bias, feedforward_out_bias, query_bias, key_bias, value_bias] + [zero] * 9
    )
    sent1, for_other = pack1(
        scal,
        query_weight,
        key_weight,
        value_weight,
        dense_weight,
        adapter_attention_down[0],
        adapter_feedforward_in_down[0],
        adapter_attention_up[0],
        adapter_dense_down[0],
        adapter_dense_up[0],
        misc_own,
        feedforward_in_bias.reshape(8, 128),
    )
    own2 = pack2(
        scal,
        feedforward_in_weight,
        feedforward_out_weight,
        adapter_feedforward_in_up[0],
        adapter_feedforward_out_down[0],
        adapter_feedforward_out_up[0],
    )
    spread = jnp.stack(spots)
    my_positions = ((spread * 2 + c) * 128)[:, None] + jnp.arange(128, dtype=jnp.int32)[None, :]
    tables = rotary_tables(my_positions.reshape(1024)) + rotary_tables(jnp.arange(2048, dtype=jnp.int32))
    tables = tables + (jnp.broadcast_to(block_row[:, None], (2048, 128)),)
    x_send = jnp.concatenate([x_own, jnp.full((128, 128), run_adapter, BF)], axis=1)

    x_up, x_down, x_side = together(up(x_send), down(x_send), across(x_send))
    other1, own2, tables = together(lax.ppermute(for_other, ("xl", "xh"), FLIP), own2, tables, x_side)[:3]
    g1 = gather_pair(sent1[:MAIN], other1[:MAIN], jnp.where(xh == xl, sent1[MAIN:], other1[MAIN:]))
    x_up_more, x_down_more, dy_side = together(
        up(jnp.concatenate([x_side, x_up[:64]], axis=0)),
        down(jnp.concatenate([x_side, x_down[64:]], axis=0)),
        across(together(dy_own, x_side)[0]),
    )
    x_far_side, dy_up, dy_down, other2 = together(
        across(jnp.concatenate([x_up_more[128:], x_down_more[128:]], axis=0)),
        *(step(together(dy_own, dy_side)[0]) for step in (up, down)),
        lax.ppermute(together(own2, dy_side)[0], "xh", SWAP),
    )
    g2 = gather_pair(own2, other2, None)
    dy_up_more, dy_down_more = together(
        up(jnp.concatenate([dy_side, dy_up[:64]], axis=0)), down(jnp.concatenate([dy_side, dy_down[64:]], axis=0))
    )
    dy_far_side = across(jnp.concatenate([dy_up_more[128:], dy_down_more[128:]], axis=0))
    x_blocks = [x_send, x_side, x_up, x_down, x_up_more, x_down_more, x_far_side]
    dy_blocks = [dy_own, dy_side, dy_up, dy_down, dy_up_more, dy_down_more, dy_far_side]

    def side_of(core):
        return jnp.stack(
            [g1[:, core, MAIN * h : MAIN * h + 64, 768:] for h in range(2)], axis=1
        ).reshape(8, 64, 256)

    ups_all = side_of(0).reshape(8, 4, 16, 256).transpose(1, 0, 2, 3).reshape(4, 128, 256)
    ups = jnp.concatenate([ups_all[0], ups_all[1], ups_all[2]], axis=1)
    dd = ups_all[3]
    small_all = side_of(1)[:, :6].astype(F32)
    misc = small_all[:, :4].transpose(1, 0, 2).reshape(4, 2048)
    head_b = lax.dynamic_index_in_dim(small_all[:, 4, :192].reshape(4, 2, 3, 64), xl, 1, keepdims=False)
    bias_qkv = head_b.transpose(1, 0, 2).reshape(1, 768)
    b1 = small_all[:, 5, :128].reshape(1, 1024)

    cos_mine, sin_mine, cos_all, sin_all, idcol = tables

    hb, inner, qkv_keep, qkv_send, aid = k1(x_blocks, scal, g1, ups, misc[:2], bias_qkv, cos_mine, sin_mine)
    qkv_recv = lax.ppermute(qkv_send, "c", SWAP)
    dob_keep, dob_send, gdense = k1b(dy_blocks, scal, aid, g1, dd)
    dob_recv = lax.ppermute(dob_send, "c", SWAP)

    idrow = jnp.broadcast_to(block_row[None, :], (8, 2048))
    att_keep, att_send = k3(scal, qkv_keep, qkv_recv, dob_keep, dob_recv, idrow, idcol, cos_all, sin_all)
    att_recv = lax.ppermute(att_send, "c", SWAP)

    fold = fold_matrix()
    gb, df, low_out, low_in, small, gup1, gd2, gdd = k2m(
        dy_blocks, scal, hb, aid, inner, gdense, att_keep, att_recv, g2, ups, dd, b1, fold
    )
    small = lax.all_to_all(small.reshape(8, 128, 128), TP, 0, 0, tiled=True)
    out_part = k2o(scal, gb, att_keep, att_recv, low_out, g1, g2)
    out_part, small, df = together(out_part, small, df)
    small = jnp.sum(small.astype(F32), axis=0).astype(BF)
    small = lax.all_to_all(jnp.broadcast_to(small[None], (8, 128, 128)), TP, 0, 0, tiled=True)
    out_sum = lax.psum_scatter(out_part.reshape(1024, 2048), TP, scatter_dimension=0, tiled=True)
    near, owns, sides, gqkv = k2h(scal, df, att_keep, att_recv, low_in, inner, g1, g2)
    near, owns, sides, small = together(near, owns, sides, small)
    shares = scatter_sum(near, owns, sides)

    keep, send = k5(scal, small, aid, hb, fold.T, gup1, gd2, gqkv, gdd, dy_blocks)
    grads = (keep + lax.ppermute(send, "c", SWAP).astype(F32)).astype(BF)
    grads = lax.all_to_all(grads, WSH, 0, 0, tiled=True)
    grads = jnp.sum(grads.astype(F32), axis=0).astype(BF)
    grads = lax.all_to_all(jnp.broadcast_to(grads[None], (8, 80, 512)), TP, 0, 0, tiled=True)
    down_qkv, up_qkv, gdd, gud, gf1d, gf1u, gf2d, gf2u = kf(scal, grads, lax.ppermute(grads, "c", SWAP))

    source = x_own.astype(F32)
    outputs = (source + out_sum.astype(F32) + misc[2:3] + misc[3:4]).astype(BF)[None]
    *shares, outputs = together(*shares, outputs)
    grad_inputs = kn(x_own, output_cotangent[0], misc[0:1], *shares)[None]
    return (
        outputs,
        grad_inputs,
        down_qkv[None],
        up_qkv[None],
        gdd[None],
        gud[None],
        gf1d[None],
        gf1u[None],
        gf2d[None],
        gf2u[None],
    )


def solution(mesh):
    fine = Mesh(np.asarray(mesh.devices).reshape(2, 4, 2, 4, 2), ("xl", "z", "c", "y", "xh"))
    tokens = P(WSH, CTX, None)
    w1 = P(WSH)
    w2 = P(WSH, None)
    w3 = P(WSH, None, None)
    w4 = P(WSH, None, None, None)
    placed = (tokens, tokens, w2, P(WSH, CTX)) + (w1, w1, w2, w2, w2, w2, w1, w1, w1, w1, w2, w1, w2, w1)
    placed = placed + (w4, w4, w3, w3, w3, w3, w3, w3)
    return jax.shard_map(
        local,
        mesh=fine,
        in_specs=placed,
        out_specs=(tokens, tokens, w4, w4, w3, w3, w3, w3, w3, w3),
        check_vma=False,
    )
```

```python
import functools

import jax
import jax.numpy as jnp
import numpy as np
from jax import lax
from jax.experimental import pallas as pl
from jax.experimental.pallas import tpu as pltpu
from jax.sharding import Mesh, PartitionSpec as P

ADAPTERS = 8
RANK = 16
EPSILON = 1e-05
GELU_SCALE = 0.7978845608028654
NEGATIVE = -1e30
SCALE = 64 ** -0.5
BF = jnp.bfloat16
F32 = jnp.float32
WSH = ("y", "xh")
TP = ("xl", "z")
CTX = ("xl", "z", "c")
VMEM_LIMIT = 58 * 1024 * 1024


def nn(a, b):
    return lax.dot_general(a, b, (((1,), (0,)), ((), ())), preferred_element_type=F32)


def nt(a, b):
    return lax.dot_general(a, b, (((1,), (1,)), ((), ())), preferred_element_type=F32)


def tn(a, b):
    return lax.dot_general(a, b, (((0,), (0,)), ((), ())), preferred_element_type=F32)


def adapter_mask(aid, columns):
    col = lax.broadcasted_iota(jnp.int32, (aid.shape[0], columns), 1)
    return (lax.shift_right_logical(col, 4) & 7) == aid.astype(jnp.int32)


def turn(values, cosine, sine):
    width = values.shape[1]
    lane = lax.broadcasted_iota(jnp.int32, values.shape, 1) & 63
    partner = jnp.where(
        lane < 16, pltpu.roll(values, width - 16, 1), pltpu.roll(values, 16, 1)
    )
    return values * cosine + partner * sine


ANY = pl.BlockSpec(memory_space=pl.ANY)
SMEM = pl.BlockSpec(memory_space=pltpu.SMEM)
VM = pl.BlockSpec(memory_space=pltpu.VMEM)
PARAMS = pltpu.CompilerParams(vmem_limit_bytes=VMEM_LIMIT)
MAIN = 208
SECOND = 288
NEAR = 1280


def whole(shape):
    return pl.BlockSpec(shape, lambda t: (0,) * len(shape), pipeline_mode=pl.Buffered(1))


def start_all(pairs, sem):
    for source, target in pairs:
        pltpu.make_async_copy(source, target, sem).start()


def wait_all(target, sem):
    pltpu.make_async_copy(target, target, sem).wait()


def token_copies(blocks, target):
    own, side, above, below, up_more, down_more, far_side = blocks
    return [
        (own, target.at[0, 0], 0),
        (side, target.at[0, 1], 1),
        (above, target.at[1, 0], 2),
        (up_more.at[pl.ds(0, 128), :], target.at[1, 1], 3),
        (below, target.at[2, 0], 4),
        (down_more.at[pl.ds(0, 128), :], target.at[2, 1], 5),
        (up_more.at[pl.ds(128, 64), :], target.at[3, 0, pl.ds(0, 64)], 6),
        (down_more.at[pl.ds(128, 64), :], target.at[3, 0, pl.ds(64, 64)], 6),
        (far_side, target.at[3, 1], 7),
    ]


def start_tokens(blocks, target, sem, first, last):
    for source, part, i in token_copies(blocks, target):
        if first <= i < last:
            pltpu.make_async_copy(source, part, sem.at[i]).start()


def wait_tokens(target, sem, step):
    for i in range(2):
        part = target.at[step, i]
        pltpu.make_async_copy(part, part, sem.at[2 * step + i]).wait()


def pieces_qkv(g1, target):
    return [
        (
            g1.at[y, c, pl.ds(MAIN * xh, 128), pl.ds(0, 768)],
            target.at[pl.ds((2 * y + xh) * 256 + c * 128, 128), :],
        )
        for y in range(4)
        for xh in range(2)
        for c in range(2)
    ]


def pieces_downs(g1, target):
    return [
        (
            g1.at[:, c, pl.ds(MAIN * xh + 128 + 32 * i + 16 * b, 16), :],
            target.at[c, i, :, xh, :, pl.ds(1024 * b, 1024)],
        )
        for c in range(2)
        for i in range(2)
        for xh in range(2)
        for b in range(2)
    ]


def pieces_rank(g, base, stride, target, row):
    return [
        (
            g.at[y, c, pl.ds(stride * xh + base, 16), :],
            target.at[pl.ds(row + (2 * y + xh) * 16, 16), pl.ds(1024 * c, 1024)],
        )
        for y in range(4)
        for xh in range(2)
        for c in range(2)
    ]


def pieces_dense(g1, target, row):
    return [
        (
            g1.at[y, c, pl.ds(2 * MAIN + 32 * b, 32), :],
            target.at[pl.ds(row + 64 * y + 32 * c, 32), pl.ds(1024 * b, 1024)],
        )
        for y in range(4)
        for c in range(2)
        for b in range(2)
    ]


def pieces_w1(g2, target):
    return [
        (
            g2.at[y, c, pl.ds(SECOND * xh, 128), :],
            target.at[pl.ds((2 * y + xh) * 256 + c * 128, 128), :],
        )
        for y in range(4)
        for xh in range(2)
        for c in range(2)
    ]


def pieces_sixteen(g2, c, target, row):
    return [
        (
            g2.at[y, c, pl.ds(SECOND * xh + 128, 16), :],
            target.at[pl.ds(row + (2 * y + xh) * 16, 16), :],
        )
        for y in range(4)
        for xh in range(2)
    ]


def pieces_w2(g2, target):
    return [
        (
            g2.at[y, c, pl.ds(SECOND * xh + 144 + 64 * b, 64), :],
            target.at[pl.ds((2 * y + xh) * 128 + c * 64, 64), pl.ds(1024 * b, 1024)],
        )
        for y in range(4)
        for xh in range(2)
        for c in range(2)
        for b in range(2)
    ]


def block_diagonal(source, target):
    target[...] = jnp.zeros_like(target)
    for p in range(3):
        cols = slice(256 * p, 256 * p + 256)
        target[128 * p : 128 * p + 128, cols] = source[:, cols]


def k1_body(*refs):
    blocks, refs = refs[:7], refs[7:]
    (scal_ref, g1_ref, up_ref, misc_ref, bias_ref, cos_ref, sin_ref,
     hb_ref, inner_ref, keep_ref, send_ref, aid_ref, x_s, w_s, down_s, up_s, x_sem, w_sem) = refs
    step = pl.program_id(0)

    @pl.when(step == 0)
    def _():
        start_tokens(blocks, x_s, x_sem, 0, 2)
        start_all(pieces_downs(g1_ref, down_s), w_sem.at[0])
        start_all(pieces_qkv(g1_ref, w_s.at[:, pl.ds(0, 768)]), w_sem.at[1])
        start_tokens(blocks, x_s, x_sem, 2, 8)

    wait_tokens(x_s, x_sem, step)
    tile = x_s[step].reshape(256, 2176)
    x = tile[:, :2048].astype(F32)
    aid_ref[...] = tile[:, 2048:]
    aid = tile[:, 2048:2049].astype(F32)
    mean = jnp.mean(x, axis=1, keepdims=True)
    center = x - mean
    spread = jnp.mean(center * center, axis=1, keepdims=True)
    h = center * lax.rsqrt(spread + EPSILON) * misc_ref[0:1, :] + misc_ref[1:2, :]
    hb = h.astype(BF)
    hb_ref[...] = hb

    @pl.when(step == 0)
    def _():
        block_diagonal(up_ref, up_s)
        wait_all(down_s, w_sem.at[0])
        w_s[:, 768:] = down_s[...].reshape(512, 2048).T
        wait_all(w_s.at[:, pl.ds(0, 768)], w_sem.at[1])

    pre_all = nn(hb, w_s[...])
    inner = jnp.where(adapter_mask(aid, 512), pre_all[:, 768:], 0.0).astype(BF)
    inner_ref[...] = inner
    pre_all = pre_all[:, :768] + nn(inner[:, :384], up_s[...]) + bias_ref[...]
    first_core = scal_ref[8] == 0
    cosine = jnp.concatenate([cos_ref[...]] * 2, axis=1)
    sine = jnp.concatenate([sin_ref[...]] * 2, axis=1)
    for p in range(3):
        cols = slice(256 * p, 256 * p + 256)
        pre = pre_all[:, cols]
        if p < 2:
            pre = turn(pre, cosine, sine)
        low = pre.astype(BF)
        keep_ref[p] = jnp.where(first_core, low[:, :128], low[:, 128:])
        send_ref[p] = jnp.where(first_core, low[:, 128:], low[:, :128])


def k1(blocks, scal, g1, ups, misc, bias, cosine, sine):
    rows = 256
    return pl.pallas_call(
        k1_body,
        grid=(4,),
        in_specs=[ANY] * 7
        + [
            SMEM,
            ANY,
            whole((128, 768)),
            whole((2, 2048)),
            whole((1, 768)),
            pl.BlockSpec((rows, 128), lambda t: (t, 0)),
            pl.BlockSpec((rows, 128), lambda t: (t, 0)),
        ],
        out_specs=[
            pl.BlockSpec((rows, 2048), lambda t: (t, 0)),
            pl.BlockSpec((rows, 512), lambda t: (t, 0)),
            pl.BlockSpec((3, rows, 128), lambda t: (0, t, 0)),
            pl.BlockSpec((3, rows, 128), lambda t: (0, t, 0)),
            pl.BlockSpec((rows, 128), lambda t: (t, 0)),
        ],
        out_shape=[
            jax.ShapeDtypeStruct((1024, 2048), BF),
            jax.ShapeDtypeStruct((1024, 512), BF),
            jax.ShapeDtypeStruct((3, 1024, 128), BF),
            jax.ShapeDtypeStruct((3, 1024, 128), BF),
            jax.ShapeDtypeStruct((1024, 128), BF),
        ],
        scratch_shapes=[
            pltpu.VMEM((4, 2, 128, 2176), BF),
            pltpu.VMEM((2048, 1280), BF),
            pltpu.VMEM((2, 2, 4, 2, 16, 2048), BF),
            pltpu.VMEM((384, 768), BF),
            pltpu.SemaphoreType.DMA((8,)),
            pltpu.SemaphoreType.DMA((2,)),
        ],
        compiler_params=PARAMS,
        cost_estimate=pl.CostEstimate(flops=6_000_000_000, bytes_accessed=20_000_000, transcendentals=0),
        name="norm_qkv",
    )(*blocks, scal, g1, ups, misc, bias, cosine, sine)


def k1b_body(*refs):
    blocks, refs = refs[:7], refs[7:]
    scal_ref, aid_ref, g1_ref, dd_ref, keep_ref, send_ref, ginner_ref, dy_s, w_s, dy_sem, w_sem = refs
    start_all(pieces_dense(g1_ref, w_s, 0) + pieces_rank(g1_ref, 192, MAIN, w_s, 256), w_sem)
    start_tokens(blocks, dy_s, dy_sem, 0, 8)
    wait_all(w_s, w_sem)
    for step in range(4):
        wait_tokens(dy_s, dy_sem, step)
    first_core = scal_ref[8] == 0
    both = nt(dy_s[...].reshape(1024, 2048), w_s[...])
    aid = aid_ref[:, 0:1].astype(F32)
    ginner = jnp.where(adapter_mask(aid, 128), both[:, 256:], 0.0).astype(BF)
    ginner_ref[...] = ginner
    dob = (both[:, :256] + nn(ginner, dd_ref[...])).astype(BF)
    keep_ref[...] = jnp.where(first_core, dob[:, :128], dob[:, 128:])
    send_ref[...] = jnp.where(first_core, dob[:, 128:], dob[:, :128])


def k1b(blocks, scal, aid, g1, dd):
    return pl.pallas_call(
        k1b_body,
        in_specs=[ANY] * 7 + [SMEM, VM, ANY, VM],
        out_specs=[VM, VM, VM],
        out_shape=[jax.ShapeDtypeStruct((1024, 128), BF)] * 3,
        scratch_shapes=[
            pltpu.VMEM((4, 2, 128, 2048), BF),
            pltpu.VMEM((384, 2048), BF),
            pltpu.SemaphoreType.DMA((8,)),
            pltpu.SemaphoreType.DMA,
        ],
        compiler_params=PARAMS,
        cost_estimate=pl.CostEstimate(flops=2_000_000_000, bytes_accessed=8_000_000, transcendentals=0),
        name="attention_output_grad",
    )(*blocks, scal, aid, g1, dd)


def k3_body(
    scal_ref, qkv_keep, qkv_recv, dob_keep, dob_recv, idrow_ref, idcol_ref, cos_ref, sin_ref,
    keep_out, send_out, x_s, out_s, kt_s, vt_s, dk_s, dv_s, sem, sem_out,
):
    core = scal_ref[8]
    copies = []
    for b in range(8):
        rows = pl.ds(128 * b, 128)
        spot = scal_ref[b]
        for side, (qkv, dob) in enumerate(((qkv_keep, dob_keep), (qkv_recv, dob_recv))):
            parity = core if side == 0 else 1 - core
            copies.append((qkv.at[:, rows, :], x_s.at[pl.ds(0, 3), spot, parity]))
            copies.append((dob.at[rows, :], x_s.at[3, spot, parity]))
    start_all(copies, sem)
    dk_s[...] = jnp.zeros_like(dk_s)
    dv_s[...] = jnp.zeros_like(dv_s)
    wait_all(x_s, sem)
    kt_s[...] = x_s[1].reshape(2048, 128).T
    vt_s[...] = x_s[2].reshape(2048, 128).T
    tile = 256
    lane = lax.broadcasted_iota(jnp.int32, (tile, 128), 1)

    def span(i, start, stop):
        return x_s[i, start // 256 : stop // 256].reshape(stop - start, 128)

    for t in range(8):
        start, stop = tile * t, tile * t + tile
        length = min(stop + tile, 2048)
        q = span(0, start, stop)
        dob = span(3, start, stop)
        zero = jnp.zeros_like(q)
        q = q * jnp.asarray(SCALE, BF)
        q2 = jnp.concatenate([jnp.where(lane < 64, q, zero), jnp.where(lane < 64, zero, q)], axis=0)
        d2 = jnp.concatenate([jnp.where(lane < 64, dob, zero), jnp.where(lane < 64, zero, dob)], axis=0)
        query_ids = idrow_ref[0:1, start:stop]
        query_ids = jnp.concatenate([query_ids, query_ids], axis=1)
        allowed = idcol_ref[start:length, 0:1] <= query_ids
        s = jnp.where(allowed, nt(span(1, start, length), q2), NEGATIVE)
        largest = jnp.max(s, axis=0, keepdims=True)
        if start:
            s_head = nt(span(1, 0, start), q2)
            largest = jnp.maximum(largest, jnp.max(s_head, axis=0, keepdims=True))
            s = jnp.concatenate([s_head, s], axis=0)
        e = jnp.exp(s - largest)
        recip = 1.0 / jnp.sum(e, axis=0, keepdims=True)
        p = e * recip
        pb = p.astype(BF)
        ot = nn(vt_s[:, :length], pb)
        dp = nt(span(2, 0, length), d2)
        o_parts = [ot[:64, :256], ot[64:, 256:]]
        dobt = dob.astype(F32).T
        delta = jnp.concatenate(
            [
                jnp.sum(o_parts[0] * dobt[:64], axis=0, keepdims=True),
                jnp.sum(o_parts[1] * dobt[64:], axis=0, keepdims=True),
            ],
            axis=1,
        )
        ds = (p * (dp - delta)).astype(BF)
        dk_s[:length] += nn(ds, q2)
        dv_s[:length] += nn(pb, d2)
        dqt = nn(kt_s[:, :length], ds)
        dq_parts = [dqt[:64, :256], dqt[64:, 256:]]
        o = jnp.concatenate(o_parts, axis=0).T
        dq = jnp.concatenate(dq_parts, axis=0).T * SCALE
        rows = slice(start, stop)
        out_s[0, t] = o.astype(BF).reshape(2, 128, 128)
        out_s[1, t] = turn(dq, cos_ref[rows], -sin_ref[rows]).astype(BF).reshape(2, 128, 128)
    out_s[2] = turn(dk_s[...], cos_ref[...], -sin_ref[...]).astype(BF).reshape(8, 2, 128, 128)
    out_s[3] = dv_s[...].astype(BF).reshape(8, 2, 128, 128)
    copies = []
    for b in range(8):
        rows = pl.ds(128 * b, 128)
        spot = scal_ref[b]
        copies.append((out_s.at[:, spot, core], keep_out.at[:, rows, :]))
        copies.append((out_s.at[:, spot, 1 - core], send_out.at[:, rows, :]))
    start_all(copies, sem_out)
    wait_all(out_s, sem_out)


def k3(scal, qkv_keep, qkv_recv, dob_keep, dob_recv, idrow, idcol, cosine, sine):
    vm = pl.BlockSpec(memory_space=pltpu.VMEM)
    return pl.pallas_call(
        k3_body,
        in_specs=[SMEM] + [ANY] * 4 + [vm] * 4,
        out_specs=[ANY, ANY],
        out_shape=[jax.ShapeDtypeStruct((4, 1024, 128), BF)] * 2,
        scratch_shapes=[
            pltpu.VMEM((4, 8, 2, 128, 128), BF),
            pltpu.VMEM((4, 8, 2, 128, 128), BF),
            pltpu.VMEM((128, 2048), BF),
            pltpu.VMEM((128, 2048), BF),
            pltpu.VMEM((2048, 128), F32),
            pltpu.VMEM((2048, 128), F32),
            pltpu.SemaphoreType.DMA,
            pltpu.SemaphoreType.DMA,
        ],
        compiler_params=PARAMS,
        cost_estimate=pl.CostEstimate(flops=15_000_000_000, bytes_accessed=8_000_000, transcendentals=5_000_000),
        name="attention",
    )(scal, qkv_keep, qkv_recv, dob_keep, dob_recv, idrow, idcol, cosine, sine)


def heads_of(keep_ref, recv_ref, i, first_core):
    a, b = keep_ref[i], recv_ref[i]
    return jnp.concatenate([jnp.where(first_core, a, b), jnp.where(first_core, b, a)], axis=1)


def tile_spec(width, rows=256):
    return pl.BlockSpec((rows, width), lambda t, s: (t, 0))


def const_spec(shape):
    return pl.BlockSpec(shape, lambda t, s: (0,) * len(shape), pipeline_mode=pl.Buffered(1))


def placed_spec(width):
    return pl.BlockSpec((2, 1, 128, width), lambda t, s: (0, s[12 + t], 0, 0))


def place(ref, xl, value):
    ref[xl, 0] = value[:128]
    ref[1 - xl, 0] = value[128:]


def accumulate(step, pairs):
    @pl.when(step == 0)
    def _():
        for ref, value in pairs:
            ref[...] = value

    @pl.when(step > 0)
    def _():
        for ref, value in pairs:
            ref[...] += value


def k2m_body(scal_ref, *refs):
    blocks, refs = refs[:7], refs[7:]
    (hb_ref, aid_ref, inner_ref, gdense_ref, keep_ref, recv_ref, g2_ref, up_ref, dd_ref, b1_ref, fold_ref,
     gb_ref, df_ref, low_out_ref, low_in_ref, small_ref, gup1_ref, gd2_ref, gdd_ref,
     dy_s, w1_s, w2_s, d2_s, up_s, dy_sem, sems) = refs
    step = pl.program_id(0)

    @pl.when(step == 0)
    def _():
        start_all(pieces_w1(g2_ref, w1_s) + pieces_sixteen(g2_ref, 0, w1_s, 2048), sems.at[0])
        start_all(pieces_sixteen(g2_ref, 1, d2_s, 0), sems.at[1])
        start_tokens(blocks, dy_s, dy_sem, 0, 2)
        start_all(pieces_w2(g2_ref, w2_s) + pieces_rank(g2_ref, 272, SECOND, w2_s, 1024), sems.at[2])
        start_tokens(blocks, dy_s, dy_sem, 2, 8)
        block_diagonal(up_ref, up_s)
        wait_all(w1_s, sems.at[0])

    aid = aid_ref[:, 0:1].astype(F32)
    first_core = scal_ref[8] == 0
    f = nn(jnp.concatenate([hb_ref[...], inner_ref[...]], axis=1), w1_s[...]) + b1_ref[...]

    @pl.when(step == 0)
    def _():
        wait_all(w2_s, sems.at[2])
        wait_all(d2_s, sems.at[1])

    wait_tokens(dy_s, dy_sem, step)
    wide = nt(dy_s[step].reshape(256, 2048), w2_s[...])
    square = f * f
    th = jnp.tanh(GELU_SCALE * f * (1.0 + 0.044715 * square))
    half = 0.5 * (1.0 + th)
    gb = (f * half).astype(BF)
    gb_ref[...] = gb
    slope = half + (0.5 * GELU_SCALE) * f * (1.0 - th * th) * (1.0 + 3 * 0.044715 * square)
    ginner2 = jnp.where(adapter_mask(aid, 128), wide[:, 1024:], 0.0).astype(BF)
    ob = heads_of(keep_ref, recv_ref, 0, first_core)
    dpre = jnp.concatenate([heads_of(keep_ref, recv_ref, p, first_core) for p in (1, 2, 3)], axis=1)
    inner2 = nt(gb, d2_s[...])
    innerd = nt(ob, dd_ref[...])
    ginner = nt(dpre, up_s[...])
    df = ((wide[:, :1024] + nn(ginner2, d2_s[...])) * slope).astype(BF)
    df_ref[...] = df
    ginner1 = nt(df, w1_s[2048:])
    low = jnp.concatenate([ginner, ginner1, innerd, inner2], axis=1)
    low = jnp.where(adapter_mask(aid, 768), low, 0.0).astype(BF)
    low_in_ref[...] = low[:, :512]
    low_out_ref[...] = low[:, 512:]
    place(small_ref, scal_ref[10], nn(low, fold_ref[...]).astype(BF))
    accumulate(
        step,
        [
            (gup1_ref, tn(inner_ref[...], df)),
            (gd2_ref, tn(ginner2, gb)),
            (gdd_ref, tn(gdense_ref[...], ob)),
        ],
    )


def att_spec(first, count):
    return pl.BlockSpec((count, 256, 128), lambda t, s: (first, t, 0))


def k2m(blocks, scal, hb, aid, inner, gdense, keep, recv, g2, ups, dd, b1, fold):
    return pl.pallas_call(
        k2m_body,
        grid_spec=pltpu.PrefetchScalarGridSpec(
            num_scalar_prefetch=1,
            grid=(4,),
            in_specs=[ANY] * 7
            + [
                tile_spec(2048),
                tile_spec(128),
                pl.BlockSpec((256, 128), lambda t, s: (t, 3)),
                tile_spec(128),
                att_spec(0, 4),
                att_spec(0, 4),
                ANY,
                const_spec((128, 768)),
                const_spec((128, 256)),
                const_spec((1, 1024)),
                const_spec((768, 128)),
            ],
            out_specs=[
                tile_spec(1024),
                tile_spec(1024),
                tile_spec(256),
                tile_spec(512),
                placed_spec(128),
                const_spec((128, 1024)),
                const_spec((128, 1024)),
                const_spec((128, 256)),
            ],
            scratch_shapes=[
                pltpu.VMEM((4, 2, 128, 2048), BF),
                pltpu.VMEM((2176, 1024), BF),
                pltpu.VMEM((1152, 2048), BF),
                pltpu.VMEM((128, 1024), BF),
                pltpu.VMEM((384, 768), BF),
                pltpu.SemaphoreType.DMA((8,)),
                pltpu.SemaphoreType.DMA((3,)),
            ],
        ),
        out_shape=[
            jax.ShapeDtypeStruct((1024, 1024), BF),
            jax.ShapeDtypeStruct((1024, 1024), BF),
            jax.ShapeDtypeStruct((1024, 256), BF),
            jax.ShapeDtypeStruct((1024, 512), BF),
            jax.ShapeDtypeStruct((2, 4, 128, 128), BF),
            jax.ShapeDtypeStruct((128, 1024), F32),
            jax.ShapeDtypeStruct((128, 1024), F32),
            jax.ShapeDtypeStruct((128, 256), F32),
        ],
        compiler_params=PARAMS,
        cost_estimate=pl.CostEstimate(flops=14_000_000_000, bytes_accessed=30_000_000, transcendentals=1_000_000),
        name="feed_forward",
    )(scal, *blocks, hb, aid, inner, gdense, keep, recv, g2, ups, dd, b1, fold)


def k2o_body(scal_ref, gb_ref, keep_ref, recv_ref, low_ref, g1_ref, g2_ref, out_ref, w_s, sem):
    step = pl.program_id(0)

    @pl.when(step == 0)
    def _():
        start_all(
            pieces_w2(g2_ref, w_s)
            + pieces_dense(g1_ref, w_s, 1024)
            + pieces_rank(g1_ref, 192, MAIN, w_s, 1280)
            + pieces_rank(g2_ref, 272, SECOND, w_s, 1408),
            sem,
        )
        wait_all(w_s, sem)

    ob = heads_of(keep_ref, recv_ref, 0, scal_ref[8] == 0)
    out = nn(jnp.concatenate([gb_ref[...], ob, low_ref[...]], axis=1), w_s[...]).astype(BF)
    place(out_ref, scal_ref[10], out)


def k2o(scal, gb, keep, recv, low_out, g1, g2):
    return pl.pallas_call(
        k2o_body,
        grid_spec=pltpu.PrefetchScalarGridSpec(
            num_scalar_prefetch=1,
            grid=(4,),
            in_specs=[tile_spec(1024), att_spec(0, 1), att_spec(0, 1), tile_spec(256), ANY, ANY],
            out_specs=[placed_spec(2048)],
            scratch_shapes=[pltpu.VMEM((1536, 2048), BF), pltpu.SemaphoreType.DMA],
        ),
        out_shape=[jax.ShapeDtypeStruct((2, 4, 128, 2048), BF)],
        compiler_params=PARAMS,
        cost_estimate=pl.CostEstimate(flops=7_000_000_000, bytes_accessed=14_000_000, transcendentals=0),
        name="out_rows",
    )(scal, gb, keep, recv, low_out, g1, g2)[0]


def k2h_body(
    scal_ref, df_ref, keep_ref, recv_ref, low_ref, inner_ref, g1_ref, g2_ref,
    near_ref, owns_ref, sides_ref, gqkv_ref, w_s, down_s, sems,
):
    step = pl.program_id(0)

    @pl.when(step == 0)
    def _():
        start_all(
            pieces_w1(g2_ref, w_s.at[:, pl.ds(0, 1024)]) + pieces_qkv(g1_ref, w_s.at[:, pl.ds(1024, 768)]), sems.at[0]
        )
        start_all(pieces_downs(g1_ref, down_s), sems.at[1])
        wait_all(w_s, sems.at[0])
        wait_all(down_s, sems.at[1])

    first_core = scal_ref[8] == 0
    dpre = [heads_of(keep_ref, recv_ref, p, first_core) for p in (1, 2, 3)]
    dh = nt(jnp.concatenate([df_ref[...]] + dpre, axis=1), w_s[...])
    dh = (dh + nn(low_ref[...], down_s[...].reshape(512, 2048))).astype(BF)
    near_ref[0] = dh[:128, :NEAR]
    near_ref[1] = dh[128:, :NEAR]
    owns_ref[0] = dh[:128, NEAR:]
    sides_ref[0] = dh[128:, NEAR:]
    gqkv = [tn(inner_ref[:, 128 * p : 128 * p + 128], dpre[p]) for p in range(3)]
    accumulate(step, [(gqkv_ref, jnp.concatenate(gqkv, axis=1))])


def k2h(scal, df, keep, recv, low_in, inner, g1, g2):
    return pl.pallas_call(
        k2h_body,
        grid_spec=pltpu.PrefetchScalarGridSpec(
            num_scalar_prefetch=1,
            grid=(4,),
            in_specs=[tile_spec(1024), att_spec(0, 4), att_spec(0, 4), tile_spec(512), tile_spec(512), ANY, ANY],
            out_specs=[
                pl.BlockSpec((2, 128, NEAR), lambda t, s: (t, 0, 0)),
                pl.BlockSpec((1, 128, 2048 - NEAR), lambda t, s: (t, 0, 0)),
                pl.BlockSpec((1, 128, 2048 - NEAR), lambda t, s: (t, 0, 0)),
                const_spec((128, 768)),
            ],
            scratch_shapes=[
                pltpu.VMEM((2048, 1792), BF),
                pltpu.VMEM((2, 2, 4, 2, 16, 2048), BF),
                pltpu.SemaphoreType.DMA((2,)),
            ],
        ),
        out_shape=[
            jax.ShapeDtypeStruct((8, 128, NEAR), BF),
            jax.ShapeDtypeStruct((4, 128, 2048 - NEAR), BF),
            jax.ShapeDtypeStruct((4, 128, 2048 - NEAR), BF),
            jax.ShapeDtypeStruct((128, 768), F32),
        ],
        compiler_params=PARAMS,
        cost_estimate=pl.CostEstimate(flops=10_000_000_000, bytes_accessed=18_000_000, transcendentals=0),
        name="hidden_grad",
    )(scal, df, keep, recv, low_in, inner, g1, g2)


def k5_body(scal_ref, small_ref, aid_ref, hb_ref, spread_ref, gup1_ref, gd2_ref, gqkv_ref, gdd_ref, *refs):
    blocks, refs = refs[:7], refs[7:]
    keep_ref, send_ref, dy_s, sem = refs
    column = pl.multiple_of(256 * scal_ref[9], 256)
    start_all(
        [(source.at[:, pl.ds(column, 256)], part) for source, part, _ in token_copies(blocks, dy_s)], sem
    )
    first_core = scal_ref[8] == 0

    def store(section, left, right):
        kept = jnp.where(first_core, left, right)
        sent = jnp.where(first_core, right, left)
        keep_ref[:, 16 * section : 16 * section + 16] = kept.reshape(8, 16, 512)
        send_ref[:, 16 * section : 16 * section + 16] = sent.astype(BF).reshape(8, 16, 512)

    small = jnp.concatenate([small_ref[scal_ref[b]] for b in range(8)], axis=0)
    aid = aid_ref[:, 0:1].astype(F32)
    wide = jnp.where(adapter_mask(aid, 768), nn(small, spread_ref[...]), 0.0).astype(BF)
    down = tn(wide[:, :512], hb_ref[...])
    store(
        0,
        jnp.concatenate([down[:128], down[128:256]], axis=1),
        jnp.concatenate([down[256:384], down[384:]], axis=1),
    )
    store(1, gqkv_ref[:, :512], jnp.concatenate([gqkv_ref[:, 512:], gdd_ref[...]], axis=1))
    store(2, gup1_ref[:, :512], gup1_ref[:, 512:])
    store(3, gd2_ref[:, :512], gd2_ref[:, 512:])
    wait_all(dy_s, sem)
    up = tn(wide[:, 512:], dy_s[...].reshape(1024, 256))
    left = jnp.concatenate([up[:128], up[128:]], axis=1)
    store(4, left, jnp.zeros_like(left))


def k5(scal, small, aid, hb, spread, gup1, gd2, gqkv, gdd, blocks):
    def const(shape):
        return pl.BlockSpec(shape, lambda t, s: (0,) * len(shape))

    return pl.pallas_call(
        k5_body,
        grid_spec=pltpu.PrefetchScalarGridSpec(
            num_scalar_prefetch=1,
            grid=(1,),
            in_specs=[
                const((8, 128, 128)),
                const((1024, 128)),
                pl.BlockSpec((1024, 256), lambda t, s: (0, s[9])),
                const((128, 768)),
                const((128, 1024)),
                const((128, 1024)),
                const((128, 768)),
                const((128, 256)),
            ]
            + [ANY] * 7,
            out_specs=[const((8, 80, 512)), const((8, 80, 512))],
            scratch_shapes=[pltpu.VMEM((4, 2, 128, 256), BF), pltpu.SemaphoreType.DMA],
        ),
        out_shape=[jax.ShapeDtypeStruct((8, 80, 512), F32), jax.ShapeDtypeStruct((8, 80, 512), BF)],
        compiler_params=PARAMS,
        cost_estimate=pl.CostEstimate(flops=1_500_000_000, bytes_accessed=6_000_000, transcendentals=0),
        name="adapter_grads",
    )(scal, small, aid, hb, spread, gup1, gd2, gqkv, gdd, *blocks)


def kf_body(scal_ref, mine_ref, theirs_ref, down_ref, up_ref, dd_ref, ud_ref, f1d_ref, f1u_ref, f2d_ref, f2u_ref):
    lane = lax.broadcasted_iota(jnp.int32, (16, 128), 1)

    core = scal_ref[8]

    def part(j, half, section, start, width):
        rows, cols = slice(16 * section, 16 * section + 16), slice(start, start + width)
        return jnp.where(core == half, mine_ref[j, rows, cols], theirs_ref[j, rows, cols]).astype(F32)

    for j in range(8):
        block = slice(256 * j, 256 * j + 256)
        down_ref[0, :, block] = part(j, 0, 0, 0, 256)
        down_ref[1, :, block] = part(j, 0, 0, 256, 256)
        down_ref[2, :, block] = part(j, 1, 0, 0, 256)
        f1d_ref[:, block] = part(j, 1, 0, 256, 256)
        ud_ref[:, block] = part(j, 0, 4, 0, 256)
        f2u_ref[:, block] = part(j, 0, 4, 256, 256)
        for w in range(8):
            spot = slice(1024 * w + 128 * j, 1024 * w + 128 * j + 128)
            f1u_ref[:, spot] = part(j, w // 4, 2, 128 * (w % 4), 128)
            f2d_ref[:, spot] = part(j, w // 4, 3, 128 * (w % 4), 128)
    for i in range(4):
        for x in range(2):
            for y in range(4):
                for h in range(2):
                    start = 256 * (i % 2) + 128 * (y // 2)
                    a = part(4 * x + 2 * h, i // 2, 1, start, 128)
                    b = part(4 * x + 2 * h + 1, i // 2, 1, start, 128)
                    if y % 2:
                        a = pltpu.roll(a, 64, 1)
                    else:
                        b = pltpu.roll(b, 64, 1)
                    value = jnp.where(lane < 64, a, b)
                    spot = slice(256 * (2 * y + x) + 128 * h, 256 * (2 * y + x) + 128 * h + 128)
                    if i < 3:
                        up_ref[i, :, spot] = value
                    else:
                        dd_ref[:, spot] = value


def kf(scal, mine, theirs):
    return pl.pallas_call(
        kf_body,
        in_specs=[SMEM, VM, VM],
        out_specs=[VM] * 8,
        out_shape=[
            jax.ShapeDtypeStruct((3, 16, 2048), F32),
            jax.ShapeDtypeStruct((3, 16, 2048), F32),
            jax.ShapeDtypeStruct((16, 2048), F32),
            jax.ShapeDtypeStruct((16, 2048), F32),
            jax.ShapeDtypeStruct((16, 2048), F32),
            jax.ShapeDtypeStruct((16, 8192), F32),
            jax.ShapeDtypeStruct((16, 8192), F32),
            jax.ShapeDtypeStruct((16, 2048), F32),
        ],
        compiler_params=PARAMS,
        name="finish",
    )(scal, mine, theirs)


def kn_body(x_ref, dy_ref, gain_ref, own_ref, up_ref, down_ref, side_ref, t_ref, up2_ref, down2_ref, out_ref):
    def total(*parts):
        return sum(p[...].astype(F32) for p in parts)

    dh = jnp.concatenate([total(own_ref, up_ref, down_ref, side_ref), total(t_ref, up2_ref, down2_ref)], axis=1)
    x = x_ref[...].astype(F32)
    center = x - jnp.mean(x, axis=1, keepdims=True)
    inv = lax.rsqrt(jnp.mean(center * center, axis=1, keepdims=True) + EPSILON)
    hn = center * inv
    e = dh * gain_ref[...]
    dx = (e - jnp.mean(e, axis=1, keepdims=True) - hn * jnp.mean(e * hn, axis=1, keepdims=True)) * inv
    out_ref[...] = (dy_ref[...].astype(F32) + dx).astype(BF)


def kn(*args):
    return pl.pallas_call(
        kn_body,
        in_specs=[VM] * 10,
        out_specs=VM,
        out_shape=jax.ShapeDtypeStruct((128, 2048), BF),
        compiler_params=PARAMS,
        name="norm_grad",
    )(*args)


def pack1_body(
    scal_ref, wq, wk, wv, wd, ad_ref, fd_ref, au_ref, dd_ref, du_ref, misc_ref, b1_ref,
    own_ref, other_ref, w_s, d_s, sem, d_sem,
):
    c, z = scal_ref[8], scal_ref[11]
    start_all([(w.at[pl.ds(128 * c, 128), :], w_s.at[i]) for i, w in enumerate((wq, wk, wv))], sem)
    start_all([(wd.at[pl.ds(64 * z + 32 * c, 32), :], d_s)], d_sem)
    first_core = c == 0
    odd = lax.rem(z, 2) == 1
    targets = ((own_ref, scal_ref[10]), (other_ref, 1 - scal_ref[10]))

    def head_pair(read, rows, i, xl):
        lane = lax.broadcasted_iota(jnp.int32, (rows, 128), 1)
        parts = []
        for k in range(2):
            start = (2 * (i + k) + xl) * 256 + (z // 2) * 128
            v = read(pl.ds(pl.multiple_of(start, 128), 128)).astype(F32)
            turned = pltpu.roll(v, 64, 1)
            parts.append(jnp.where(odd, turned, v) if k == 0 else jnp.where(odd, v, turned))
        return jnp.where(lane < 64, parts[0], parts[1]).astype(BF)

    half = pl.ds(pl.multiple_of((z // 2) * 128, 128), 128)
    row = lax.broadcasted_iota(jnp.int32, (16, 128), 0)
    lane = lax.broadcasted_iota(jnp.int32, (16, 128), 1)

    def biases(xl):
        plain = misc_ref[:, :128].astype(F32), misc_ref[:, 128:256].astype(F32)
        mine = misc_ref[:, half].astype(F32)
        turned = pltpu.roll(mine, 64, 1)
        low = jnp.where(odd, turned, mine)
        high = jnp.where(odd, mine, turned)
        query_key = jnp.where(lane[:1] < 64, low[4:5], high[5:6])
        value = jnp.where(lane[:1] < 64, low[6:7], 0.0)
        hidden = jnp.where(row[:8] == xl * 4 + z, b1_ref[...].astype(F32), 0.0)
        hidden = jnp.sum(hidden, axis=0, keepdims=True)
        left = jnp.where(row < 4, plain[0], jnp.where(row == 4, query_key, hidden))
        right = jnp.where(row < 4, plain[1], value)
        return left.astype(BF), right.astype(BF)

    a = jnp.where(first_core, ad_ref[0], ad_ref[2])
    b = jnp.where(first_core, ad_ref[1], fd_ref[...])
    du = jnp.where(first_core, du_ref[:, :1024], du_ref[:, 1024:])
    for out_ref, xl in targets:
        rows_of = biases(xl)
        for p in range(4):
            for i in (0, 2):
                read = (lambda s, p=p: au_ref[p, :, s]) if p < 3 else (lambda s: dd_ref[:, s])
                value = head_pair(read, 16, i, xl)
                rows = slice(16 * p, 16 * p + 16)
                if p == 0:
                    value = jnp.where(first_core, value, rows_of[i // 2])
                out_ref[rows, 768 + 64 * i : 768 + 64 * i + 128] = value
        out_ref[64:128, 768:] = jnp.zeros((64, 256), BF)
        out_ref[128:144] = a[:, :1024]
        out_ref[144:160] = a[:, 1024:]
        out_ref[160:176] = b[:, :1024]
        out_ref[176:192] = b[:, 1024:]
        out_ref[192:208] = du
    wait_all(d_s, d_sem)
    for out_ref, _ in targets:
        out_ref[208:240] = d_s[:, :1024]
        out_ref[240:272] = d_s[:, 1024:]
    wait_all(w_s, sem)
    for p in range(3):
        for i in (0, 2):
            start = 256 * p + 64 * i
            for out_ref, xl in targets:
                out_ref[:128, start : start + 128] = head_pair(lambda s, p=p: w_s[p, :, s], 128, i, xl)


def pack1(scal, wq, wk, wv, wd, ad, fd, au, dd, du, misc, b1):
    return pl.pallas_call(
        pack1_body,
        in_specs=[SMEM] + [ANY] * 4 + [VM] * 7,
        out_specs=[VM, VM],
        out_shape=[jax.ShapeDtypeStruct((272, 1024), BF)] * 2,
        scratch_shapes=[
            pltpu.VMEM((3, 128, 2048), BF),
            pltpu.VMEM((32, 2048), BF),
            pltpu.SemaphoreType.DMA,
            pltpu.SemaphoreType.DMA,
        ],
        compiler_params=PARAMS,
        cost_estimate=pl.CostEstimate(flops=1_000_000, bytes_accessed=4_000_000, transcendentals=0),
        name="pack_qkv",
    )(scal, wq, wk, wv, wd, ad, fd, au, dd, du, misc, b1)


def pack2_body(scal_ref, w1, w2, up_ref, down_ref, up2_ref, own_ref, other_ref, w1_s, w2_s, sem, sem2):
    c, z = scal_ref[8], scal_ref[11]
    places = [scal_ref[10] * 4 + z, (1 - scal_ref[10]) * 4 + z]
    start_all([(w1.at[pl.ds(128 * c, 128), :], w1_s)], sem)
    start_all([(w2.at[pl.ds(128 * places[i] + 64 * c, 64), :], w2_s.at[i]) for i in range(2)], sem2)
    first_core = c == 0
    up2 = jnp.where(first_core, up2_ref[:, :1024], up2_ref[:, 1024:])

    def column(w, i):
        return pl.ds(pl.multiple_of(1024 * w + 128 * places[i], 128), 128)

    for i, out_ref in enumerate((own_ref, other_ref)):
        out_ref[272:288] = up2
        for w in range(8):
            out_ref[128:144, 128 * w : 128 * w + 128] = jnp.where(
                first_core, up_ref[:, column(w, i)], down_ref[:, column(w, i)]
            )
    wait_all(w2_s, sem2)
    for i, out_ref in enumerate((own_ref, other_ref)):
        out_ref[144:208] = w2_s[i, :, :1024]
        out_ref[208:272] = w2_s[i, :, 1024:]
    wait_all(w1_s, sem)
    for i, out_ref in enumerate((own_ref, other_ref)):
        for w in range(8):
            out_ref[:128, 128 * w : 128 * w + 128] = w1_s[:, column(w, i)]


def pack2(scal, w1, w2, up, down, up2):
    return pl.pallas_call(
        pack2_body,
        in_specs=[SMEM, ANY, ANY, VM, VM, VM],
        out_specs=[VM, VM],
        out_shape=[jax.ShapeDtypeStruct((288, 1024), BF)] * 2,
        scratch_shapes=[
            pltpu.VMEM((128, 8192), BF),
            pltpu.VMEM((2, 64, 2048), BF),
            pltpu.SemaphoreType.DMA,
            pltpu.SemaphoreType.DMA,
        ],
        compiler_params=PARAMS,
        cost_estimate=pl.CostEstimate(flops=1_000_000, bytes_accessed=5_000_000, transcendentals=0),
        name="pack_hidden",
    )(scal, w1, w2, up, down, up2)


def rotary_tables(positions):
    lane = np.arange(128) % 64
    rate = np.where(lane < 32, 10000.0 ** (-2.0 * (lane % 16) / 32.0), 0.0).astype(np.float32)
    sign = np.where(lane < 16, -1.0, 1.0).astype(np.float32)
    angles = positions.astype(F32)[:, None] * jnp.asarray(rate)[None, :]
    return jnp.cos(angles), jnp.sin(angles) * jnp.asarray(sign)[None, :]


def fold_matrix():
    row = np.arange(768)
    target = (row // 128) * 16 + row % 16
    return jnp.asarray((target[:, None] == np.arange(128)[None, :]).astype(np.float32)).astype(BF)


def halves(a):
    m = a.shape[1] // 2
    return jnp.concatenate([a[:, :m], a[:, m:]], axis=0)


SWAP = [(0, 1), (1, 0)]
FLIP = [(i, 3 - i) for i in range(4)]
UP = [(i, (i + 1) % 4) for i in range(4)]
DOWN = [(i, (i + 3) % 4) for i in range(4)]
Z_OFFSETS = (0, -1, 1, 2)


def together(*values):
    return lax.optimization_barrier(values)


def up(a):
    return lax.ppermute(a, "z", UP)


def down(a):
    return lax.ppermute(a, "z", DOWN)


def across(a):
    return lax.ppermute(a, "xl", SWAP)


def gather_pair(own, other, single):
    xh = lax.axis_index("xh")
    parts = [jnp.where(xh == 0, own, other), jnp.where(xh == 0, other, own)]
    if single is not None:
        parts.append(single)
    packed = jnp.concatenate(parts, axis=0)
    g = lax.all_gather(packed, ("y", "c"), axis=0, tiled=False)
    return g.reshape((4, 2) + packed.shape)


def add(*terms):
    return sum(t.astype(F32) for t in terms)


def scatter_sum(near, owns, sides):
    own, side, down_own, down_side, up_own, up_side, far_own, far_side = [near[b] for b in range(8)]
    from_side = lax.ppermute(sides, "xl", SWAP)
    via_below = lax.ppermute(far_own, "z", UP)
    via_above = lax.ppermute(far_side, "z", DOWN)
    up_side = lax.ppermute(up_side, "z", UP)
    down_own = lax.ppermute(down_own, "z", DOWN)
    up_own = lax.ppermute(add(up_own, via_below).astype(BF), "z", UP)
    down_side = lax.ppermute(add(down_side, via_above).astype(BF), "z", DOWN)
    side = lax.ppermute(add(side, up_side, down_side).astype(BF), "xl", SWAP)
    t = add(owns, from_side)
    far = t[3].astype(BF)
    half_up = lax.ppermute(far[:64], "z", UP)
    half_down = lax.ppermute(far[64:], "z", DOWN)
    up = jnp.concatenate([t[2, :64] + half_up.astype(F32), t[2, 64:]], axis=0).astype(BF)
    down = jnp.concatenate([t[1, :64], t[1, 64:] + half_down.astype(F32)], axis=0).astype(BF)
    return own, up_own, down_own, side, t[0], lax.ppermute(up, "z", UP), lax.ppermute(down, "z", DOWN)


def local(
    inputs,
    output_cotangent,
    block_index_per_position,
    adapter_index_per_run,
    norm_gain,
    norm_bias,
    query_weight,
    key_weight,
    value_weight,
    dense_weight,
    query_bias,
    key_bias,
    value_bias,
    dense_bias,
    feedforward_in_weight,
    feedforward_in_bias,
    feedforward_out_weight,
    feedforward_out_bias,
    adapter_attention_down,
    adapter_attention_up,
    adapter_dense_down,
    adapter_dense_up,
    adapter_feedforward_in_down,
    adapter_feedforward_in_up,
    adapter_feedforward_out_down,
    adapter_feedforward_out_up,
):
    xl, z, c = lax.axis_index("xl"), lax.axis_index("z"), lax.axis_index("c")
    xh = lax.axis_index("xh")
    j = xl * 4 + z
    x_own = inputs[0]
    dy_own = output_cotangent[0]
    run_adapter = adapter_index_per_run[0, 0].astype(F32).astype(BF)
    block_row = block_index_per_position[0]
    z_of = [lax.rem(z + o + 4, 4) for o in Z_OFFSETS]
    spots = [(xl if side == 0 else 1 - xl) * 4 + zz for zz in z_of for side in range(2)]
    scal = jnp.stack(spots + [c, j, xl, z] + z_of).astype(jnp.int32)

    zero = jnp.zeros((256,), BF)
    misc_own = jnp.stack(
        [norm_gain, norm_bias, dense_bias, feedforward_out_bias, query_bias, key_bias, value_bias] + [zero] * 9
    )
    sent1, for_other = pack1(
        scal,
        query_weight,
        key_weight,
        value_weight,
        dense_weight,
        adapter_attention_down[0],
        adapter_feedforward_in_down[0],
        adapter_attention_up[0],
        adapter_dense_down[0],
        adapter_dense_up[0],
        misc_own,
        feedforward_in_bias.reshape(8, 128),
    )
    own2, own2_for_other = pack2(
        scal,
        feedforward_in_weight,
        feedforward_out_weight,
        adapter_feedforward_in_up[0],
        adapter_feedforward_out_down[0],
        adapter_feedforward_out_up[0],
    )
    spread = jnp.stack(spots)
    my_positions = ((spread * 2 + c) * 128)[:, None] + jnp.arange(128, dtype=jnp.int32)[None, :]
    tables = rotary_tables(my_positions.reshape(1024)) + rotary_tables(jnp.arange(2048, dtype=jnp.int32))
    tables = tables + (jnp.broadcast_to(block_row[:, None], (2048, 128)),)
    x_send = jnp.concatenate([x_own, jnp.full((128, 128), run_adapter, BF)], axis=1)

    x_up, x_down, x_side = together(up(x_send), down(x_send), across(x_send))
    other1 = lax.ppermute(for_other, ("xl", "xh"), FLIP)
    x_up_more, x_down_more, dy_side = together(
        up(jnp.concatenate([x_side, x_up[:64]], axis=0)),
        down(jnp.concatenate([x_side, x_down[64:]], axis=0)),
        across(together(dy_own, x_side)[0]),
    )
    other1, own2, own2_for_other, tables, x_up_more, x_down_more, dy_side = together(
        other1, own2, own2_for_other, tables, x_up_more, x_down_more, dy_side
    )
    g1 = gather_pair(sent1[:MAIN], other1[:MAIN], jnp.where(xh == xl, sent1[MAIN:], other1[MAIN:]))
    x_far_side, dy_up, dy_down, other2 = together(
        across(jnp.concatenate([x_up_more[128:], x_down_more[128:]], axis=0)),
        up(together(dy_own, dy_side)[0]),
        down(together(dy_own, dy_side)[0]),
        lax.ppermute(own2_for_other, ("xl", "xh"), FLIP),
    )
    g2 = gather_pair(own2, other2, None)
    dy_up_more, dy_down_more = together(
        up(jnp.concatenate([dy_side, dy_up[:64]], axis=0)), down(jnp.concatenate([dy_side, dy_down[64:]], axis=0))
    )
    dy_far_side = across(jnp.concatenate([dy_up_more[128:], dy_down_more[128:]], axis=0))
    x_blocks = [x_send, x_side, x_up, x_down, x_up_more, x_down_more, x_far_side]
    dy_blocks = [dy_own, dy_side, dy_up, dy_down, dy_up_more, dy_down_more, dy_far_side]

    def side_of(core):
        return jnp.stack(
            [g1[:, core, MAIN * h : MAIN * h + 64, 768:] for h in range(2)], axis=1
        ).reshape(8, 64, 256)

    ups_all = side_of(0).reshape(8, 4, 16, 256).transpose(1, 0, 2, 3).reshape(4, 128, 256)
    ups = jnp.concatenate([ups_all[0], ups_all[1], ups_all[2]], axis=1)
    dd = ups_all[3]
    small_all = side_of(1)[:, :6].astype(F32)
    misc = small_all[:, :4].transpose(1, 0, 2).reshape(4, 2048)
    head_b = lax.dynamic_index_in_dim(small_all[:, 4, :192].reshape(4, 2, 3, 64), xl, 1, keepdims=False)
    bias_qkv = head_b.transpose(1, 0, 2).reshape(1, 768)
    b1 = small_all[:, 5, :128].reshape(1, 1024)

    cos_mine, sin_mine, cos_all, sin_all, idcol = tables

    hb, inner, qkv_keep, qkv_send, aid = k1(x_blocks, scal, g1, ups, misc[:2], bias_qkv, cos_mine, sin_mine)
    qkv_recv = lax.ppermute(qkv_send, "c", SWAP)
    dob_keep, dob_send, gdense = k1b(dy_blocks, scal, aid, g1, dd)
    dob_recv = lax.ppermute(dob_send, "c", SWAP)

    idrow = jnp.broadcast_to(block_row[None, :], (8, 2048))
    att_keep, att_send = k3(scal, qkv_keep, qkv_recv, dob_keep, dob_recv, idrow, idcol, cos_all, sin_all)
    att_recv = lax.ppermute(att_send, "c", SWAP)

    fold = fold_matrix()
    gb, df, low_out, low_in, small, gup1, gd2, gdd = k2m(
        dy_blocks, scal, hb, aid, inner, gdense, att_keep, att_recv, g2, ups, dd, b1, fold
    )
    small = lax.all_to_all(small.reshape(8, 128, 128), TP, 0, 0, tiled=True)
    out_part = k2o(scal, gb, att_keep, att_recv, low_out, g1, g2)
    out_part, small, df = together(out_part, small, df)
    small = jnp.sum(small.astype(F32), axis=0).astype(BF)
    small = lax.all_to_all(jnp.broadcast_to(small[None], (8, 128, 128)), TP, 0, 0, tiled=True)
    out_sum = lax.psum_scatter(out_part.reshape(1024, 2048), TP, scatter_dimension=0, tiled=True)
    near, owns, sides, gqkv = k2h(scal, df, att_keep, att_recv, low_in, inner, g1, g2)
    near, owns, sides, small = together(near, owns, sides, small)
    shares = scatter_sum(near, owns, sides)

    keep, send = k5(scal, small, aid, hb, fold.T, gup1, gd2, gqkv, gdd, dy_blocks)
    grads = (keep + lax.ppermute(send, "c", SWAP).astype(F32)).astype(BF)
    grads = lax.all_to_all(grads, WSH, 0, 0, tiled=True)
    grads = jnp.sum(grads.astype(F32), axis=0).astype(BF)
    grads = lax.all_to_all(jnp.broadcast_to(grads[None], (8, 80, 512)), TP, 0, 0, tiled=True)
    down_qkv, up_qkv, gdd, gud, gf1d, gf1u, gf2d, gf2u = kf(scal, grads, lax.ppermute(grads, "c", SWAP))

    source = x_own.astype(F32)
    outputs = (source + out_sum.astype(F32) + misc[2:3] + misc[3:4]).astype(BF)[None]
    *shares, outputs = together(*shares, outputs)
    grad_inputs = kn(x_own, output_cotangent[0], misc[0:1], *shares)[None]
    return (
        outputs,
        grad_inputs,
        down_qkv[None],
        up_qkv[None],
        gdd[None],
        gud[None],
        gf1d[None],
        gf1u[None],
        gf2d[None],
        gf2u[None],
    )


def solution(mesh):
    fine = Mesh(np.asarray(mesh.devices).reshape(2, 4, 2, 4, 2), ("xl", "z", "c", "y", "xh"))
    tokens = P(WSH, CTX, None)
    w1 = P(WSH)
    w2 = P(WSH, None)
    w3 = P(WSH, None, None)
    w4 = P(WSH, None, None, None)
    placed = (tokens, tokens, w2, P(WSH, CTX)) + (w1, w1, w2, w2, w2, w2, w1, w1, w1, w1, w2, w1, w2, w1)
    placed = placed + (w4, w4, w3, w3, w3, w3, w3, w3)
    return jax.shard_map(
        local,
        mesh=fine,
        in_specs=placed,
        out_specs=(tokens, tokens, w4, w4, w3, w3, w3, w3, w3, w3),
        check_vma=False,
    )
```

```python
import functools

import jax
import jax.numpy as jnp
import numpy as np
from jax import lax
from jax.experimental import pallas as pl
from jax.experimental.pallas import tpu as pltpu
from jax.sharding import Mesh, PartitionSpec as P

ADAPTERS = 8
RANK = 16
EPSILON = 1e-05
GELU_SCALE = 0.7978845608028654
NEGATIVE = -1e30
SCALE = 64 ** -0.5
BF = jnp.bfloat16
F32 = jnp.float32
WSH = ("y", "xh")
TP = ("xl", "z")
CTX = ("xl", "z", "c")
VMEM_LIMIT = 58 * 1024 * 1024


def nn(a, b):
    return lax.dot_general(a, b, (((1,), (0,)), ((), ())), preferred_element_type=F32)


def nt(a, b):
    return lax.dot_general(a, b, (((1,), (1,)), ((), ())), preferred_element_type=F32)


def tn(a, b):
    return lax.dot_general(a, b, (((0,), (0,)), ((), ())), preferred_element_type=F32)


def adapter_mask(aid, columns):
    col = lax.broadcasted_iota(jnp.int32, (aid.shape[0], columns), 1)
    return (lax.shift_right_logical(col, 4) & 7) == aid.astype(jnp.int32)


def turn(values, cosine, sine):
    width = values.shape[1]
    lane = lax.broadcasted_iota(jnp.int32, values.shape, 1) & 63
    partner = jnp.where(
        lane < 16, pltpu.roll(values, width - 16, 1), pltpu.roll(values, 16, 1)
    )
    return values * cosine + partner * sine


ANY = pl.BlockSpec(memory_space=pl.ANY)
SMEM = pl.BlockSpec(memory_space=pltpu.SMEM)
VM = pl.BlockSpec(memory_space=pltpu.VMEM)
PARAMS = pltpu.CompilerParams(vmem_limit_bytes=VMEM_LIMIT)
MAIN = 208
SECOND = 288
NEAR = 1024


def whole(shape):
    return pl.BlockSpec(shape, lambda t: (0,) * len(shape), pipeline_mode=pl.Buffered(1))


def start_all(pairs, sem):
    for source, target in pairs:
        pltpu.make_async_copy(source, target, sem).start()


def wait_all(target, sem):
    pltpu.make_async_copy(target, target, sem).wait()


def token_copies(blocks, target):
    own, side, above, below, up_more, down_more, far_side = blocks
    return [
        (own, target.at[0, 0], 0),
        (side, target.at[0, 1], 1),
        (above, target.at[1, 0], 2),
        (up_more.at[pl.ds(0, 128), :], target.at[1, 1], 3),
        (below, target.at[2, 0], 4),
        (down_more.at[pl.ds(0, 128), :], target.at[2, 1], 5),
        (up_more.at[pl.ds(128, 64), :], target.at[3, 0, pl.ds(0, 64)], 6),
        (down_more.at[pl.ds(128, 64), :], target.at[3, 0, pl.ds(64, 64)], 6),
        (far_side, target.at[3, 1], 7),
    ]


def start_tokens(blocks, target, sem, first, last):
    for source, part, i in token_copies(blocks, target):
        if first <= i < last:
            pltpu.make_async_copy(source, part, sem.at[i]).start()


def wait_tokens(target, sem, step):
    for i in range(2):
        part = target.at[step, i]
        pltpu.make_async_copy(part, part, sem.at[2 * step + i]).wait()


def pieces_qkv(g1, target):
    return [
        (
            g1.at[y, c, pl.ds(MAIN * xh, 128), pl.ds(0, 768)],
            target.at[pl.ds((2 * y + xh) * 256 + c * 128, 128), :],
        )
        for y in range(4)
        for xh in range(2)
        for c in range(2)
    ]


def pieces_downs(g1, target):
    return [
        (
            g1.at[:, c, pl.ds(MAIN * xh + 128 + 32 * i + 16 * b, 16), :],
            target.at[c, i, :, xh, :, pl.ds(1024 * b, 1024)],
        )
        for c in range(2)
        for i in range(2)
        for xh in range(2)
        for b in range(2)
    ]


def pieces_rank(g, base, stride, target, row):
    return [
        (
            g.at[y, c, pl.ds(stride * xh + base, 16), :],
            target.at[pl.ds(row + (2 * y + xh) * 16, 16), pl.ds(1024 * c, 1024)],
        )
        for y in range(4)
        for xh in range(2)
        for c in range(2)
    ]


def pieces_dense(g1, target, row):
    return [
        (
            g1.at[y, c, pl.ds(2 * MAIN + 32 * b, 32), :],
            target.at[pl.ds(row + 64 * y + 32 * c, 32), pl.ds(1024 * b, 1024)],
        )
        for y in range(4)
        for c in range(2)
        for b in range(2)
    ]


def pieces_w1(g2, target):
    return [
        (
            g2.at[y, c, pl.ds(SECOND * xh, 128), :],
            target.at[pl.ds((2 * y + xh) * 256 + c * 128, 128), :],
        )
        for y in range(4)
        for xh in range(2)
        for c in range(2)
    ]


def pieces_sixteen(g2, c, target, row):
    return [
        (
            g2.at[y, c, pl.ds(SECOND * xh + 128, 16), :],
            target.at[pl.ds(row + (2 * y + xh) * 16, 16), :],
        )
        for y in range(4)
        for xh in range(2)
    ]


def pieces_w2(g2, target):
    return [
        (
            g2.at[y, c, pl.ds(SECOND * xh + 144 + 64 * b, 64), :],
            target.at[pl.ds((2 * y + xh) * 128 + c * 64, 64), pl.ds(1024 * b, 1024)],
        )
        for y in range(4)
        for xh in range(2)
        for c in range(2)
        for b in range(2)
    ]


def block_diagonal(source, target):
    target[...] = jnp.zeros_like(target)
    for p in range(3):
        cols = slice(256 * p, 256 * p + 256)
        target[128 * p : 128 * p + 128, cols] = source[:, cols]


def k1_body(*refs):
    blocks, refs = refs[:7], refs[7:]
    (scal_ref, g1_ref, up_ref, misc_ref, bias_ref, cos_ref, sin_ref,
     hb_ref, inner_ref, keep_ref, send_ref, aid_ref, x_s, w_s, down_s, up_s, x_sem, w_sem) = refs
    step = pl.program_id(0)

    @pl.when(step == 0)
    def _():
        start_tokens(blocks, x_s, x_sem, 0, 2)
        start_all(pieces_downs(g1_ref, down_s), w_sem.at[0])
        start_all(pieces_qkv(g1_ref, w_s.at[:, pl.ds(0, 768)]), w_sem.at[1])
        start_tokens(blocks, x_s, x_sem, 2, 8)

    wait_tokens(x_s, x_sem, step)
    tile = x_s[step].reshape(256, 2176)
    x = tile[:, :2048].astype(F32)
    aid_ref[...] = tile[:, 2048:]
    aid = tile[:, 2048:2049].astype(F32)
    mean = jnp.mean(x, axis=1, keepdims=True)
    center = x - mean
    spread = jnp.mean(center * center, axis=1, keepdims=True)
    h = center * lax.rsqrt(spread + EPSILON) * misc_ref[0:1, :] + misc_ref[1:2, :]
    hb = h.astype(BF)
    hb_ref[...] = hb

    @pl.when(step == 0)
    def _():
        block_diagonal(up_ref, up_s)
        wait_all(down_s, w_sem.at[0])
        w_s[:, 768:] = down_s[...].reshape(512, 2048).T
        wait_all(w_s.at[:, pl.ds(0, 768)], w_sem.at[1])

    pre_all = nn(hb, w_s[...])
    inner = jnp.where(adapter_mask(aid, 512), pre_all[:, 768:], 0.0).astype(BF)
    inner_ref[...] = inner
    pre_all = pre_all[:, :768] + nn(inner[:, :384], up_s[...]) + bias_ref[...]
    first_core = scal_ref[8] == 0
    cosine = jnp.concatenate([cos_ref[...]] * 2, axis=1)
    sine = jnp.concatenate([sin_ref[...]] * 2, axis=1)
    for p in range(3):
        cols = slice(256 * p, 256 * p + 256)
        pre = pre_all[:, cols]
        if p < 2:
            pre = turn(pre, cosine, sine)
        low = pre.astype(BF)
        keep_ref[p] = jnp.where(first_core, low[:, :128], low[:, 128:])
        send_ref[p] = jnp.where(first_core, low[:, 128:], low[:, :128])


def k1(blocks, scal, g1, ups, misc, bias, cosine, sine):
    rows = 256
    return pl.pallas_call(
        k1_body,
        grid=(4,),
        in_specs=[ANY] * 7
        + [
            SMEM,
            ANY,
            whole((128, 768)),
            whole((2, 2048)),
            whole((1, 768)),
            pl.BlockSpec((rows, 128), lambda t: (t, 0)),
            pl.BlockSpec((rows, 128), lambda t: (t, 0)),
        ],
        out_specs=[
            pl.BlockSpec((rows, 2048), lambda t: (t, 0)),
            pl.BlockSpec((rows, 512), lambda t: (t, 0)),
            pl.BlockSpec((3, rows, 128), lambda t: (0, t, 0)),
            pl.BlockSpec((3, rows, 128), lambda t: (0, t, 0)),
            pl.BlockSpec((rows, 128), lambda t: (t, 0)),
        ],
        out_shape=[
            jax.ShapeDtypeStruct((1024, 2048), BF),
            jax.ShapeDtypeStruct((1024, 512), BF),
            jax.ShapeDtypeStruct((3, 1024, 128), BF),
            jax.ShapeDtypeStruct((3, 1024, 128), BF),
            jax.ShapeDtypeStruct((1024, 128), BF),
        ],
        scratch_shapes=[
            pltpu.VMEM((4, 2, 128, 2176), BF),
            pltpu.VMEM((2048, 1280), BF),
            pltpu.VMEM((2, 2, 4, 2, 16, 2048), BF),
            pltpu.VMEM((384, 768), BF),
            pltpu.SemaphoreType.DMA((8,)),
            pltpu.SemaphoreType.DMA((2,)),
        ],
        compiler_params=PARAMS,
        cost_estimate=pl.CostEstimate(flops=6_000_000_000, bytes_accessed=20_000_000, transcendentals=0),
        name="norm_qkv",
    )(*blocks, scal, g1, ups, misc, bias, cosine, sine)


def k1b_body(*refs):
    blocks, refs = refs[:7], refs[7:]
    scal_ref, aid_ref, g1_ref, dd_ref, keep_ref, send_ref, ginner_ref, dy_s, w_s, dy_sem, w_sem = refs
    start_all(pieces_dense(g1_ref, w_s, 0) + pieces_rank(g1_ref, 192, MAIN, w_s, 256), w_sem)
    start_tokens(blocks, dy_s, dy_sem, 0, 8)
    wait_all(w_s, w_sem)
    for step in range(4):
        wait_tokens(dy_s, dy_sem, step)
    first_core = scal_ref[8] == 0
    both = nt(dy_s[...].reshape(1024, 2048), w_s[...])
    aid = aid_ref[:, 0:1].astype(F32)
    ginner = jnp.where(adapter_mask(aid, 128), both[:, 256:], 0.0).astype(BF)
    ginner_ref[...] = ginner
    dob = (both[:, :256] + nn(ginner, dd_ref[...])).astype(BF)
    keep_ref[...] = jnp.where(first_core, dob[:, :128], dob[:, 128:])
    send_ref[...] = jnp.where(first_core, dob[:, 128:], dob[:, :128])


def k1b(blocks, scal, aid, g1, dd):
    return pl.pallas_call(
        k1b_body,
        in_specs=[ANY] * 7 + [SMEM, VM, ANY, VM],
        out_specs=[VM, VM, VM],
        out_shape=[jax.ShapeDtypeStruct((1024, 128), BF)] * 3,
        scratch_shapes=[
            pltpu.VMEM((4, 2, 128, 2048), BF),
            pltpu.VMEM((384, 2048), BF),
            pltpu.SemaphoreType.DMA((8,)),
            pltpu.SemaphoreType.DMA,
        ],
        compiler_params=PARAMS,
        cost_estimate=pl.CostEstimate(flops=2_000_000_000, bytes_accessed=8_000_000, transcendentals=0),
        name="attention_output_grad",
    )(*blocks, scal, aid, g1, dd)


def k3_body(
    scal_ref, qkv_keep, qkv_recv, dob_keep, dob_recv, idrow_ref, idcol_ref, cos_ref, sin_ref,
    keep_out, send_out, x_s, out_s, kt_s, vt_s, dk_s, dv_s, sem, sem_out,
):
    core = scal_ref[8]
    copies = []
    for b in range(8):
        rows = pl.ds(128 * b, 128)
        spot = scal_ref[b]
        for side, (qkv, dob) in enumerate(((qkv_keep, dob_keep), (qkv_recv, dob_recv))):
            parity = core if side == 0 else 1 - core
            copies.append((qkv.at[:, rows, :], x_s.at[pl.ds(0, 3), spot, parity]))
            copies.append((dob.at[rows, :], x_s.at[3, spot, parity]))
    start_all(copies, sem)
    dk_s[...] = jnp.zeros_like(dk_s)
    dv_s[...] = jnp.zeros_like(dv_s)
    wait_all(x_s, sem)
    kt_s[...] = x_s[1].reshape(2048, 128).T
    vt_s[...] = x_s[2].reshape(2048, 128).T
    tile = 256
    lane = lax.broadcasted_iota(jnp.int32, (tile, 128), 1)

    def span(i, start, stop):
        return x_s[i, start // 256 : stop // 256].reshape(stop - start, 128)

    for t in range(8):
        start, stop = tile * t, tile * t + tile
        length = min(stop + tile, 2048)
        q = span(0, start, stop)
        dob = span(3, start, stop)
        zero = jnp.zeros_like(q)
        q = q * jnp.asarray(SCALE, BF)
        q2 = jnp.concatenate([jnp.where(lane < 64, q, zero), jnp.where(lane < 64, zero, q)], axis=0)
        d2 = jnp.concatenate([jnp.where(lane < 64, dob, zero), jnp.where(lane < 64, zero, dob)], axis=0)
        query_ids = idrow_ref[0:1, start:stop]
        query_ids = jnp.concatenate([query_ids, query_ids], axis=1)
        allowed = idcol_ref[start:length, 0:1] <= query_ids
        s = jnp.where(allowed, nt(span(1, start, length), q2), NEGATIVE)
        largest = jnp.max(s, axis=0, keepdims=True)
        if start:
            s_head = nt(span(1, 0, start), q2)
            largest = jnp.maximum(largest, jnp.max(s_head, axis=0, keepdims=True))
            s = jnp.concatenate([s_head, s], axis=0)
        e = jnp.exp(s - largest)
        recip = 1.0 / jnp.sum(e, axis=0, keepdims=True)
        p = e * recip
        pb = p.astype(BF)
        ot = nn(vt_s[:, :length], pb)
        dp = nt(span(2, 0, length), d2)
        o_parts = [ot[:64, :256], ot[64:, 256:]]
        dobt = dob.astype(F32).T
        delta = jnp.concatenate(
            [
                jnp.sum(o_parts[0] * dobt[:64], axis=0, keepdims=True),
                jnp.sum(o_parts[1] * dobt[64:], axis=0, keepdims=True),
            ],
            axis=1,
        )
        ds = (p * (dp - delta)).astype(BF)
        dk_s[:length] += nn(ds, q2)
        dv_s[:length] += nn(pb, d2)
        dqt = nn(kt_s[:, :length], ds)
        dq_parts = [dqt[:64, :256], dqt[64:, 256:]]
        o = jnp.concatenate(o_parts, axis=0).T
        dq = jnp.concatenate(dq_parts, axis=0).T * SCALE
        rows = slice(start, stop)
        out_s[0, t] = o.astype(BF).reshape(2, 128, 128)
        out_s[1, t] = turn(dq, cos_ref[rows], -sin_ref[rows]).astype(BF).reshape(2, 128, 128)
    out_s[2] = turn(dk_s[...], cos_ref[...], -sin_ref[...]).astype(BF).reshape(8, 2, 128, 128)
    out_s[3] = dv_s[...].astype(BF).reshape(8, 2, 128, 128)
    copies = []
    for b in range(8):
        rows = pl.ds(128 * b, 128)
        spot = scal_ref[b]
        copies.append((out_s.at[:, spot, core], keep_out.at[:, rows, :]))
        copies.append((out_s.at[:, spot, 1 - core], send_out.at[:, rows, :]))
    start_all(copies, sem_out)
    wait_all(out_s, sem_out)


def k3(scal, qkv_keep, qkv_recv, dob_keep, dob_recv, idrow, idcol, cosine, sine):
    vm = pl.BlockSpec(memory_space=pltpu.VMEM)
    return pl.pallas_call(
        k3_body,
        in_specs=[SMEM] + [ANY] * 4 + [vm] * 4,
        out_specs=[ANY, ANY],
        out_shape=[jax.ShapeDtypeStruct((4, 1024, 128), BF)] * 2,
        scratch_shapes=[
            pltpu.VMEM((4, 8, 2, 128, 128), BF),
            pltpu.VMEM((4, 8, 2, 128, 128), BF),
            pltpu.VMEM((128, 2048), BF),
            pltpu.VMEM((128, 2048), BF),
            pltpu.VMEM((2048, 128), F32),
            pltpu.VMEM((2048, 128), F32),
            pltpu.SemaphoreType.DMA,
            pltpu.SemaphoreType.DMA,
        ],
        compiler_params=PARAMS,
        cost_estimate=pl.CostEstimate(flops=15_000_000_000, bytes_accessed=8_000_000, transcendentals=5_000_000),
        name="attention",
    )(scal, qkv_keep, qkv_recv, dob_keep, dob_recv, idrow, idcol, cosine, sine)


def heads_of(keep_ref, recv_ref, i, first_core):
    a, b = keep_ref[i], recv_ref[i]
    return jnp.concatenate([jnp.where(first_core, a, b), jnp.where(first_core, b, a)], axis=1)


def tile_spec(width, rows=256):
    return pl.BlockSpec((rows, width), lambda t, s: (t, 0))


def const_spec(shape):
    return pl.BlockSpec(shape, lambda t, s: (0,) * len(shape), pipeline_mode=pl.Buffered(1))


def placed_spec(width):
    return pl.BlockSpec((2, 1, 128, width), lambda t, s: (0, s[12 + t], 0, 0))


def place(ref, xl, value):
    ref[xl, 0] = value[:128]
    ref[1 - xl, 0] = value[128:]


def accumulate(step, pairs):
    @pl.when(step == 0)
    def _():
        for ref, value in pairs:
            ref[...] = value

    @pl.when(step > 0)
    def _():
        for ref, value in pairs:
            ref[...] += value


def k2m_body(scal_ref, *refs):
    blocks, refs = refs[:7], refs[7:]
    (hb_ref, aid_ref, inner_ref, gdense_ref, keep_ref, recv_ref, g2_ref, up_ref, dd_ref, b1_ref, fold_ref,
     gb_ref, df_ref, low_out_ref, low_in_ref, small_ref, gup1_ref, gd2_ref, gdd_ref,
     dy_s, w1_s, w2_s, d2_s, up_s, dy_sem, sems) = refs
    step = pl.program_id(0)

    @pl.when(step == 0)
    def _():
        start_all(pieces_w1(g2_ref, w1_s) + pieces_sixteen(g2_ref, 0, w1_s, 2048), sems.at[0])
        start_all(pieces_sixteen(g2_ref, 1, d2_s, 0), sems.at[1])
        start_tokens(blocks, dy_s, dy_sem, 0, 2)
        start_all(pieces_w2(g2_ref, w2_s) + pieces_rank(g2_ref, 272, SECOND, w2_s, 1024), sems.at[2])
        start_tokens(blocks, dy_s, dy_sem, 2, 8)
        block_diagonal(up_ref, up_s)
        wait_all(w1_s, sems.at[0])

    aid = aid_ref[:, 0:1].astype(F32)
    first_core = scal_ref[8] == 0
    f = nn(jnp.concatenate([hb_ref[...], inner_ref[...]], axis=1), w1_s[...]) + b1_ref[...]

    @pl.when(step == 0)
    def _():
        wait_all(w2_s, sems.at[2])
        wait_all(d2_s, sems.at[1])

    wait_tokens(dy_s, dy_sem, step)
    wide = nt(dy_s[step].reshape(256, 2048), w2_s[...])
    square = f * f
    th = jnp.tanh(GELU_SCALE * f * (1.0 + 0.044715 * square))
    half = 0.5 * (1.0 + th)
    gb = (f * half).astype(BF)
    gb_ref[...] = gb
    slope = half + (0.5 * GELU_SCALE) * f * (1.0 - th * th) * (1.0 + 3 * 0.044715 * square)
    ginner2 = jnp.where(adapter_mask(aid, 128), wide[:, 1024:], 0.0).astype(BF)
    ob = heads_of(keep_ref, recv_ref, 0, first_core)
    dpre = jnp.concatenate([heads_of(keep_ref, recv_ref, p, first_core) for p in (1, 2, 3)], axis=1)
    inner2 = nt(gb, d2_s[...])
    innerd = nt(ob, dd_ref[...])
    ginner = nt(dpre, up_s[...])
    df = ((wide[:, :1024] + nn(ginner2, d2_s[...])) * slope).astype(BF)
    df_ref[...] = df
    ginner1 = nt(df, w1_s[2048:])
    low = jnp.concatenate([ginner, ginner1, innerd, inner2], axis=1)
    low = jnp.where(adapter_mask(aid, 768), low, 0.0).astype(BF)
    low_in_ref[...] = low[:, :512]
    low_out_ref[...] = low[:, 512:]
    place(small_ref, scal_ref[10], nn(low, fold_ref[...]).astype(BF))
    accumulate(
        step,
        [
            (gup1_ref, tn(inner_ref[...], df)),
            (gd2_ref, tn(ginner2, gb)),
            (gdd_ref, tn(gdense_ref[...], ob)),
        ],
    )


def att_spec(first, count):
    return pl.BlockSpec((count, 256, 128), lambda t, s: (first, t, 0))


def k2m(blocks, scal, hb, aid, inner, gdense, keep, recv, g2, ups, dd, b1, fold):
    return pl.pallas_call(
        k2m_body,
        grid_spec=pltpu.PrefetchScalarGridSpec(
            num_scalar_prefetch=1,
            grid=(4,),
            in_specs=[ANY] * 7
            + [
                tile_spec(2048),
                tile_spec(128),
                pl.BlockSpec((256, 128), lambda t, s: (t, 3)),
                tile_spec(128),
                att_spec(0, 4),
                att_spec(0, 4),
                ANY,
                const_spec((128, 768)),
                const_spec((128, 256)),
                const_spec((1, 1024)),
                const_spec((768, 128)),
            ],
            out_specs=[
                tile_spec(1024),
                tile_spec(1024),
                tile_spec(256),
                tile_spec(512),
                placed_spec(128),
                const_spec((128, 1024)),
                const_spec((128, 1024)),
                const_spec((128, 256)),
            ],
            scratch_shapes=[
                pltpu.VMEM((4, 2, 128, 2048), BF),
                pltpu.VMEM((2176, 1024), BF),
                pltpu.VMEM((1152, 2048), BF),
                pltpu.VMEM((128, 1024), BF),
                pltpu.VMEM((384, 768), BF),
                pltpu.SemaphoreType.DMA((8,)),
                pltpu.SemaphoreType.DMA((3,)),
            ],
        ),
        out_shape=[
            jax.ShapeDtypeStruct((1024, 1024), BF),
            jax.ShapeDtypeStruct((1024, 1024), BF),
            jax.ShapeDtypeStruct((1024, 256), BF),
            jax.ShapeDtypeStruct((1024, 512), BF),
            jax.ShapeDtypeStruct((2, 4, 128, 128), BF),
            jax.ShapeDtypeStruct((128, 1024), F32),
            jax.ShapeDtypeStruct((128, 1024), F32),
            jax.ShapeDtypeStruct((128, 256), F32),
        ],
        compiler_params=PARAMS,
        cost_estimate=pl.CostEstimate(flops=14_000_000_000, bytes_accessed=30_000_000, transcendentals=1_000_000),
        name="feed_forward",
    )(scal, *blocks, hb, aid, inner, gdense, keep, recv, g2, ups, dd, b1, fold)


def k2o_body(scal_ref, gb_ref, keep_ref, recv_ref, low_ref, g1_ref, g2_ref, out_ref, w_s, sem):
    step = pl.program_id(0)

    @pl.when(step == 0)
    def _():
        start_all(
            pieces_w2(g2_ref, w_s)
            + pieces_dense(g1_ref, w_s, 1024)
            + pieces_rank(g1_ref, 192, MAIN, w_s, 1280)
            + pieces_rank(g2_ref, 272, SECOND, w_s, 1408),
            sem,
        )
        wait_all(w_s, sem)

    ob = heads_of(keep_ref, recv_ref, 0, scal_ref[8] == 0)
    out = nn(jnp.concatenate([gb_ref[...], ob, low_ref[...]], axis=1), w_s[...]).astype(BF)
    place(out_ref, scal_ref[10], out)


def k2o(scal, gb, keep, recv, low_out, g1, g2):
    return pl.pallas_call(
        k2o_body,
        grid_spec=pltpu.PrefetchScalarGridSpec(
            num_scalar_prefetch=1,
            grid=(4,),
            in_specs=[tile_spec(1024), att_spec(0, 1), att_spec(0, 1), tile_spec(256), ANY, ANY],
            out_specs=[placed_spec(2048)],
            scratch_shapes=[pltpu.VMEM((1536, 2048), BF), pltpu.SemaphoreType.DMA],
        ),
        out_shape=[jax.ShapeDtypeStruct((2, 4, 128, 2048), BF)],
        compiler_params=PARAMS,
        cost_estimate=pl.CostEstimate(flops=7_000_000_000, bytes_accessed=14_000_000, transcendentals=0),
        name="out_rows",
    )(scal, gb, keep, recv, low_out, g1, g2)[0]


def k2h_body(
    scal_ref, df_ref, keep_ref, recv_ref, low_ref, inner_ref, g1_ref, g2_ref,
    near_ref, owns_ref, sides_ref, gqkv_ref, w_s, down_s, sems,
):
    step = pl.program_id(0)

    @pl.when(step == 0)
    def _():
        start_all(
            pieces_w1(g2_ref, w_s.at[:, pl.ds(0, 1024)]) + pieces_qkv(g1_ref, w_s.at[:, pl.ds(1024, 768)]), sems.at[0]
        )
        start_all(pieces_downs(g1_ref, down_s), sems.at[1])
        wait_all(w_s, sems.at[0])
        wait_all(down_s, sems.at[1])

    first_core = scal_ref[8] == 0
    dpre = [heads_of(keep_ref, recv_ref, p, first_core) for p in (1, 2, 3)]
    dh = nt(jnp.concatenate([df_ref[...]] + dpre, axis=1), w_s[...])
    dh = (dh + nn(low_ref[...], down_s[...].reshape(512, 2048))).astype(BF)
    near_ref[0] = dh[:128, :NEAR]
    near_ref[1] = dh[128:, :NEAR]
    owns_ref[0] = dh[:128, NEAR:]
    sides_ref[0] = dh[128:, NEAR:]
    gqkv = [tn(inner_ref[:, 128 * p : 128 * p + 128], dpre[p]) for p in range(3)]
    accumulate(step, [(gqkv_ref, jnp.concatenate(gqkv, axis=1))])


def k2h(scal, df, keep, recv, low_in, inner, g1, g2):
    return pl.pallas_call(
        k2h_body,
        grid_spec=pltpu.PrefetchScalarGridSpec(
            num_scalar_prefetch=1,
            grid=(4,),
            in_specs=[tile_spec(1024), att_spec(0, 4), att_spec(0, 4), tile_spec(512), tile_spec(512), ANY, ANY],
            out_specs=[
                pl.BlockSpec((2, 128, NEAR), lambda t, s: (t, 0, 0)),
                pl.BlockSpec((1, 128, 2048 - NEAR), lambda t, s: (t, 0, 0)),
                pl.BlockSpec((1, 128, 2048 - NEAR), lambda t, s: (t, 0, 0)),
                const_spec((128, 768)),
            ],
            scratch_shapes=[
                pltpu.VMEM((2048, 1792), BF),
                pltpu.VMEM((2, 2, 4, 2, 16, 2048), BF),
                pltpu.SemaphoreType.DMA((2,)),
            ],
        ),
        out_shape=[
            jax.ShapeDtypeStruct((8, 128, NEAR), BF),
            jax.ShapeDtypeStruct((4, 128, 2048 - NEAR), BF),
            jax.ShapeDtypeStruct((4, 128, 2048 - NEAR), BF),
            jax.ShapeDtypeStruct((128, 768), F32),
        ],
        compiler_params=PARAMS,
        cost_estimate=pl.CostEstimate(flops=10_000_000_000, bytes_accessed=18_000_000, transcendentals=0),
        name="hidden_grad",
    )(scal, df, keep, recv, low_in, inner, g1, g2)


def k5_body(scal_ref, small_ref, aid_ref, hb_ref, spread_ref, gup1_ref, gd2_ref, gqkv_ref, gdd_ref, *refs):
    blocks, refs = refs[:7], refs[7:]
    keep_ref, send_ref, dy_s, sem = refs
    column = pl.multiple_of(256 * scal_ref[9], 256)
    start_all(
        [(source.at[:, pl.ds(column, 256)], part) for source, part, _ in token_copies(blocks, dy_s)], sem
    )
    first_core = scal_ref[8] == 0

    def store(section, left, right):
        kept = jnp.where(first_core, left, right)
        sent = jnp.where(first_core, right, left)
        keep_ref[:, 16 * section : 16 * section + 16] = kept.reshape(8, 16, 512)
        send_ref[:, 16 * section : 16 * section + 16] = sent.astype(BF).reshape(8, 16, 512)

    small = jnp.concatenate([small_ref[scal_ref[b]] for b in range(8)], axis=0)
    aid = aid_ref[:, 0:1].astype(F32)
    wide = jnp.where(adapter_mask(aid, 768), nn(small, spread_ref[...]), 0.0).astype(BF)
    down = tn(wide[:, :512], hb_ref[...])
    store(
        0,
        jnp.concatenate([down[:128], down[128:256]], axis=1),
        jnp.concatenate([down[256:384], down[384:]], axis=1),
    )
    store(1, gqkv_ref[:, :512], jnp.concatenate([gqkv_ref[:, 512:], gdd_ref[...]], axis=1))
    store(2, gup1_ref[:, :512], gup1_ref[:, 512:])
    store(3, gd2_ref[:, :512], gd2_ref[:, 512:])
    wait_all(dy_s, sem)
    up = tn(wide[:, 512:], dy_s[...].reshape(1024, 256))
    left = jnp.concatenate([up[:128], up[128:]], axis=1)
    store(4, left, jnp.zeros_like(left))


def k5(scal, small, aid, hb, spread, gup1, gd2, gqkv, gdd, blocks):
    def const(shape):
        return pl.BlockSpec(shape, lambda t, s: (0,) * len(shape))

    return pl.pallas_call(
        k5_body,
        grid_spec=pltpu.PrefetchScalarGridSpec(
            num_scalar_prefetch=1,
            grid=(1,),
            in_specs=[
                const((8, 128, 128)),
                const((1024, 128)),
                pl.BlockSpec((1024, 256), lambda t, s: (0, s[9])),
                const((128, 768)),
                const((128, 1024)),
                const((128, 1024)),
                const((128, 768)),
                const((128, 256)),
            ]
            + [ANY] * 7,
            out_specs=[const((8, 80, 512)), const((8, 80, 512))],
            scratch_shapes=[pltpu.VMEM((4, 2, 128, 256), BF), pltpu.SemaphoreType.DMA],
        ),
        out_shape=[jax.ShapeDtypeStruct((8, 80, 512), F32), jax.ShapeDtypeStruct((8, 80, 512), BF)],
        compiler_params=PARAMS,
        cost_estimate=pl.CostEstimate(flops=1_500_000_000, bytes_accessed=6_000_000, transcendentals=0),
        name="adapter_grads",
    )(scal, small, aid, hb, spread, gup1, gd2, gqkv, gdd, *blocks)


def kf_body(scal_ref, mine_ref, theirs_ref, down_ref, up_ref, dd_ref, ud_ref, f1d_ref, f1u_ref, f2d_ref, f2u_ref):
    lane = lax.broadcasted_iota(jnp.int32, (16, 128), 1)

    core = scal_ref[8]

    def part(j, half, section, start, width):
        rows, cols = slice(16 * section, 16 * section + 16), slice(start, start + width)
        return jnp.where(core == half, mine_ref[j, rows, cols], theirs_ref[j, rows, cols]).astype(F32)

    for j in range(8):
        block = slice(256 * j, 256 * j + 256)
        down_ref[0, :, block] = part(j, 0, 0, 0, 256)
        down_ref[1, :, block] = part(j, 0, 0, 256, 256)
        down_ref[2, :, block] = part(j, 1, 0, 0, 256)
        f1d_ref[:, block] = part(j, 1, 0, 256, 256)
        ud_ref[:, block] = part(j, 0, 4, 0, 256)
        f2u_ref[:, block] = part(j, 0, 4, 256, 256)
        for w in range(8):
            spot = slice(1024 * w + 128 * j, 1024 * w + 128 * j + 128)
            f1u_ref[:, spot] = part(j, w // 4, 2, 128 * (w % 4), 128)
            f2d_ref[:, spot] = part(j, w // 4, 3, 128 * (w % 4), 128)
    for i in range(4):
        for x in range(2):
            for y in range(4):
                for h in range(2):
                    start = 256 * (i % 2) + 128 * (y // 2)
                    a = part(4 * x + 2 * h, i // 2, 1, start, 128)
                    b = part(4 * x + 2 * h + 1, i // 2, 1, start, 128)
                    if y % 2:
                        a = pltpu.roll(a, 64, 1)
                    else:
                        b = pltpu.roll(b, 64, 1)
                    value = jnp.where(lane < 64, a, b)
                    spot = slice(256 * (2 * y + x) + 128 * h, 256 * (2 * y + x) + 128 * h + 128)
                    if i < 3:
                        up_ref[i, :, spot] = value
                    else:
                        dd_ref[:, spot] = value


def kf(scal, mine, theirs):
    return pl.pallas_call(
        kf_body,
        in_specs=[SMEM, VM, VM],
        out_specs=[VM] * 8,
        out_shape=[
            jax.ShapeDtypeStruct((3, 16, 2048), F32),
            jax.ShapeDtypeStruct((3, 16, 2048), F32),
            jax.ShapeDtypeStruct((16, 2048), F32),
            jax.ShapeDtypeStruct((16, 2048), F32),
            jax.ShapeDtypeStruct((16, 2048), F32),
            jax.ShapeDtypeStruct((16, 8192), F32),
            jax.ShapeDtypeStruct((16, 8192), F32),
            jax.ShapeDtypeStruct((16, 2048), F32),
        ],
        compiler_params=PARAMS,
        name="finish",
    )(scal, mine, theirs)


def kn_body(
    x_ref, dy_ref, gain_ref, own_ref, up_ref, down_ref, far_ref, side_ref, t_ref, up2_ref, down2_ref, far2_ref, out_ref
):
    def total(*parts):
        return sum(p.astype(F32) for p in parts)

    first = total(own_ref[0], up_ref[0], down_ref[0], far_ref[0], side_ref[...])
    second = total(t_ref[0], up2_ref[...], down2_ref[...], far2_ref[...])
    dh = jnp.concatenate([first, second], axis=1)
    x = x_ref[...].astype(F32)
    center = x - jnp.mean(x, axis=1, keepdims=True)
    inv = lax.rsqrt(jnp.mean(center * center, axis=1, keepdims=True) + EPSILON)
    hn = center * inv
    e = dh * gain_ref[...]
    dx = (e - jnp.mean(e, axis=1, keepdims=True) - hn * jnp.mean(e * hn, axis=1, keepdims=True)) * inv
    out_ref[...] = (dy_ref[...].astype(F32) + dx).astype(BF)


def kn(*args):
    def flat(width, rows=128):
        return pl.BlockSpec((rows, width), lambda i: (0, 0))

    def first(width):
        return pl.BlockSpec((1, 128, width), lambda i: (0, 0, 0))

    rest = 2048 - NEAR
    return pl.pallas_call(
        kn_body,
        grid=(1,),
        in_specs=[flat(2048), flat(2048), flat(2048, 1)]
        + [first(NEAR)] * 4
        + [flat(NEAR), first(rest), flat(rest), flat(rest), flat(rest)],
        out_specs=flat(2048),
        out_shape=jax.ShapeDtypeStruct((128, 2048), BF),
        compiler_params=PARAMS,
        name="norm_grad",
    )(*args)


def pack1_body(
    scal_ref, wq, wk, wv, wd, ad_ref, fd_ref, au_ref, dd_ref, du_ref, misc_ref, b1_ref,
    own_ref, other_ref, w_s, d_s, sem, d_sem,
):
    c, z = scal_ref[8], scal_ref[11]
    start_all([(w.at[pl.ds(128 * c, 128), :], w_s.at[i]) for i, w in enumerate((wq, wk, wv))], sem)
    start_all([(wd.at[pl.ds(64 * z + 32 * c, 32), :], d_s)], d_sem)
    first_core = c == 0
    odd = lax.rem(z, 2) == 1
    targets = ((own_ref, scal_ref[10]), (other_ref, 1 - scal_ref[10]))

    def head_pair(read, rows, i, xl):
        lane = lax.broadcasted_iota(jnp.int32, (rows, 128), 1)
        parts = []
        for k in range(2):
            start = (2 * (i + k) + xl) * 256 + (z // 2) * 128
            v = read(pl.ds(pl.multiple_of(start, 128), 128)).astype(F32)
            turned = pltpu.roll(v, 64, 1)
            parts.append(jnp.where(odd, turned, v) if k == 0 else jnp.where(odd, v, turned))
        return jnp.where(lane < 64, parts[0], parts[1]).astype(BF)

    half = pl.ds(pl.multiple_of((z // 2) * 128, 128), 128)
    row = lax.broadcasted_iota(jnp.int32, (16, 128), 0)
    lane = lax.broadcasted_iota(jnp.int32, (16, 128), 1)

    def biases(xl):
        plain = misc_ref[:, :128].astype(F32), misc_ref[:, 128:256].astype(F32)
        mine = misc_ref[:, half].astype(F32)
        turned = pltpu.roll(mine, 64, 1)
        low = jnp.where(odd, turned, mine)
        high = jnp.where(odd, mine, turned)
        query_key = jnp.where(lane[:1] < 64, low[4:5], high[5:6])
        value = jnp.where(lane[:1] < 64, low[6:7], 0.0)
        hidden = jnp.where(row[:8] == xl * 4 + z, b1_ref[...].astype(F32), 0.0)
        hidden = jnp.sum(hidden, axis=0, keepdims=True)
        left = jnp.where(row < 4, plain[0], jnp.where(row == 4, query_key, hidden))
        right = jnp.where(row < 4, plain[1], value)
        return left.astype(BF), right.astype(BF)

    a = jnp.where(first_core, ad_ref[0], ad_ref[2])
    b = jnp.where(first_core, ad_ref[1], fd_ref[...])
    du = jnp.where(first_core, du_ref[:, :1024], du_ref[:, 1024:])
    for out_ref, xl in targets:
        rows_of = biases(xl)
        for p in range(4):
            for i in (0, 2):
                read = (lambda s, p=p: au_ref[p, :, s]) if p < 3 else (lambda s: dd_ref[:, s])
                value = head_pair(read, 16, i, xl)
                rows = slice(16 * p, 16 * p + 16)
                if p == 0:
                    value = jnp.where(first_core, value, rows_of[i // 2])
                out_ref[rows, 768 + 64 * i : 768 + 64 * i + 128] = value
        out_ref[64:128, 768:] = jnp.zeros((64, 256), BF)
        out_ref[128:144] = a[:, :1024]
        out_ref[144:160] = a[:, 1024:]
        out_ref[160:176] = b[:, :1024]
        out_ref[176:192] = b[:, 1024:]
        out_ref[192:208] = du
    wait_all(d_s, d_sem)
    for out_ref, _ in targets:
        out_ref[208:240] = d_s[:, :1024]
        out_ref[240:272] = d_s[:, 1024:]
    wait_all(w_s, sem)
    for p in range(3):
        for i in (0, 2):
            start = 256 * p + 64 * i
            for out_ref, xl in targets:
                out_ref[:128, start : start + 128] = head_pair(lambda s, p=p: w_s[p, :, s], 128, i, xl)


def pack1(scal, wq, wk, wv, wd, ad, fd, au, dd, du, misc, b1):
    return pl.pallas_call(
        pack1_body,
        in_specs=[SMEM] + [ANY] * 4 + [VM] * 7,
        out_specs=[VM, VM],
        out_shape=[jax.ShapeDtypeStruct((272, 1024), BF)] * 2,
        scratch_shapes=[
            pltpu.VMEM((3, 128, 2048), BF),
            pltpu.VMEM((32, 2048), BF),
            pltpu.SemaphoreType.DMA,
            pltpu.SemaphoreType.DMA,
        ],
        compiler_params=PARAMS,
        cost_estimate=pl.CostEstimate(flops=1_000_000, bytes_accessed=4_000_000, transcendentals=0),
        name="pack_qkv",
    )(scal, wq, wk, wv, wd, ad, fd, au, dd, du, misc, b1)


def pack2_body(scal_ref, w1, w2, up_ref, down_ref, up2_ref, own_ref, other_ref, w1_s, w2_s, sem, sem2):
    c, z = scal_ref[8], scal_ref[11]
    places = [scal_ref[10] * 4 + z, (1 - scal_ref[10]) * 4 + z]
    start_all([(w1.at[pl.ds(128 * c, 128), :], w1_s)], sem)
    start_all([(w2.at[pl.ds(128 * places[i] + 64 * c, 64), :], w2_s.at[i]) for i in range(2)], sem2)
    first_core = c == 0
    up2 = jnp.where(first_core, up2_ref[:, :1024], up2_ref[:, 1024:])

    def column(w, i):
        return pl.ds(pl.multiple_of(1024 * w + 128 * places[i], 128), 128)

    for i, out_ref in enumerate((own_ref, other_ref)):
        out_ref[272:288] = up2
        for w in range(8):
            out_ref[128:144, 128 * w : 128 * w + 128] = jnp.where(
                first_core, up_ref[:, column(w, i)], down_ref[:, column(w, i)]
            )
    wait_all(w2_s, sem2)
    for i, out_ref in enumerate((own_ref, other_ref)):
        out_ref[144:208] = w2_s[i, :, :1024]
        out_ref[208:272] = w2_s[i, :, 1024:]
    wait_all(w1_s, sem)
    for i, out_ref in enumerate((own_ref, other_ref)):
        for w in range(8):
            out_ref[:128, 128 * w : 128 * w + 128] = w1_s[:, column(w, i)]


def pack2(scal, w1, w2, up, down, up2):
    return pl.pallas_call(
        pack2_body,
        in_specs=[SMEM, ANY, ANY, VM, VM, VM],
        out_specs=[VM, VM],
        out_shape=[jax.ShapeDtypeStruct((288, 1024), BF)] * 2,
        scratch_shapes=[
            pltpu.VMEM((128, 8192), BF),
            pltpu.VMEM((2, 64, 2048), BF),
            pltpu.SemaphoreType.DMA,
            pltpu.SemaphoreType.DMA,
        ],
        compiler_params=PARAMS,
        cost_estimate=pl.CostEstimate(flops=1_000_000, bytes_accessed=5_000_000, transcendentals=0),
        name="pack_hidden",
    )(scal, w1, w2, up, down, up2)


def rotary_tables(positions):
    lane = np.arange(128) % 64
    rate = np.where(lane < 32, 10000.0 ** (-2.0 * (lane % 16) / 32.0), 0.0).astype(np.float32)
    sign = np.where(lane < 16, -1.0, 1.0).astype(np.float32)
    angles = positions.astype(F32)[:, None] * jnp.asarray(rate)[None, :]
    return jnp.cos(angles), jnp.sin(angles) * jnp.asarray(sign)[None, :]


def fold_matrix():
    row = np.arange(768)
    target = (row // 128) * 16 + row % 16
    return jnp.asarray((target[:, None] == np.arange(128)[None, :]).astype(np.float32)).astype(BF)


def halves(a):
    m = a.shape[1] // 2
    return jnp.concatenate([a[:, :m], a[:, m:]], axis=0)


SWAP = [(0, 1), (1, 0)]
FLIP = [(i, 3 - i) for i in range(4)]
UP = [(i, (i + 1) % 4) for i in range(4)]
DOWN = [(i, (i + 3) % 4) for i in range(4)]
FAR = [(i, (i + 2) % 4) for i in range(4)]
Z_OFFSETS = (0, -1, 1, 2)


def together(*values):
    return lax.optimization_barrier(values)


def up(a):
    return lax.ppermute(a, "z", UP)


def down(a):
    return lax.ppermute(a, "z", DOWN)


def across(a):
    return lax.ppermute(a, "xl", SWAP)


def gather_pair(own, other, single):
    xh = lax.axis_index("xh")
    parts = [jnp.where(xh == 0, own, other), jnp.where(xh == 0, other, own)]
    if single is not None:
        parts.append(single)
    packed = jnp.concatenate(parts, axis=0)
    g = lax.all_gather(packed, ("y", "c"), axis=0, tiled=False)
    return g.reshape((4, 2) + packed.shape)


def add(*terms):
    return sum(t.astype(F32) for t in terms)


def scatter_sum(near, owns, sides):
    from_side = lax.ppermute(sides, "xl", SWAP)
    above = lax.ppermute(near[4:6], "z", UP)
    below = lax.ppermute(near[2:4], "z", DOWN)
    far = lax.ppermute(near[6:8], "z", FAR)
    t = add(owns, from_side)
    low = t.astype(BF)
    side = lax.ppermute(add(near[1], above[1], below[1], far[1]).astype(BF), "xl", SWAP)
    above2 = lax.ppermute(low[2], "z", UP)
    below2 = lax.ppermute(low[1], "z", DOWN)
    far2 = lax.ppermute(low[3], "z", FAR)
    return near, above, below, far, side, t, above2, below2, far2


def local(
    inputs,
    output_cotangent,
    block_index_per_position,
    adapter_index_per_run,
    norm_gain,
    norm_bias,
    query_weight,
    key_weight,
    value_weight,
    dense_weight,
    query_bias,
    key_bias,
    value_bias,
    dense_bias,
    feedforward_in_weight,
    feedforward_in_bias,
    feedforward_out_weight,
    feedforward_out_bias,
    adapter_attention_down,
    adapter_attention_up,
    adapter_dense_down,
    adapter_dense_up,
    adapter_feedforward_in_down,
    adapter_feedforward_in_up,
    adapter_feedforward_out_down,
    adapter_feedforward_out_up,
):
    xl, z, c = lax.axis_index("xl"), lax.axis_index("z"), lax.axis_index("c")
    xh = lax.axis_index("xh")
    j = xl * 4 + z
    x_own = inputs[0]
    dy_own = output_cotangent[0]
    run_adapter = adapter_index_per_run[0, 0].astype(F32).astype(BF)
    block_row = block_index_per_position[0]
    z_of = [lax.rem(z + o + 4, 4) for o in Z_OFFSETS]
    spots = [(xl if side == 0 else 1 - xl) * 4 + zz for zz in z_of for side in range(2)]
    scal = jnp.stack(spots + [c, j, xl, z] + z_of).astype(jnp.int32)

    misc_own = jnp.concatenate(
        [norm_gain, norm_bias, dense_bias, feedforward_out_bias, query_bias, key_bias, value_bias]
        + [jnp.zeros((9 * 256,), BF)]
    ).reshape(16, 256)
    sent1, for_other = pack1(
        scal,
        query_weight,
        key_weight,
        value_weight,
        dense_weight,
        adapter_attention_down[0],
        adapter_feedforward_in_down[0],
        adapter_attention_up[0],
        adapter_dense_down[0],
        adapter_dense_up[0],
        misc_own,
        feedforward_in_bias.reshape(8, 128),
    )
    own2, own2_for_other = pack2(
        scal,
        feedforward_in_weight,
        feedforward_out_weight,
        adapter_feedforward_in_up[0],
        adapter_feedforward_out_down[0],
        adapter_feedforward_out_up[0],
    )
    spread = jnp.stack(spots)
    my_positions = ((spread * 2 + c) * 128)[:, None] + jnp.arange(128, dtype=jnp.int32)[None, :]
    tables = rotary_tables(my_positions.reshape(1024)) + rotary_tables(jnp.arange(2048, dtype=jnp.int32))
    tables = tables + (jnp.broadcast_to(block_row[:, None], (2048, 128)),)
    x_send = jnp.concatenate([x_own, jnp.full((128, 128), run_adapter, BF)], axis=1)

    x_up, x_down, x_side = together(up(x_send), down(x_send), across(x_send))
    other1 = lax.ppermute(for_other, ("xl", "xh"), FLIP)
    x_up_more = up(jnp.concatenate([x_side, x_up[:64]], axis=0))
    x_down_more = down(jnp.concatenate([x_side, x_down[64:]], axis=0))
    dy_side = across(together(dy_own, x_side)[0])
    own2, own2_for_other, tables, x_up_more, x_down_more = together(
        own2, own2_for_other, tables, x_up_more, x_down_more
    )
    other1 = together(other1, dy_side)[0]
    g1 = gather_pair(sent1[:MAIN], other1[:MAIN], jnp.where(xh == xl, sent1[MAIN:], other1[MAIN:]))
    x_far_side, dy_up, dy_down, other2 = together(
        across(jnp.concatenate([x_up_more[128:], x_down_more[128:]], axis=0)),
        up(together(dy_own, x_up_more)[0]),
        down(together(dy_own, x_down_more)[0]),
        lax.ppermute(own2_for_other, ("xl", "xh"), FLIP),
    )
    g2 = gather_pair(own2, other2, None)
    dy_up_more, dy_down_more = together(
        up(jnp.concatenate([dy_side, dy_up[:64]], axis=0)), down(jnp.concatenate([dy_side, dy_down[64:]], axis=0))
    )
    dy_far_side = across(jnp.concatenate([dy_up_more[128:], dy_down_more[128:]], axis=0))
    x_blocks = [x_send, x_side, x_up, x_down, x_up_more, x_down_more, x_far_side]
    dy_blocks = [dy_own, dy_side, dy_up, dy_down, dy_up_more, dy_down_more, dy_far_side]

    def side_of(core):
        return jnp.stack(
            [g1[:, core, MAIN * h : MAIN * h + 64, 768:] for h in range(2)], axis=1
        ).reshape(8, 64, 256)

    ups_all = side_of(0).reshape(8, 4, 16, 256).transpose(1, 0, 2, 3).reshape(4, 128, 256)
    ups = jnp.concatenate([ups_all[0], ups_all[1], ups_all[2]], axis=1)
    dd = ups_all[3]
    small_all = side_of(1)[:, :6].astype(F32)
    misc = small_all[:, :4].transpose(1, 0, 2).reshape(4, 2048)
    head_b = lax.dynamic_index_in_dim(small_all[:, 4, :192].reshape(4, 2, 3, 64), xl, 1, keepdims=False)
    bias_qkv = head_b.transpose(1, 0, 2).reshape(1, 768)
    b1 = small_all[:, 5, :128].reshape(1, 1024)

    cos_mine, sin_mine, cos_all, sin_all, idcol = tables

    hb, inner, qkv_keep, qkv_send, aid = k1(x_blocks, scal, g1, ups, misc[:2], bias_qkv, cos_mine, sin_mine)
    qkv_recv = lax.ppermute(qkv_send, "c", SWAP)
    dob_keep, dob_send, gdense = k1b(dy_blocks, scal, aid, g1, dd)
    dob_recv = lax.ppermute(dob_send, "c", SWAP)

    idrow = jnp.broadcast_to(block_row[None, :], (8, 2048))
    att_keep, att_send = k3(scal, qkv_keep, qkv_recv, dob_keep, dob_recv, idrow, idcol, cos_all, sin_all)
    att_recv = lax.ppermute(att_send, "c", SWAP)

    fold = fold_matrix()
    gb, df, low_out, low_in, small, gup1, gd2, gdd = k2m(
        dy_blocks, scal, hb, aid, inner, gdense, att_keep, att_recv, g2, ups, dd, b1, fold
    )
    small = lax.all_to_all(small.reshape(8, 128, 128), TP, 0, 0, tiled=True)
    out_part = k2o(scal, gb, att_keep, att_recv, low_out, g1, g2)
    out_part, small, df = together(out_part, small, df)
    small = jnp.sum(small.astype(F32), axis=0).astype(BF)
    small = lax.all_to_all(jnp.broadcast_to(small[None], (8, 128, 128)), TP, 0, 0, tiled=True)
    out_sum = lax.psum_scatter(out_part.reshape(1024, 2048), TP, scatter_dimension=0, tiled=True)
    near, owns, sides, gqkv = k2h(scal, df, att_keep, att_recv, low_in, inner, g1, g2)
    near, owns, sides, small = together(near, owns, sides, small)
    shares = scatter_sum(near, owns, sides)

    keep, send = k5(scal, small, aid, hb, fold.T, gup1, gd2, gqkv, gdd, dy_blocks)
    grads = (keep + lax.ppermute(send, "c", SWAP).astype(F32)).astype(BF)
    grads = lax.all_to_all(grads, WSH, 0, 0, tiled=True)
    grads = jnp.sum(grads.astype(F32), axis=0).astype(BF)
    grads = together(grads, *shares[1:4], shares[5])[0]
    grads = lax.all_to_all(jnp.broadcast_to(grads[None], (8, 80, 512)), TP, 0, 0, tiled=True)
    down_qkv, up_qkv, gdd, gud, gf1d, gf1u, gf2d, gf2u = kf(scal, grads, lax.ppermute(grads, "c", SWAP))

    source = x_own.astype(F32)
    outputs = (source + out_sum.astype(F32) + misc[2:3] + misc[3:4]).astype(BF)[None]
    *shares, outputs = together(*shares, outputs)
    grad_inputs = kn(x_own, output_cotangent[0], misc[0:1], *shares)[None]
    return (
        outputs,
        grad_inputs,
        down_qkv[None],
        up_qkv[None],
        gdd[None],
        gud[None],
        gf1d[None],
        gf1u[None],
        gf2d[None],
        gf2u[None],
    )


def solution(mesh):
    fine = Mesh(np.asarray(mesh.devices).reshape(2, 4, 2, 4, 2), ("xl", "z", "c", "y", "xh"))
    tokens = P(WSH, CTX, None)
    w1 = P(WSH)
    w2 = P(WSH, None)
    w3 = P(WSH, None, None)
    w4 = P(WSH, None, None, None)
    placed = (tokens, tokens, w2, P(WSH, CTX)) + (w1, w1, w2, w2, w2, w2, w1, w1, w1, w1, w2, w1, w2, w1)
    placed = placed + (w4, w4, w3, w3, w3, w3, w3, w3)
    return jax.shard_map(
        local,
        mesh=fine,
        in_specs=placed,
        out_specs=(tokens, tokens, w4, w4, w3, w3, w3, w3, w3, w3),
        check_vma=False,
    )
```

```python
import functools

import jax
import jax.numpy as jnp
import numpy as np
from jax import lax
from jax.experimental import pallas as pl
from jax.experimental.pallas import tpu as pltpu
from jax.sharding import Mesh, PartitionSpec as P

ADAPTERS = 8
RANK = 16
EPSILON = 1e-05
GELU_SCALE = 0.7978845608028654
NEGATIVE = -1e30
SCALE = 64 ** -0.5
BF = jnp.bfloat16
F32 = jnp.float32
WSH = ("y", "xh")
TP = ("xl", "z")
CTX = ("xl", "z", "c")
VMEM_LIMIT = 58 * 1024 * 1024


def nn(a, b):
    return lax.dot_general(a, b, (((1,), (0,)), ((), ())), preferred_element_type=F32)


def nt(a, b):
    return lax.dot_general(a, b, (((1,), (1,)), ((), ())), preferred_element_type=F32)


def tn(a, b):
    return lax.dot_general(a, b, (((0,), (0,)), ((), ())), preferred_element_type=F32)


def adapter_mask(aid, columns):
    col = lax.broadcasted_iota(jnp.int32, (aid.shape[0], columns), 1)
    return (lax.shift_right_logical(col, 4) & 7) == aid.astype(jnp.int32)


def turn(values, cosine, sine):
    width = values.shape[1]
    lane = lax.broadcasted_iota(jnp.int32, values.shape, 1) & 63
    partner = jnp.where(
        lane < 16, pltpu.roll(values, width - 16, 1), pltpu.roll(values, 16, 1)
    )
    return values * cosine + partner * sine


ANY = pl.BlockSpec(memory_space=pl.ANY)
SMEM = pl.BlockSpec(memory_space=pltpu.SMEM)
VM = pl.BlockSpec(memory_space=pltpu.VMEM)
PARAMS = pltpu.CompilerParams(vmem_limit_bytes=VMEM_LIMIT)
MAIN = 208
SECOND = 288
NEAR = 1280


def whole(shape):
    return pl.BlockSpec(shape, lambda t: (0,) * len(shape), pipeline_mode=pl.Buffered(1))


def start_all(pairs, sem):
    for source, target in pairs:
        pltpu.make_async_copy(source, target, sem).start()


def wait_all(target, sem):
    pltpu.make_async_copy(target, target, sem).wait()


def token_copies(blocks, target):
    if len(blocks) == 7:
        own, side, above, below, up_more, down_more, far_side = blocks
        side_above, far_a = up_more.at[pl.ds(0, 128), :], up_more.at[pl.ds(128, 64), :]
        side_below, far_b = down_more.at[pl.ds(0, 128), :], down_more.at[pl.ds(128, 64), :]
    else:
        own, side, above, below, side_above, side_below, far_a, far_b, far_side = blocks
    return [
        (own, target.at[0, 0], 0),
        (side, target.at[0, 1], 1),
        (above, target.at[1, 0], 2),
        (side_above, target.at[1, 1], 3),
        (below, target.at[2, 0], 4),
        (side_below, target.at[2, 1], 5),
        (far_a, target.at[3, 0, pl.ds(0, 64)], 6),
        (far_b, target.at[3, 0, pl.ds(64, 64)], 6),
        (far_side, target.at[3, 1], 7),
    ]


def start_tokens(blocks, target, sem, first, last):
    for source, part, i in token_copies(blocks, target):
        if first <= i < last:
            pltpu.make_async_copy(source, part, sem.at[i]).start()


def wait_tokens(target, sem, step):
    for i in range(2):
        part = target.at[step, i]
        pltpu.make_async_copy(part, part, sem.at[2 * step + i]).wait()


def pieces_qkv(g1, target):
    return [
        (
            g1.at[y, c, pl.ds(MAIN * xh, 128), pl.ds(0, 768)],
            target.at[pl.ds((2 * y + xh) * 256 + c * 128, 128), :],
        )
        for y in range(4)
        for xh in range(2)
        for c in range(2)
    ]


def pieces_downs(g1, target):
    return [
        (
            g1.at[:, c, pl.ds(MAIN * xh + 128 + 32 * i + 16 * b, 16), :],
            target.at[c, i, :, xh, :, pl.ds(1024 * b, 1024)],
        )
        for c in range(2)
        for i in range(2)
        for xh in range(2)
        for b in range(2)
    ]


def pieces_rank(g, base, stride, target, row):
    return [
        (
            g.at[y, c, pl.ds(stride * xh + base, 16), :],
            target.at[pl.ds(row + (2 * y + xh) * 16, 16), pl.ds(1024 * c, 1024)],
        )
        for y in range(4)
        for xh in range(2)
        for c in range(2)
    ]


def pieces_dense(g1, target, row):
    return [
        (
            g1.at[y, c, pl.ds(2 * MAIN + 32 * b, 32), :],
            target.at[pl.ds(row + 64 * y + 32 * c, 32), pl.ds(1024 * b, 1024)],
        )
        for y in range(4)
        for c in range(2)
        for b in range(2)
    ]


def pieces_w1(g2, target):
    return [
        (
            g2.at[y, c, pl.ds(SECOND * xh, 128), :],
            target.at[pl.ds((2 * y + xh) * 256 + c * 128, 128), :],
        )
        for y in range(4)
        for xh in range(2)
        for c in range(2)
    ]


def pieces_sixteen(g2, c, target, row):
    return [
        (
            g2.at[y, c, pl.ds(SECOND * xh + 128, 16), :],
            target.at[pl.ds(row + (2 * y + xh) * 16, 16), :],
        )
        for y in range(4)
        for xh in range(2)
    ]


def pieces_w2(g2, target):
    return [
        (
            g2.at[y, c, pl.ds(SECOND * xh + 144 + 64 * b, 64), :],
            target.at[pl.ds((2 * y + xh) * 128 + c * 64, 64), pl.ds(1024 * b, 1024)],
        )
        for y in range(4)
        for xh in range(2)
        for c in range(2)
        for b in range(2)
    ]


def block_diagonal(source, target):
    target[...] = jnp.zeros_like(target)
    for p in range(3):
        cols = slice(256 * p, 256 * p + 256)
        target[128 * p : 128 * p + 128, cols] = source[:, cols]


def k1_body(*refs):
    blocks, refs = refs[:9], refs[9:]
    (scal_ref, g1_ref, up_ref, misc_ref, bias_ref, cos_ref, sin_ref,
     hb_ref, inner_ref, keep_ref, send_ref, aid_ref, x_s, w_s, down_s, up_s, x_sem, w_sem) = refs
    step = pl.program_id(0)

    @pl.when(step == 0)
    def _():
        start_tokens(blocks, x_s, x_sem, 0, 2)
        start_all(pieces_downs(g1_ref, down_s), w_sem.at[0])
        start_all(pieces_qkv(g1_ref, w_s.at[:, pl.ds(0, 768)]), w_sem.at[1])
        start_tokens(blocks, x_s, x_sem, 2, 8)

    wait_tokens(x_s, x_sem, step)
    tile = x_s[step].reshape(256, 2176)
    x = tile[:, :2048].astype(F32)
    aid_ref[...] = tile[:, 2048:]
    aid = tile[:, 2048:2049].astype(F32)
    mean = jnp.mean(x, axis=1, keepdims=True)
    center = x - mean
    spread = jnp.mean(center * center, axis=1, keepdims=True)
    h = center * lax.rsqrt(spread + EPSILON) * misc_ref[0:1, :] + misc_ref[1:2, :]
    hb = h.astype(BF)
    hb_ref[...] = hb

    @pl.when(step == 0)
    def _():
        block_diagonal(up_ref, up_s)
        wait_all(down_s, w_sem.at[0])
        w_s[:, 768:] = down_s[...].reshape(512, 2048).T
        wait_all(w_s.at[:, pl.ds(0, 768)], w_sem.at[1])

    pre_all = nn(hb, w_s[...])
    inner = jnp.where(adapter_mask(aid, 512), pre_all[:, 768:], 0.0).astype(BF)
    inner_ref[...] = inner
    pre_all = pre_all[:, :768] + nn(inner[:, :384], up_s[...]) + bias_ref[...]
    first_core = scal_ref[8] == 0
    cosine = jnp.concatenate([cos_ref[...]] * 2, axis=1)
    sine = jnp.concatenate([sin_ref[...]] * 2, axis=1)
    for p in range(3):
        cols = slice(256 * p, 256 * p + 256)
        pre = pre_all[:, cols]
        if p < 2:
            pre = turn(pre, cosine, sine)
        low = pre.astype(BF)
        keep_ref[p] = jnp.where(first_core, low[:, :128], low[:, 128:])
        send_ref[p] = jnp.where(first_core, low[:, 128:], low[:, :128])


def k1(blocks, scal, g1, ups, misc, bias, cosine, sine):
    rows = 256
    return pl.pallas_call(
        k1_body,
        grid=(4,),
        in_specs=[ANY] * 9
        + [
            SMEM,
            ANY,
            whole((128, 768)),
            whole((2, 2048)),
            whole((1, 768)),
            pl.BlockSpec((rows, 128), lambda t: (t, 0)),
            pl.BlockSpec((rows, 128), lambda t: (t, 0)),
        ],
        out_specs=[
            pl.BlockSpec((rows, 2048), lambda t: (t, 0)),
            pl.BlockSpec((rows, 512), lambda t: (t, 0)),
            pl.BlockSpec((3, rows, 128), lambda t: (0, t, 0)),
            pl.BlockSpec((3, rows, 128), lambda t: (0, t, 0)),
            pl.BlockSpec((rows, 128), lambda t: (t, 0)),
        ],
        out_shape=[
            jax.ShapeDtypeStruct((1024, 2048), BF),
            jax.ShapeDtypeStruct((1024, 512), BF),
            jax.ShapeDtypeStruct((3, 1024, 128), BF),
            jax.ShapeDtypeStruct((3, 1024, 128), BF),
            jax.ShapeDtypeStruct((1024, 128), BF),
        ],
        scratch_shapes=[
            pltpu.VMEM((4, 2, 128, 2176), BF),
            pltpu.VMEM((2048, 1280), BF),
            pltpu.VMEM((2, 2, 4, 2, 16, 2048), BF),
            pltpu.VMEM((384, 768), BF),
            pltpu.SemaphoreType.DMA((8,)),
            pltpu.SemaphoreType.DMA((2,)),
        ],
        compiler_params=PARAMS,
        cost_estimate=pl.CostEstimate(flops=6_000_000_000, bytes_accessed=20_000_000, transcendentals=0),
        name="norm_qkv",
    )(*blocks, scal, g1, ups, misc, bias, cosine, sine)


def k1b_body(*refs):
    blocks, refs = refs[:7], refs[7:]
    scal_ref, aid_ref, g1_ref, dd_ref, keep_ref, send_ref, ginner_ref, dy_s, w_s, dy_sem, w_sem = refs
    start_all(pieces_dense(g1_ref, w_s, 0) + pieces_rank(g1_ref, 192, MAIN, w_s, 256), w_sem)
    start_tokens(blocks, dy_s, dy_sem, 0, 8)
    wait_all(w_s, w_sem)
    for step in range(4):
        wait_tokens(dy_s, dy_sem, step)
    first_core = scal_ref[8] == 0
    both = nt(dy_s[...].reshape(1024, 2048), w_s[...])
    aid = aid_ref[:, 0:1].astype(F32)
    ginner = jnp.where(adapter_mask(aid, 128), both[:, 256:], 0.0).astype(BF)
    ginner_ref[...] = ginner
    dob = (both[:, :256] + nn(ginner, dd_ref[...])).astype(BF)
    keep_ref[...] = jnp.where(first_core, dob[:, :128], dob[:, 128:])
    send_ref[...] = jnp.where(first_core, dob[:, 128:], dob[:, :128])


def k1b(blocks, scal, aid, g1, dd):
    return pl.pallas_call(
        k1b_body,
        in_specs=[ANY] * 7 + [SMEM, VM, ANY, VM],
        out_specs=[VM, VM, VM],
        out_shape=[jax.ShapeDtypeStruct((1024, 128), BF)] * 3,
        scratch_shapes=[
            pltpu.VMEM((4, 2, 128, 2048), BF),
            pltpu.VMEM((384, 2048), BF),
            pltpu.SemaphoreType.DMA((8,)),
            pltpu.SemaphoreType.DMA,
        ],
        compiler_params=PARAMS,
        cost_estimate=pl.CostEstimate(flops=2_000_000_000, bytes_accessed=8_000_000, transcendentals=0),
        name="attention_output_grad",
    )(*blocks, scal, aid, g1, dd)


def k3_body(
    scal_ref, qkv_keep, qkv_recv, dob_keep, dob_recv, idrow_ref, idcol_ref, cos_ref, sin_ref,
    keep_out, send_out, x_s, out_s, kt_s, vt_s, dk_s, dv_s, sem, sem_out,
):
    core = scal_ref[8]
    copies = []
    for b in range(8):
        rows = pl.ds(128 * b, 128)
        spot = scal_ref[b]
        for side, (qkv, dob) in enumerate(((qkv_keep, dob_keep), (qkv_recv, dob_recv))):
            parity = core if side == 0 else 1 - core
            copies.append((qkv.at[:, rows, :], x_s.at[pl.ds(0, 3), spot, parity]))
            copies.append((dob.at[rows, :], x_s.at[3, spot, parity]))
    start_all(copies, sem)
    dk_s[...] = jnp.zeros_like(dk_s)
    dv_s[...] = jnp.zeros_like(dv_s)
    wait_all(x_s, sem)
    kt_s[...] = x_s[1].reshape(2048, 128).T
    vt_s[...] = x_s[2].reshape(2048, 128).T
    tile = 256
    lane = lax.broadcasted_iota(jnp.int32, (tile, 128), 1)

    def span(i, start, stop):
        return x_s[i, start // 256 : stop // 256].reshape(stop - start, 128)

    for t in range(8):
        start, stop = tile * t, tile * t + tile
        length = min(stop + tile, 2048)
        q = span(0, start, stop)
        dob = span(3, start, stop)
        zero = jnp.zeros_like(q)
        q = q * jnp.asarray(SCALE, BF)
        q2 = jnp.concatenate([jnp.where(lane < 64, q, zero), jnp.where(lane < 64, zero, q)], axis=0)
        d2 = jnp.concatenate([jnp.where(lane < 64, dob, zero), jnp.where(lane < 64, zero, dob)], axis=0)
        query_ids = idrow_ref[0:1, start:stop]
        query_ids = jnp.concatenate([query_ids, query_ids], axis=1)
        allowed = idcol_ref[start:length, 0:1] <= query_ids
        s = jnp.where(allowed, nt(span(1, start, length), q2), NEGATIVE)
        largest = jnp.max(s, axis=0, keepdims=True)
        if start:
            s_head = nt(span(1, 0, start), q2)
            largest = jnp.maximum(largest, jnp.max(s_head, axis=0, keepdims=True))
            s = jnp.concatenate([s_head, s], axis=0)
        e = jnp.exp(s - largest)
        recip = 1.0 / jnp.sum(e, axis=0, keepdims=True)
        p = e * recip
        pb = p.astype(BF)
        ot = nn(vt_s[:, :length], pb)
        dp = nt(span(2, 0, length), d2)
        o_parts = [ot[:64, :256], ot[64:, 256:]]
        dobt = dob.astype(F32).T
        delta = jnp.concatenate(
            [
                jnp.sum(o_parts[0] * dobt[:64], axis=0, keepdims=True),
                jnp.sum(o_parts[1] * dobt[64:], axis=0, keepdims=True),
            ],
            axis=1,
        )
        ds = (p * (dp - delta)).astype(BF)
        dk_s[:length] += nn(ds, q2)
        dv_s[:length] += nn(pb, d2)
        dqt = nn(kt_s[:, :length], ds)
        dq_parts = [dqt[:64, :256], dqt[64:, 256:]]
        o = jnp.concatenate(o_parts, axis=0).T
        dq = jnp.concatenate(dq_parts, axis=0).T * SCALE
        rows = slice(start, stop)
        out_s[0, t] = o.astype(BF).reshape(2, 128, 128)
        out_s[1, t] = turn(dq, cos_ref[rows], -sin_ref[rows]).astype(BF).reshape(2, 128, 128)
    out_s[2] = turn(dk_s[...], cos_ref[...], -sin_ref[...]).astype(BF).reshape(8, 2, 128, 128)
    out_s[3] = dv_s[...].astype(BF).reshape(8, 2, 128, 128)
    copies = []
    for b in range(8):
        rows = pl.ds(128 * b, 128)
        spot = scal_ref[b]
        copies.append((out_s.at[:, spot, core], keep_out.at[:, rows, :]))
        copies.append((out_s.at[:, spot, 1 - core], send_out.at[:, rows, :]))
    start_all(copies, sem_out)
    wait_all(out_s, sem_out)


def k3(scal, qkv_keep, qkv_recv, dob_keep, dob_recv, idrow, idcol, cosine, sine):
    vm = pl.BlockSpec(memory_space=pltpu.VMEM)
    return pl.pallas_call(
        k3_body,
        in_specs=[SMEM] + [ANY] * 4 + [vm] * 4,
        out_specs=[ANY, ANY],
        out_shape=[jax.ShapeDtypeStruct((4, 1024, 128), BF)] * 2,
        scratch_shapes=[
            pltpu.VMEM((4, 8, 2, 128, 128), BF),
            pltpu.VMEM((4, 8, 2, 128, 128), BF),
            pltpu.VMEM((128, 2048), BF),
            pltpu.VMEM((128, 2048), BF),
            pltpu.VMEM((2048, 128), F32),
            pltpu.VMEM((2048, 128), F32),
            pltpu.SemaphoreType.DMA,
            pltpu.SemaphoreType.DMA,
        ],
        compiler_params=PARAMS,
        cost_estimate=pl.CostEstimate(flops=15_000_000_000, bytes_accessed=8_000_000, transcendentals=5_000_000),
        name="attention",
    )(scal, qkv_keep, qkv_recv, dob_keep, dob_recv, idrow, idcol, cosine, sine)


def heads_of(keep_ref, recv_ref, i, first_core):
    a, b = keep_ref[i], recv_ref[i]
    return jnp.concatenate([jnp.where(first_core, a, b), jnp.where(first_core, b, a)], axis=1)


def tile_spec(width, rows=256):
    return pl.BlockSpec((rows, width), lambda t, s: (t, 0))


def const_spec(shape):
    return pl.BlockSpec(shape, lambda t, s: (0,) * len(shape), pipeline_mode=pl.Buffered(1))


def placed_spec(width):
    return pl.BlockSpec((2, 1, 128, width), lambda t, s: (0, s[12 + t], 0, 0))


def place(ref, xl, value):
    ref[xl, 0] = value[:128]
    ref[1 - xl, 0] = value[128:]


def accumulate(step, pairs):
    @pl.when(step == 0)
    def _():
        for ref, value in pairs:
            ref[...] = value

    @pl.when(step > 0)
    def _():
        for ref, value in pairs:
            ref[...] += value


def k2m_body(scal_ref, *refs):
    blocks, refs = refs[:7], refs[7:]
    (hb_ref, aid_ref, inner_ref, gdense_ref, keep_ref, recv_ref, g2_ref, up_ref, dd_ref, b1_ref, fold_ref,
     gb_ref, df_ref, low_out_ref, low_in_ref, small_ref, gup1_ref, gd2_ref, gdd_ref,
     dy_s, w1_s, w2_s, d2_s, up_s, dy_sem, sems) = refs
    step = pl.program_id(0)

    @pl.when(step == 0)
    def _():
        start_all(pieces_w1(g2_ref, w1_s) + pieces_sixteen(g2_ref, 0, w1_s, 2048), sems.at[0])
        start_all(pieces_sixteen(g2_ref, 1, d2_s, 0), sems.at[1])
        start_tokens(blocks, dy_s, dy_sem, 0, 2)
        start_all(pieces_w2(g2_ref, w2_s) + pieces_rank(g2_ref, 272, SECOND, w2_s, 1024), sems.at[2])
        start_tokens(blocks, dy_s, dy_sem, 2, 8)
        block_diagonal(up_ref, up_s)
        wait_all(w1_s, sems.at[0])

    aid = aid_ref[:, 0:1].astype(F32)
    first_core = scal_ref[8] == 0
    f = nn(jnp.concatenate([hb_ref[...], inner_ref[...]], axis=1), w1_s[...]) + b1_ref[...]

    @pl.when(step == 0)
    def _():
        wait_all(w2_s, sems.at[2])
        wait_all(d2_s, sems.at[1])

    wait_tokens(dy_s, dy_sem, step)
    wide = nt(dy_s[step].reshape(256, 2048), w2_s[...])
    square = f * f
    th = jnp.tanh(GELU_SCALE * f * (1.0 + 0.044715 * square))
    half = 0.5 * (1.0 + th)
    gb = (f * half).astype(BF)
    gb_ref[...] = gb
    slope = half + (0.5 * GELU_SCALE) * f * (1.0 - th * th) * (1.0 + 3 * 0.044715 * square)
    ginner2 = jnp.where(adapter_mask(aid, 128), wide[:, 1024:], 0.0).astype(BF)
    ob = heads_of(keep_ref, recv_ref, 0, first_core)
    dpre = jnp.concatenate([heads_of(keep_ref, recv_ref, p, first_core) for p in (1, 2, 3)], axis=1)
    inner2 = nt(gb, d2_s[...])
    innerd = nt(ob, dd_ref[...])
    ginner = nt(dpre, up_s[...])
    df = ((wide[:, :1024] + nn(ginner2, d2_s[...])) * slope).astype(BF)
    df_ref[...] = df
    ginner1 = nt(df, w1_s[2048:])
    low = jnp.concatenate([ginner, ginner1, innerd, inner2], axis=1)
    low = jnp.where(adapter_mask(aid, 768), low, 0.0).astype(BF)
    low_in_ref[...] = low[:, :512]
    low_out_ref[...] = low[:, 512:]
    place(small_ref, scal_ref[10], nn(low, fold_ref[...]).astype(BF))
    accumulate(
        step,
        [
            (gup1_ref, tn(inner_ref[...], df)),
            (gd2_ref, tn(ginner2, gb)),
            (gdd_ref, tn(gdense_ref[...], ob)),
        ],
    )


def att_spec(first, count):
    return pl.BlockSpec((count, 256, 128), lambda t, s: (first, t, 0))


def k2m(blocks, scal, hb, aid, inner, gdense, keep, recv, g2, ups, dd, b1, fold):
    return pl.pallas_call(
        k2m_body,
        grid_spec=pltpu.PrefetchScalarGridSpec(
            num_scalar_prefetch=1,
            grid=(4,),
            in_specs=[ANY] * 7
            + [
                tile_spec(2048),
                tile_spec(128),
                pl.BlockSpec((256, 128), lambda t, s: (t, 3)),
                tile_spec(128),
                att_spec(0, 4),
                att_spec(0, 4),
                ANY,
                const_spec((128, 768)),
                const_spec((128, 256)),
                const_spec((1, 1024)),
                const_spec((768, 128)),
            ],
            out_specs=[
                tile_spec(1024),
                tile_spec(1024),
                tile_spec(256),
                tile_spec(512),
                placed_spec(128),
                const_spec((128, 1024)),
                const_spec((128, 1024)),
                const_spec((128, 256)),
            ],
            scratch_shapes=[
                pltpu.VMEM((4, 2, 128, 2048), BF),
                pltpu.VMEM((2176, 1024), BF),
                pltpu.VMEM((1152, 2048), BF),
                pltpu.VMEM((128, 1024), BF),
                pltpu.VMEM((384, 768), BF),
                pltpu.SemaphoreType.DMA((8,)),
                pltpu.SemaphoreType.DMA((3,)),
            ],
        ),
        out_shape=[
            jax.ShapeDtypeStruct((1024, 1024), BF),
            jax.ShapeDtypeStruct((1024, 1024), BF),
            jax.ShapeDtypeStruct((1024, 256), BF),
            jax.ShapeDtypeStruct((1024, 512), BF),
            jax.ShapeDtypeStruct((2, 4, 128, 128), BF),
            jax.ShapeDtypeStruct((128, 1024), F32),
            jax.ShapeDtypeStruct((128, 1024), F32),
            jax.ShapeDtypeStruct((128, 256), F32),
        ],
        compiler_params=PARAMS,
        cost_estimate=pl.CostEstimate(flops=14_000_000_000, bytes_accessed=30_000_000, transcendentals=1_000_000),
        name="feed_forward",
    )(scal, *blocks, hb, aid, inner, gdense, keep, recv, g2, ups, dd, b1, fold)


def k2o_body(scal_ref, gb_ref, keep_ref, recv_ref, low_ref, g1_ref, g2_ref, out_ref, w_s, sem):
    step = pl.program_id(0)

    @pl.when(step == 0)
    def _():
        start_all(
            pieces_w2(g2_ref, w_s)
            + pieces_dense(g1_ref, w_s, 1024)
            + pieces_rank(g1_ref, 192, MAIN, w_s, 1280)
            + pieces_rank(g2_ref, 272, SECOND, w_s, 1408),
            sem,
        )
        wait_all(w_s, sem)

    ob = heads_of(keep_ref, recv_ref, 0, scal_ref[8] == 0)
    out = nn(jnp.concatenate([gb_ref[...], ob, low_ref[...]], axis=1), w_s[...]).astype(BF)
    place(out_ref, scal_ref[10], out)


def k2o(scal, gb, keep, recv, low_out, g1, g2):
    return pl.pallas_call(
        k2o_body,
        grid_spec=pltpu.PrefetchScalarGridSpec(
            num_scalar_prefetch=1,
            grid=(4,),
            in_specs=[tile_spec(1024), att_spec(0, 1), att_spec(0, 1), tile_spec(256), ANY, ANY],
            out_specs=[placed_spec(2048)],
            scratch_shapes=[pltpu.VMEM((1536, 2048), BF), pltpu.SemaphoreType.DMA],
        ),
        out_shape=[jax.ShapeDtypeStruct((2, 4, 128, 2048), BF)],
        compiler_params=PARAMS,
        cost_estimate=pl.CostEstimate(flops=7_000_000_000, bytes_accessed=14_000_000, transcendentals=0),
        name="out_rows",
    )(scal, gb, keep, recv, low_out, g1, g2)[0]


def k2h_body(
    scal_ref, df_ref, keep_ref, recv_ref, low_ref, inner_ref, g1_ref, g2_ref,
    near_ref, owns_ref, sides_ref, gqkv_ref, w_s, down_s, sems,
):
    step = pl.program_id(0)

    @pl.when(step == 0)
    def _():
        start_all(
            pieces_w1(g2_ref, w_s.at[:, pl.ds(0, 1024)]) + pieces_qkv(g1_ref, w_s.at[:, pl.ds(1024, 768)]), sems.at[0]
        )
        start_all(pieces_downs(g1_ref, down_s), sems.at[1])
        wait_all(w_s, sems.at[0])
        wait_all(down_s, sems.at[1])

    first_core = scal_ref[8] == 0
    dpre = [heads_of(keep_ref, recv_ref, p, first_core) for p in (1, 2, 3)]
    dh = nt(jnp.concatenate([df_ref[...]] + dpre, axis=1), w_s[...])
    dh = (dh + nn(low_ref[...], down_s[...].reshape(512, 2048))).astype(BF)
    near_ref[0] = dh[:128, :NEAR]
    near_ref[1] = dh[128:, :NEAR]
    owns_ref[0] = dh[:128, NEAR:]
    sides_ref[0] = dh[128:, NEAR:]
    gqkv = [tn(inner_ref[:, 128 * p : 128 * p + 128], dpre[p]) for p in range(3)]
    accumulate(step, [(gqkv_ref, jnp.concatenate(gqkv, axis=1))])


def k2h(scal, df, keep, recv, low_in, inner, g1, g2):
    return pl.pallas_call(
        k2h_body,
        grid_spec=pltpu.PrefetchScalarGridSpec(
            num_scalar_prefetch=1,
            grid=(4,),
            in_specs=[tile_spec(1024), att_spec(0, 4), att_spec(0, 4), tile_spec(512), tile_spec(512), ANY, ANY],
            out_specs=[
                pl.BlockSpec((2, 128, NEAR), lambda t, s: (t, 0, 0)),
                pl.BlockSpec((1, 128, 2048 - NEAR), lambda t, s: (t, 0, 0)),
                pl.BlockSpec((1, 128, 2048 - NEAR), lambda t, s: (t, 0, 0)),
                const_spec((128, 768)),
            ],
            scratch_shapes=[
                pltpu.VMEM((2048, 1792), BF),
                pltpu.VMEM((2, 2, 4, 2, 16, 2048), BF),
                pltpu.SemaphoreType.DMA((2,)),
            ],
        ),
        out_shape=[
            jax.ShapeDtypeStruct((8, 128, NEAR), BF),
            jax.ShapeDtypeStruct((4, 128, 2048 - NEAR), BF),
            jax.ShapeDtypeStruct((4, 128, 2048 - NEAR), BF),
            jax.ShapeDtypeStruct((128, 768), F32),
        ],
        compiler_params=PARAMS,
        cost_estimate=pl.CostEstimate(flops=10_000_000_000, bytes_accessed=18_000_000, transcendentals=0),
        name="hidden_grad",
    )(scal, df, keep, recv, low_in, inner, g1, g2)


def k5_body(scal_ref, small_ref, aid_ref, hb_ref, spread_ref, gup1_ref, gd2_ref, gqkv_ref, gdd_ref, *refs):
    blocks, refs = refs[:7], refs[7:]
    keep_ref, send_ref, dy_s, sem = refs
    column = pl.multiple_of(256 * scal_ref[9], 256)
    start_all(
        [(source.at[:, pl.ds(column, 256)], part) for source, part, _ in token_copies(blocks, dy_s)], sem
    )
    first_core = scal_ref[8] == 0

    def store(section, left, right):
        kept = jnp.where(first_core, left, right)
        sent = jnp.where(first_core, right, left)
        keep_ref[:, 16 * section : 16 * section + 16] = kept.reshape(8, 16, 512)
        send_ref[:, 16 * section : 16 * section + 16] = sent.astype(BF).reshape(8, 16, 512)

    small = jnp.concatenate([small_ref[scal_ref[b]] for b in range(8)], axis=0)
    aid = aid_ref[:, 0:1].astype(F32)
    wide = jnp.where(adapter_mask(aid, 768), nn(small, spread_ref[...]), 0.0).astype(BF)
    down = tn(wide[:, :512], hb_ref[...])
    store(
        0,
        jnp.concatenate([down[:128], down[128:256]], axis=1),
        jnp.concatenate([down[256:384], down[384:]], axis=1),
    )
    store(1, gqkv_ref[:, :512], jnp.concatenate([gqkv_ref[:, 512:], gdd_ref[...]], axis=1))
    store(2, gup1_ref[:, :512], gup1_ref[:, 512:])
    store(3, gd2_ref[:, :512], gd2_ref[:, 512:])
    wait_all(dy_s, sem)
    up = tn(wide[:, 512:], dy_s[...].reshape(1024, 256))
    left = jnp.concatenate([up[:128], up[128:]], axis=1)
    store(4, left, jnp.zeros_like(left))


def k5(scal, small, aid, hb, spread, gup1, gd2, gqkv, gdd, blocks):
    def const(shape):
        return pl.BlockSpec(shape, lambda t, s: (0,) * len(shape))

    return pl.pallas_call(
        k5_body,
        grid_spec=pltpu.PrefetchScalarGridSpec(
            num_scalar_prefetch=1,
            grid=(1,),
            in_specs=[
                const((8, 128, 128)),
                const((1024, 128)),
                pl.BlockSpec((1024, 256), lambda t, s: (0, s[9])),
                const((128, 768)),
                const((128, 1024)),
                const((128, 1024)),
                const((128, 768)),
                const((128, 256)),
            ]
            + [ANY] * 7,
            out_specs=[const((8, 80, 512)), const((8, 80, 512))],
            scratch_shapes=[pltpu.VMEM((4, 2, 128, 256), BF), pltpu.SemaphoreType.DMA],
        ),
        out_shape=[jax.ShapeDtypeStruct((8, 80, 512), F32), jax.ShapeDtypeStruct((8, 80, 512), BF)],
        compiler_params=PARAMS,
        cost_estimate=pl.CostEstimate(flops=1_500_000_000, bytes_accessed=6_000_000, transcendentals=0),
        name="adapter_grads",
    )(scal, small, aid, hb, spread, gup1, gd2, gqkv, gdd, *blocks)


def kf_body(scal_ref, mine_ref, theirs_ref, down_ref, up_ref, dd_ref, ud_ref, f1d_ref, f1u_ref, f2d_ref, f2u_ref):
    lane = lax.broadcasted_iota(jnp.int32, (16, 128), 1)

    core = scal_ref[8]

    def part(j, half, section, start, width):
        rows, cols = slice(16 * section, 16 * section + 16), slice(start, start + width)
        return jnp.where(core == half, mine_ref[j, rows, cols], theirs_ref[j, rows, cols]).astype(F32)

    for j in range(8):
        block = slice(256 * j, 256 * j + 256)
        down_ref[0, :, block] = part(j, 0, 0, 0, 256)
        down_ref[1, :, block] = part(j, 0, 0, 256, 256)
        down_ref[2, :, block] = part(j, 1, 0, 0, 256)
        f1d_ref[:, block] = part(j, 1, 0, 256, 256)
        ud_ref[:, block] = part(j, 0, 4, 0, 256)
        f2u_ref[:, block] = part(j, 0, 4, 256, 256)
        for w in range(8):
            spot = slice(1024 * w + 128 * j, 1024 * w + 128 * j + 128)
            f1u_ref[:, spot] = part(j, w // 4, 2, 128 * (w % 4), 128)
            f2d_ref[:, spot] = part(j, w // 4, 3, 128 * (w % 4), 128)
    for i in range(4):
        for x in range(2):
            for y in range(4):
                for h in range(2):
                    start = 256 * (i % 2) + 128 * (y // 2)
                    a = part(4 * x + 2 * h, i // 2, 1, start, 128)
                    b = part(4 * x + 2 * h + 1, i // 2, 1, start, 128)
                    if y % 2:
                        a = pltpu.roll(a, 64, 1)
                    else:
                        b = pltpu.roll(b, 64, 1)
                    value = jnp.where(lane < 64, a, b)
                    spot = slice(256 * (2 * y + x) + 128 * h, 256 * (2 * y + x) + 128 * h + 128)
                    if i < 3:
                        up_ref[i, :, spot] = value
                    else:
                        dd_ref[:, spot] = value


def kf(scal, mine, theirs):
    return pl.pallas_call(
        kf_body,
        in_specs=[SMEM, VM, VM],
        out_specs=[VM] * 8,
        out_shape=[
            jax.ShapeDtypeStruct((3, 16, 2048), F32),
            jax.ShapeDtypeStruct((3, 16, 2048), F32),
            jax.ShapeDtypeStruct((16, 2048), F32),
            jax.ShapeDtypeStruct((16, 2048), F32),
            jax.ShapeDtypeStruct((16, 2048), F32),
            jax.ShapeDtypeStruct((16, 8192), F32),
            jax.ShapeDtypeStruct((16, 8192), F32),
            jax.ShapeDtypeStruct((16, 2048), F32),
        ],
        compiler_params=PARAMS,
        name="finish",
    )(scal, mine, theirs)


def kn_body(x_ref, dy_ref, gain_ref, own_ref, up_ref, down_ref, side_ref, t_ref, up2_ref, down2_ref, out_ref):
    def total(*parts):
        return sum(p[...].astype(F32) for p in parts)

    dh = jnp.concatenate([total(own_ref, up_ref, down_ref, side_ref), total(t_ref, up2_ref, down2_ref)], axis=1)
    x = x_ref[...].astype(F32)
    center = x - jnp.mean(x, axis=1, keepdims=True)
    inv = lax.rsqrt(jnp.mean(center * center, axis=1, keepdims=True) + EPSILON)
    hn = center * inv
    e = dh * gain_ref[...]
    dx = (e - jnp.mean(e, axis=1, keepdims=True) - hn * jnp.mean(e * hn, axis=1, keepdims=True)) * inv
    out_ref[...] = (dy_ref[...].astype(F32) + dx).astype(BF)


def kn(*args):
    return pl.pallas_call(
        kn_body,
        in_specs=[VM] * 10,
        out_specs=VM,
        out_shape=jax.ShapeDtypeStruct((128, 2048), BF),
        compiler_params=PARAMS,
        name="norm_grad",
    )(*args)


def pack1_body(
    scal_ref, wq, wk, wv, wd, ad_ref, fd_ref, au_ref, dd_ref, du_ref, misc_ref, b1_ref,
    own_ref, other_ref, w_s, d_s, sem, d_sem,
):
    c, z = scal_ref[8], scal_ref[11]
    start_all([(w.at[pl.ds(128 * c, 128), :], w_s.at[i]) for i, w in enumerate((wq, wk, wv))], sem)
    start_all([(wd.at[pl.ds(64 * z + 32 * c, 32), :], d_s)], d_sem)
    first_core = c == 0
    odd = lax.rem(z, 2) == 1
    targets = ((own_ref, scal_ref[10]), (other_ref, 1 - scal_ref[10]))

    def head_pair(read, rows, i, xl):
        lane = lax.broadcasted_iota(jnp.int32, (rows, 128), 1)
        parts = []
        for k in range(2):
            start = (2 * (i + k) + xl) * 256 + (z // 2) * 128
            v = read(pl.ds(pl.multiple_of(start, 128), 128)).astype(F32)
            turned = pltpu.roll(v, 64, 1)
            parts.append(jnp.where(odd, turned, v) if k == 0 else jnp.where(odd, v, turned))
        return jnp.where(lane < 64, parts[0], parts[1]).astype(BF)

    half = pl.ds(pl.multiple_of((z // 2) * 128, 128), 128)
    row = lax.broadcasted_iota(jnp.int32, (16, 128), 0)
    lane = lax.broadcasted_iota(jnp.int32, (16, 128), 1)

    def biases(xl):
        plain = misc_ref[:, :128].astype(F32), misc_ref[:, 128:256].astype(F32)
        mine = misc_ref[:, half].astype(F32)
        turned = pltpu.roll(mine, 64, 1)
        low = jnp.where(odd, turned, mine)
        high = jnp.where(odd, mine, turned)
        query_key = jnp.where(lane[:1] < 64, low[4:5], high[5:6])
        value = jnp.where(lane[:1] < 64, low[6:7], 0.0)
        hidden = jnp.where(row[:8] == xl * 4 + z, b1_ref[...].astype(F32), 0.0)
        hidden = jnp.sum(hidden, axis=0, keepdims=True)
        left = jnp.where(row < 4, plain[0], jnp.where(row == 4, query_key, hidden))
        right = jnp.where(row < 4, plain[1], value)
        return left.astype(BF), right.astype(BF)

    a = jnp.where(first_core, ad_ref[0], ad_ref[2])
    b = jnp.where(first_core, ad_ref[1], fd_ref[...])
    du = jnp.where(first_core, du_ref[:, :1024], du_ref[:, 1024:])
    for out_ref, xl in targets:
        rows_of = biases(xl)
        for p in range(4):
            for i in (0, 2):
                read = (lambda s, p=p: au_ref[p, :, s]) if p < 3 else (lambda s: dd_ref[:, s])
                value = head_pair(read, 16, i, xl)
                rows = slice(16 * p, 16 * p + 16)
                if p == 0:
                    value = jnp.where(first_core, value, rows_of[i // 2])
                out_ref[rows, 768 + 64 * i : 768 + 64 * i + 128] = value
        out_ref[64:128, 768:] = jnp.zeros((64, 256), BF)
        out_ref[128:144] = a[:, :1024]
        out_ref[144:160] = a[:, 1024:]
        out_ref[160:176] = b[:, :1024]
        out_ref[176:192] = b[:, 1024:]
        out_ref[192:208] = du
    wait_all(d_s, d_sem)
    for out_ref, _ in targets:
        out_ref[208:240] = d_s[:, :1024]
        out_ref[240:272] = d_s[:, 1024:]
    wait_all(w_s, sem)
    for p in range(3):
        for i in (0, 2):
            start = 256 * p + 64 * i
            for out_ref, xl in targets:
                out_ref[:128, start : start + 128] = head_pair(lambda s, p=p: w_s[p, :, s], 128, i, xl)


def pack1(scal, wq, wk, wv, wd, ad, fd, au, dd, du, misc, b1):
    return pl.pallas_call(
        pack1_body,
        in_specs=[SMEM] + [ANY] * 4 + [VM] * 7,
        out_specs=[VM, VM],
        out_shape=[jax.ShapeDtypeStruct((272, 1024), BF)] * 2,
        scratch_shapes=[
            pltpu.VMEM((3, 128, 2048), BF),
            pltpu.VMEM((32, 2048), BF),
            pltpu.SemaphoreType.DMA,
            pltpu.SemaphoreType.DMA,
        ],
        compiler_params=PARAMS,
        cost_estimate=pl.CostEstimate(flops=1_000_000, bytes_accessed=4_000_000, transcendentals=0),
        name="pack_qkv",
    )(scal, wq, wk, wv, wd, ad, fd, au, dd, du, misc, b1)


def pack2_body(scal_ref, w1, w2, up_ref, down_ref, up2_ref, own_ref, other_ref, w1_s, w2_s, sem, sem2):
    c, z = scal_ref[8], scal_ref[11]
    places = [scal_ref[10] * 4 + z, (1 - scal_ref[10]) * 4 + z]
    start_all([(w1.at[pl.ds(128 * c, 128), :], w1_s)], sem)
    start_all([(w2.at[pl.ds(128 * places[i] + 64 * c, 64), :], w2_s.at[i]) for i in range(2)], sem2)
    first_core = c == 0
    up2 = jnp.where(first_core, up2_ref[:, :1024], up2_ref[:, 1024:])

    def column(w, i):
        return pl.ds(pl.multiple_of(1024 * w + 128 * places[i], 128), 128)

    for i, out_ref in enumerate((own_ref, other_ref)):
        out_ref[272:288] = up2
        for w in range(8):
            out_ref[128:144, 128 * w : 128 * w + 128] = jnp.where(
                first_core, up_ref[:, column(w, i)], down_ref[:, column(w, i)]
            )
    wait_all(w2_s, sem2)
    for i, out_ref in enumerate((own_ref, other_ref)):
        out_ref[144:208] = w2_s[i, :, :1024]
        out_ref[208:272] = w2_s[i, :, 1024:]
    wait_all(w1_s, sem)
    for i, out_ref in enumerate((own_ref, other_ref)):
        for w in range(8):
            out_ref[:128, 128 * w : 128 * w + 128] = w1_s[:, column(w, i)]


def pack2(scal, w1, w2, up, down, up2):
    return pl.pallas_call(
        pack2_body,
        in_specs=[SMEM, ANY, ANY, VM, VM, VM],
        out_specs=[VM, VM],
        out_shape=[jax.ShapeDtypeStruct((288, 1024), BF)] * 2,
        scratch_shapes=[
            pltpu.VMEM((128, 8192), BF),
            pltpu.VMEM((2, 64, 2048), BF),
            pltpu.SemaphoreType.DMA,
            pltpu.SemaphoreType.DMA,
        ],
        compiler_params=PARAMS,
        cost_estimate=pl.CostEstimate(flops=1_000_000, bytes_accessed=5_000_000, transcendentals=0),
        name="pack_hidden",
    )(scal, w1, w2, up, down, up2)


def rotary_tables(positions):
    lane = np.arange(128) % 64
    rate = np.where(lane < 32, 10000.0 ** (-2.0 * (lane % 16) / 32.0), 0.0).astype(np.float32)
    sign = np.where(lane < 16, -1.0, 1.0).astype(np.float32)
    angles = positions.astype(F32)[:, None] * jnp.asarray(rate)[None, :]
    return jnp.cos(angles), jnp.sin(angles) * jnp.asarray(sign)[None, :]


def fold_matrix():
    row = np.arange(768)
    target = (row // 128) * 16 + row % 16
    return jnp.asarray((target[:, None] == np.arange(128)[None, :]).astype(np.float32)).astype(BF)


def halves(a):
    m = a.shape[1] // 2
    return jnp.concatenate([a[:, :m], a[:, m:]], axis=0)


SWAP = [(0, 1), (1, 0)]
FLIP = [(i, 3 - i) for i in range(4)]
UP = [(i, (i + 1) % 4) for i in range(4)]
DOWN = [(i, (i + 3) % 4) for i in range(4)]
Z_OFFSETS = (0, -1, 1, 2)


def together(*values):
    return lax.optimization_barrier(values)


def up(a):
    return lax.ppermute(a, "z", UP)


def down(a):
    return lax.ppermute(a, "z", DOWN)


def across(a):
    return lax.ppermute(a, "xl", SWAP)


def gather_pair(own, other, single):
    xh = lax.axis_index("xh")
    parts = [jnp.where(xh == 0, own, other), jnp.where(xh == 0, other, own)]
    if single is not None:
        parts.append(single)
    packed = jnp.concatenate(parts, axis=0)
    g = lax.all_gather(packed, ("y", "c"), axis=0, tiled=False)
    return g.reshape((4, 2) + packed.shape)


def add(*terms):
    return sum(t.astype(F32) for t in terms)


def scatter_sum(near, owns, sides):
    own, side, down_own, down_side, up_own, up_side, far_own, far_side = [near[b] for b in range(8)]
    from_side = lax.ppermute(sides, "xl", SWAP)
    via_below = lax.ppermute(far_own, "z", UP)
    via_above = lax.ppermute(far_side, "z", DOWN)
    up_side = lax.ppermute(up_side, "z", UP)
    down_own = lax.ppermute(down_own, "z", DOWN)
    up_own = lax.ppermute(add(up_own, via_below).astype(BF), "z", UP)
    down_side = lax.ppermute(add(down_side, via_above).astype(BF), "z", DOWN)
    side = lax.ppermute(add(side, up_side, down_side).astype(BF), "xl", SWAP)
    t = add(owns, from_side)
    far = t[3].astype(BF)
    half_up = lax.ppermute(far[:64], "z", UP)
    half_down = lax.ppermute(far[64:], "z", DOWN)
    up = jnp.concatenate([t[2, :64] + half_up.astype(F32), t[2, 64:]], axis=0).astype(BF)
    down = jnp.concatenate([t[1, :64], t[1, 64:] + half_down.astype(F32)], axis=0).astype(BF)
    return own, up_own, down_own, side, t[0], lax.ppermute(up, "z", UP), lax.ppermute(down, "z", DOWN)


def local(
    inputs,
    output_cotangent,
    block_index_per_position,
    adapter_index_per_run,
    norm_gain,
    norm_bias,
    query_weight,
    key_weight,
    value_weight,
    dense_weight,
    query_bias,
    key_bias,
    value_bias,
    dense_bias,
    feedforward_in_weight,
    feedforward_in_bias,
    feedforward_out_weight,
    feedforward_out_bias,
    adapter_attention_down,
    adapter_attention_up,
    adapter_dense_down,
    adapter_dense_up,
    adapter_feedforward_in_down,
    adapter_feedforward_in_up,
    adapter_feedforward_out_down,
    adapter_feedforward_out_up,
):
    xl, z, c = lax.axis_index("xl"), lax.axis_index("z"), lax.axis_index("c")
    xh = lax.axis_index("xh")
    j = xl * 4 + z
    x_own = inputs[0]
    dy_own = output_cotangent[0]
    run_adapter = adapter_index_per_run[0, 0].astype(F32).astype(BF)
    block_row = block_index_per_position[0]
    z_of = [lax.rem(z + o + 4, 4) for o in Z_OFFSETS]
    spots = [(xl if side == 0 else 1 - xl) * 4 + zz for zz in z_of for side in range(2)]
    scal = jnp.stack(spots + [c, j, xl, z] + z_of).astype(jnp.int32)

    zero = jnp.zeros((256,), BF)
    misc_own = jnp.stack(
        [norm_gain, norm_bias, dense_bias, feedforward_out_bias, query_bias, key_bias, value_bias] + [zero] * 9
    )
    sent1, for_other = pack1(
        scal,
        query_weight,
        key_weight,
        value_weight,
        dense_weight,
        adapter_attention_down[0],
        adapter_feedforward_in_down[0],
        adapter_attention_up[0],
        adapter_dense_down[0],
        adapter_dense_up[0],
        misc_own,
        feedforward_in_bias.reshape(8, 128),
    )
    own2, own2_for_other = pack2(
        scal,
        feedforward_in_weight,
        feedforward_out_weight,
        adapter_feedforward_in_up[0],
        adapter_feedforward_out_down[0],
        adapter_feedforward_out_up[0],
    )
    spread = jnp.stack(spots)
    my_positions = ((spread * 2 + c) * 128)[:, None] + jnp.arange(128, dtype=jnp.int32)[None, :]
    tables = rotary_tables(my_positions.reshape(1024)) + rotary_tables(jnp.arange(2048, dtype=jnp.int32))
    tables = tables + (jnp.broadcast_to(block_row[:, None], (2048, 128)),)
    x_send = jnp.concatenate([x_own, jnp.full((128, 128), run_adapter, BF)], axis=1)

    x_up, x_down, x_side = together(up(x_send), down(x_send), across(x_send), for_other)[:3]
    other1 = lax.ppermute(for_other, ("xl", "xh"), FLIP)
    x_up_side, x_down_side, dy_side = together(up(x_side), down(x_side), across(together(dy_own, x_side)[0]))
    other1, own2, own2_for_other, x_up, x_down, dy_side = together(
        other1, own2, own2_for_other, x_up, x_down, dy_side, x_up_side, x_down_side
    )[:6]
    g1 = gather_pair(sent1[:MAIN], other1[:MAIN], jnp.where(xh == xl, sent1[MAIN:], other1[MAIN:]))
    dy_own = together(dy_own, dy_side)[0]
    x_far_a, x_far_b, dy_up, dy_down, other2, tables = together(
        up(x_up[:64]),
        down(x_down[64:]),
        up(dy_own),
        down(dy_own),
        lax.ppermute(own2_for_other, ("xl", "xh"), FLIP),
        tables,
    )
    g2 = gather_pair(own2, other2, None)
    x_far_side = across(jnp.concatenate([x_far_a, x_far_b], axis=0))
    dy_up_more, dy_down_more, x_far_side = together(
        up(jnp.concatenate([dy_side, dy_up[:64]], axis=0)),
        down(jnp.concatenate([dy_side, dy_down[64:]], axis=0)),
        x_far_side,
    )
    dy_far_side = across(jnp.concatenate([dy_up_more[128:], dy_down_more[128:]], axis=0))
    x_blocks = [x_send, x_side, x_up, x_down, x_up_side, x_down_side, x_far_a, x_far_b, x_far_side]
    dy_blocks = [dy_own, dy_side, dy_up, dy_down, dy_up_more, dy_down_more, dy_far_side]

    def side_of(core):
        return jnp.stack(
            [g1[:, core, MAIN * h : MAIN * h + 64, 768:] for h in range(2)], axis=1
        ).reshape(8, 64, 256)

    ups_all = side_of(0).reshape(8, 4, 16, 256).transpose(1, 0, 2, 3).reshape(4, 128, 256)
    ups = jnp.concatenate([ups_all[0], ups_all[1], ups_all[2]], axis=1)
    dd = ups_all[3]
    small_all = side_of(1)[:, :6].astype(F32)
    misc = small_all[:, :4].transpose(1, 0, 2).reshape(4, 2048)
    head_b = lax.dynamic_index_in_dim(small_all[:, 4, :192].reshape(4, 2, 3, 64), xl, 1, keepdims=False)
    bias_qkv = head_b.transpose(1, 0, 2).reshape(1, 768)
    b1 = small_all[:, 5, :128].reshape(1, 1024)

    cos_mine, sin_mine, cos_all, sin_all, idcol = tables

    hb, inner, qkv_keep, qkv_send, aid = k1(x_blocks, scal, g1, ups, misc[:2], bias_qkv, cos_mine, sin_mine)
    qkv_recv = lax.ppermute(qkv_send, "c", SWAP)
    dob_keep, dob_send, gdense = k1b(dy_blocks, scal, aid, g1, dd)
    dob_recv = lax.ppermute(dob_send, "c", SWAP)

    idrow = jnp.broadcast_to(block_row[None, :], (8, 2048))
    att_keep, att_send = k3(scal, qkv_keep, qkv_recv, dob_keep, dob_recv, idrow, idcol, cos_all, sin_all)
    att_recv = lax.ppermute(att_send, "c", SWAP)

    fold = fold_matrix()
    gb, df, low_out, low_in, small, gup1, gd2, gdd = k2m(
        dy_blocks, scal, hb, aid, inner, gdense, att_keep, att_recv, g2, ups, dd, b1, fold
    )
    small = lax.all_to_all(small.reshape(8, 128, 128), TP, 0, 0, tiled=True)
    out_part = k2o(scal, gb, att_keep, att_recv, low_out, g1, g2)
    out_part, small, df = together(out_part, small, df)
    small = jnp.sum(small.astype(F32), axis=0).astype(BF)
    small = lax.all_to_all(jnp.broadcast_to(small[None], (8, 128, 128)), TP, 0, 0, tiled=True)
    out_sum = lax.psum_scatter(out_part.reshape(1024, 2048), TP, scatter_dimension=0, tiled=True)
    near, owns, sides, gqkv = k2h(scal, df, att_keep, att_recv, low_in, inner, g1, g2)
    shares = scatter_sum(near, owns, sides)

    keep, send = k5(scal, small, aid, hb, fold.T, gup1, gd2, gqkv, gdd, dy_blocks)
    grads = (keep + lax.ppermute(send, "c", SWAP).astype(F32)).astype(BF)
    grads = lax.all_to_all(grads, WSH, 0, 0, tiled=True)
    grads = jnp.sum(grads.astype(F32), axis=0).astype(BF)
    grads = lax.all_to_all(jnp.broadcast_to(grads[None], (8, 80, 512)), TP, 0, 0, tiled=True)
    down_qkv, up_qkv, gdd, gud, gf1d, gf1u, gf2d, gf2u = kf(scal, grads, lax.ppermute(grads, "c", SWAP))

    source = x_own.astype(F32)
    outputs = (source + out_sum.astype(F32) + misc[2:3] + misc[3:4]).astype(BF)[None]
    *shares, outputs = together(*shares, outputs)
    grad_inputs = kn(x_own, output_cotangent[0], misc[0:1], *shares)[None]
    return (
        outputs,
        grad_inputs,
        down_qkv[None],
        up_qkv[None],
        gdd[None],
        gud[None],
        gf1d[None],
        gf1u[None],
        gf2d[None],
        gf2u[None],
    )


def solution(mesh):
    fine = Mesh(np.asarray(mesh.devices).reshape(2, 4, 2, 4, 2), ("xl", "z", "c", "y", "xh"))
    tokens = P(WSH, CTX, None)
    w1 = P(WSH)
    w2 = P(WSH, None)
    w3 = P(WSH, None, None)
    w4 = P(WSH, None, None, None)
    placed = (tokens, tokens, w2, P(WSH, CTX)) + (w1, w1, w2, w2, w2, w2, w1, w1, w1, w1, w2, w1, w2, w1)
    placed = placed + (w4, w4, w3, w3, w3, w3, w3, w3)
    return jax.shard_map(
        local,
        mesh=fine,
        in_specs=placed,
        out_specs=(tokens, tokens, w4, w4, w3, w3, w3, w3, w3, w3),
        check_vma=False,
    )
```

```python
import functools

import jax
import jax.numpy as jnp
import numpy as np
from jax import lax
from jax.experimental import pallas as pl
from jax.experimental.pallas import tpu as pltpu
from jax.sharding import Mesh, PartitionSpec as P

ADAPTERS = 8
RANK = 16
EPSILON = 1e-05
GELU_SCALE = 0.7978845608028654
NEGATIVE = -1e30
SCALE = 64 ** -0.5
BF = jnp.bfloat16
F32 = jnp.float32
WSH = ("y", "xh")
TP = ("xl", "z")
CTX = ("xl", "z", "c")
VMEM_LIMIT = 58 * 1024 * 1024


def nn(a, b):
    return lax.dot_general(a, b, (((1,), (0,)), ((), ())), preferred_element_type=F32)


def nt(a, b):
    return lax.dot_general(a, b, (((1,), (1,)), ((), ())), preferred_element_type=F32)


def tn(a, b):
    return lax.dot_general(a, b, (((0,), (0,)), ((), ())), preferred_element_type=F32)


def adapter_mask(aid, columns):
    col = lax.broadcasted_iota(jnp.int32, (aid.shape[0], columns), 1)
    return (lax.shift_right_logical(col, 4) & 7) == aid.astype(jnp.int32)


def turn(values, cosine, sine):
    width = values.shape[1]
    lane = lax.broadcasted_iota(jnp.int32, values.shape, 1) & 63
    partner = jnp.where(
        lane < 16, pltpu.roll(values, width - 16, 1), pltpu.roll(values, 16, 1)
    )
    return values * cosine + partner * sine


ANY = pl.BlockSpec(memory_space=pl.ANY)
SMEM = pl.BlockSpec(memory_space=pltpu.SMEM)
VM = pl.BlockSpec(memory_space=pltpu.VMEM)
PARAMS = pltpu.CompilerParams(vmem_limit_bytes=VMEM_LIMIT)
MAIN = 208
SECOND = 288
NEAR = 1280


def whole(shape):
    return pl.BlockSpec(shape, lambda t: (0,) * len(shape), pipeline_mode=pl.Buffered(1))


def start_all(pairs, sem):
    for source, target in pairs:
        pltpu.make_async_copy(source, target, sem).start()


def wait_all(target, sem):
    pltpu.make_async_copy(target, target, sem).wait()


def token_copies(blocks, target):
    if len(blocks) == 7:
        own, side, above, below, up_more, down_more, far_side = blocks
        side_above, far_a = up_more.at[pl.ds(0, 128), :], up_more.at[pl.ds(128, 64), :]
        side_below, far_b = down_more.at[pl.ds(0, 128), :], down_more.at[pl.ds(128, 64), :]
    else:
        own, side, above, below, side_above, side_below, far_a, far_b, far_side = blocks
    return [
        (own, target.at[0, 0], 0),
        (side, target.at[0, 1], 1),
        (above, target.at[1, 0], 2),
        (side_above, target.at[1, 1], 3),
        (below, target.at[2, 0], 4),
        (side_below, target.at[2, 1], 5),
        (far_a, target.at[3, 0, pl.ds(0, 64)], 6),
        (far_b, target.at[3, 0, pl.ds(64, 64)], 6),
        (far_side, target.at[3, 1], 7),
    ]


def start_tokens(blocks, target, sem, first, last):
    for source, part, i in token_copies(blocks, target):
        if first <= i < last:
            pltpu.make_async_copy(source, part, sem.at[i]).start()


def wait_tokens(target, sem, step):
    for i in range(2):
        part = target.at[step, i]
        pltpu.make_async_copy(part, part, sem.at[2 * step + i]).wait()


def pieces_qkv(g1, target):
    return [
        (
            g1.at[y, c, pl.ds(MAIN * xh, 128), pl.ds(0, 768)],
            target.at[pl.ds((2 * y + xh) * 256 + c * 128, 128), :],
        )
        for y in range(4)
        for xh in range(2)
        for c in range(2)
    ]


def pieces_downs(g1, target):
    return [
        (
            g1.at[:, c, pl.ds(MAIN * xh + 128 + 32 * i + 16 * b, 16), :],
            target.at[c, i, :, xh, :, pl.ds(1024 * b, 1024)],
        )
        for c in range(2)
        for i in range(2)
        for xh in range(2)
        for b in range(2)
    ]


def pieces_rank(g, base, stride, target, row):
    return [
        (
            g.at[y, c, pl.ds(stride * xh + base, 16), :],
            target.at[pl.ds(row + (2 * y + xh) * 16, 16), pl.ds(1024 * c, 1024)],
        )
        for y in range(4)
        for xh in range(2)
        for c in range(2)
    ]


def pieces_dense(g1, target, row):
    return [
        (
            g1.at[y, c, pl.ds(2 * MAIN + 32 * b, 32), :],
            target.at[pl.ds(row + 64 * y + 32 * c, 32), pl.ds(1024 * b, 1024)],
        )
        for y in range(4)
        for c in range(2)
        for b in range(2)
    ]


def pieces_w1(g2, target):
    return [
        (
            g2.at[y, c, pl.ds(SECOND * xh, 128), :],
            target.at[pl.ds((2 * y + xh) * 256 + c * 128, 128), :],
        )
        for y in range(4)
        for xh in range(2)
        for c in range(2)
    ]


def pieces_sixteen(g2, c, target, row):
    return [
        (
            g2.at[y, c, pl.ds(SECOND * xh + 128, 16), :],
            target.at[pl.ds(row + (2 * y + xh) * 16, 16), :],
        )
        for y in range(4)
        for xh in range(2)
    ]


def pieces_w2(g2, target):
    return [
        (
            g2.at[y, c, pl.ds(SECOND * xh + 144 + 64 * b, 64), :],
            target.at[pl.ds((2 * y + xh) * 128 + c * 64, 64), pl.ds(1024 * b, 1024)],
        )
        for y in range(4)
        for xh in range(2)
        for c in range(2)
        for b in range(2)
    ]


def block_diagonal(source, target):
    target[...] = jnp.zeros_like(target)
    for p in range(3):
        cols = slice(256 * p, 256 * p + 256)
        target[128 * p : 128 * p + 128, cols] = source[:, cols]


def k1_body(*refs):
    blocks, refs = refs[:9], refs[9:]
    (scal_ref, g1_ref, up_ref, misc_ref, bias_ref, cos_ref, sin_ref,
     hb_ref, inner_ref, keep_ref, send_ref, aid_ref, x_s, w_s, down_s, up_s, x_sem, w_sem) = refs
    step = pl.program_id(0)

    @pl.when(step == 0)
    def _():
        start_tokens(blocks, x_s, x_sem, 0, 2)
        start_all(pieces_downs(g1_ref, down_s), w_sem.at[0])
        start_all(pieces_qkv(g1_ref, w_s.at[:, pl.ds(0, 768)]), w_sem.at[1])
        start_tokens(blocks, x_s, x_sem, 2, 8)

    wait_tokens(x_s, x_sem, step)
    tile = x_s[step].reshape(256, 2176)
    x = tile[:, :2048].astype(F32)
    aid_ref[...] = tile[:, 2048:]
    aid = tile[:, 2048:2049].astype(F32)
    mean = jnp.mean(x, axis=1, keepdims=True)
    center = x - mean
    spread = jnp.mean(center * center, axis=1, keepdims=True)
    h = center * lax.rsqrt(spread + EPSILON) * misc_ref[0:1, :] + misc_ref[1:2, :]
    hb = h.astype(BF)
    hb_ref[...] = hb

    @pl.when(step == 0)
    def _():
        block_diagonal(up_ref, up_s)
        wait_all(down_s, w_sem.at[0])
        w_s[:, 768:] = down_s[...].reshape(512, 2048).T
        wait_all(w_s.at[:, pl.ds(0, 768)], w_sem.at[1])

    pre_all = nn(hb, w_s[...])
    inner = jnp.where(adapter_mask(aid, 512), pre_all[:, 768:], 0.0).astype(BF)
    inner_ref[...] = inner
    pre_all = pre_all[:, :768] + nn(inner[:, :384], up_s[...]) + bias_ref[...]
    first_core = scal_ref[8] == 0
    cosine = jnp.concatenate([cos_ref[...]] * 2, axis=1)
    sine = jnp.concatenate([sin_ref[...]] * 2, axis=1)
    for p in range(3):
        cols = slice(256 * p, 256 * p + 256)
        pre = pre_all[:, cols]
        if p < 2:
            pre = turn(pre, cosine, sine)
        low = pre.astype(BF)
        keep_ref[p] = jnp.where(first_core, low[:, :128], low[:, 128:])
        send_ref[p] = jnp.where(first_core, low[:, 128:], low[:, :128])


def k1(blocks, scal, g1, ups, misc, bias, cosine, sine):
    rows = 256
    return pl.pallas_call(
        k1_body,
        grid=(4,),
        in_specs=[ANY] * 9
        + [
            SMEM,
            ANY,
            whole((128, 768)),
            whole((2, 2048)),
            whole((1, 768)),
            pl.BlockSpec((rows, 128), lambda t: (t, 0)),
            pl.BlockSpec((rows, 128), lambda t: (t, 0)),
        ],
        out_specs=[
            pl.BlockSpec((rows, 2048), lambda t: (t, 0)),
            pl.BlockSpec((rows, 512), lambda t: (t, 0)),
            pl.BlockSpec((3, rows, 128), lambda t: (0, t, 0)),
            pl.BlockSpec((3, rows, 128), lambda t: (0, t, 0)),
            pl.BlockSpec((rows, 128), lambda t: (t, 0)),
        ],
        out_shape=[
            jax.ShapeDtypeStruct((1024, 2048), BF),
            jax.ShapeDtypeStruct((1024, 512), BF),
            jax.ShapeDtypeStruct((3, 1024, 128), BF),
            jax.ShapeDtypeStruct((3, 1024, 128), BF),
            jax.ShapeDtypeStruct((1024, 128), BF),
        ],
        scratch_shapes=[
            pltpu.VMEM((4, 2, 128, 2176), BF),
            pltpu.VMEM((2048, 1280), BF),
            pltpu.VMEM((2, 2, 4, 2, 16, 2048), BF),
            pltpu.VMEM((384, 768), BF),
            pltpu.SemaphoreType.DMA((8,)),
            pltpu.SemaphoreType.DMA((2,)),
        ],
        compiler_params=PARAMS,
        cost_estimate=pl.CostEstimate(flops=6_000_000_000, bytes_accessed=20_000_000, transcendentals=0),
        name="norm_qkv",
    )(*blocks, scal, g1, ups, misc, bias, cosine, sine)


def k1b_body(*refs):
    blocks, refs = refs[:7], refs[7:]
    scal_ref, aid_ref, g1_ref, dd_ref, keep_ref, send_ref, ginner_ref, dy_s, w_s, dy_sem, w_sem = refs
    start_all(pieces_dense(g1_ref, w_s, 0) + pieces_rank(g1_ref, 192, MAIN, w_s, 256), w_sem)
    start_tokens(blocks, dy_s, dy_sem, 0, 8)
    wait_all(w_s, w_sem)
    for step in range(4):
        wait_tokens(dy_s, dy_sem, step)
    first_core = scal_ref[8] == 0
    both = nt(dy_s[...].reshape(1024, 2048), w_s[...])
    aid = aid_ref[:, 0:1].astype(F32)
    ginner = jnp.where(adapter_mask(aid, 128), both[:, 256:], 0.0).astype(BF)
    ginner_ref[...] = ginner
    dob = (both[:, :256] + nn(ginner, dd_ref[...])).astype(BF)
    keep_ref[...] = jnp.where(first_core, dob[:, :128], dob[:, 128:])
    send_ref[...] = jnp.where(first_core, dob[:, 128:], dob[:, :128])


def k1b(blocks, scal, aid, g1, dd):
    return pl.pallas_call(
        k1b_body,
        in_specs=[ANY] * 7 + [SMEM, VM, ANY, VM],
        out_specs=[VM, VM, VM],
        out_shape=[jax.ShapeDtypeStruct((1024, 128), BF)] * 3,
        scratch_shapes=[
            pltpu.VMEM((4, 2, 128, 2048), BF),
            pltpu.VMEM((384, 2048), BF),
            pltpu.SemaphoreType.DMA((8,)),
            pltpu.SemaphoreType.DMA,
        ],
        compiler_params=PARAMS,
        cost_estimate=pl.CostEstimate(flops=2_000_000_000, bytes_accessed=8_000_000, transcendentals=0),
        name="attention_output_grad",
    )(*blocks, scal, aid, g1, dd)


def k3_body(
    scal_ref, qkv_keep, qkv_recv, dob_keep, dob_recv, idrow_ref, idcol_ref, cos_ref, sin_ref,
    keep_out, send_out, x_s, out_s, kt_s, vt_s, dk_s, dv_s, sem, sem_out,
):
    core = scal_ref[8]
    copies = []
    for b in range(8):
        rows = pl.ds(128 * b, 128)
        spot = scal_ref[b]
        for side, (qkv, dob) in enumerate(((qkv_keep, dob_keep), (qkv_recv, dob_recv))):
            parity = core if side == 0 else 1 - core
            copies.append((qkv.at[:, rows, :], x_s.at[pl.ds(0, 3), spot, parity]))
            copies.append((dob.at[rows, :], x_s.at[3, spot, parity]))
    start_all(copies, sem)
    dk_s[...] = jnp.zeros_like(dk_s)
    dv_s[...] = jnp.zeros_like(dv_s)
    wait_all(x_s, sem)
    kt_s[...] = x_s[1].reshape(2048, 128).T
    vt_s[...] = x_s[2].reshape(2048, 128).T
    tile = 256
    lane = lax.broadcasted_iota(jnp.int32, (tile, 128), 1)

    def span(i, start, stop):
        return x_s[i, start // 256 : stop // 256].reshape(stop - start, 128)

    for t in range(8):
        start, stop = tile * t, tile * t + tile
        length = min(stop + tile, 2048)
        q = span(0, start, stop)
        dob = span(3, start, stop)
        zero = jnp.zeros_like(q)
        q = q * jnp.asarray(SCALE, BF)
        q2 = jnp.concatenate([jnp.where(lane < 64, q, zero), jnp.where(lane < 64, zero, q)], axis=0)
        d2 = jnp.concatenate([jnp.where(lane < 64, dob, zero), jnp.where(lane < 64, zero, dob)], axis=0)
        query_ids = idrow_ref[0:1, start:stop]
        query_ids = jnp.concatenate([query_ids, query_ids], axis=1)
        allowed = idcol_ref[start:length, 0:1] <= query_ids
        s = jnp.where(allowed, nt(span(1, start, length), q2), NEGATIVE)
        largest = jnp.max(s, axis=0, keepdims=True)
        if start:
            s_head = nt(span(1, 0, start), q2)
            largest = jnp.maximum(largest, jnp.max(s_head, axis=0, keepdims=True))
            s = jnp.concatenate([s_head, s], axis=0)
        e = jnp.exp(s - largest)
        recip = 1.0 / jnp.sum(e, axis=0, keepdims=True)
        p = e * recip
        pb = p.astype(BF)
        ot = nn(vt_s[:, :length], pb)
        dp = nt(span(2, 0, length), d2)
        o_parts = [ot[:64, :256], ot[64:, 256:]]
        dobt = dob.astype(F32).T
        delta = jnp.concatenate(
            [
                jnp.sum(o_parts[0] * dobt[:64], axis=0, keepdims=True),
                jnp.sum(o_parts[1] * dobt[64:], axis=0, keepdims=True),
            ],
            axis=1,
        )
        ds = (p * (dp - delta)).astype(BF)
        dk_s[:length] += nn(ds, q2)
        dv_s[:length] += nn(pb, d2)
        dqt = nn(kt_s[:, :length], ds)
        dq_parts = [dqt[:64, :256], dqt[64:, 256:]]
        o = jnp.concatenate(o_parts, axis=0).T
        dq = jnp.concatenate(dq_parts, axis=0).T * SCALE
        rows = slice(start, stop)
        out_s[0, t] = o.astype(BF).reshape(2, 128, 128)
        out_s[1, t] = turn(dq, cos_ref[rows], -sin_ref[rows]).astype(BF).reshape(2, 128, 128)
    out_s[2] = turn(dk_s[...], cos_ref[...], -sin_ref[...]).astype(BF).reshape(8, 2, 128, 128)
    out_s[3] = dv_s[...].astype(BF).reshape(8, 2, 128, 128)
    copies = []
    for b in range(8):
        rows = pl.ds(128 * b, 128)
        spot = scal_ref[b]
        copies.append((out_s.at[:, spot, core], keep_out.at[:, rows, :]))
        copies.append((out_s.at[:, spot, 1 - core], send_out.at[:, rows, :]))
    start_all(copies, sem_out)
    wait_all(out_s, sem_out)


def k3(scal, qkv_keep, qkv_recv, dob_keep, dob_recv, idrow, idcol, cosine, sine):
    vm = pl.BlockSpec(memory_space=pltpu.VMEM)
    return pl.pallas_call(
        k3_body,
        in_specs=[SMEM] + [ANY] * 4 + [vm] * 4,
        out_specs=[ANY, ANY],
        out_shape=[jax.ShapeDtypeStruct((4, 1024, 128), BF)] * 2,
        scratch_shapes=[
            pltpu.VMEM((4, 8, 2, 128, 128), BF),
            pltpu.VMEM((4, 8, 2, 128, 128), BF),
            pltpu.VMEM((128, 2048), BF),
            pltpu.VMEM((128, 2048), BF),
            pltpu.VMEM((2048, 128), F32),
            pltpu.VMEM((2048, 128), F32),
            pltpu.SemaphoreType.DMA,
            pltpu.SemaphoreType.DMA,
        ],
        compiler_params=PARAMS,
        cost_estimate=pl.CostEstimate(flops=15_000_000_000, bytes_accessed=8_000_000, transcendentals=5_000_000),
        name="attention",
    )(scal, qkv_keep, qkv_recv, dob_keep, dob_recv, idrow, idcol, cosine, sine)


def heads_of(keep_ref, recv_ref, i, first_core):
    a, b = keep_ref[i], recv_ref[i]
    return jnp.concatenate([jnp.where(first_core, a, b), jnp.where(first_core, b, a)], axis=1)


def tile_spec(width, rows=256):
    return pl.BlockSpec((rows, width), lambda t, s: (t, 0))


def const_spec(shape):
    return pl.BlockSpec(shape, lambda t, s: (0,) * len(shape), pipeline_mode=pl.Buffered(1))


def placed_spec(width):
    return pl.BlockSpec((2, 1, 128, width), lambda t, s: (0, s[12 + t], 0, 0))


def place(ref, xl, value):
    ref[xl, 0] = value[:128]
    ref[1 - xl, 0] = value[128:]


def accumulate(step, pairs):
    @pl.when(step == 0)
    def _():
        for ref, value in pairs:
            ref[...] = value

    @pl.when(step > 0)
    def _():
        for ref, value in pairs:
            ref[...] += value


def k2m_body(scal_ref, *refs):
    blocks, refs = refs[:7], refs[7:]
    (hb_ref, aid_ref, inner_ref, gdense_ref, keep_ref, recv_ref, g2_ref, up_ref, dd_ref, b1_ref, fold_ref,
     gb_ref, df_ref, low_out_ref, low_in_ref, small_ref, gup1_ref, gd2_ref, gdd_ref,
     dy_s, w1_s, w2_s, d2_s, up_s, dy_sem, sems) = refs
    step = pl.program_id(0)

    @pl.when(step == 0)
    def _():
        start_all(pieces_w1(g2_ref, w1_s) + pieces_sixteen(g2_ref, 0, w1_s, 2048), sems.at[0])
        start_all(pieces_sixteen(g2_ref, 1, d2_s, 0), sems.at[1])
        start_tokens(blocks, dy_s, dy_sem, 0, 2)
        start_all(pieces_w2(g2_ref, w2_s) + pieces_rank(g2_ref, 272, SECOND, w2_s, 1024), sems.at[2])
        start_tokens(blocks, dy_s, dy_sem, 2, 8)
        block_diagonal(up_ref, up_s)
        wait_all(w1_s, sems.at[0])

    aid = aid_ref[:, 0:1].astype(F32)
    first_core = scal_ref[8] == 0
    f = nn(jnp.concatenate([hb_ref[...], inner_ref[...]], axis=1), w1_s[...]) + b1_ref[...]

    @pl.when(step == 0)
    def _():
        wait_all(w2_s, sems.at[2])
        wait_all(d2_s, sems.at[1])

    wait_tokens(dy_s, dy_sem, step)
    wide = nt(dy_s[step].reshape(256, 2048), w2_s[...])
    square = f * f
    th = jnp.tanh(GELU_SCALE * f * (1.0 + 0.044715 * square))
    half = 0.5 * (1.0 + th)
    gb = (f * half).astype(BF)
    gb_ref[...] = gb
    slope = half + (0.5 * GELU_SCALE) * f * (1.0 - th * th) * (1.0 + 3 * 0.044715 * square)
    ginner2 = jnp.where(adapter_mask(aid, 128), wide[:, 1024:], 0.0).astype(BF)
    ob = heads_of(keep_ref, recv_ref, 0, first_core)
    dpre = jnp.concatenate([heads_of(keep_ref, recv_ref, p, first_core) for p in (1, 2, 3)], axis=1)
    inner2 = nt(gb, d2_s[...])
    innerd = nt(ob, dd_ref[...])
    ginner = nt(dpre, up_s[...])
    df = ((wide[:, :1024] + nn(ginner2, d2_s[...])) * slope).astype(BF)
    df_ref[...] = df
    ginner1 = nt(df, w1_s[2048:])
    low = jnp.concatenate([ginner, ginner1, innerd, inner2], axis=1)
    low = jnp.where(adapter_mask(aid, 768), low, 0.0).astype(BF)
    low_in_ref[...] = low[:, :512]
    low_out_ref[...] = low[:, 512:]
    place(small_ref, scal_ref[10], nn(low, fold_ref[...]).astype(BF))
    accumulate(
        step,
        [
            (gup1_ref, tn(inner_ref[...], df)),
            (gd2_ref, tn(ginner2, gb)),
            (gdd_ref, tn(gdense_ref[...], ob)),
        ],
    )


def att_spec(first, count):
    return pl.BlockSpec((count, 256, 128), lambda t, s: (first, t, 0))


def k2m(blocks, scal, hb, aid, inner, gdense, keep, recv, g2, ups, dd, b1, fold):
    return pl.pallas_call(
        k2m_body,
        grid_spec=pltpu.PrefetchScalarGridSpec(
            num_scalar_prefetch=1,
            grid=(4,),
            in_specs=[ANY] * 7
            + [
                tile_spec(2048),
                tile_spec(128),
                pl.BlockSpec((256, 128), lambda t, s: (t, 3)),
                tile_spec(128),
                att_spec(0, 4),
                att_spec(0, 4),
                ANY,
                const_spec((128, 768)),
                const_spec((128, 256)),
                const_spec((1, 1024)),
                const_spec((768, 128)),
            ],
            out_specs=[
                tile_spec(1024),
                tile_spec(1024),
                tile_spec(256),
                tile_spec(512),
                placed_spec(128),
                const_spec((128, 1024)),
                const_spec((128, 1024)),
                const_spec((128, 256)),
            ],
            scratch_shapes=[
                pltpu.VMEM((4, 2, 128, 2048), BF),
                pltpu.VMEM((2176, 1024), BF),
                pltpu.VMEM((1152, 2048), BF),
                pltpu.VMEM((128, 1024), BF),
                pltpu.VMEM((384, 768), BF),
                pltpu.SemaphoreType.DMA((8,)),
                pltpu.SemaphoreType.DMA((3,)),
            ],
        ),
        out_shape=[
            jax.ShapeDtypeStruct((1024, 1024), BF),
            jax.ShapeDtypeStruct((1024, 1024), BF),
            jax.ShapeDtypeStruct((1024, 256), BF),
            jax.ShapeDtypeStruct((1024, 512), BF),
            jax.ShapeDtypeStruct((2, 4, 128, 128), BF),
            jax.ShapeDtypeStruct((128, 1024), F32),
            jax.ShapeDtypeStruct((128, 1024), F32),
            jax.ShapeDtypeStruct((128, 256), F32),
        ],
        compiler_params=PARAMS,
        cost_estimate=pl.CostEstimate(flops=14_000_000_000, bytes_accessed=30_000_000, transcendentals=1_000_000),
        name="feed_forward",
    )(scal, *blocks, hb, aid, inner, gdense, keep, recv, g2, ups, dd, b1, fold)


def k2o_body(scal_ref, gb_ref, keep_ref, recv_ref, low_ref, g1_ref, g2_ref, out_ref, w_s, sem):
    step = pl.program_id(0)

    @pl.when(step == 0)
    def _():
        start_all(
            pieces_w2(g2_ref, w_s)
            + pieces_dense(g1_ref, w_s, 1024)
            + pieces_rank(g1_ref, 192, MAIN, w_s, 1280)
            + pieces_rank(g2_ref, 272, SECOND, w_s, 1408),
            sem,
        )
        wait_all(w_s, sem)

    ob = heads_of(keep_ref, recv_ref, 0, scal_ref[8] == 0)
    out = nn(jnp.concatenate([gb_ref[...], ob, low_ref[...]], axis=1), w_s[...]).astype(BF)
    place(out_ref, scal_ref[10], out)


def k2o(scal, gb, keep, recv, low_out, g1, g2):
    return pl.pallas_call(
        k2o_body,
        grid_spec=pltpu.PrefetchScalarGridSpec(
            num_scalar_prefetch=1,
            grid=(4,),
            in_specs=[tile_spec(1024), att_spec(0, 1), att_spec(0, 1), tile_spec(256), ANY, ANY],
            out_specs=[placed_spec(2048)],
            scratch_shapes=[pltpu.VMEM((1536, 2048), BF), pltpu.SemaphoreType.DMA],
        ),
        out_shape=[jax.ShapeDtypeStruct((2, 4, 128, 2048), BF)],
        compiler_params=PARAMS,
        cost_estimate=pl.CostEstimate(flops=7_000_000_000, bytes_accessed=14_000_000, transcendentals=0),
        name="out_rows",
    )(scal, gb, keep, recv, low_out, g1, g2)[0]


def k2h_body(
    scal_ref, df_ref, keep_ref, recv_ref, low_ref, inner_ref, g1_ref, g2_ref,
    near_ref, owns_ref, sides_ref, gqkv_ref, w_s, down_s, sems,
):
    step = pl.program_id(0)

    @pl.when(step == 0)
    def _():
        start_all(
            pieces_w1(g2_ref, w_s.at[:, pl.ds(0, 1024)]) + pieces_qkv(g1_ref, w_s.at[:, pl.ds(1024, 768)]), sems.at[0]
        )
        start_all(pieces_downs(g1_ref, down_s), sems.at[1])
        wait_all(w_s, sems.at[0])
        wait_all(down_s, sems.at[1])

    first_core = scal_ref[8] == 0
    dpre = [heads_of(keep_ref, recv_ref, p, first_core) for p in (1, 2, 3)]
    dh = nt(jnp.concatenate([df_ref[...]] + dpre, axis=1), w_s[...])
    dh = (dh + nn(low_ref[...], down_s[...].reshape(512, 2048))).astype(BF)
    near_ref[0] = dh[:128, :NEAR]
    near_ref[1] = dh[128:, :NEAR]
    owns_ref[0] = dh[:128, NEAR:]
    sides_ref[0] = dh[128:, NEAR:]
    gqkv = [tn(inner_ref[:, 128 * p : 128 * p + 128], dpre[p]) for p in range(3)]
    accumulate(step, [(gqkv_ref, jnp.concatenate(gqkv, axis=1))])


def k2h(scal, df, keep, recv, low_in, inner, g1, g2):
    return pl.pallas_call(
        k2h_body,
        grid_spec=pltpu.PrefetchScalarGridSpec(
            num_scalar_prefetch=1,
            grid=(4,),
            in_specs=[tile_spec(1024), att_spec(0, 4), att_spec(0, 4), tile_spec(512), tile_spec(512), ANY, ANY],
            out_specs=[
                pl.BlockSpec((2, 128, NEAR), lambda t, s: (t, 0, 0)),
                pl.BlockSpec((1, 128, 2048 - NEAR), lambda t, s: (t, 0, 0)),
                pl.BlockSpec((1, 128, 2048 - NEAR), lambda t, s: (t, 0, 0)),
                const_spec((128, 768)),
            ],
            scratch_shapes=[
                pltpu.VMEM((2048, 1792), BF),
                pltpu.VMEM((2, 2, 4, 2, 16, 2048), BF),
                pltpu.SemaphoreType.DMA((2,)),
            ],
        ),
        out_shape=[
            jax.ShapeDtypeStruct((8, 128, NEAR), BF),
            jax.ShapeDtypeStruct((4, 128, 2048 - NEAR), BF),
            jax.ShapeDtypeStruct((4, 128, 2048 - NEAR), BF),
            jax.ShapeDtypeStruct((128, 768), F32),
        ],
        compiler_params=PARAMS,
        cost_estimate=pl.CostEstimate(flops=10_000_000_000, bytes_accessed=18_000_000, transcendentals=0),
        name="hidden_grad",
    )(scal, df, keep, recv, low_in, inner, g1, g2)


def k5_body(scal_ref, small_ref, aid_ref, hb_ref, spread_ref, gup1_ref, gd2_ref, gqkv_ref, gdd_ref, *refs):
    blocks, refs = refs[:7], refs[7:]
    keep_ref, send_ref, dy_s, sem = refs
    column = pl.multiple_of(256 * scal_ref[9], 256)
    start_all(
        [(source.at[:, pl.ds(column, 256)], part) for source, part, _ in token_copies(blocks, dy_s)], sem
    )
    first_core = scal_ref[8] == 0

    def store(section, left, right):
        kept = jnp.where(first_core, left, right)
        sent = jnp.where(first_core, right, left)
        keep_ref[:, 16 * section : 16 * section + 16] = kept.reshape(8, 16, 512)
        send_ref[:, 16 * section : 16 * section + 16] = sent.astype(BF).reshape(8, 16, 512)

    small = jnp.concatenate([small_ref[scal_ref[b]] for b in range(8)], axis=0)
    aid = aid_ref[:, 0:1].astype(F32)
    wide = jnp.where(adapter_mask(aid, 768), nn(small, spread_ref[...]), 0.0).astype(BF)
    down = tn(wide[:, :512], hb_ref[...])
    store(
        0,
        jnp.concatenate([down[:128], down[128:256]], axis=1),
        jnp.concatenate([down[256:384], down[384:]], axis=1),
    )
    store(1, gqkv_ref[:, :512], jnp.concatenate([gqkv_ref[:, 512:], gdd_ref[...]], axis=1))
    store(2, gup1_ref[:, :512], gup1_ref[:, 512:])
    store(3, gd2_ref[:, :512], gd2_ref[:, 512:])
    wait_all(dy_s, sem)
    up = tn(wide[:, 512:], dy_s[...].reshape(1024, 256))
    left = jnp.concatenate([up[:128], up[128:]], axis=1)
    store(4, left, jnp.zeros_like(left))


def k5(scal, small, aid, hb, spread, gup1, gd2, gqkv, gdd, blocks):
    def const(shape):
        return pl.BlockSpec(shape, lambda t, s: (0,) * len(shape))

    return pl.pallas_call(
        k5_body,
        grid_spec=pltpu.PrefetchScalarGridSpec(
            num_scalar_prefetch=1,
            grid=(1,),
            in_specs=[
                const((8, 128, 128)),
                const((1024, 128)),
                pl.BlockSpec((1024, 256), lambda t, s: (0, s[9])),
                const((128, 768)),
                const((128, 1024)),
                const((128, 1024)),
                const((128, 768)),
                const((128, 256)),
            ]
            + [ANY] * 7,
            out_specs=[const((8, 80, 512)), const((8, 80, 512))],
            scratch_shapes=[pltpu.VMEM((4, 2, 128, 256), BF), pltpu.SemaphoreType.DMA],
        ),
        out_shape=[jax.ShapeDtypeStruct((8, 80, 512), F32), jax.ShapeDtypeStruct((8, 80, 512), BF)],
        compiler_params=PARAMS,
        cost_estimate=pl.CostEstimate(flops=1_500_000_000, bytes_accessed=6_000_000, transcendentals=0),
        name="adapter_grads",
    )(scal, small, aid, hb, spread, gup1, gd2, gqkv, gdd, *blocks)


def kf_body(scal_ref, mine_ref, theirs_ref, down_ref, up_ref, dd_ref, ud_ref, f1d_ref, f1u_ref, f2d_ref, f2u_ref):
    lane = lax.broadcasted_iota(jnp.int32, (16, 128), 1)

    core = scal_ref[8]

    def part(j, half, section, start, width):
        rows, cols = slice(16 * section, 16 * section + 16), slice(start, start + width)
        return jnp.where(core == half, mine_ref[j, rows, cols], theirs_ref[j, rows, cols]).astype(F32)

    for j in range(8):
        block = slice(256 * j, 256 * j + 256)
        down_ref[0, :, block] = part(j, 0, 0, 0, 256)
        down_ref[1, :, block] = part(j, 0, 0, 256, 256)
        down_ref[2, :, block] = part(j, 1, 0, 0, 256)
        f1d_ref[:, block] = part(j, 1, 0, 256, 256)
        ud_ref[:, block] = part(j, 0, 4, 0, 256)
        f2u_ref[:, block] = part(j, 0, 4, 256, 256)
        for w in range(8):
            spot = slice(1024 * w + 128 * j, 1024 * w + 128 * j + 128)
            f1u_ref[:, spot] = part(j, w // 4, 2, 128 * (w % 4), 128)
            f2d_ref[:, spot] = part(j, w // 4, 3, 128 * (w % 4), 128)
    for i in range(4):
        for x in range(2):
            for y in range(4):
                for h in range(2):
                    start = 256 * (i % 2) + 128 * (y // 2)
                    a = part(4 * x + 2 * h, i // 2, 1, start, 128)
                    b = part(4 * x + 2 * h + 1, i // 2, 1, start, 128)
                    if y % 2:
                        a = pltpu.roll(a, 64, 1)
                    else:
                        b = pltpu.roll(b, 64, 1)
                    value = jnp.where(lane < 64, a, b)
                    spot = slice(256 * (2 * y + x) + 128 * h, 256 * (2 * y + x) + 128 * h + 128)
                    if i < 3:
                        up_ref[i, :, spot] = value
                    else:
                        dd_ref[:, spot] = value


def kf(scal, mine, theirs):
    return pl.pallas_call(
        kf_body,
        in_specs=[SMEM, VM, VM],
        out_specs=[VM] * 8,
        out_shape=[
            jax.ShapeDtypeStruct((3, 16, 2048), F32),
            jax.ShapeDtypeStruct((3, 16, 2048), F32),
            jax.ShapeDtypeStruct((16, 2048), F32),
            jax.ShapeDtypeStruct((16, 2048), F32),
            jax.ShapeDtypeStruct((16, 2048), F32),
            jax.ShapeDtypeStruct((16, 8192), F32),
            jax.ShapeDtypeStruct((16, 8192), F32),
            jax.ShapeDtypeStruct((16, 2048), F32),
        ],
        compiler_params=PARAMS,
        name="finish",
    )(scal, mine, theirs)


def kn_body(x_ref, dy_ref, gain_ref, own_ref, up_ref, down_ref, side_ref, t_ref, up2_ref, down2_ref, out_ref):
    def total(*parts):
        return sum(p[...].astype(F32) for p in parts)

    dh = jnp.concatenate([total(own_ref, up_ref, down_ref, side_ref), total(t_ref, up2_ref, down2_ref)], axis=1)
    x = x_ref[...].astype(F32)
    center = x - jnp.mean(x, axis=1, keepdims=True)
    inv = lax.rsqrt(jnp.mean(center * center, axis=1, keepdims=True) + EPSILON)
    hn = center * inv
    e = dh * gain_ref[...]
    dx = (e - jnp.mean(e, axis=1, keepdims=True) - hn * jnp.mean(e * hn, axis=1, keepdims=True)) * inv
    out_ref[...] = (dy_ref[...].astype(F32) + dx).astype(BF)


def kn(*args):
    return pl.pallas_call(
        kn_body,
        in_specs=[VM] * 10,
        out_specs=VM,
        out_shape=jax.ShapeDtypeStruct((128, 2048), BF),
        compiler_params=PARAMS,
        name="norm_grad",
    )(*args)


def pack1_body(
    scal_ref, wq, wk, wv, wd, ad_ref, fd_ref, au_ref, dd_ref, du_ref, misc_ref, b1_ref,
    own_ref, other_ref, w_s, d_s, sem, d_sem,
):
    c, z = scal_ref[8], scal_ref[11]
    start_all([(w.at[pl.ds(128 * c, 128), :], w_s.at[i]) for i, w in enumerate((wq, wk, wv))], sem)
    start_all([(wd.at[pl.ds(64 * z + 32 * c, 32), :], d_s)], d_sem)
    first_core = c == 0
    odd = lax.rem(z, 2) == 1
    targets = ((own_ref, scal_ref[10]), (other_ref, 1 - scal_ref[10]))

    def head_pair(read, rows, i, xl):
        lane = lax.broadcasted_iota(jnp.int32, (rows, 128), 1)
        parts = []
        for k in range(2):
            start = (2 * (i + k) + xl) * 256 + (z // 2) * 128
            v = read(pl.ds(pl.multiple_of(start, 128), 128)).astype(F32)
            turned = pltpu.roll(v, 64, 1)
            parts.append(jnp.where(odd, turned, v) if k == 0 else jnp.where(odd, v, turned))
        return jnp.where(lane < 64, parts[0], parts[1]).astype(BF)

    half = pl.ds(pl.multiple_of((z // 2) * 128, 128), 128)
    row = lax.broadcasted_iota(jnp.int32, (16, 128), 0)
    lane = lax.broadcasted_iota(jnp.int32, (16, 128), 1)

    def biases(xl):
        plain = misc_ref[:, :128].astype(F32), misc_ref[:, 128:256].astype(F32)
        mine = misc_ref[:, half].astype(F32)
        turned = pltpu.roll(mine, 64, 1)
        low = jnp.where(odd, turned, mine)
        high = jnp.where(odd, mine, turned)
        query_key = jnp.where(lane[:1] < 64, low[4:5], high[5:6])
        value = jnp.where(lane[:1] < 64, low[6:7], 0.0)
        hidden = jnp.where(row[:8] == xl * 4 + z, b1_ref[...].astype(F32), 0.0)
        hidden = jnp.sum(hidden, axis=0, keepdims=True)
        left = jnp.where(row < 4, plain[0], jnp.where(row == 4, query_key, hidden))
        right = jnp.where(row < 4, plain[1], value)
        return left.astype(BF), right.astype(BF)

    a = jnp.where(first_core, ad_ref[0], ad_ref[2])
    b = jnp.where(first_core, ad_ref[1], fd_ref[...])
    du = jnp.where(first_core, du_ref[:, :1024], du_ref[:, 1024:])
    for out_ref, xl in targets:
        rows_of = biases(xl)
        for p in range(4):
            for i in (0, 2):
                read = (lambda s, p=p: au_ref[p, :, s]) if p < 3 else (lambda s: dd_ref[:, s])
                value = head_pair(read, 16, i, xl)
                rows = slice(16 * p, 16 * p + 16)
                if p == 0:
                    value = jnp.where(first_core, value, rows_of[i // 2])
                out_ref[rows, 768 + 64 * i : 768 + 64 * i + 128] = value
        out_ref[64:128, 768:] = jnp.zeros((64, 256), BF)
        out_ref[128:144] = a[:, :1024]
        out_ref[144:160] = a[:, 1024:]
        out_ref[160:176] = b[:, :1024]
        out_ref[176:192] = b[:, 1024:]
        out_ref[192:208] = du
    wait_all(d_s, d_sem)
    for out_ref, _ in targets:
        out_ref[208:240] = d_s[:, :1024]
        out_ref[240:272] = d_s[:, 1024:]
    wait_all(w_s, sem)
    for p in range(3):
        for i in (0, 2):
            start = 256 * p + 64 * i
            for out_ref, xl in targets:
                out_ref[:128, start : start + 128] = head_pair(lambda s, p=p: w_s[p, :, s], 128, i, xl)


def pack1(scal, wq, wk, wv, wd, ad, fd, au, dd, du, misc, b1):
    return pl.pallas_call(
        pack1_body,
        in_specs=[SMEM] + [ANY] * 4 + [VM] * 7,
        out_specs=[VM, VM],
        out_shape=[jax.ShapeDtypeStruct((272, 1024), BF)] * 2,
        scratch_shapes=[
            pltpu.VMEM((3, 128, 2048), BF),
            pltpu.VMEM((32, 2048), BF),
            pltpu.SemaphoreType.DMA,
            pltpu.SemaphoreType.DMA,
        ],
        compiler_params=PARAMS,
        cost_estimate=pl.CostEstimate(flops=1_000_000, bytes_accessed=4_000_000, transcendentals=0),
        name="pack_qkv",
    )(scal, wq, wk, wv, wd, ad, fd, au, dd, du, misc, b1)


def pack2_body(scal_ref, w1, w2, up_ref, down_ref, up2_ref, own_ref, other_ref, w1_s, w2_s, sem, sem2):
    c, z = scal_ref[8], scal_ref[11]
    places = [scal_ref[10] * 4 + z, (1 - scal_ref[10]) * 4 + z]
    start_all([(w1.at[pl.ds(128 * c, 128), :], w1_s)], sem)
    start_all([(w2.at[pl.ds(128 * places[i] + 64 * c, 64), :], w2_s.at[i]) for i in range(2)], sem2)
    first_core = c == 0
    up2 = jnp.where(first_core, up2_ref[:, :1024], up2_ref[:, 1024:])

    def column(w, i):
        return pl.ds(pl.multiple_of(1024 * w + 128 * places[i], 128), 128)

    for i, out_ref in enumerate((own_ref, other_ref)):
        out_ref[272:288] = up2
        for w in range(8):
            out_ref[128:144, 128 * w : 128 * w + 128] = jnp.where(
                first_core, up_ref[:, column(w, i)], down_ref[:, column(w, i)]
            )
    wait_all(w2_s, sem2)
    for i, out_ref in enumerate((own_ref, other_ref)):
        out_ref[144:208] = w2_s[i, :, :1024]
        out_ref[208:272] = w2_s[i, :, 1024:]
    wait_all(w1_s, sem)
    for i, out_ref in enumerate((own_ref, other_ref)):
        for w in range(8):
            out_ref[:128, 128 * w : 128 * w + 128] = w1_s[:, column(w, i)]


def pack2(scal, w1, w2, up, down, up2):
    return pl.pallas_call(
        pack2_body,
        in_specs=[SMEM, ANY, ANY, VM, VM, VM],
        out_specs=[VM, VM],
        out_shape=[jax.ShapeDtypeStruct((288, 1024), BF)] * 2,
        scratch_shapes=[
            pltpu.VMEM((128, 8192), BF),
            pltpu.VMEM((2, 64, 2048), BF),
            pltpu.SemaphoreType.DMA,
            pltpu.SemaphoreType.DMA,
        ],
        compiler_params=PARAMS,
        cost_estimate=pl.CostEstimate(flops=1_000_000, bytes_accessed=5_000_000, transcendentals=0),
        name="pack_hidden",
    )(scal, w1, w2, up, down, up2)


def rotary_tables(positions):
    lane = np.arange(128) % 64
    rate = np.where(lane < 32, 10000.0 ** (-2.0 * (lane % 16) / 32.0), 0.0).astype(np.float32)
    sign = np.where(lane < 16, -1.0, 1.0).astype(np.float32)
    angles = positions.astype(F32)[:, None] * jnp.asarray(rate)[None, :]
    return jnp.cos(angles), jnp.sin(angles) * jnp.asarray(sign)[None, :]


def fold_matrix():
    row = np.arange(768)
    target = (row // 128) * 16 + row % 16
    return jnp.asarray((target[:, None] == np.arange(128)[None, :]).astype(np.float32)).astype(BF)


def halves(a):
    m = a.shape[1] // 2
    return jnp.concatenate([a[:, :m], a[:, m:]], axis=0)


SWAP = [(0, 1), (1, 0)]
FLIP = [(i, 3 - i) for i in range(4)]
UP = [(i, (i + 1) % 4) for i in range(4)]
DOWN = [(i, (i + 3) % 4) for i in range(4)]
Z_OFFSETS = (0, -1, 1, 2)


def together(*values):
    return lax.optimization_barrier(values)


def up(a):
    return lax.ppermute(a, "z", UP)


def down(a):
    return lax.ppermute(a, "z", DOWN)


def across(a):
    return lax.ppermute(a, "xl", SWAP)


def gather_pair(own, other, single):
    xh = lax.axis_index("xh")
    parts = [jnp.where(xh == 0, own, other), jnp.where(xh == 0, other, own)]
    if single is not None:
        parts.append(single)
    packed = jnp.concatenate(parts, axis=0)
    g = lax.all_gather(packed, ("y", "c"), axis=0, tiled=False)
    return g.reshape((4, 2) + packed.shape)


def add(*terms):
    return sum(t.astype(F32) for t in terms)


def scatter_sum(near, owns, sides):
    own, side, down_own, down_side, up_own, up_side, far_own, far_side = [near[b] for b in range(8)]
    from_side = lax.ppermute(sides, "xl", SWAP)
    via_below = lax.ppermute(far_own, "z", UP)
    via_above = lax.ppermute(far_side, "z", DOWN)
    via_below, via_above, from_side = together(via_below, via_above, from_side)
    up_side = lax.ppermute(up_side, "z", UP)
    down_own = lax.ppermute(down_own, "z", DOWN)
    up_own = lax.ppermute(add(up_own, via_below).astype(BF), "z", UP)
    down_side = lax.ppermute(add(down_side, via_above).astype(BF), "z", DOWN)
    side = lax.ppermute(add(side, up_side, down_side).astype(BF), "xl", SWAP)
    t = add(owns, from_side)
    far = t[3].astype(BF)
    half_up = lax.ppermute(far[:64], "z", UP)
    half_down = lax.ppermute(far[64:], "z", DOWN)
    up = jnp.concatenate([t[2, :64] + half_up.astype(F32), t[2, 64:]], axis=0).astype(BF)
    down = jnp.concatenate([t[1, :64], t[1, 64:] + half_down.astype(F32)], axis=0).astype(BF)
    return own, up_own, down_own, side, t[0], lax.ppermute(up, "z", UP), lax.ppermute(down, "z", DOWN)


def local(
    inputs,
    output_cotangent,
    block_index_per_position,
    adapter_index_per_run,
    norm_gain,
    norm_bias,
    query_weight,
    key_weight,
    value_weight,
    dense_weight,
    query_bias,
    key_bias,
    value_bias,
    dense_bias,
    feedforward_in_weight,
    feedforward_in_bias,
    feedforward_out_weight,
    feedforward_out_bias,
    adapter_attention_down,
    adapter_attention_up,
    adapter_dense_down,
    adapter_dense_up,
    adapter_feedforward_in_down,
    adapter_feedforward_in_up,
    adapter_feedforward_out_down,
    adapter_feedforward_out_up,
):
    xl, z, c = lax.axis_index("xl"), lax.axis_index("z"), lax.axis_index("c")
    xh = lax.axis_index("xh")
    j = xl * 4 + z
    x_own = inputs[0]
    dy_own = output_cotangent[0]
    run_adapter = adapter_index_per_run[0, 0].astype(F32).astype(BF)
    block_row = block_index_per_position[0]
    z_of = [lax.rem(z + o + 4, 4) for o in Z_OFFSETS]
    spots = [(xl if side == 0 else 1 - xl) * 4 + zz for zz in z_of for side in range(2)]
    scal = jnp.stack(spots + [c, j, xl, z] + z_of).astype(jnp.int32)

    zero = jnp.zeros((256,), BF)
    misc_own = jnp.stack(
        [norm_gain, norm_bias, dense_bias, feedforward_out_bias, query_bias, key_bias, value_bias] + [zero] * 9
    )
    sent1, for_other = pack1(
        scal,
        query_weight,
        key_weight,
        value_weight,
        dense_weight,
        adapter_attention_down[0],
        adapter_feedforward_in_down[0],
        adapter_attention_up[0],
        adapter_dense_down[0],
        adapter_dense_up[0],
        misc_own,
        feedforward_in_bias.reshape(8, 128),
    )
    own2, own2_for_other = pack2(
        scal,
        feedforward_in_weight,
        feedforward_out_weight,
        adapter_feedforward_in_up[0],
        adapter_feedforward_out_down[0],
        adapter_feedforward_out_up[0],
    )
    spread = jnp.stack(spots)
    my_positions = ((spread * 2 + c) * 128)[:, None] + jnp.arange(128, dtype=jnp.int32)[None, :]
    tables = rotary_tables(my_positions.reshape(1024)) + rotary_tables(jnp.arange(2048, dtype=jnp.int32))
    tables = tables + (jnp.broadcast_to(block_row[:, None], (2048, 128)),)
    x_send = jnp.concatenate([x_own, jnp.full((128, 128), run_adapter, BF)], axis=1)

    x_up, x_down, x_side = together(up(x_send), down(x_send), across(x_send), for_other)[:3]
    other1 = lax.ppermute(for_other, ("xl", "xh"), FLIP)
    x_up_side, x_down_side, dy_side = together(up(x_side), down(x_side), across(together(dy_own, x_side)[0]))
    other1, own2, own2_for_other, x_up, x_down, dy_side = together(
        other1, own2, own2_for_other, x_up, x_down, dy_side, x_up_side, x_down_side
    )[:6]
    g1 = gather_pair(sent1[:MAIN], other1[:MAIN], jnp.where(xh == xl, sent1[MAIN:], other1[MAIN:]))
    dy_own = together(dy_own, dy_side)[0]
    x_far_a, x_far_b, dy_up, dy_down, other2, tables = together(
        up(x_up[:64]),
        down(x_down[64:]),
        up(dy_own),
        down(dy_own),
        lax.ppermute(own2_for_other, ("xl", "xh"), FLIP),
        tables,
    )
    g2 = gather_pair(own2, other2, None)
    x_far_side = across(jnp.concatenate([x_far_a, x_far_b], axis=0))
    dy_up_more, dy_down_more, x_far_side = together(
        up(jnp.concatenate([dy_side, dy_up[:64]], axis=0)),
        down(jnp.concatenate([dy_side, dy_down[64:]], axis=0)),
        x_far_side,
    )
    dy_far_side = across(jnp.concatenate([dy_up_more[128:], dy_down_more[128:]], axis=0))
    x_blocks = [x_send, x_side, x_up, x_down, x_up_side, x_down_side, x_far_a, x_far_b, x_far_side]
    dy_blocks = [dy_own, dy_side, dy_up, dy_down, dy_up_more, dy_down_more, dy_far_side]

    def side_of(core):
        return jnp.stack(
            [g1[:, core, MAIN * h : MAIN * h + 64, 768:] for h in range(2)], axis=1
        ).reshape(8, 64, 256)

    ups_all = side_of(0).reshape(8, 4, 16, 256).transpose(1, 0, 2, 3).reshape(4, 128, 256)
    ups = jnp.concatenate([ups_all[0], ups_all[1], ups_all[2]], axis=1)
    dd = ups_all[3]
    small_all = side_of(1)[:, :6].astype(F32)
    misc = small_all[:, :4].transpose(1, 0, 2).reshape(4, 2048)
    head_b = lax.dynamic_index_in_dim(small_all[:, 4, :192].reshape(4, 2, 3, 64), xl, 1, keepdims=False)
    bias_qkv = head_b.transpose(1, 0, 2).reshape(1, 768)
    b1 = small_all[:, 5, :128].reshape(1, 1024)

    cos_mine, sin_mine, cos_all, sin_all, idcol = tables

    hb, inner, qkv_keep, qkv_send, aid = k1(x_blocks, scal, g1, ups, misc[:2], bias_qkv, cos_mine, sin_mine)
    qkv_recv = lax.ppermute(qkv_send, "c", SWAP)
    dob_keep, dob_send, gdense = k1b(dy_blocks, scal, aid, g1, dd)
    dob_recv = lax.ppermute(dob_send, "c", SWAP)

    idrow = jnp.broadcast_to(block_row[None, :], (8, 2048))
    att_keep, att_send = k3(scal, qkv_keep, qkv_recv, dob_keep, dob_recv, idrow, idcol, cos_all, sin_all)
    att_recv = lax.ppermute(att_send, "c", SWAP)

    fold = fold_matrix()
    gb, df, low_out, low_in, small, gup1, gd2, gdd = k2m(
        dy_blocks, scal, hb, aid, inner, gdense, att_keep, att_recv, g2, ups, dd, b1, fold
    )
    small = lax.all_to_all(small.reshape(8, 128, 128), TP, 0, 0, tiled=True)
    out_part = k2o(scal, gb, att_keep, att_recv, low_out, g1, g2)
    out_part, small, df = together(out_part, small, df)
    small = jnp.sum(small.astype(F32), axis=0).astype(BF)
    small = lax.all_to_all(jnp.broadcast_to(small[None], (8, 128, 128)), TP, 0, 0, tiled=True)
    out_sum = lax.psum_scatter(out_part.reshape(1024, 2048), TP, scatter_dimension=0, tiled=True)
    near, owns, sides, gqkv = k2h(scal, df, att_keep, att_recv, low_in, inner, g1, g2)
    shares = scatter_sum(near, owns, sides)

    keep, send = k5(scal, small, aid, hb, fold.T, gup1, gd2, gqkv, gdd, dy_blocks)
    grads = (keep + lax.ppermute(send, "c", SWAP).astype(F32)).astype(BF)
    grads = lax.all_to_all(grads, WSH, 0, 0, tiled=True)
    grads = jnp.sum(grads.astype(F32), axis=0).astype(BF)
    grads = lax.all_to_all(jnp.broadcast_to(grads[None], (8, 80, 512)), TP, 0, 0, tiled=True)
    down_qkv, up_qkv, gdd, gud, gf1d, gf1u, gf2d, gf2u = kf(scal, grads, lax.ppermute(grads, "c", SWAP))

    source = x_own.astype(F32)
    outputs = (source + out_sum.astype(F32) + misc[2:3] + misc[3:4]).astype(BF)[None]
    *shares, outputs = together(*shares, outputs)
    grad_inputs = kn(x_own, output_cotangent[0], misc[0:1], *shares)[None]
    return (
        outputs,
        grad_inputs,
        down_qkv[None],
        up_qkv[None],
        gdd[None],
        gud[None],
        gf1d[None],
        gf1u[None],
        gf2d[None],
        gf2u[None],
    )


def solution(mesh):
    fine = Mesh(np.asarray(mesh.devices).reshape(2, 4, 2, 4, 2), ("xl", "z", "c", "y", "xh"))
    tokens = P(WSH, CTX, None)
    w1 = P(WSH)
    w2 = P(WSH, None)
    w3 = P(WSH, None, None)
    w4 = P(WSH, None, None, None)
    placed = (tokens, tokens, w2, P(WSH, CTX)) + (w1, w1, w2, w2, w2, w2, w1, w1, w1, w1, w2, w1, w2, w1)
    placed = placed + (w4, w4, w3, w3, w3, w3, w3, w3)
    return jax.shard_map(
        local,
        mesh=fine,
        in_specs=placed,
        out_specs=(tokens, tokens, w4, w4, w3, w3, w3, w3, w3, w3),
        check_vma=False,
    )
```
